32 devices in a mesh: seq: 16 (over z, y, x), head: 2 (over core).
Axes of the slice: x: 2, y: 2, z: 4, core: 2. Of those that a mesh axis runs over, the one named last changes fastest.
Arguments:
- queries: bfloat16 [17408, 512], P('seq', 'head'), may hold values from -50 to 50
- keys: bfloat16 [17408, 512], P('seq', 'head'), may hold values from -6 to 6
- values: bfloat16 [17408, 512], P('seq', 'head'), may hold values from -48 to 48
- rand_group: int32 [272, 3], replicated, may hold values from 0 to 15, all different within a row; in each aligned block of 17 rows (0 to 16, 17 to 33, ...) at most 4 rows name the same one
- rand_offset: int32 [272, 3], replicated, may hold values from 0 to 16
- glob_blocks: int32 [2], replicated, may hold values from 0 to 271
- w_out: bfloat16 [512, 4096], P(None, 'head'), may hold values from -0.25 to 0.25
Outputs:
- layer_out: bfloat16 [17408, 4096], P('seq', 'head')
The draws below stay inside these ranges and needn't reach their ends.
Inputs may be any that keep to these rules, and one draw needn't show every extreme that they name: `rand_group`: each row names 3 different groups. Among the 17 rows of one aligned block of 17 rows, no group is named more than 4 times, and in every draw some group is named exactly 4 times in some such block.
All inputs are finite; a program needn't handle non-finite values.
Results may differ from the reference program's by a relative error of at most 0.0056.
Values may be sent and summed in bfloat16 or wider, within the bound.
No kernel may reach another device: no remote copies, remote signals or barrier semaphores. Data moves between devices by JAX's collectives and lax.ppermute only.
A program may use at most 128 MiB of HBM per device.

```python
import math
import jax
import jax.numpy as jnp
import numpy as np
from jax import lax

D = 4096
DH = 128
BLOCK = 64
R = 3
G = 2
TOKENS = 17408
NB = 272
BPD = 17
CAP = 4
HEADS = 4
N_SEQ = 16


def draw_keys(key, part):
    result = jnp.clip(jax.random.normal(jax.random.fold_in(key, 11), (TOKENS, HEADS * DH), jnp.float32), -6.0, 6.0)
    return result.astype(jnp.bfloat16)


def draw_queries(key, part):
    result = jnp.clip(jax.random.normal(jax.random.fold_in(key, 23), (TOKENS, HEADS * DH), jnp.float32), -6.0, 6.0)
    return result.astype(jnp.bfloat16)


def with_ends(entries, key, smallest, largest):
    extent = entries.shape
    index_at = [jax.random.randint(jax.random.fold_in(key, axis), (), 0, extent[axis]) for axis in range(len(extent))]
    entries = entries.at[tuple(index_at)].set(smallest)
    longest = extent.index(max(extent))
    index_at[longest] = (index_at[longest] + 1) % extent[longest]
    return entries.at[tuple(index_at)].set(largest)


def block_levels(own_key, extent, pieces, low, high):
    factor_of, own = 1.0, jax.random.fold_in(own_key, 6)
    for position, shards_of in pieces:
        heights = jnp.exp(jax.random.uniform(jax.random.fold_in(own, position), (shards_of,), jnp.float32, low / len(pieces), high / len(pieces)))
        factor_of = factor_of * jnp.repeat(heights, extent[position] // shards_of).reshape([-1 if axis == position else 1 for axis in range(len(extent))])
    return factor_of


def deal_out(own_key, own, number, rows, amount, top, reach, lean):
    sequence = jax.random.permutation(own_key, amount)
    packed, common = shares(amount, rows * top, reach, lean, True), shares(amount, rows * top, reach, lean, False)
    places = jnp.arange(amount)

    def named(tallies, turn):
        used = int((tallies > 0).sum())
        fixed = max(1, used // 4)
        shifted = fixed + (places - fixed + turn * (used - fixed)) % max(1, amount - fixed)
        return jnp.zeros((amount,), jnp.int32).at[sequence[jnp.where(places < fixed, places, shifted)]].set(jnp.asarray(tallies, jnp.int32))

    tallies = jnp.where(number % 4 == 0, named(packed, number // 4), named(common, number - number // 4 - 1))
    mixed = jax.random.permutation(jax.random.fold_in(own, 3), amount)
    giver, receiver = mixed[0:amount // 2 * 2:2], mixed[1:amount // 2 * 2:2]
    slack = jnp.minimum(tallies[giver] - 1, reach - tallies[receiver]) // 2
    slack = jnp.where((giver == sequence[0]) | (receiver == sequence[0]) | (tallies[receiver] == 0), 0, jnp.maximum(slack, 0))
    shifted = jax.random.randint(jax.random.fold_in(own, 4), (amount // 2,), 0, 1 << 20) % (slack + 1)
    tallies = tallies.at[giver].add(-shifted).at[receiver].add(shifted)
    labels = jnp.searchsorted(jnp.cumsum(tallies), jnp.arange(rows * top), side="right").astype(jnp.int32)
    grid = labels.reshape(top, rows).T
    grid = grid[jax.random.permutation(jax.random.fold_in(own, 1), rows)]
    turn = jax.random.randint(jax.random.fold_in(own, 2), (rows, 1), 0, top)
    return jnp.take_along_axis(grid, (jnp.arange(top)[None, :] + turn) % top, axis=1)


def shares(number_of, total, limit, skew, full):
    weights = [(1 << 20) // math.isqrt(grade ** skew) + 1 for grade in range(1, number_of + 1)]
    largest = limit if full else min(limit, max(-(-total // number_of), total * weights[0] // sum(weights)))
    least = 1 if total - largest >= number_of - 1 else 0
    holding, spare = [largest] + [least] * (number_of - 1), total - largest - least * (number_of - 1)
    while spare > 0:
        free = [i for i in range(1, number_of) if holding[i] < largest] or [i for i in range(1, number_of) if holding[i] < limit]
        whole, left = sum([weights[i] for i in free]), spare
        for i in free:
            extra = min(limit - holding[i], max(1, left * weights[i] // whole), spare)
            holding[i] = holding[i] + extra
            spare = spare - extra
    return np.array(holding)


def noise(stream_key, shape, deviation, limit, pieces=(), kind=jnp.bfloat16):
    values = jax.random.normal(stream_key, shape, jnp.float32) * deviation
    if len(pieces) > 0:
        values = block_levels(stream_key, shape, pieces, -0.22, 0.18) * values
    return jnp.clip(values, min=-limit, max=limit).astype(kind)


def setup_inputs(seed: int = 0) -> dict:
    seeds = jax.random.split(jax.random.key(seed), 8)
    queries = draw_queries(jax.random.fold_in(seeds[7], 71), 0)
    keys = draw_keys(jax.random.fold_in(seeds[7], 71), 0)
    values = noise(seeds[2], (TOKENS, HEADS * DH), 8.0, 48.0, ((0, 16), (1, 2)))
    rand_group_keys = jax.random.split(jax.random.fold_in(seeds[3], 1), NB // BPD)
    rand_group_turns = jax.random.permutation(jax.random.fold_in(seeds[3], 3), NB // BPD)
    rand_group = jax.vmap(lambda own, number: deal_out(jax.random.fold_in(seeds[3], 2), own, number, BPD, N_SEQ, R, CAP, 2))(rand_group_keys, rand_group_turns).reshape((NB, R))
    rand_offset = with_ends(jax.random.randint(seeds[4], (NB, R), 0, BPD), jax.random.fold_in(seeds[4], 1), 0, BPD - 1).astype(jnp.int32)
    glob_blocks = jax.random.randint(seeds[5], (G,), 0, NB).astype(jnp.int32)
    w_out = noise(seeds[6], (HEADS * DH, D), (HEADS * DH) ** -0.5, 0.25, ((1, 2),))
    return {"queries": queries, "keys": keys, "values": values, "rand_group": rand_group, "rand_offset": rand_offset, "glob_blocks": glob_blocks, "w_out": w_out}


def attend_blocks(query_rows, key_rows, value_rows):
    score_scale = 1.0 / math.sqrt(DH)
    scores = jnp.einsum('nqhd,nkhd->nhqk', query_rows.astype(jnp.float32), key_rows.astype(jnp.float32)) * score_scale
    row_max = lax.optimization_barrier(jnp.max(scores, axis=-1, keepdims=True))
    weights = jnp.exp(scores - row_max)
    row_total = lax.optimization_barrier(jnp.sum(weights, axis=-1))
    probs = lax.optimization_barrier(weights.astype(jnp.bfloat16))
    weighted = jnp.einsum('nhqk,nkhd->nqhd', probs.astype(jnp.float32), value_rows.astype(jnp.float32))
    return (weighted / jnp.transpose(row_total, (0, 2, 1))[..., None]).astype(jnp.bfloat16)

def reference(queries, keys, values, rand_group, rand_offset, glob_blocks, w_out):
    columns = HEADS * DH
    block_count = TOKENS // BLOCK
    pair_blocks = jnp.concatenate([keys, values], axis=1).reshape(block_count, BLOCK, 2 * columns)
    query_blocks = queries.reshape(block_count, BLOCK, HEADS, DH)
    block_index = jnp.arange(block_count, dtype=jnp.int32)
    window_ids = jnp.stack([(block_index - 1) % block_count, block_index, (block_index + 1) % block_count], axis=1)
    global_ids = jnp.broadcast_to(glob_blocks[None, :].astype(jnp.int32), (block_count, G))
    random_ids = (rand_group * BPD + rand_offset).astype(jnp.int32)
    key_ids = jnp.concatenate([window_ids, global_ids, random_ids], axis=1).astype(jnp.int32)
    group_count = block_count // BPD

    def one_group(group_index):
        first_block = (group_index * BPD).astype(jnp.int32)
        chosen_ids = lax.dynamic_slice_in_dim(key_ids, first_block, BPD, 0)
        gathered = jnp.take(pair_blocks, chosen_ids.reshape(-1), axis=0).reshape(BPD, -1, 2 * columns)
        key_rows = gathered[..., :columns].reshape(BPD, -1, HEADS, DH)
        value_rows = gathered[..., columns:].reshape(BPD, -1, HEADS, DH)
        query_rows = lax.dynamic_slice_in_dim(query_blocks, first_block, BPD, 0)
        return attend_blocks(query_rows, key_rows, value_rows)
    context = lax.map(one_group, jnp.arange(group_count, dtype=jnp.int32)).reshape(TOKENS, columns)
    return jnp.dot(context, w_out, preferred_element_type=jnp.float32).astype(jnp.bfloat16)
```

```python
import functools
import math

import jax
import jax.numpy as jnp
from jax import lax
from jax.experimental import pallas as pl
from jax.experimental.pallas import tpu as pltpu
from jax.sharding import PartitionSpec as P

DH = 128
BLOCK = 64
R = 3
G = 2
VMEM = pltpu.MemorySpace.VMEM
SMEM = pltpu.MemorySpace.SMEM
BF16 = jnp.bfloat16
F32 = jnp.float32
I32 = jnp.int32


def params(mib):
    return pltpu.CompilerParams(vmem_limit_bytes=mib * 1024 * 1024)


def cost(flops, size):
    return pl.CostEstimate(flops=int(flops), bytes_accessed=int(size), transcendentals=0)


def spec(space=VMEM):
    return pl.BlockSpec(memory_space=space)


def rank_kernel(n, per, cap, g_ref, o_ref, spot_ref, arrive_ref, g_pad, o_pad):
    me = lax.axis_index("seq")
    nb = g_ref.shape[1]
    wide = g_pad.shape[1]
    g_pad[...] = jnp.full(g_pad.shape, -1, I32)
    o_pad[...] = jnp.zeros(o_pad.shape, I32)
    g_pad[:R, :nb] = g_ref[...]
    o_pad[:R, :nb] = o_ref[...]
    g = g_pad[...]
    lane = lax.broadcasted_iota(I32, g.shape, 1)
    place = lane
    for d in range(1, n):
        place = jnp.where(lane >= d * per, lane - d * per, place)
    rank = jnp.zeros(g.shape, I32)
    for s in range(1, per):
        back = pltpu.roll(g, s, axis=1)
        ahead = place >= s
        for r in range(R):
            same = jnp.broadcast_to(back[r : r + 1, :], g.shape) == g
            rank = rank + jnp.where(ahead & same, 1, 0)
    arrive_ref[...] = g * cap + rank
    named = jnp.where(g == me, o_pad[...], 0)
    row = lax.broadcasted_iota(I32, (8, wide), 0)
    spots = jnp.zeros((8, wide), F32)
    for s in range(cap):
        picked = jnp.where(rank == s, named, 0).astype(F32)
        total = jnp.sum(picked, axis=0, keepdims=True)
        spots = spots + jnp.where(row == s, jnp.broadcast_to(total, (8, wide)), 0.0)
    token = lax.broadcasted_iota(I32, (wide, 128), 0)
    first = lax.broadcasted_iota(I32, (wide, 128), 1) * per
    belongs = jnp.where((token >= first) & (token < first + per), 1.0, 0.0)
    spot_ref[...] = jnp.dot(
        spots.astype(BF16), belongs.astype(BF16), preferred_element_type=F32
    ).astype(I32)


def ranks(n, per, cap, groups, offsets):
    nb = groups.shape[1]
    wide = -(-nb // 128) * 128
    return pl.pallas_call(
        functools.partial(rank_kernel, n, per, cap),
        out_shape=(
            jax.ShapeDtypeStruct((8, 128), I32),
            jax.ShapeDtypeStruct((8, wide), I32),
        ),
        in_specs=[spec(), spec()],
        out_specs=(spec(), spec()),
        scratch_shapes=[pltpu.VMEM((8, wide), I32), pltpu.VMEM((8, wide), I32)],
        compiler_params=params(16),
        name="ranks",
    )(groups, offsets)


def gather_kernel(n, cap, spot_ref, rows_ref, out_ref, sem):
    def one(d, carry):
        for s in range(cap):
            start = pl.multiple_of(spot_ref[s, d] * BLOCK, BLOCK)
            slot = pl.multiple_of((d * cap + s) * BLOCK, BLOCK)
            pltpu.make_async_copy(
                rows_ref.at[pl.ds(start, BLOCK)], out_ref.at[pl.ds(slot, BLOCK)], sem
            ).start()
        return carry

    lax.fori_loop(0, n, one, 0)
    pltpu.make_async_copy(out_ref, out_ref, sem).wait()


def gather(n, cap, spots, rows):
    columns = rows.shape[1]
    return pl.pallas_call(
        functools.partial(gather_kernel, n, cap),
        out_shape=jax.ShapeDtypeStruct((n * cap * BLOCK, columns), BF16),
        in_specs=[spec(SMEM), spec()],
        out_specs=spec(pl.ANY),
        scratch_shapes=[pltpu.SemaphoreType.DMA],
        compiler_params=params(16),
        cost_estimate=cost(0, 2 * n * cap * BLOCK * columns * 2),
        name="gather_blocks",
    )(spots, rows)


def fetch_blocks(per, arrive_ref, source_ref, held, sems):
    me = lax.axis_index("seq")

    def one(i, carry):
        for r in range(R):
            start = pl.multiple_of(arrive_ref[r, me * per + i] * BLOCK, BLOCK)
            slot = pl.multiple_of((i * R + r) * BLOCK, BLOCK)
            pltpu.make_async_copy(
                source_ref.at[pl.ds(start, BLOCK)], held.at[pl.ds(slot, BLOCK)], sems.at[i]
            ).start()
        return carry

    lax.fori_loop(0, per, one, 0)


def wait_blocks(i, held, sems):
    part = held.at[pl.ds(pl.multiple_of(i * R * BLOCK, BLOCK), R * BLOCK)]
    pltpu.make_async_copy(part, part, sems.at[i]).wait()


def dot_t(a, b):
    return lax.dot_general(a, b, (((1,), (1,)), ((), ())), preferred_element_type=F32)


def scores_kernel(
    per, heads, arrive_ref, q_ref, k_ref, v_ref, before_ref, after_ref, glob_ref, rand_ref,
    prob_ref, part_ref, total_ref, keys, vals, held, sems,
):
    fetch_blocks(per, arrive_ref, rand_ref, held, sems)
    rows = per * BLOCK
    keys[:BLOCK] = before_ref[:BLOCK]
    vals[:BLOCK] = before_ref[BLOCK:]
    keys[pl.ds(BLOCK, rows)] = k_ref[...]
    vals[pl.ds(BLOCK, rows)] = v_ref[...]
    keys[pl.ds(BLOCK + rows, BLOCK)] = after_ref[:BLOCK]
    vals[pl.ds(BLOCK + rows, BLOCK)] = after_ref[BLOCK:]
    scale = 1.0 / math.sqrt(DH)

    def one(i, carry):
        wait_blocks(i, held, sems)
        at = pl.ds(pl.multiple_of(i * BLOCK, BLOCK), BLOCK)
        window = pl.ds(pl.multiple_of(i * BLOCK, BLOCK), 3 * BLOCK)
        chosen = pl.ds(pl.multiple_of(i * R * BLOCK, BLOCK), R * BLOCK)
        for h in range(heads):
            cols = pl.ds(h * DH, DH)
            q = q_ref[at, cols]
            s_w = dot_t(q, keys[window, cols]) * scale
            s_g = dot_t(q, glob_ref[: G * BLOCK, cols]) * scale
            s_r = dot_t(q, held[chosen, cols]) * scale
            top = jnp.maximum(
                jnp.max(s_g, axis=1, keepdims=True),
                jnp.maximum(
                    jnp.max(s_w, axis=1, keepdims=True), jnp.max(s_r, axis=1, keepdims=True)
                ),
            )
            w_w, w_g, w_r = jnp.exp(s_w - top), jnp.exp(s_g - top), jnp.exp(s_r - top)
            total = (
                jnp.sum(w_w, axis=1, keepdims=True)
                + jnp.sum(w_g, axis=1, keepdims=True)
                + jnp.sum(w_r, axis=1, keepdims=True)
            )
            part = jnp.dot(w_w.astype(BF16), vals[window, cols], preferred_element_type=F32)
            part = part + jnp.dot(
                w_g.astype(BF16), glob_ref[G * BLOCK :, cols], preferred_element_type=F32
            )
            prob_ref[at, pl.ds(h * 256, R * BLOCK)] = w_r.astype(BF16)
            part_ref[at, cols] = part
            total_ref[at, cols] = jnp.broadcast_to(total, (BLOCK, DH))
        return carry

    lax.fori_loop(0, per, one, 0)


def scores(per, arrive, q, k, v, before, after, glob, rand):
    rows, columns = q.shape
    heads = columns // DH
    return pl.pallas_call(
        functools.partial(scores_kernel, per, heads),
        out_shape=(
            jax.ShapeDtypeStruct((rows, heads * 256), BF16),
            jax.ShapeDtypeStruct((rows, columns), F32),
            jax.ShapeDtypeStruct((rows, columns), F32),
        ),
        in_specs=[spec(SMEM)] + [spec()] * 6 + [spec(pl.ANY)],
        out_specs=(spec(), spec(), spec()),
        scratch_shapes=[
            pltpu.VMEM((rows + 2 * BLOCK, columns), BF16),
            pltpu.VMEM((rows + 2 * BLOCK, columns), BF16),
            pltpu.VMEM((rows * R, columns), BF16),
            pltpu.SemaphoreType.DMA((per,)),
        ],
        compiler_params=params(32),
        cost_estimate=cost(rows * 13 * BLOCK * columns * 2, rows * columns * 30),
        name="scores",
    )(arrive, q, k, v, before, after, glob, rand)


def context_kernel(
    per, heads, arrive_ref, prob_ref, part_ref, total_ref, rand_ref, out_ref, held, sems
):
    fetch_blocks(per, arrive_ref, rand_ref, held, sems)

    def one(i, carry):
        wait_blocks(i, held, sems)
        at = pl.ds(pl.multiple_of(i * BLOCK, BLOCK), BLOCK)
        chosen = pl.ds(pl.multiple_of(i * R * BLOCK, BLOCK), R * BLOCK)
        for h in range(heads):
            cols = pl.ds(h * DH, DH)
            weighted = part_ref[at, cols] + jnp.dot(
                prob_ref[at, pl.ds(h * 256, R * BLOCK)],
                held[chosen, cols],
                preferred_element_type=F32,
            )
            out_ref[at, cols] = (weighted / total_ref[at, cols]).astype(BF16)
        return carry

    lax.fori_loop(0, per, one, 0)


def contexts(per, arrive, prob, part, total, rand):
    rows, columns = part.shape
    heads = columns // DH
    return pl.pallas_call(
        functools.partial(context_kernel, per, heads),
        out_shape=jax.ShapeDtypeStruct((rows, columns), BF16),
        in_specs=[spec(SMEM)] + [spec()] * 3 + [spec(pl.ANY)],
        out_specs=spec(),
        scratch_shapes=[
            pltpu.VMEM((rows * R, columns), BF16),
            pltpu.SemaphoreType.DMA((per,)),
        ],
        compiler_params=params(32),
        cost_estimate=cost(rows * 3 * BLOCK * columns * 2, rows * columns * 18),
        name="contexts",
    )(arrive, prob, part, total, rand)


def project_kernel(own_ref, other_refs, w_ref, out_ref):
    me = lax.axis_index("head")
    count = lax.axis_size("head")
    columns = own_ref.shape[1]
    total = None
    for step, rows_ref in enumerate([own_ref] + list(other_refs)):
        owner = lax.rem(me + step, count)
        at = pl.ds(pl.multiple_of(owner * columns, columns), columns)
        term = jnp.dot(rows_ref[...], w_ref[at, :], preferred_element_type=F32)
        total = term if total is None else total + term
    out_ref[...] = total.astype(BF16)


def project(own, others, w_out):
    rows, columns = own.shape
    wide = w_out.shape[1]
    tile = rows // 4
    block = pl.BlockSpec((tile, columns), lambda i: (i, 0))

    def kernel(own_ref, *refs):
        project_kernel(own_ref, refs[: len(others)], refs[-2], refs[-1])

    return pl.pallas_call(
        kernel,
        grid=(4,),
        out_shape=jax.ShapeDtypeStruct((rows, wide), BF16),
        in_specs=[block] * (1 + len(others)) + [spec()],
        out_specs=pl.BlockSpec((tile, wide), lambda i: (i, 0)),
        compiler_params=params(48),
        cost_estimate=cost(
            2 * rows * w_out.shape[0] * wide, rows * wide * 2 + w_out.size * 2 + rows * columns * 4
        ),
        name="project",
    )(own, *others, w_out)


def spread(rows, owners, my_index, seq_count):
    shape = rows.shape
    bit = 0
    while (1 << bit) < seq_count:
        pairs = [(i, i ^ (1 << bit)) for i in range(seq_count)]
        got = lax.ppermute(rows, "seq", pairs)
        have = ((owners ^ my_index) >> bit) == 0
        rows = jnp.where(have[None, :, None, None], rows.reshape(2, G, BLOCK, -1),
                         got.reshape(2, G, BLOCK, -1)).reshape(shape)
        bit += 1
    return rows


def on_device(queries, keys, values, rand_group, rand_offset, glob_blocks, w_out):
    tokens_dev, columns = queries.shape
    per = tokens_dev // BLOCK
    n = lax.axis_size("seq")
    heads = lax.axis_size("head")
    me = lax.axis_index("seq")
    cap = max(2, (rand_group.shape[0] // n * R + n - 1) // n)

    up = [(i, (i + 1) % n) for i in range(n)]
    down = [(j, i) for i, j in up]
    last = jnp.concatenate([keys[-BLOCK:], values[-BLOCK:]], axis=0)
    first = jnp.concatenate([keys[:BLOCK], values[:BLOCK]], axis=0)
    before = lax.ppermute(last, "seq", up)
    after = lax.ppermute(first, "seq", down)

    owners = glob_blocks // per
    starts = (glob_blocks % per) * BLOCK
    held = [
        lax.dynamic_slice(rows, (starts[g], 0), (BLOCK, columns))
        for rows in (keys, values)
        for g in range(G)
    ]
    glob = spread(jnp.concatenate(held, axis=0), owners, me, n)

    spots, arrive = ranks(n, per, cap, rand_group.T, rand_offset.T)
    out_k = gather(n, cap, spots, keys)
    out_k, glob, before, after = lax.optimization_barrier((out_k, glob, before, after))
    rand_k = lax.all_to_all(
        out_k.reshape(n, cap * BLOCK, columns), "seq", split_axis=0, concat_axis=0, tiled=True
    ).reshape(n * cap * BLOCK, columns)
    out_v = gather(n, cap, spots, values)
    rand_v = lax.all_to_all(
        out_v.reshape(n, cap * BLOCK, columns), "seq", split_axis=0, concat_axis=0, tiled=True
    ).reshape(n * cap * BLOCK, columns)
    prob, part, total = scores(
        per, arrive, queries, keys, values, before, after, glob, rand_k
    )
    context = contexts(per, arrive, prob, part, total, rand_v)
    others = [
        lax.ppermute(context, "head", [((i + s) % heads, i) for i in range(heads)])
        for s in range(1, heads)
    ]
    return project(context, others, w_out)


def solution(mesh):
    return jax.shard_map(
        on_device,
        mesh=mesh,
        in_specs=(
            P("seq", "head"),
            P("seq", "head"),
            P("seq", "head"),
            P(),
            P(),
            P(),
            P(None, "head"),
        ),
        out_specs=P("seq", "head"),
        check_vma=False,
    )
```

```python
import functools
import math

import jax
import jax.numpy as jnp
from jax import lax
from jax.experimental import pallas as pl
from jax.experimental.pallas import tpu as pltpu
from jax.sharding import PartitionSpec as P

DH = 128
BLOCK = 64
R = 3
G = 2
VMEM = pltpu.MemorySpace.VMEM
SMEM = pltpu.MemorySpace.SMEM
BF16 = jnp.bfloat16
F32 = jnp.float32
I32 = jnp.int32


def params(mib):
    return pltpu.CompilerParams(vmem_limit_bytes=mib * 1024 * 1024)


def cost(flops, size):
    return pl.CostEstimate(flops=int(flops), bytes_accessed=int(size), transcendentals=0)


def spec(space=VMEM):
    return pl.BlockSpec(memory_space=space)


def rank_kernel(n, per, cap, g_ref, o_ref, spot_ref, arrive_ref, g_pad, o_pad):
    me = lax.axis_index("seq")
    nb = g_ref.shape[1]
    wide = g_pad.shape[1]
    tall = spot_ref.shape[0]
    g_pad[...] = jnp.full(g_pad.shape, -1, I32)
    o_pad[...] = jnp.zeros(o_pad.shape, I32)
    g_pad[:R, :nb] = g_ref[...]
    o_pad[:R, :nb] = o_ref[...]
    g = g_pad[...]
    lane = lax.broadcasted_iota(I32, g.shape, 1)
    place = lane
    for d in range(1, n):
        place = jnp.where(lane >= d * per, lane - d * per, place)
    rank = jnp.zeros(g.shape, I32)
    for s in range(1, per):
        back = pltpu.roll(g, s, axis=1)
        ahead = place >= s
        for r in range(R):
            same = jnp.broadcast_to(back[r : r + 1, :], g.shape) == g
            rank = rank + jnp.where(ahead & same, 1, 0)
    arrive_ref[...] = g * cap + rank
    row = lax.broadcasted_iota(I32, (tall, wide), 0)
    spots = jnp.zeros((tall, wide), F32)
    for side in range(2):
        group = lax.rem(me + side * (n // 2), n)
        named = jnp.where(g == group, o_pad[...], 0)
        for s in range(cap):
            picked = jnp.where(rank == s, named, 0).astype(F32)
            total = jnp.sum(picked, axis=0, keepdims=True)
            here = row == side * cap + s
            spots = spots + jnp.where(here, jnp.broadcast_to(total, (tall, wide)), 0.0)
    token = lax.broadcasted_iota(I32, (wide, 128), 0)
    first = lax.broadcasted_iota(I32, (wide, 128), 1) * per
    belongs = jnp.where((token >= first) & (token < first + per), 1.0, 0.0)
    spot_ref[...] = jnp.dot(
        spots.astype(BF16), belongs.astype(BF16), preferred_element_type=F32
    ).astype(I32)


def ranks(n, per, cap, groups, offsets):
    nb = groups.shape[1]
    wide = -(-nb // 128) * 128
    tall = -(-2 * cap // 8) * 8
    return pl.pallas_call(
        functools.partial(rank_kernel, n, per, cap),
        out_shape=(
            jax.ShapeDtypeStruct((tall, 128), I32),
            jax.ShapeDtypeStruct((8, wide), I32),
        ),
        in_specs=[spec(), spec()],
        out_specs=(spec(), spec()),
        scratch_shapes=[pltpu.VMEM((8, wide), I32), pltpu.VMEM((8, wide), I32)],
        compiler_params=params(4),
        name="ranks",
    )(groups, offsets)


def gather_kernel(n, cap, row, count, spot_ref, *refs):
    sources, out_ref, held, sem = refs[:count], refs[count], refs[count + 1], refs[count + 2]
    half = n // 2
    base = jnp.where(lax.axis_index("seq") >= half, half, 0)
    size = count * cap * BLOCK

    def one(j, carry):
        for c, source in enumerate(sources):
            for s in range(cap):
                start = pl.multiple_of(spot_ref[row + s, base + j] * BLOCK, BLOCK)
                slot = pl.multiple_of(j * size + (c * cap + s) * BLOCK, BLOCK)
                held[pl.ds(slot, BLOCK)] = source[pl.ds(start, BLOCK)]
        part = pl.ds(pl.multiple_of(j * size, size), size)
        pltpu.make_async_copy(held.at[part], out_ref.at[part], sem).start()
        return carry

    lax.fori_loop(0, half, one, 0)
    pltpu.make_async_copy(held, out_ref, sem).wait()


def gather(n, cap, row, spots, *sources):
    columns = sources[0].shape[1]
    count = len(sources)
    rows = n // 2 * cap * BLOCK * count
    return pl.pallas_call(
        functools.partial(gather_kernel, n, cap, row, count),
        out_shape=jax.ShapeDtypeStruct((rows, columns), BF16),
        in_specs=[spec(SMEM)] + [spec()] * count,
        out_specs=spec(pltpu.MemorySpace.HBM),
        scratch_shapes=[pltpu.VMEM((rows, columns), BF16), pltpu.SemaphoreType.DMA],
        compiler_params=params(8),
        cost_estimate=cost(0, 2 * rows * columns * 2),
        name="gather_blocks",
    )(spots, *sources)


def half_all_to_all(rows, n, size):
    groups = [list(range(n // 2)), list(range(n // 2, n))]
    columns = rows.shape[1]
    return lax.all_to_all(
        rows.reshape(n // 2, size, columns), "seq", 0, 0, axis_index_groups=groups, tiled=True
    )


def pack_kernel(per, glob_ref, k_ref, v_ref, first_ref, last_ref, cand_ref):
    rows = per * BLOCK
    for c, source in enumerate((k_ref, v_ref)):
        at = pl.ds(c * BLOCK, BLOCK)
        first_ref[at] = source[:BLOCK]
        last_ref[at] = source[rows - BLOCK :]
        for g in range(G):
            start = pl.multiple_of(lax.rem(glob_ref[g], per) * BLOCK, BLOCK)
            cand_ref[pl.ds((c * G + g) * BLOCK, BLOCK)] = source[pl.ds(start, BLOCK)]


def pack(per, glob, k, v):
    columns = k.shape[1]
    edge = jax.ShapeDtypeStruct((2 * BLOCK, columns), BF16)
    return pl.pallas_call(
        functools.partial(pack_kernel, per),
        out_shape=(edge, edge, jax.ShapeDtypeStruct((2 * G * BLOCK, columns), BF16)),
        in_specs=[spec(SMEM), spec(), spec()],
        out_specs=(spec(), spec(), spec()),
        compiler_params=params(4),
        name="pack",
    )(glob, k, v)


def merge_kernel(per, known, glob_ref, own_ref, got_ref, out_ref):
    me = lax.axis_index("seq")
    for g in range(G):
        differ = lax.bitwise_xor(me, lax.div(glob_ref[g], per))
        have = lax.bitwise_and(differ, jnp.int32(~known)) == 0
        for c in range(2):
            at = pl.ds((c * G + g) * BLOCK, BLOCK)
            out_ref[at] = jnp.where(have, own_ref[at], got_ref[at])


def spread(rows, glob, per, n):
    known = 0
    for bit in reversed(range(n.bit_length() - 1)):
        pairs = [(i, i ^ (1 << bit)) for i in range(n)]
        got = lax.ppermute(rows, "seq", pairs)
        rows = pl.pallas_call(
            functools.partial(merge_kernel, per, known),
            out_shape=jax.ShapeDtypeStruct(rows.shape, BF16),
            in_specs=[spec(SMEM), spec(), spec()],
            out_specs=spec(),
            compiler_params=params(4),
            name="merge",
        )(glob, rows, got)
        known |= 1 << bit
    return rows


def answer(n, cap, arrive_ref, i, r, own_ref, skip, other_ref):
    half = n // 2
    me = lax.axis_index("seq")
    spot = arrive_ref[r, i]
    group = lax.div(spot, cap)
    slot = spot - group * cap
    own_side = (group >= half) == (me >= half)
    place = jnp.where(group >= half, group - half, group)
    at = pl.ds(pl.multiple_of(slot * BLOCK, BLOCK), BLOCK)
    at_own = pl.ds(pl.multiple_of(skip + slot * BLOCK, BLOCK), BLOCK)
    return jnp.where(own_side, own_ref[place, at_own, :], other_ref[place, at, :])


def dot_t(a, b):
    return lax.dot_general(a, b, (((1,), (1,)), ((), ())), preferred_element_type=F32)


def scores_kernel(
    n, cap, per, heads, arrive_ref, q_ref, k_ref, v_ref, before_ref, after_ref, glob_ref,
    own_ref, other_ref, prob_ref, part_ref, total_ref, keys, vals, chosen,
):
    me = lax.axis_index("seq")
    rows = per * BLOCK
    keys[:BLOCK] = before_ref[:BLOCK]
    vals[:BLOCK] = before_ref[BLOCK:]
    keys[pl.ds(BLOCK, rows)] = k_ref[...]
    vals[pl.ds(BLOCK, rows)] = v_ref[...]
    keys[pl.ds(BLOCK + rows, BLOCK)] = after_ref[:BLOCK]
    vals[pl.ds(BLOCK + rows, BLOCK)] = after_ref[BLOCK:]
    scale = 1.0 / math.sqrt(DH)
    for i in range(per):
        at = pl.ds(i * BLOCK, BLOCK)
        window = pl.ds(i * BLOCK, 3 * BLOCK)
        picked = pl.ds(i * R * BLOCK, R * BLOCK)
        for r in range(R):
            chosen[pl.ds((i * R + r) * BLOCK, BLOCK)] = answer(
                n, cap, arrive_ref, me * per + i, r, own_ref, 0, other_ref
            )
        for h in range(heads):
            cols = pl.ds(h * DH, DH)
            q = q_ref[at, cols]
            s_w = dot_t(q, keys[window, cols]) * scale
            s_g = dot_t(q, glob_ref[: G * BLOCK, cols]) * scale
            s_r = dot_t(q, chosen[picked, cols]) * scale
            top = jnp.maximum(
                jnp.max(s_g, axis=1, keepdims=True),
                jnp.maximum(
                    jnp.max(s_w, axis=1, keepdims=True), jnp.max(s_r, axis=1, keepdims=True)
                ),
            )
            w_w, w_g, w_r = jnp.exp(s_w - top), jnp.exp(s_g - top), jnp.exp(s_r - top)
            total = (
                jnp.sum(w_w, axis=1, keepdims=True)
                + jnp.sum(w_g, axis=1, keepdims=True)
                + jnp.sum(w_r, axis=1, keepdims=True)
            )
            part = jnp.dot(w_w.astype(BF16), vals[window, cols], preferred_element_type=F32)
            part = part + jnp.dot(
                w_g.astype(BF16), glob_ref[G * BLOCK :, cols], preferred_element_type=F32
            )
            prob_ref[at, pl.ds(h * 256, R * BLOCK)] = w_r.astype(BF16)
            part_ref[at, cols] = part
            total_ref[at, cols] = jnp.broadcast_to(total, (BLOCK, DH))


def scores(n, cap, per, arrive, q, k, v, before, after, glob, own, other):
    rows, columns = q.shape
    heads = columns // DH
    return pl.pallas_call(
        functools.partial(scores_kernel, n, cap, per, heads),
        out_shape=(
            jax.ShapeDtypeStruct((rows, heads * 256), BF16),
            jax.ShapeDtypeStruct((rows, columns), F32),
            jax.ShapeDtypeStruct((rows, columns), F32),
        ),
        in_specs=[spec(SMEM)] + [spec()] * 8,
        out_specs=(spec(), spec(), spec()),
        scratch_shapes=[
            pltpu.VMEM((rows + 2 * BLOCK, columns), BF16),
            pltpu.VMEM((rows + 2 * BLOCK, columns), BF16),
            pltpu.VMEM((rows * R, columns), BF16),
        ],
        compiler_params=params(16),
        cost_estimate=cost(rows * 13 * BLOCK * columns * 2, rows * columns * 30),
        name="scores",
    )(arrive, q, k, v, before, after, glob, own, other)


def context_kernel(
    n, cap, per, heads, arrive_ref, prob_ref, part_ref, total_ref, own_ref, other_ref,
    out_ref, chosen,
):
    me = lax.axis_index("seq")
    for i in range(per):
        at = pl.ds(i * BLOCK, BLOCK)
        picked = pl.ds(i * R * BLOCK, R * BLOCK)
        for r in range(R):
            chosen[pl.ds((i * R + r) * BLOCK, BLOCK)] = answer(
                n, cap, arrive_ref, me * per + i, r, own_ref, cap * BLOCK, other_ref
            )
        for h in range(heads):
            cols = pl.ds(h * DH, DH)
            weighted = part_ref[at, cols] + jnp.dot(
                prob_ref[at, pl.ds(h * 256, R * BLOCK)],
                chosen[picked, cols],
                preferred_element_type=F32,
            )
            out_ref[at, cols] = (weighted / total_ref[at, cols]).astype(BF16)


def contexts(n, cap, per, arrive, prob, part, total, own, other):
    rows, columns = part.shape
    heads = columns // DH
    return pl.pallas_call(
        functools.partial(context_kernel, n, cap, per, heads),
        out_shape=jax.ShapeDtypeStruct((rows, columns), BF16),
        in_specs=[spec(SMEM)] + [spec()] * 5,
        out_specs=spec(),
        scratch_shapes=[pltpu.VMEM((rows * R, columns), BF16)],
        compiler_params=params(16),
        cost_estimate=cost(rows * 3 * BLOCK * columns * 2, rows * columns * 18),
        name="contexts",
    )(arrive, prob, part, total, own, other)


def project_kernel(own_ref, other_refs, w_ref, out_ref):
    me = lax.axis_index("head")
    count = lax.axis_size("head")
    columns = own_ref.shape[1]
    total = None
    for step, rows_ref in enumerate([own_ref] + list(other_refs)):
        owner = lax.rem(me + step, count)
        at = pl.ds(pl.multiple_of(owner * columns, columns), columns)
        term = jnp.dot(rows_ref[...], w_ref[at, :], preferred_element_type=F32)
        total = term if total is None else total + term
    out_ref[...] = total.astype(BF16)


def project(own, others, w_out):
    rows, columns = own.shape
    wide = w_out.shape[1]
    tile = rows // 4
    block = pl.BlockSpec((tile, columns), lambda i: (i, 0))

    def kernel(own_ref, *refs):
        project_kernel(own_ref, refs[: len(others)], refs[-2], refs[-1])

    return pl.pallas_call(
        kernel,
        grid=(4,),
        out_shape=jax.ShapeDtypeStruct((rows, wide), BF16),
        in_specs=[block] * (1 + len(others)) + [spec()],
        out_specs=pl.BlockSpec((tile, wide), lambda i: (i, 0)),
        compiler_params=params(16),
        cost_estimate=cost(
            2 * rows * w_out.shape[0] * wide, rows * wide * 2 + w_out.size * 2 + rows * columns * 4
        ),
        name="project",
    )(own, *others, w_out)


def on_device(queries, keys, values, rand_group, rand_offset, glob_blocks, w_out):
    tokens_dev = queries.shape[0]
    per = tokens_dev // BLOCK
    n = lax.axis_size("seq")
    heads = lax.axis_size("head")
    cap = max(2, (rand_group.shape[0] // n * R + n - 1) // n)

    up = [(i, (i + 1) % n) for i in range(n)]
    down = [(j, i) for i, j in up]
    partners = [(i, (i + n // 2) % n) for i in range(n)]
    first, last, cand = pack(per, glob_blocks, keys, values)
    before = lax.ppermute(last, "seq", up)
    after = lax.ppermute(first, "seq", down)
    far_k = lax.ppermute(keys, "seq", partners)
    far_v = lax.ppermute(values, "seq", partners)
    glob = spread(cand, glob_blocks, per, n)

    spots, arrive = ranks(n, per, cap, rand_group.T, rand_offset.T)
    slots = cap * BLOCK
    near = half_all_to_all(gather(n, cap, 0, spots, keys, values), n, 2 * slots)
    rand_k = half_all_to_all(gather(n, cap, cap, spots, far_k), n, slots)
    rand_v = half_all_to_all(gather(n, cap, cap, spots, far_v), n, slots)
    prob, part, total = scores(
        n, cap, per, arrive, queries, keys, values, before, after, glob, near, rand_k
    )
    context = contexts(n, cap, per, arrive, prob, part, total, near, rand_v)
    others = [
        lax.ppermute(context, "head", [((i + s) % heads, i) for i in range(heads)])
        for s in range(1, heads)
    ]
    return project(context, others, w_out)


def solution(mesh):
    return jax.shard_map(
        on_device,
        mesh=mesh,
        in_specs=(
            P("seq", "head"),
            P("seq", "head"),
            P("seq", "head"),
            P(),
            P(),
            P(),
            P(None, "head"),
        ),
        out_specs=P("seq", "head"),
        check_vma=False,
    )
```

```python
import functools
import math

import jax
import jax.numpy as jnp
from jax import lax
from jax.experimental import pallas as pl
from jax.experimental.pallas import tpu as pltpu
from jax.sharding import PartitionSpec as P

DH = 128
BLOCK = 64
R = 3
G = 2
VMEM = pltpu.MemorySpace.VMEM
SMEM = pltpu.MemorySpace.SMEM
BF16 = jnp.bfloat16
F32 = jnp.float32
I32 = jnp.int32


def params(mib):
    return pltpu.CompilerParams(vmem_limit_bytes=mib * 1024 * 1024)


def cost(flops, size):
    return pl.CostEstimate(flops=int(flops), bytes_accessed=int(size), transcendentals=0)


def spec(space=VMEM):
    return pl.BlockSpec(memory_space=space)


def rank_kernel(n, per, cap, g_ref, o_ref, spot_ref, arrive_ref, g_pad, o_pad):
    me = lax.axis_index("seq")
    nb = g_ref.shape[1]
    wide = g_pad.shape[1]
    tall = spot_ref.shape[0]
    g_pad[...] = jnp.full(g_pad.shape, -1, I32)
    o_pad[...] = jnp.zeros(o_pad.shape, I32)
    g_pad[:R, :nb] = g_ref[...]
    o_pad[:R, :nb] = o_ref[...]
    g = g_pad[...]
    lane = lax.broadcasted_iota(I32, g.shape, 1)
    place = lane
    for d in range(1, n):
        place = jnp.where(lane >= d * per, lane - d * per, place)
    rank = jnp.zeros(g.shape, I32)
    for s in range(1, per):
        back = pltpu.roll(g, s, axis=1)
        ahead = place >= s
        for r in range(R):
            same = jnp.broadcast_to(back[r : r + 1, :], g.shape) == g
            rank = rank + jnp.where(ahead & same, 1, 0)
    arrive_ref[...] = g * cap + rank
    row = lax.broadcasted_iota(I32, (tall, wide), 0)
    spots = jnp.zeros((tall, wide), F32)
    for side in range(2):
        group = lax.rem(me + side * (n // 2), n)
        named = jnp.where(g == group, o_pad[...], 0)
        for s in range(cap):
            picked = jnp.where(rank == s, named, 0).astype(F32)
            total = jnp.sum(picked, axis=0, keepdims=True)
            here = row == side * cap + s
            spots = spots + jnp.where(here, jnp.broadcast_to(total, (tall, wide)), 0.0)
    token = lax.broadcasted_iota(I32, (wide, 128), 0)
    first = lax.broadcasted_iota(I32, (wide, 128), 1) * per
    belongs = jnp.where((token >= first) & (token < first + per), 1.0, 0.0)
    spot_ref[...] = jnp.dot(
        spots.astype(BF16), belongs.astype(BF16), preferred_element_type=F32
    ).astype(I32)


def ranks(n, per, cap, groups, offsets):
    nb = groups.shape[1]
    wide = -(-nb // 128) * 128
    tall = -(-2 * cap // 8) * 8
    return pl.pallas_call(
        functools.partial(rank_kernel, n, per, cap),
        out_shape=(
            jax.ShapeDtypeStruct((tall, 128), I32),
            jax.ShapeDtypeStruct((8, wide), I32),
        ),
        in_specs=[spec(), spec()],
        out_specs=(spec(), spec()),
        scratch_shapes=[pltpu.VMEM((8, wide), I32), pltpu.VMEM((8, wide), I32)],
        compiler_params=params(4),
        name="ranks",
    )(groups, offsets)


def gather_kernel(n, cap, row, count, spot_ref, *refs):
    sources, (out_ref, held, sem) = refs[:count], refs[-3:]
    half = n // 2
    base = jnp.where(lax.axis_index("seq") >= half, half, 0)
    size = count * cap * BLOCK

    def one(j, carry):
        for c, source in enumerate(sources):
            for s in range(cap):
                start = pl.multiple_of(spot_ref[row + s, base + j] * BLOCK, BLOCK)
                slot = pl.multiple_of(j * size + (c * cap + s) * BLOCK, BLOCK)
                held[pl.ds(slot, BLOCK)] = source[pl.ds(start, BLOCK)]
        part = pl.ds(pl.multiple_of(j * size, size), size)
        pltpu.make_async_copy(held.at[part], out_ref.at[part], sem).start()
        return carry

    lax.fori_loop(0, half, one, 0)
    pltpu.make_async_copy(held, out_ref, sem).wait()


def gather(n, cap, row, spots, sources, earlier=()):
    columns = sources[0].shape[1]
    count = len(sources)
    rows = n // 2 * cap * BLOCK * count
    return pl.pallas_call(
        functools.partial(gather_kernel, n, cap, row, count),
        out_shape=jax.ShapeDtypeStruct((rows, columns), BF16),
        in_specs=[spec(SMEM)] + [spec()] * count + [spec(pl.ANY)] * len(earlier),
        out_specs=spec(pltpu.MemorySpace.HBM),
        scratch_shapes=[pltpu.VMEM((rows, columns), BF16), pltpu.SemaphoreType.DMA],
        compiler_params=params(8),
        cost_estimate=cost(0, 2 * rows * columns * 2),
        name="gather_blocks",
    )(spots, *sources, *earlier)


def half_all_to_all(rows, n, size):
    groups = [list(range(n // 2)), list(range(n // 2, n))]
    columns = rows.shape[1]
    return lax.all_to_all(
        rows.reshape(n // 2, size, columns), "seq", 0, 0, axis_index_groups=groups, tiled=True
    )


def pack_kernel(per, glob_ref, k_ref, v_ref, first_ref, last_ref, cand_ref):
    rows = per * BLOCK
    for c, source in enumerate((k_ref, v_ref)):
        at = pl.ds(c * BLOCK, BLOCK)
        first_ref[at] = source[:BLOCK]
        last_ref[at] = source[rows - BLOCK :]
        for g in range(G):
            start = pl.multiple_of(lax.rem(glob_ref[g], per) * BLOCK, BLOCK)
            cand_ref[pl.ds((c * G + g) * BLOCK, BLOCK)] = source[pl.ds(start, BLOCK)]


def pack(per, glob, k, v):
    columns = k.shape[1]
    edge = jax.ShapeDtypeStruct((2 * BLOCK, columns), BF16)
    return pl.pallas_call(
        functools.partial(pack_kernel, per),
        out_shape=(edge, edge, jax.ShapeDtypeStruct((2 * G * BLOCK, columns), BF16)),
        in_specs=[spec(SMEM), spec(), spec()],
        out_specs=(spec(), spec(), spec()),
        compiler_params=params(4),
        name="pack",
    )(glob, k, v)


def merge_kernel(per, known, glob_ref, own_ref, got_ref, out_ref):
    me = lax.axis_index("seq")
    for g in range(G):
        differ = lax.bitwise_xor(me, lax.div(glob_ref[g], per))
        have = lax.bitwise_and(differ, jnp.int32(~known)) == 0
        for c in range(2):
            at = pl.ds((c * G + g) * BLOCK, BLOCK)
            out_ref[at] = jnp.where(have, own_ref[at], got_ref[at])


def spread(rows, glob, per, n):
    known, steps = 0, []
    for bit in reversed(range(n.bit_length() - 1)):
        pairs = [(i, i ^ (1 << bit)) for i in range(n)]
        got = lax.ppermute(rows, "seq", pairs)
        rows = pl.pallas_call(
            functools.partial(merge_kernel, per, known),
            out_shape=jax.ShapeDtypeStruct(rows.shape, BF16),
            in_specs=[spec(SMEM), spec(), spec()],
            out_specs=spec(),
            compiler_params=params(4),
            name="merge",
        )(glob, rows, got)
        known |= 1 << bit
        steps.append(rows)
    return steps


def answer(n, cap, arrive_ref, i, r, own_ref, skip, other_ref):
    half = n // 2
    me = lax.axis_index("seq")
    spot = arrive_ref[r, i]
    group = lax.div(spot, cap)
    slot = spot - group * cap
    own_side = (group >= half) == (me >= half)
    place = jnp.where(group >= half, group - half, group)
    at = pl.ds(pl.multiple_of(slot * BLOCK, BLOCK), BLOCK)
    at_own = pl.ds(pl.multiple_of(skip + slot * BLOCK, BLOCK), BLOCK)
    return jnp.where(own_side, own_ref[place, at_own, :], other_ref[place, at, :])


def dot_t(a, b):
    return lax.dot_general(a, b, (((1,), (1,)), ((), ())), preferred_element_type=F32)


def scores_kernel(
    n, cap, per, heads, arrive_ref, q_ref, k_ref, v_ref, before_ref, after_ref, glob_ref,
    own_ref, other_ref, prob_ref, part_ref, total_ref, keys, vals, chosen,
):
    me = lax.axis_index("seq")
    rows = per * BLOCK
    keys[:BLOCK] = before_ref[:BLOCK]
    vals[:BLOCK] = before_ref[BLOCK:]
    keys[pl.ds(BLOCK, rows)] = k_ref[...]
    vals[pl.ds(BLOCK, rows)] = v_ref[...]
    keys[pl.ds(BLOCK + rows, BLOCK)] = after_ref[:BLOCK]
    vals[pl.ds(BLOCK + rows, BLOCK)] = after_ref[BLOCK:]
    scale = 1.0 / math.sqrt(DH)
    for i in range(per):
        at = pl.ds(i * BLOCK, BLOCK)
        window = pl.ds(i * BLOCK, 3 * BLOCK)
        picked = pl.ds(i * R * BLOCK, R * BLOCK)
        for r in range(R):
            chosen[pl.ds((i * R + r) * BLOCK, BLOCK)] = answer(
                n, cap, arrive_ref, me * per + i, r, own_ref, 0, other_ref
            )
        for h in range(heads):
            cols = pl.ds(h * DH, DH)
            q = q_ref[at, cols]
            s_w = dot_t(q, keys[window, cols]) * scale
            s_g = dot_t(q, glob_ref[: G * BLOCK, cols]) * scale
            s_r = dot_t(q, chosen[picked, cols]) * scale
            top = jnp.maximum(
                jnp.max(s_g, axis=1, keepdims=True),
                jnp.maximum(
                    jnp.max(s_w, axis=1, keepdims=True), jnp.max(s_r, axis=1, keepdims=True)
                ),
            )
            w_w, w_g, w_r = jnp.exp(s_w - top), jnp.exp(s_g - top), jnp.exp(s_r - top)
            total = (
                jnp.sum(w_w, axis=1, keepdims=True)
                + jnp.sum(w_g, axis=1, keepdims=True)
                + jnp.sum(w_r, axis=1, keepdims=True)
            )
            part = jnp.dot(w_w.astype(BF16), vals[window, cols], preferred_element_type=F32)
            part = part + jnp.dot(
                w_g.astype(BF16), glob_ref[G * BLOCK :, cols], preferred_element_type=F32
            )
            prob_ref[at, pl.ds(h * 256, R * BLOCK)] = w_r.astype(BF16)
            part_ref[at, cols] = part
            total_ref[at, cols] = jnp.broadcast_to(total, (BLOCK, DH))


def scores(n, cap, per, arrive, q, k, v, before, after, glob, own, other):
    rows, columns = q.shape
    heads = columns // DH
    return pl.pallas_call(
        functools.partial(scores_kernel, n, cap, per, heads),
        out_shape=(
            jax.ShapeDtypeStruct((rows, heads * 256), BF16),
            jax.ShapeDtypeStruct((rows, columns), F32),
            jax.ShapeDtypeStruct((rows, columns), F32),
        ),
        in_specs=[spec(SMEM)] + [spec()] * 8,
        out_specs=(spec(), spec(), spec()),
        scratch_shapes=[
            pltpu.VMEM((rows + 2 * BLOCK, columns), BF16),
            pltpu.VMEM((rows + 2 * BLOCK, columns), BF16),
            pltpu.VMEM((rows * R, columns), BF16),
        ],
        compiler_params=params(16),
        cost_estimate=cost(rows * 13 * BLOCK * columns * 2, rows * columns * 30),
        name="scores",
    )(arrive, q, k, v, before, after, glob, own, other)


def context_kernel(
    n, cap, per, heads, arrive_ref, prob_ref, part_ref, total_ref, own_ref, other_ref,
    out_ref, chosen,
):
    me = lax.axis_index("seq")
    for i in range(per):
        at = pl.ds(i * BLOCK, BLOCK)
        picked = pl.ds(i * R * BLOCK, R * BLOCK)
        for r in range(R):
            chosen[pl.ds((i * R + r) * BLOCK, BLOCK)] = answer(
                n, cap, arrive_ref, me * per + i, r, own_ref, cap * BLOCK, other_ref
            )
        for h in range(heads):
            cols = pl.ds(h * DH, DH)
            weighted = part_ref[at, cols] + jnp.dot(
                prob_ref[at, pl.ds(h * 256, R * BLOCK)],
                chosen[picked, cols],
                preferred_element_type=F32,
            )
            out_ref[at, cols] = (weighted / total_ref[at, cols]).astype(BF16)


def contexts(n, cap, per, arrive, prob, part, total, own, other):
    rows, columns = part.shape
    heads = columns // DH
    return pl.pallas_call(
        functools.partial(context_kernel, n, cap, per, heads),
        out_shape=jax.ShapeDtypeStruct((rows, columns), BF16),
        in_specs=[spec(SMEM)] + [spec()] * 5,
        out_specs=spec(),
        scratch_shapes=[pltpu.VMEM((rows * R, columns), BF16)],
        compiler_params=params(16),
        cost_estimate=cost(rows * 3 * BLOCK * columns * 2, rows * columns * 18),
        name="contexts",
    )(arrive, prob, part, total, own, other)


def project_kernel(own_ref, other_refs, w_ref, out_ref):
    me = lax.axis_index("head")
    count = lax.axis_size("head")
    columns = own_ref.shape[1]
    total = None
    for step, rows_ref in enumerate([own_ref] + list(other_refs)):
        owner = lax.rem(me + step, count)
        at = pl.ds(pl.multiple_of(owner * columns, columns), columns)
        term = jnp.dot(rows_ref[...], w_ref[at, :], preferred_element_type=F32)
        total = term if total is None else total + term
    out_ref[...] = total.astype(BF16)


def project(own, others, w_out):
    rows, columns = own.shape
    wide = w_out.shape[1]
    tile = rows // 4
    block = pl.BlockSpec((tile, columns), lambda i: (i, 0))

    def kernel(own_ref, *refs):
        project_kernel(own_ref, refs[: len(others)], refs[-2], refs[-1])

    return pl.pallas_call(
        kernel,
        grid=(4,),
        out_shape=jax.ShapeDtypeStruct((rows, wide), BF16),
        in_specs=[block] * (1 + len(others)) + [spec()],
        out_specs=pl.BlockSpec((tile, wide), lambda i: (i, 0)),
        compiler_params=params(16),
        cost_estimate=cost(
            2 * rows * w_out.shape[0] * wide, rows * wide * 2 + w_out.size * 2 + rows * columns * 4
        ),
        name="project",
    )(own, *others, w_out)


def on_device(queries, keys, values, rand_group, rand_offset, glob_blocks, w_out):
    tokens_dev = queries.shape[0]
    per = tokens_dev // BLOCK
    n = lax.axis_size("seq")
    heads = lax.axis_size("head")
    cap = max(2, (rand_group.shape[0] // n * R + n - 1) // n)

    up = [(i, (i + 1) % n) for i in range(n)]
    down = [(j, i) for i, j in up]
    partners = [(i, (i + n // 2) % n) for i in range(n)]
    first, last, cand = pack(per, glob_blocks, keys, values)
    before = lax.ppermute(last, "seq", up)
    after = lax.ppermute(first, "seq", down)
    far_k = lax.ppermute(keys, "seq", partners)
    later_v, _ = lax.optimization_barrier((values, far_k))
    far_v = lax.ppermute(later_v, "seq", partners)
    steps = spread(cand, glob_blocks, per, n)
    glob = steps[-1]

    spots, arrive = ranks(n, per, cap, rand_group.T, rand_offset.T)
    slots = cap * BLOCK
    own = gather(n, cap, 0, spots, [keys, values], [steps[0]])
    near = half_all_to_all(own, n, 2 * slots)
    own = gather(n, cap, cap, spots, [far_k], [near, before, after, steps[-2]])
    rand_k = half_all_to_all(own, n, slots)
    own = gather(n, cap, cap, spots, [far_v], [rand_k, glob])
    rand_v = half_all_to_all(own, n, slots)
    prob, part, total = scores(
        n, cap, per, arrive, queries, keys, values, before, after, glob, near, rand_k
    )
    context = contexts(n, cap, per, arrive, prob, part, total, near, rand_v)
    others = [
        lax.ppermute(context, "head", [((i + s) % heads, i) for i in range(heads)])
        for s in range(1, heads)
    ]
    return project(context, others, w_out)


def solution(mesh):
    return jax.shard_map(
        on_device,
        mesh=mesh,
        in_specs=(
            P("seq", "head"),
            P("seq", "head"),
            P("seq", "head"),
            P(),
            P(),
            P(),
            P(None, "head"),
        ),
        out_specs=P("seq", "head"),
        check_vma=False,
    )
```

```python
import functools
import math

import jax
import jax.numpy as jnp
from jax import lax
from jax.experimental import pallas as pl
from jax.experimental.pallas import tpu as pltpu
from jax.sharding import PartitionSpec as P

DH = 128
BLOCK = 64
R = 3
G = 2
VMEM = pltpu.MemorySpace.VMEM
SMEM = pltpu.MemorySpace.SMEM
BF16 = jnp.bfloat16
F32 = jnp.float32
I32 = jnp.int32
NONE = -1e30


def params(mib):
    return pltpu.CompilerParams(vmem_limit_bytes=mib * 1024 * 1024)


def cost(flops, size):
    return pl.CostEstimate(flops=int(flops), bytes_accessed=int(size), transcendentals=0)


def spec(space=VMEM):
    return pl.BlockSpec(memory_space=space)


def rank_kernel(n, per, cap, g_ref, o_ref, spot_ref, arrive_ref, g_pad, o_pad):
    me = lax.axis_index("seq")
    nb = g_ref.shape[1]
    wide = g_pad.shape[1]
    tall = spot_ref.shape[0]
    g_pad[...] = jnp.full(g_pad.shape, -1, I32)
    o_pad[...] = jnp.zeros(o_pad.shape, I32)
    g_pad[:R, :nb] = g_ref[...]
    o_pad[:R, :nb] = o_ref[...]
    g = g_pad[...]
    lane = lax.broadcasted_iota(I32, g.shape, 1)
    place = lane
    for d in range(1, n):
        place = jnp.where(lane >= d * per, lane - d * per, place)
    rank = jnp.zeros(g.shape, I32)
    for s in range(1, per):
        back = pltpu.roll(g, s, axis=1)
        ahead = place >= s
        for r in range(R):
            same = jnp.broadcast_to(back[r : r + 1, :], g.shape) == g
            rank = rank + jnp.where(ahead & same, 1, 0)
    arrive_ref[...] = g * cap + rank
    row = lax.broadcasted_iota(I32, (tall, wide), 0)
    spots = jnp.zeros((tall, wide), F32)
    named = jnp.where(g == me, o_pad[...], 0)
    for s in range(cap):
        picked = jnp.where(rank == s, named, 0).astype(F32)
        total = jnp.sum(picked, axis=0, keepdims=True)
        spots = spots + jnp.where(row == s, jnp.broadcast_to(total, (tall, wide)), 0.0)
    token = lax.broadcasted_iota(I32, (wide, 128), 0)
    first = lax.broadcasted_iota(I32, (wide, 128), 1) * per
    belongs = jnp.where((token >= first) & (token < first + per), 1.0, 0.0)
    spot_ref[...] = jnp.dot(
        spots.astype(BF16), belongs.astype(BF16), preferred_element_type=F32
    ).astype(I32)


def ranks(n, per, cap, groups, offsets):
    nb = groups.shape[1]
    wide = -(-nb // 128) * 128
    tall = -(-cap // 8) * 8
    return pl.pallas_call(
        functools.partial(rank_kernel, n, per, cap),
        out_shape=(
            jax.ShapeDtypeStruct((tall, 128), I32),
            jax.ShapeDtypeStruct((8, wide), I32),
        ),
        in_specs=[spec(), spec()],
        out_specs=(spec(), spec()),
        scratch_shapes=[pltpu.VMEM((8, wide), I32), pltpu.VMEM((8, wide), I32)],
        compiler_params=params(4),
        name="ranks",
    )(groups, offsets)


def gather_kernel(n, cap, far, spot_ref, k_ref, v_ref, *refs):
    out_ref, held, sem = refs[-3:]
    half = n // 2
    low = lax.axis_index("seq") < half
    base = jnp.where(low != far, 0, half)
    size = 2 * cap * BLOCK

    def one(j, carry):
        for c, source in enumerate((k_ref, v_ref)):
            for s in range(cap):
                start = pl.multiple_of(spot_ref[s, base + j] * BLOCK, BLOCK)
                slot = pl.multiple_of(j * size + (c * cap + s) * BLOCK, BLOCK)
                held[pl.ds(slot, BLOCK)] = source[pl.ds(start, BLOCK)]
        part = pl.ds(pl.multiple_of(j * size, size), size)
        pltpu.make_async_copy(held.at[part], out_ref.at[part], sem).start()
        return carry

    lax.fori_loop(0, half, one, 0)
    pltpu.make_async_copy(held, out_ref, sem).wait()


def gather(n, cap, far, spots, k, v, earlier=()):
    columns = k.shape[1]
    rows = n // 2 * 2 * cap * BLOCK
    return pl.pallas_call(
        functools.partial(gather_kernel, n, cap, far),
        out_shape=jax.ShapeDtypeStruct((rows, columns), BF16),
        in_specs=[spec(SMEM), spec(), spec()] + [spec(pl.ANY)] * len(earlier),
        out_specs=spec(pltpu.MemorySpace.HBM),
        scratch_shapes=[pltpu.VMEM((rows, columns), BF16), pltpu.SemaphoreType.DMA],
        compiler_params=params(8),
        cost_estimate=cost(0, 2 * rows * columns * 2),
        name="gather_blocks",
    )(spots, k, v, *earlier)


def half_all_to_all(rows, n, size):
    groups = [list(range(n // 2)), list(range(n // 2, n))]
    columns = rows.shape[1]
    return lax.all_to_all(
        rows.reshape(n // 2, size, columns), "seq", 0, 0, axis_index_groups=groups, tiled=True
    )


def pack_kernel(per, glob_ref, k_ref, v_ref, first_ref, last_ref, cand_ref):
    rows = per * BLOCK
    for c, source in enumerate((k_ref, v_ref)):
        at = pl.ds(c * BLOCK, BLOCK)
        first_ref[at] = source[:BLOCK]
        last_ref[at] = source[rows - BLOCK :]
        for g in range(G):
            start = pl.multiple_of(lax.rem(glob_ref[g], per) * BLOCK, BLOCK)
            cand_ref[pl.ds((c * G + g) * BLOCK, BLOCK)] = source[pl.ds(start, BLOCK)]


def pack(per, glob, k, v):
    columns = k.shape[1]
    edge = jax.ShapeDtypeStruct((2 * BLOCK, columns), BF16)
    return pl.pallas_call(
        functools.partial(pack_kernel, per),
        out_shape=(edge, edge, jax.ShapeDtypeStruct((2 * G * BLOCK, columns), BF16)),
        in_specs=[spec(SMEM), spec(), spec()],
        out_specs=(spec(), spec(), spec()),
        compiler_params=params(4),
        name="pack",
    )(glob, k, v)


def merge_kernel(per, known, glob_ref, own_ref, got_ref, out_ref):
    me = lax.axis_index("seq")
    for g in range(G):
        differ = lax.bitwise_xor(me, lax.div(glob_ref[g], per))
        have = lax.bitwise_and(differ, jnp.int32(~known)) == 0
        for c in range(2):
            at = pl.ds((c * G + g) * BLOCK, BLOCK)
            out_ref[at] = jnp.where(have, own_ref[at], got_ref[at])


def spread(rows, glob, per, n):
    known, steps = 0, []
    for bit in reversed(range(n.bit_length() - 1)):
        pairs = [(i, i ^ (1 << bit)) for i in range(n)]
        got = lax.ppermute(rows, "seq", pairs)
        rows = pl.pallas_call(
            functools.partial(merge_kernel, per, known),
            out_shape=jax.ShapeDtypeStruct(rows.shape, BF16),
            in_specs=[spec(SMEM), spec(), spec()],
            out_specs=spec(),
            compiler_params=params(4),
            name="merge",
        )(glob, rows, got)
        known |= 1 << bit
        steps.append(rows)
    return steps


def choose(n, cap, per, arrive_ref, d, i, got_ref, key_at, val_at, into):
    half = n // 2
    low = lax.axis_index("seq") < half
    biases = []
    for r in range(R):
        spot = arrive_ref[r, d * per + i]
        group = lax.div(spot, cap)
        here = (group < half) == low
        slot = jnp.where(here, spot - group * cap, 0)
        place = jnp.where(here, jnp.where(low, group, group - half), 0)
        at = pl.ds(into + r * BLOCK, BLOCK)
        key_at[at] = got_ref[place, pl.ds(pl.multiple_of(slot * BLOCK, BLOCK), BLOCK), :]
        val_at[at] = got_ref[place, pl.ds(pl.multiple_of((cap + slot) * BLOCK, BLOCK), BLOCK), :]
        biases.append(jnp.where(here, 0.0, NONE))
    lane = lax.broadcasted_iota(I32, (1, R * BLOCK), 1)
    bias = jnp.full((1, R * BLOCK), biases[-1], F32)
    for r in reversed(range(R - 1)):
        bias = jnp.where(lane < (r + 1) * BLOCK, biases[r], bias)
    return bias


def dot_t(a, b):
    return lax.dot_general(a, b, (((1,), (1,)), ((), ())), preferred_element_type=F32)


def eye():
    shape = (BLOCK, BLOCK)
    return lax.broadcasted_iota(I32, shape, 0) == lax.broadcasted_iota(I32, shape, 1)


def far_kernel(n, cap, per, heads, arrive_ref, q_ref, got_ref, out_ref, stat_ref, keys, vals):
    d = lax.bitwise_xor(lax.axis_index("seq"), n // 2)
    scale = 1.0 / math.sqrt(DH)
    diagonal = eye()
    stat_ref[...] = jnp.zeros_like(stat_ref)
    for i in range(per):
        at = pl.ds(i * BLOCK, BLOCK)
        picked = pl.ds(i * R * BLOCK, R * BLOCK)
        bias = choose(n, cap, per, arrive_ref, d, i, got_ref, keys, vals, i * R * BLOCK)
        for h in range(heads):
            cols = pl.ds(h * DH, DH)
            s = dot_t(q_ref[at, cols], keys[picked, cols]) * scale + bias
            top = jnp.max(s, axis=1, keepdims=True)
            w = jnp.exp(s - top)
            total = jnp.sum(w, axis=1, keepdims=True)
            part = jnp.dot(w.astype(BF16), vals[picked, cols], preferred_element_type=F32)
            out_ref[at, cols] = (part / total).astype(BF16)
            row = pl.ds(i * heads + h, 1)
            for c, column in enumerate((top, total)):
                flat = jnp.sum(jnp.where(diagonal, column, 0.0), axis=0, keepdims=True)
                stat_ref[row, pl.ds(c * BLOCK, BLOCK)] = flat


def far_part(n, cap, per, arrive, q, got):
    rows, columns = q.shape
    heads = columns // DH
    return pl.pallas_call(
        functools.partial(far_kernel, n, cap, per, heads),
        out_shape=(
            jax.ShapeDtypeStruct((rows, columns), BF16),
            jax.ShapeDtypeStruct((-(-per * heads // 8) * 8, 128), F32),
        ),
        in_specs=[spec(SMEM), spec(), spec()],
        out_specs=(spec(), spec()),
        scratch_shapes=[pltpu.VMEM((rows * R, columns), BF16)] * 2,
        compiler_params=params(16),
        cost_estimate=cost(rows * 6 * BLOCK * columns * 2, rows * columns * 16),
        name="far_part",
    )(arrive, q, got)


def near_kernel(
    per, heads, q_ref, k_ref, v_ref, before_ref, after_ref, glob_ref, part_ref, stat_ref,
    keys, vals,
):
    rows = per * BLOCK
    keys[:BLOCK] = before_ref[:BLOCK]
    vals[:BLOCK] = before_ref[BLOCK:]
    keys[pl.ds(BLOCK, rows)] = k_ref[...]
    vals[pl.ds(BLOCK, rows)] = v_ref[...]
    keys[pl.ds(BLOCK + rows, BLOCK)] = after_ref[:BLOCK]
    vals[pl.ds(BLOCK + rows, BLOCK)] = after_ref[BLOCK:]
    scale = 1.0 / math.sqrt(DH)
    for i in range(per):
        at = pl.ds(i * BLOCK, BLOCK)
        window = pl.ds(i * BLOCK, 3 * BLOCK)
        for h in range(heads):
            cols = pl.ds(h * DH, DH)
            q = q_ref[at, cols]
            s_w = dot_t(q, keys[window, cols]) * scale
            s_g = dot_t(q, glob_ref[: G * BLOCK, cols]) * scale
            top = jnp.maximum(
                jnp.max(s_g, axis=1, keepdims=True), jnp.max(s_w, axis=1, keepdims=True)
            )
            w_w, w_g = jnp.exp(s_w - top), jnp.exp(s_g - top)
            total = jnp.sum(w_w, axis=1, keepdims=True) + jnp.sum(w_g, axis=1, keepdims=True)
            part = jnp.dot(w_w.astype(BF16), vals[window, cols], preferred_element_type=F32)
            part_ref[at, cols] = part + jnp.dot(
                w_g.astype(BF16), glob_ref[G * BLOCK :, cols], preferred_element_type=F32
            )
            stat_ref[at, 2 * h : 2 * h + 1] = top
            stat_ref[at, 2 * h + 1 : 2 * h + 2] = total


def near_part(per, q, k, v, before, after, glob):
    rows, columns = q.shape
    heads = columns // DH
    return pl.pallas_call(
        functools.partial(near_kernel, per, heads),
        out_shape=(
            jax.ShapeDtypeStruct((rows, columns), F32),
            jax.ShapeDtypeStruct((rows, 128), F32),
        ),
        in_specs=[spec()] * 6,
        out_specs=(spec(), spec()),
        scratch_shapes=[pltpu.VMEM((rows + 2 * BLOCK, columns), BF16)] * 2,
        compiler_params=params(16),
        cost_estimate=cost(rows * 10 * BLOCK * columns * 2, rows * columns * 16),
        name="near_part",
    )(q, k, v, before, after, glob)


def context_kernel(
    n, cap, per, heads, arrive_ref, q_ref, got_ref, part_ref, stat_ref, far_ref, far_stat_ref,
    out_ref, keys, vals,
):
    d = lax.axis_index("seq")
    scale = 1.0 / math.sqrt(DH)
    diagonal = eye()
    for i in range(per):
        at = pl.ds(i * BLOCK, BLOCK)
        picked = pl.ds(i * R * BLOCK, R * BLOCK)
        bias = choose(n, cap, per, arrive_ref, d, i, got_ref, keys, vals, i * R * BLOCK)
        for h in range(heads):
            cols = pl.ds(h * DH, DH)
            s = dot_t(q_ref[at, cols], keys[picked, cols]) * scale + bias
            row = pl.ds(i * heads + h, 1)
            far_top, far_total = [
                jnp.sum(
                    jnp.where(diagonal, far_stat_ref[row, pl.ds(c * BLOCK, BLOCK)], 0.0),
                    axis=1, keepdims=True,
                )
                for c in range(2)
            ]
            near_top = stat_ref[at, 2 * h : 2 * h + 1]
            near_total = stat_ref[at, 2 * h + 1 : 2 * h + 2]
            top = jnp.maximum(
                jnp.max(s, axis=1, keepdims=True), jnp.maximum(near_top, far_top)
            )
            w = jnp.exp(s - top)
            near_w = jnp.exp(near_top - top)
            far_w = jnp.exp(far_top - top) * far_total
            total = jnp.sum(w, axis=1, keepdims=True) + near_w * near_total + far_w
            weighted = jnp.dot(w.astype(BF16), vals[picked, cols], preferred_element_type=F32)
            weighted = weighted + part_ref[at, cols] * near_w
            weighted = weighted + far_ref[at, cols].astype(F32) * far_w
            out_ref[at, cols] = (weighted / total).astype(BF16)


def contexts(n, cap, per, arrive, q, got, part, stat, far, far_stat):
    rows, columns = q.shape
    heads = columns // DH
    return pl.pallas_call(
        functools.partial(context_kernel, n, cap, per, heads),
        out_shape=jax.ShapeDtypeStruct((rows, columns), BF16),
        in_specs=[spec(SMEM)] + [spec()] * 6,
        out_specs=spec(),
        scratch_shapes=[pltpu.VMEM((rows * R, columns), BF16)] * 2,
        compiler_params=params(16),
        cost_estimate=cost(rows * 6 * BLOCK * columns * 2, rows * columns * 18),
        name="contexts",
    )(arrive, q, got, part, stat, far, far_stat)


def project_kernel(own_ref, other_refs, w_ref, out_ref):
    me = lax.axis_index("head")
    count = lax.axis_size("head")
    columns = own_ref.shape[1]
    total = None
    for step, rows_ref in enumerate([own_ref] + list(other_refs)):
        owner = lax.rem(me + step, count)
        at = pl.ds(pl.multiple_of(owner * columns, columns), columns)
        term = jnp.dot(rows_ref[...], w_ref[at, :], preferred_element_type=F32)
        total = term if total is None else total + term
    out_ref[...] = total.astype(BF16)


def project(own, others, w_out):
    rows, columns = own.shape
    wide = w_out.shape[1]
    tile = rows // 4
    block = pl.BlockSpec((tile, columns), lambda i: (i, 0))

    def kernel(own_ref, *refs):
        project_kernel(own_ref, refs[: len(others)], refs[-2], refs[-1])

    return pl.pallas_call(
        kernel,
        grid=(4,),
        out_shape=jax.ShapeDtypeStruct((rows, wide), BF16),
        in_specs=[block] * (1 + len(others)) + [spec()],
        out_specs=pl.BlockSpec((tile, wide), lambda i: (i, 0)),
        compiler_params=params(16),
        cost_estimate=cost(
            2 * rows * w_out.shape[0] * wide, rows * wide * 2 + w_out.size * 2 + rows * columns * 4
        ),
        name="project",
    )(own, *others, w_out)


def on_device(queries, keys, values, rand_group, rand_offset, glob_blocks, w_out):
    tokens_dev = queries.shape[0]
    per = tokens_dev // BLOCK
    n = lax.axis_size("seq")
    heads = lax.axis_size("head")
    cap = max(2, (rand_group.shape[0] // n * R + n - 1) // n)

    up = [(i, (i + 1) % n) for i in range(n)]
    down = [(j, i) for i, j in up]
    partners = [(i, (i + n // 2) % n) for i in range(n)]
    first, last, cand = pack(per, glob_blocks, keys, values)
    before = lax.ppermute(last, "seq", up)
    after = lax.ppermute(first, "seq", down)
    far_q = lax.ppermute(queries, "seq", partners)
    steps = spread(cand, glob_blocks, per, n)

    spots, arrive = ranks(n, per, cap, rand_group.T, rand_offset.T)
    size = 2 * cap * BLOCK
    got_far = half_all_to_all(gather(n, cap, True, spots, keys, values), n, size)
    own = gather(
        n, cap, False, spots, keys, values, [got_far, before, after, steps[-2]]
    )
    got_own = half_all_to_all(own, n, size)
    far, far_stat = far_part(n, cap, per, arrive, far_q, got_far)
    far = lax.ppermute(far, "seq", partners)
    far_stat = lax.ppermute(far_stat, "seq", partners)
    part, stat = near_part(per, queries, keys, values, before, after, steps[-1])
    context = contexts(n, cap, per, arrive, queries, got_own, part, stat, far, far_stat)
    others = [
        lax.ppermute(context, "head", [((i + s) % heads, i) for i in range(heads)])
        for s in range(1, heads)
    ]
    return project(context, others, w_out)


def solution(mesh):
    return jax.shard_map(
        on_device,
        mesh=mesh,
        in_specs=(
            P("seq", "head"),
            P("seq", "head"),
            P("seq", "head"),
            P(),
            P(),
            P(),
            P(None, "head"),
        ),
        out_specs=P("seq", "head"),
        check_vma=False,
    )
```

```python
import functools
import math

import jax
import jax.numpy as jnp
from jax import lax
from jax.experimental import pallas as pl
from jax.experimental.pallas import tpu as pltpu
from jax.sharding import PartitionSpec as P

DH = 128
BLOCK = 64
R = 3
G = 2
VMEM = pltpu.MemorySpace.VMEM
SMEM = pltpu.MemorySpace.SMEM
BF16 = jnp.bfloat16
F32 = jnp.float32
I32 = jnp.int32


def params(mib):
    return pltpu.CompilerParams(vmem_limit_bytes=mib * 1024 * 1024)


def cost(flops, size):
    return pl.CostEstimate(flops=int(flops), bytes_accessed=int(size), transcendentals=0)


def spec(space=VMEM):
    return pl.BlockSpec(memory_space=space)


def rank_kernel(n, per, cap, g_ref, o_ref, spot_ref, arrive_ref, g_pad, o_pad):
    me = lax.axis_index("seq")
    nb = g_ref.shape[1]
    wide = g_pad.shape[1]
    tall = spot_ref.shape[0]
    g_pad[...] = jnp.full(g_pad.shape, -1, I32)
    o_pad[...] = jnp.zeros(o_pad.shape, I32)
    g_pad[:R, :nb] = g_ref[...]
    o_pad[:R, :nb] = o_ref[...]
    g = g_pad[...]
    lane = lax.broadcasted_iota(I32, g.shape, 1)
    place = lane
    for d in range(1, n):
        place = jnp.where(lane >= d * per, lane - d * per, place)
    rank = jnp.zeros(g.shape, I32)
    for s in range(1, per):
        back = pltpu.roll(g, s, axis=1)
        ahead = place >= s
        for r in range(R):
            same = jnp.broadcast_to(back[r : r + 1, :], g.shape) == g
            rank = rank + jnp.where(ahead & same, 1, 0)
    arrive_ref[...] = g * cap + rank
    row = lax.broadcasted_iota(I32, (tall, wide), 0)
    spots = jnp.zeros((tall, wide), F32)
    named = jnp.where(g == me, o_pad[...], 0)
    for s in range(cap):
        picked = jnp.where(rank == s, named, 0).astype(F32)
        total = jnp.sum(picked, axis=0, keepdims=True)
        spots = spots + jnp.where(row == s, jnp.broadcast_to(total, (tall, wide)), 0.0)
    token = lax.broadcasted_iota(I32, (wide, 128), 0)
    first = lax.broadcasted_iota(I32, (wide, 128), 1) * per
    belongs = jnp.where((token >= first) & (token < first + per), 1.0, 0.0)
    spot_ref[...] = jnp.dot(
        spots.astype(BF16), belongs.astype(BF16), preferred_element_type=F32
    ).astype(I32)


def ranks(n, per, cap, groups, offsets):
    nb = groups.shape[1]
    wide = -(-nb // 128) * 128
    tall = -(-cap // 8) * 8
    return pl.pallas_call(
        functools.partial(rank_kernel, n, per, cap),
        out_shape=(
            jax.ShapeDtypeStruct((tall, 128), I32),
            jax.ShapeDtypeStruct((8, wide), I32),
        ),
        in_specs=[spec(), spec()],
        out_specs=(spec(), spec()),
        scratch_shapes=[pltpu.VMEM((8, wide), I32), pltpu.VMEM((8, wide), I32)],
        compiler_params=params(4),
        name="ranks",
    )(groups, offsets)


def gather_kernel(n, cap, spot_ref, rows_ref, *refs):
    out_ref, held, sem = refs[-3:]
    size = cap * BLOCK

    def one(d, carry):
        for s in range(cap):
            start = pl.multiple_of(spot_ref[s, d] * BLOCK, BLOCK)
            slot = pl.multiple_of(d * size + s * BLOCK, BLOCK)
            held[pl.ds(slot, BLOCK)] = rows_ref[pl.ds(start, BLOCK)]
        part = pl.ds(pl.multiple_of(d * size, size), size)
        pltpu.make_async_copy(held.at[part], out_ref.at[part], sem).start()
        return carry

    lax.fori_loop(0, n, one, 0)
    pltpu.make_async_copy(held, out_ref, sem).wait()


def gather(n, cap, spots, source, earlier=()):
    columns = source.shape[1]
    rows = n * cap * BLOCK
    return pl.pallas_call(
        functools.partial(gather_kernel, n, cap),
        out_shape=jax.ShapeDtypeStruct((rows, columns), BF16),
        in_specs=[spec(SMEM), spec()] + [spec(pl.ANY)] * len(earlier),
        out_specs=spec(pltpu.MemorySpace.HBM),
        scratch_shapes=[pltpu.VMEM((rows, columns), BF16), pltpu.SemaphoreType.DMA],
        compiler_params=params(8),
        cost_estimate=cost(0, 2 * rows * columns * 2),
        name="gather_blocks",
    )(spots, source, *earlier)


def exchange(rows, n):
    rows = rows.reshape(n, -1, rows.shape[1])
    return lax.all_to_all(rows, "seq", split_axis=0, concat_axis=0, tiled=True)


def pack_kernel(per, glob_ref, k_ref, v_ref, first_ref, last_ref, cand_ref):
    rows = per * BLOCK
    for c, source in enumerate((k_ref, v_ref)):
        at = pl.ds(c * BLOCK, BLOCK)
        first_ref[at] = source[:BLOCK]
        last_ref[at] = source[rows - BLOCK :]
        for g in range(G):
            start = pl.multiple_of(lax.rem(glob_ref[g], per) * BLOCK, BLOCK)
            cand_ref[pl.ds((c * G + g) * BLOCK, BLOCK)] = source[pl.ds(start, BLOCK)]


def pack(per, glob, k, v):
    columns = k.shape[1]
    edge = jax.ShapeDtypeStruct((2 * BLOCK, columns), BF16)
    return pl.pallas_call(
        functools.partial(pack_kernel, per),
        out_shape=(edge, edge, jax.ShapeDtypeStruct((2 * G * BLOCK, columns), BF16)),
        in_specs=[spec(SMEM), spec(), spec()],
        out_specs=(spec(), spec(), spec()),
        compiler_params=params(4),
        name="pack",
    )(glob, k, v)


def merge_kernel(per, known, glob_ref, own_ref, got_ref, out_ref):
    me = lax.axis_index("seq")
    for g in range(G):
        differ = lax.bitwise_xor(me, lax.div(glob_ref[g], per))
        have = lax.bitwise_and(differ, jnp.int32(~known)) == 0
        for c in range(2):
            at = pl.ds((c * G + g) * BLOCK, BLOCK)
            out_ref[at] = jnp.where(have, own_ref[at], got_ref[at])


def spread(rows, glob, per, n):
    known, steps = 0, []
    for bit in reversed(range(n.bit_length() - 1)):
        pairs = [(i, i ^ (1 << bit)) for i in range(n)]
        got = lax.ppermute(rows, "seq", pairs)
        rows = pl.pallas_call(
            functools.partial(merge_kernel, per, known),
            out_shape=jax.ShapeDtypeStruct(rows.shape, BF16),
            in_specs=[spec(SMEM), spec(), spec()],
            out_specs=spec(),
            compiler_params=params(4),
            name="merge",
        )(glob, rows, got)
        known |= 1 << bit
        steps.append(rows)
    return steps


def choose(cap, per, arrive_ref, i, got_ref, chosen):
    me = lax.axis_index("seq")
    for r in range(R):
        spot = arrive_ref[r, me * per + i]
        group = lax.div(spot, cap)
        at = pl.ds(pl.multiple_of((spot - group * cap) * BLOCK, BLOCK), BLOCK)
        chosen[pl.ds((i * R + r) * BLOCK, BLOCK)] = got_ref[group, at, :]


def dot_t(a, b):
    return lax.dot_general(a, b, (((1,), (1,)), ((), ())), preferred_element_type=F32)


def scores_kernel(
    cap, per, heads, arrive_ref, q_ref, k_ref, v_ref, before_ref, after_ref, glob_ref, got_ref,
    prob_ref, part_ref, total_ref, keys, vals, chosen,
):
    rows = per * BLOCK
    keys[:BLOCK] = before_ref[:BLOCK]
    vals[:BLOCK] = before_ref[BLOCK:]
    keys[pl.ds(BLOCK, rows)] = k_ref[...]
    vals[pl.ds(BLOCK, rows)] = v_ref[...]
    keys[pl.ds(BLOCK + rows, BLOCK)] = after_ref[:BLOCK]
    vals[pl.ds(BLOCK + rows, BLOCK)] = after_ref[BLOCK:]
    scale = 1.0 / math.sqrt(DH)
    for i in range(per):
        choose(cap, per, arrive_ref, i, got_ref, chosen)
        at = pl.ds(i * BLOCK, BLOCK)
        window = pl.ds(i * BLOCK, 3 * BLOCK)
        picked = pl.ds(i * R * BLOCK, R * BLOCK)
        for h in range(heads):
            cols = pl.ds(h * DH, DH)
            q = q_ref[at, cols]
            s_w = dot_t(q, keys[window, cols]) * scale
            s_g = dot_t(q, glob_ref[: G * BLOCK, cols]) * scale
            s_r = dot_t(q, chosen[picked, cols]) * scale
            top = jnp.maximum(
                jnp.max(s_g, axis=1, keepdims=True),
                jnp.maximum(
                    jnp.max(s_w, axis=1, keepdims=True), jnp.max(s_r, axis=1, keepdims=True)
                ),
            )
            w_w, w_g, w_r = jnp.exp(s_w - top), jnp.exp(s_g - top), jnp.exp(s_r - top)
            total = (
                jnp.sum(w_w, axis=1, keepdims=True)
                + jnp.sum(w_g, axis=1, keepdims=True)
                + jnp.sum(w_r, axis=1, keepdims=True)
            )
            part = jnp.dot(w_w.astype(BF16), vals[window, cols], preferred_element_type=F32)
            part_ref[at, cols] = part + jnp.dot(
                w_g.astype(BF16), glob_ref[G * BLOCK :, cols], preferred_element_type=F32
            )
            prob_ref[at, pl.ds(h * 256, R * BLOCK)] = w_r.astype(BF16)
            prob_ref[at, pl.ds(h * 256 + R * BLOCK, BLOCK)] = jnp.zeros((BLOCK, BLOCK), BF16)
            total_ref[at, cols] = jnp.broadcast_to(total, (BLOCK, DH))


def scores(cap, per, arrive, q, k, v, before, after, glob, got):
    rows, columns = q.shape
    heads = columns // DH
    return pl.pallas_call(
        functools.partial(scores_kernel, cap, per, heads),
        out_shape=(
            jax.ShapeDtypeStruct((rows, heads * 256), BF16),
            jax.ShapeDtypeStruct((rows, columns), F32),
            jax.ShapeDtypeStruct((rows, columns), F32),
        ),
        in_specs=[spec(SMEM)] + [spec()] * 7,
        out_specs=(spec(), spec(), spec()),
        scratch_shapes=[
            pltpu.VMEM((rows + 2 * BLOCK, columns), BF16),
            pltpu.VMEM((rows + 2 * BLOCK, columns), BF16),
            pltpu.VMEM((rows * R, columns), BF16),
        ],
        compiler_params=params(16),
        cost_estimate=cost(rows * 13 * BLOCK * columns * 2, rows * columns * 30),
        name="scores",
    )(arrive, q, k, v, before, after, glob, got)


def context_kernel(
    cap, per, heads, arrive_ref, got_ref, prob_hbm, part_hbm, total_hbm, out_ref,
    prob_ref, part_ref, total_ref, chosen, sems,
):
    copies = [
        pltpu.make_async_copy(source, target, sems.at[c])
        for c, (source, target) in enumerate(
            [(prob_hbm, prob_ref), (part_hbm, part_ref), (total_hbm, total_ref)]
        )
    ]
    for copy in copies:
        copy.start()
    for i in range(per):
        choose(cap, per, arrive_ref, i, got_ref, chosen)
    for copy in copies:
        copy.wait()
    for i in range(per):
        at = pl.ds(i * BLOCK, BLOCK)
        picked = pl.ds(i * R * BLOCK, R * BLOCK)
        for h in range(heads):
            cols = pl.ds(h * DH, DH)
            weighted = part_ref[at, cols] + jnp.dot(
                prob_ref[at, pl.ds(h * 256, R * BLOCK)],
                chosen[picked, cols],
                preferred_element_type=F32,
            )
            out_ref[at, cols] = (weighted / total_ref[at, cols]).astype(BF16)


def contexts(cap, per, arrive, got, prob, part, total):
    rows, columns = part.shape
    heads = columns // DH
    return pl.pallas_call(
        functools.partial(context_kernel, cap, per, heads),
        out_shape=jax.ShapeDtypeStruct((rows, columns), BF16),
        in_specs=[spec(SMEM), spec()] + [spec(pl.ANY)] * 3,
        out_specs=spec(),
        scratch_shapes=[
            pltpu.VMEM(prob.shape, BF16),
            pltpu.VMEM(part.shape, F32),
            pltpu.VMEM(total.shape, F32),
            pltpu.VMEM((rows * R, columns), BF16),
            pltpu.SemaphoreType.DMA((3,)),
        ],
        compiler_params=params(16),
        cost_estimate=cost(rows * 3 * BLOCK * columns * 2, rows * columns * 18),
        name="contexts",
    )(arrive, got, prob, part, total)


def project_kernel(own_ref, other_refs, w_ref, out_ref):
    me = lax.axis_index("head")
    count = lax.axis_size("head")
    columns = own_ref.shape[1]
    total = None
    for step, rows_ref in enumerate([own_ref] + list(other_refs)):
        owner = lax.rem(me + step, count)
        at = pl.ds(pl.multiple_of(owner * columns, columns), columns)
        term = jnp.dot(rows_ref[...], w_ref[at, :], preferred_element_type=F32)
        total = term if total is None else total + term
    out_ref[...] = total.astype(BF16)


def project(own, others, w_out):
    rows, columns = own.shape
    wide = w_out.shape[1]
    tile = rows // 4
    block = pl.BlockSpec((tile, columns), lambda i: (i, 0))

    def kernel(own_ref, *refs):
        project_kernel(own_ref, refs[: len(others)], refs[-2], refs[-1])

    return pl.pallas_call(
        kernel,
        grid=(4,),
        out_shape=jax.ShapeDtypeStruct((rows, wide), BF16),
        in_specs=[block] * (1 + len(others)) + [spec()],
        out_specs=pl.BlockSpec((tile, wide), lambda i: (i, 0)),
        compiler_params=params(16),
        cost_estimate=cost(
            2 * rows * w_out.shape[0] * wide, rows * wide * 2 + w_out.size * 2 + rows * columns * 4
        ),
        name="project",
    )(own, *others, w_out)


def on_device(queries, keys, values, rand_group, rand_offset, glob_blocks, w_out):
    tokens_dev = queries.shape[0]
    per = tokens_dev // BLOCK
    n = lax.axis_size("seq")
    heads = lax.axis_size("head")
    cap = max(2, (rand_group.shape[0] // n * R + n - 1) // n)

    up = [(i, (i + 1) % n) for i in range(n)]
    down = [(j, i) for i, j in up]
    first, last, cand = pack(per, glob_blocks, keys, values)
    steps = spread(cand, glob_blocks, per, n)
    before = lax.ppermute(last, "seq", up)
    after = lax.ppermute(first, "seq", down)

    spots, arrive = ranks(n, per, cap, rand_group.T, rand_offset.T)
    got_k = exchange(gather(n, cap, spots, keys, [steps[0]]), n)
    got_v = exchange(gather(n, cap, spots, values, [got_k]), n)
    prob, part, total = scores(
        cap, per, arrive, queries, keys, values, before, after, steps[-1], got_k
    )
    context = contexts(cap, per, arrive, got_v, prob, part, total)
    others = [
        lax.ppermute(context, "head", [((i + s) % heads, i) for i in range(heads)])
        for s in range(1, heads)
    ]
    return project(context, others, w_out)


def solution(mesh):
    return jax.shard_map(
        on_device,
        mesh=mesh,
        in_specs=(
            P("seq", "head"),
            P("seq", "head"),
            P("seq", "head"),
            P(),
            P(),
            P(),
            P(None, "head"),
        ),
        out_specs=P("seq", "head"),
        check_vma=False,
    )
```

```python
import functools
import math

import jax
import jax.numpy as jnp
from jax import lax
from jax.experimental import pallas as pl
from jax.experimental.pallas import tpu as pltpu
from jax.sharding import PartitionSpec as P

DH = 128
BLOCK = 64
R = 3
G = 2
VMEM = pltpu.MemorySpace.VMEM
SMEM = pltpu.MemorySpace.SMEM
BF16 = jnp.bfloat16
F32 = jnp.float32
I32 = jnp.int32
NONE = -1e30


def params(mib):
    return pltpu.CompilerParams(vmem_limit_bytes=mib * 1024 * 1024)


LIGHT = pl.CostEstimate(flops=1, bytes_accessed=1, transcendentals=0)


def spec(space=VMEM):
    return pl.BlockSpec(memory_space=space)


def rank_kernel(n, per, cap, g_ref, o_ref, spot_ref, arrive_ref, g_pad, o_pad):
    me = lax.axis_index("seq")
    nb = g_ref.shape[1]
    wide = g_pad.shape[1]
    tall = spot_ref.shape[0]
    g_pad[...] = jnp.full(g_pad.shape, -1, I32)
    o_pad[...] = jnp.zeros(o_pad.shape, I32)
    g_pad[:R, :nb] = g_ref[...]
    o_pad[:R, :nb] = o_ref[...]
    g = g_pad[...]
    lane = lax.broadcasted_iota(I32, g.shape, 1)
    place = lane
    for d in range(1, n):
        place = jnp.where(lane >= d * per, lane - d * per, place)
    rank = jnp.zeros(g.shape, I32)
    for s in range(1, per):
        back = pltpu.roll(g, s, axis=1)
        ahead = place >= s
        for r in range(R):
            same = jnp.broadcast_to(back[r : r + 1, :], g.shape) == g
            rank = rank + jnp.where(ahead & same, 1, 0)
    arrive_ref[...] = g * cap + rank
    row = lax.broadcasted_iota(I32, (tall, wide), 0)
    spots = jnp.zeros((tall, wide), F32)
    named = jnp.where(g == me, o_pad[...], 0)
    for s in range(cap):
        picked = jnp.where(rank == s, named, 0).astype(F32)
        total = jnp.sum(picked, axis=0, keepdims=True)
        spots = spots + jnp.where(row == s, jnp.broadcast_to(total, (tall, wide)), 0.0)
    token = lax.broadcasted_iota(I32, (wide, 128), 0)
    first = lax.broadcasted_iota(I32, (wide, 128), 1) * per
    belongs = jnp.where((token >= first) & (token < first + per), 1.0, 0.0)
    spot_ref[...] = jnp.dot(
        spots.astype(BF16), belongs.astype(BF16), preferred_element_type=F32
    ).astype(I32)


def ranks(n, per, cap, groups, offsets):
    nb = groups.shape[1]
    wide = -(-nb // 128) * 128
    tall = -(-cap // 8) * 8
    return pl.pallas_call(
        functools.partial(rank_kernel, n, per, cap),
        out_shape=(
            jax.ShapeDtypeStruct((tall, 128), I32),
            jax.ShapeDtypeStruct((8, wide), I32),
        ),
        in_specs=[spec(), spec()],
        out_specs=(spec(), spec()),
        scratch_shapes=[pltpu.VMEM((8, wide), I32), pltpu.VMEM((8, wide), I32)],
        compiler_params=params(4),
        cost_estimate=LIGHT,
        name="ranks",
    )(groups, offsets)


def gather_kernel(n, cap, far, spot_ref, k_ref, v_ref, *refs):
    half = n // 2
    me = lax.axis_index("seq")
    low = me < half
    base = jnp.where(low != far, 0, half)
    place = jnp.where(low, me, me - half)
    for k, out_ref in enumerate(refs[-half:]):
        d = base + lax.bitwise_xor(place, k)
        for s in range(cap):
            rows = pl.ds(pl.multiple_of(spot_ref[s, d] * BLOCK, BLOCK), BLOCK)
            out_ref[pl.ds(s * BLOCK, BLOCK)] = k_ref[rows]
            out_ref[pl.ds((cap + s) * BLOCK, BLOCK)] = v_ref[rows]


def gather(n, cap, far, spots, k, v, earlier=()):
    half = n // 2
    out = jax.ShapeDtypeStruct((2 * cap * BLOCK, k.shape[1]), BF16)
    return pl.pallas_call(
        functools.partial(gather_kernel, n, cap, far),
        out_shape=(out,) * half,
        in_specs=[spec(SMEM), spec(), spec()] + [spec(pl.ANY)] * len(earlier),
        out_specs=(spec(),) * half,
        compiler_params=params(8),
        cost_estimate=LIGHT,
        name="gather_blocks",
    )(spots, k, v, *earlier)


def exchange(parts, n):
    got = [parts[0]]
    for k in range(1, n // 2):
        got.append(lax.ppermute(parts[k], "seq", [(i, i ^ k) for i in range(n)]))
    return got


def pack_kernel(per, glob_ref, k_ref, v_ref, first_ref, last_ref, cand_ref):
    rows = per * BLOCK
    for c, source in enumerate((k_ref, v_ref)):
        at = pl.ds(c * BLOCK, BLOCK)
        first_ref[at] = source[:BLOCK]
        last_ref[at] = source[rows - BLOCK :]
        for g in range(G):
            start = pl.multiple_of(lax.rem(glob_ref[g], per) * BLOCK, BLOCK)
            cand_ref[pl.ds((c * G + g) * BLOCK, BLOCK)] = source[pl.ds(start, BLOCK)]


def pack(per, glob, k, v):
    columns = k.shape[1]
    edge = jax.ShapeDtypeStruct((2 * BLOCK, columns), BF16)
    return pl.pallas_call(
        functools.partial(pack_kernel, per),
        out_shape=(edge, edge, jax.ShapeDtypeStruct((2 * G * BLOCK, columns), BF16)),
        in_specs=[spec(SMEM), spec(), spec()],
        out_specs=(spec(), spec(), spec()),
        compiler_params=params(4),
        cost_estimate=LIGHT,
        name="pack",
    )(glob, k, v)


def merge_kernel(per, known, glob_ref, own_ref, got_ref, out_ref):
    me = lax.axis_index("seq")
    for g in range(G):
        differ = lax.bitwise_xor(me, lax.div(glob_ref[g], per))
        have = lax.bitwise_and(differ, jnp.int32(~known)) == 0
        for c in range(2):
            at = pl.ds((c * G + g) * BLOCK, BLOCK)
            out_ref[at] = jnp.where(have, own_ref[at], got_ref[at])


def spread(rows, glob, per, n):
    known, steps = 0, []
    for bit in reversed(range(n.bit_length() - 1)):
        pairs = [(i, i ^ (1 << bit)) for i in range(n)]
        got = lax.ppermute(rows, "seq", pairs)
        rows = pl.pallas_call(
            functools.partial(merge_kernel, per, known),
            out_shape=jax.ShapeDtypeStruct(rows.shape, BF16),
            in_specs=[spec(SMEM), spec(), spec()],
            out_specs=spec(),
            compiler_params=params(4),
            cost_estimate=LIGHT,
            name="merge",
        )(glob, rows, got)
        known |= 1 << bit
        steps.append(rows)
    return steps


def choose(n, cap, per, arrive_ref, d, got_refs, held, keys, vals):
    half = n // 2
    me = lax.axis_index("seq")
    low = me < half
    mine = jnp.where(low, me, me - half)
    for k, got_ref in enumerate(got_refs):
        held[k] = got_ref[...]
    biases = []
    for i in range(per):
        row = []
        for r in range(R):
            spot = arrive_ref[r, d * per + i]
            group = lax.div(spot, cap)
            here = (group < half) == low
            slot = jnp.where(here, spot - group * cap, 0)
            place = jnp.where(here, jnp.where(low, group, group - half), mine)
            k = lax.bitwise_xor(place, mine)
            at = pl.ds((i * R + r) * BLOCK, BLOCK)
            keys[at] = held[k, pl.ds(pl.multiple_of(slot * BLOCK, BLOCK), BLOCK), :]
            vals[at] = held[k, pl.ds(pl.multiple_of((cap + slot) * BLOCK, BLOCK), BLOCK), :]
            row.append(jnp.where(here, 0.0, NONE))
        biases.append(row)
    return biases


def widen(biases):
    lane = lax.broadcasted_iota(I32, (1, R * BLOCK), 1)
    bias = jnp.full((1, R * BLOCK), biases[-1], F32)
    for r in reversed(range(R - 1)):
        bias = jnp.where(lane < (r + 1) * BLOCK, biases[r], bias)
    return bias


def batches(per, heads, step):
    for first in range(0, per, step):
        yield [(i, h) for i in range(first, min(per, first + step)) for h in range(heads)]


def rows_of(i):
    return pl.ds(i * BLOCK, BLOCK)


def picked_of(i):
    return pl.ds(i * R * BLOCK, R * BLOCK)


def cols_of(h):
    return pl.ds(h * DH, DH)


def dot_t(a, b):
    return lax.dot_general(a, b, (((1,), (1,)), ((), ())), preferred_element_type=F32)


def eye():
    shape = (BLOCK, BLOCK)
    return lax.broadcasted_iota(I32, shape, 0) == lax.broadcasted_iota(I32, shape, 1)


def far_kernel(n, cap, per, heads, arrive_ref, q_ref, *refs):
    half = n // 2
    got_refs, (out_ref, stat_ref, held, keys, vals) = refs[:half], refs[-5:]
    d = lax.bitwise_xor(lax.axis_index("seq"), half)
    scale = 1.0 / math.sqrt(DH)
    diagonal = eye()
    stat_ref[...] = jnp.zeros_like(stat_ref)
    biases = choose(n, cap, per, arrive_ref, d, got_refs, held, keys, vals)
    for pairs in batches(per, heads, 4):
        s = [
            dot_t(q_ref[rows_of(i), cols_of(h)], keys[picked_of(i), cols_of(h)]) * scale
            + widen(biases[i])
            for i, h in pairs
        ]
        top = [jnp.max(x, axis=1, keepdims=True) for x in s]
        w = [jnp.exp(x - t) for x, t in zip(s, top)]
        total = [jnp.sum(x, axis=1, keepdims=True) for x in w]
        part = [
            jnp.dot(x.astype(BF16), vals[picked_of(i), cols_of(h)], preferred_element_type=F32)
            for x, (i, h) in zip(w, pairs)
        ]
        for x, t, (i, h) in zip(part, total, pairs):
            out_ref[rows_of(i), cols_of(h)] = (x / t).astype(BF16)
        for c, columns in enumerate((top, total)):
            flat = [
                jnp.sum(jnp.where(diagonal, x, 0.0), axis=0, keepdims=True) for x in columns
            ]
            for x, (i, h) in zip(flat, pairs):
                stat_ref[pl.ds(i * heads + h, 1), pl.ds(c * BLOCK, BLOCK)] = x


def far_part(n, cap, per, arrive, q, got, earlier):
    rows, columns = q.shape
    heads = columns // DH
    return pl.pallas_call(
        functools.partial(far_kernel, n, cap, per, heads),
        out_shape=(
            jax.ShapeDtypeStruct((rows, columns), BF16),
            jax.ShapeDtypeStruct((-(-per * heads // 8) * 8, 128), F32),
        ),
        in_specs=[spec(SMEM), spec()] + [spec()] * len(got) + [spec(pl.ANY)] * len(earlier),
        out_specs=(spec(), spec()),
        scratch_shapes=[pltpu.VMEM((n // 2,) + got[0].shape, BF16)]
        + [pltpu.VMEM((rows * R, columns), BF16)] * 2,
        compiler_params=params(16),
        cost_estimate=LIGHT,
        name="far_part",
    )(arrive, q, *got, *earlier)


def near_kernel(
    per, heads, q_ref, k_ref, v_ref, before_ref, after_ref, glob_ref, part_ref, stat_ref,
    keys, vals,
):
    rows = per * BLOCK
    keys[:BLOCK] = before_ref[:BLOCK]
    vals[:BLOCK] = before_ref[BLOCK:]
    keys[pl.ds(BLOCK, rows)] = k_ref[...]
    vals[pl.ds(BLOCK, rows)] = v_ref[...]
    keys[pl.ds(BLOCK + rows, BLOCK)] = after_ref[:BLOCK]
    vals[pl.ds(BLOCK + rows, BLOCK)] = after_ref[BLOCK:]
    scale = 1.0 / math.sqrt(DH)
    for i in range(per):
        at = pl.ds(i * BLOCK, BLOCK)
        window = pl.ds(i * BLOCK, 3 * BLOCK)
        for h in range(heads):
            cols = pl.ds(h * DH, DH)
            q = q_ref[at, cols]
            s_w = dot_t(q, keys[window, cols]) * scale
            s_g = dot_t(q, glob_ref[: G * BLOCK, cols]) * scale
            top = jnp.maximum(
                jnp.max(s_g, axis=1, keepdims=True), jnp.max(s_w, axis=1, keepdims=True)
            )
            w_w, w_g = jnp.exp(s_w - top), jnp.exp(s_g - top)
            total = jnp.sum(w_w, axis=1, keepdims=True) + jnp.sum(w_g, axis=1, keepdims=True)
            part = jnp.dot(w_w.astype(BF16), vals[window, cols], preferred_element_type=F32)
            part_ref[at, cols] = part + jnp.dot(
                w_g.astype(BF16), glob_ref[G * BLOCK :, cols], preferred_element_type=F32
            )
            stat_ref[at, 2 * h : 2 * h + 1] = top
            stat_ref[at, 2 * h + 1 : 2 * h + 2] = total


def near_part(per, q, k, v, before, after, glob):
    rows, columns = q.shape
    heads = columns // DH
    return pl.pallas_call(
        functools.partial(near_kernel, per, heads),
        out_shape=(
            jax.ShapeDtypeStruct((rows, columns), F32),
            jax.ShapeDtypeStruct((rows, 128), F32),
        ),
        in_specs=[spec()] * 6,
        out_specs=(spec(), spec()),
        scratch_shapes=[pltpu.VMEM((rows + 2 * BLOCK, columns), BF16)] * 2,
        compiler_params=params(16),
        cost_estimate=LIGHT,
        name="near_part",
    )(q, k, v, before, after, glob)


def own_kernel(n, cap, per, heads, arrive_ref, q_ref, near_ref, near_stat_ref, *refs):
    half = n // 2
    got_refs, (part_ref, stat_ref, held, keys, vals) = refs[:half], refs[-5:]
    d = lax.axis_index("seq")
    scale = 1.0 / math.sqrt(DH)
    biases = choose(n, cap, per, arrive_ref, d, got_refs, held, keys, vals)
    for pairs in batches(per, heads, 4):
        s = [
            dot_t(q_ref[rows_of(i), cols_of(h)], keys[picked_of(i), cols_of(h)]) * scale
            + widen(biases[i])
            for i, h in pairs
        ]
        near_top = [near_stat_ref[rows_of(i), 2 * h : 2 * h + 1] for i, h in pairs]
        top = [jnp.maximum(jnp.max(x, axis=1, keepdims=True), t) for x, t in zip(s, near_top)]
        w = [jnp.exp(x - t) for x, t in zip(s, top)]
        near_w = [jnp.exp(x - t) for x, t in zip(near_top, top)]
        total = [
            jnp.sum(x, axis=1, keepdims=True)
            + y * near_stat_ref[rows_of(i), 2 * h + 1 : 2 * h + 2]
            for x, y, (i, h) in zip(w, near_w, pairs)
        ]
        part = [
            jnp.dot(x.astype(BF16), vals[picked_of(i), cols_of(h)], preferred_element_type=F32)
            for x, (i, h) in zip(w, pairs)
        ]
        for j, (i, h) in enumerate(pairs):
            part_ref[rows_of(i), cols_of(h)] = (
                part[j] + near_ref[rows_of(i), cols_of(h)] * near_w[j]
            )
            stat_ref[rows_of(i), 2 * h : 2 * h + 1] = top[j]
            stat_ref[rows_of(i), 2 * h + 1 : 2 * h + 2] = total[j]


def own_part(n, cap, per, arrive, q, near, near_stat, got):
    rows, columns = q.shape
    heads = columns // DH
    return pl.pallas_call(
        functools.partial(own_kernel, n, cap, per, heads),
        out_shape=(
            jax.ShapeDtypeStruct((rows, columns), F32),
            jax.ShapeDtypeStruct((rows, 128), F32),
        ),
        in_specs=[spec(SMEM)] + [spec()] * (3 + len(got)),
        out_specs=(spec(), spec()),
        scratch_shapes=[pltpu.VMEM((n // 2,) + got[0].shape, BF16)]
        + [pltpu.VMEM((rows * R, columns), BF16)] * 2,
        compiler_params=params(16),
        cost_estimate=LIGHT,
        name="own_part",
    )(arrive, q, near, near_stat, *got)


def merge_kernel_far(per, heads, part_ref, stat_ref, far_ref, far_stat_ref, out_ref):
    diagonal = eye()
    for pairs in batches(per, heads, 4):
        far_top, far_total = [
            [
                jnp.sum(
                    jnp.where(
                        diagonal,
                        far_stat_ref[pl.ds(i * heads + h, 1), pl.ds(c * BLOCK, BLOCK)],
                        0.0,
                    ),
                    axis=1, keepdims=True,
                )
                for i, h in pairs
            ]
            for c in range(2)
        ]
        for j, (i, h) in enumerate(pairs):
            own_top = stat_ref[rows_of(i), 2 * h : 2 * h + 1]
            own_total = stat_ref[rows_of(i), 2 * h + 1 : 2 * h + 2]
            top = jnp.maximum(own_top, far_top[j])
            own_w = jnp.exp(own_top - top)
            far_w = jnp.exp(far_top[j] - top) * far_total[j]
            total = own_w * own_total + far_w
            out_ref[rows_of(i), cols_of(h)] = (
                part_ref[rows_of(i), cols_of(h)] * (own_w / total)
                + far_ref[rows_of(i), cols_of(h)].astype(F32) * (far_w / total)
            ).astype(BF16)


def contexts(per, part, stat, far, far_stat):
    rows, columns = part.shape
    heads = columns // DH
    return pl.pallas_call(
        functools.partial(merge_kernel_far, per, heads),
        out_shape=jax.ShapeDtypeStruct((rows, columns), BF16),
        in_specs=[spec()] * 4,
        out_specs=spec(),
        compiler_params=params(8),
        cost_estimate=LIGHT,
        name="contexts",
    )(part, stat, far, far_stat)


def project_kernel(own_ref, other_refs, w_ref, out_ref):
    me = lax.axis_index("head")
    count = lax.axis_size("head")
    columns = own_ref.shape[1]
    total = None
    for step, rows_ref in enumerate([own_ref] + list(other_refs)):
        owner = lax.rem(me + step, count)
        at = pl.ds(pl.multiple_of(owner * columns, columns), columns)
        term = jnp.dot(rows_ref[...], w_ref[at, :], preferred_element_type=F32)
        total = term if total is None else total + term
    out_ref[...] = total.astype(BF16)


def project(own, others, w_out):
    rows, columns = own.shape
    wide = w_out.shape[1]
    tile = rows // 4
    block = pl.BlockSpec((tile, columns), lambda i: (i, 0))

    def kernel(own_ref, *refs):
        project_kernel(own_ref, refs[: len(others)], refs[-2], refs[-1])

    return pl.pallas_call(
        kernel,
        grid=(4,),
        out_shape=jax.ShapeDtypeStruct((rows, wide), BF16),
        in_specs=[block] * (1 + len(others)) + [spec()],
        out_specs=pl.BlockSpec((tile, wide), lambda i: (i, 0)),
        compiler_params=params(16),
        cost_estimate=LIGHT,
        name="project",
    )(own, *others, w_out)


def on_device(queries, keys, values, rand_group, rand_offset, glob_blocks, w_out):
    tokens_dev = queries.shape[0]
    per = tokens_dev // BLOCK
    n = lax.axis_size("seq")
    heads = lax.axis_size("head")
    cap = max(2, (rand_group.shape[0] // n * R + n - 1) // n)

    up = [(i, (i + 1) % n) for i in range(n)]
    down = [(j, i) for i, j in up]
    partners = [(i, (i + n // 2) % n) for i in range(n)]
    first, last, cand = pack(per, glob_blocks, keys, values)
    before = lax.ppermute(last, "seq", up)
    after = lax.ppermute(first, "seq", down)
    far_q = lax.ppermute(queries, "seq", partners)
    steps = spread(cand, glob_blocks, per, n)

    spots, arrive = ranks(n, per, cap, rand_group.T, rand_offset.T)
    got_far = exchange(gather(n, cap, True, spots, keys, values), n)
    own = gather(n, cap, False, spots, keys, values)
    got_own = exchange(own, n)
    far, far_stat = far_part(n, cap, per, arrive, far_q, got_far, [own[1]])
    far = lax.ppermute(far, "seq", partners)
    far_stat = lax.ppermute(far_stat, "seq", partners)
    near, near_stat = near_part(per, queries, keys, values, before, after, steps[-1])
    part, stat = own_part(n, cap, per, arrive, queries, near, near_stat, got_own)
    context = contexts(per, part, stat, far, far_stat)
    others = [
        lax.ppermute(context, "head", [((i + s) % heads, i) for i in range(heads)])
        for s in range(1, heads)
    ]
    return project(context, others, w_out)


def solution(mesh):
    return jax.shard_map(
        on_device,
        mesh=mesh,
        in_specs=(
            P("seq", "head"),
            P("seq", "head"),
            P("seq", "head"),
            P(),
            P(),
            P(),
            P(None, "head"),
        ),
        out_specs=P("seq", "head"),
        check_vma=False,
    )
```

```python
import functools
import math

import jax
import jax.numpy as jnp
from jax import lax
from jax.experimental import pallas as pl
from jax.experimental.pallas import tpu as pltpu
from jax.sharding import PartitionSpec as P

DH = 128
BLOCK = 64
R = 3
G = 2
VMEM = pltpu.MemorySpace.VMEM
SMEM = pltpu.MemorySpace.SMEM
BF16 = jnp.bfloat16
F32 = jnp.float32
I32 = jnp.int32
NONE = -1e30


def params(mib):
    return pltpu.CompilerParams(vmem_limit_bytes=mib * 1024 * 1024)


LIGHT = pl.CostEstimate(flops=1, bytes_accessed=1, transcendentals=0)


def spec(space=VMEM):
    return pl.BlockSpec(memory_space=space)


def rank_kernel(n, per, cap, g_ref, o_ref, spot_ref, arrive_ref, g_pad, o_pad):
    me = lax.axis_index("seq")
    nb = g_ref.shape[1]
    wide = g_pad.shape[1]
    tall = spot_ref.shape[0]
    g_pad[...] = jnp.full(g_pad.shape, -1, I32)
    o_pad[...] = jnp.zeros(o_pad.shape, I32)
    g_pad[:R, :nb] = g_ref[...]
    o_pad[:R, :nb] = o_ref[...]
    g = g_pad[...]
    lane = lax.broadcasted_iota(I32, g.shape, 1)
    place = lane
    for d in range(1, n):
        place = jnp.where(lane >= d * per, lane - d * per, place)
    rank = jnp.zeros(g.shape, I32)
    for s in range(1, per):
        back = pltpu.roll(g, s, axis=1)
        ahead = place >= s
        for r in range(R):
            same = jnp.broadcast_to(back[r : r + 1, :], g.shape) == g
            rank = rank + jnp.where(ahead & same, 1, 0)
    arrive_ref[...] = g * cap + rank
    row = lax.broadcasted_iota(I32, (tall, wide), 0)
    spots = jnp.zeros((tall, wide), F32)
    for side in range(2):
        named = jnp.where(g == lax.bitwise_xor(me, side * (n // 4)), o_pad[...], 0)
        for s in range(cap):
            picked = jnp.where(rank == s, named, 0).astype(F32)
            total = jnp.sum(picked, axis=0, keepdims=True)
            here = row == side * cap + s
            spots = spots + jnp.where(here, jnp.broadcast_to(total, (tall, wide)), 0.0)
    token = lax.broadcasted_iota(I32, (wide, 128), 0)
    first = lax.broadcasted_iota(I32, (wide, 128), 1) * per
    belongs = jnp.where((token >= first) & (token < first + per), 1.0, 0.0)
    spot_ref[...] = jnp.dot(
        spots.astype(BF16), belongs.astype(BF16), preferred_element_type=F32
    ).astype(I32)


def ranks(n, per, cap, groups, offsets):
    nb = groups.shape[1]
    wide = -(-nb // 128) * 128
    tall = -(-2 * cap // 8) * 8
    return pl.pallas_call(
        functools.partial(rank_kernel, n, per, cap),
        out_shape=(
            jax.ShapeDtypeStruct((tall, 128), I32),
            jax.ShapeDtypeStruct((8, wide), I32),
        ),
        in_specs=[spec(), spec()],
        out_specs=(spec(), spec()),
        scratch_shapes=[pltpu.VMEM((8, wide), I32), pltpu.VMEM((8, wide), I32)],
        compiler_params=params(4),
        cost_estimate=LIGHT,
        name="ranks",
    )(groups, offsets)


def gather_kernel(n, cap, side, users, glob, spot_ref, k_ref, v_ref, *refs):
    plane = n // 4
    me = lax.axis_index("seq")
    size = 2 * cap * BLOCK
    for k, out_ref in enumerate(refs[-plane:]):
        for u, far in enumerate(users):
            d = lax.bitwise_xor(me, k + (n // 2 if far else 0))
            for s in range(cap):
                start = spot_ref[side * cap + s, d] * BLOCK
                rows = pl.ds(pl.multiple_of(start, BLOCK), BLOCK)
                out_ref[pl.ds(u * size + s * BLOCK, BLOCK)] = k_ref[rows]
                out_ref[pl.ds(u * size + (cap + s) * BLOCK, BLOCK)] = v_ref[rows]
        if glob:
            out_ref[pl.ds(len(users) * size, 2 * G * BLOCK)] = refs[0][...]


def gather(n, cap, side, users, spots, k, v, glob=None, earlier=()):
    plane = n // 4
    extra = [] if glob is None else [glob]
    rows = 2 * cap * BLOCK * len(users) + 2 * G * BLOCK * len(extra)
    out = jax.ShapeDtypeStruct((rows, k.shape[1]), BF16)
    return pl.pallas_call(
        functools.partial(gather_kernel, n, cap, side, users, bool(extra)),
        out_shape=(out,) * plane,
        in_specs=[spec(SMEM)] + [spec()] * (2 + len(extra)) + [spec(pl.ANY)] * len(earlier),
        out_specs=(spec(),) * plane,
        compiler_params=params(8),
        cost_estimate=LIGHT,
        name="gather_blocks",
    )(spots, k, v, *extra, *earlier)


def exchange(parts, n):
    got = [parts[0]]
    for k in range(1, n // 4):
        got.append(lax.ppermute(parts[k], "seq", [(i, i ^ k) for i in range(n)]))
    return got


def pack_kernel(per, glob_ref, k_ref, v_ref, first_ref, last_ref, cand_ref):
    rows = per * BLOCK
    for c, source in enumerate((k_ref, v_ref)):
        at = pl.ds(c * BLOCK, BLOCK)
        first_ref[at] = source[:BLOCK]
        last_ref[at] = source[rows - BLOCK :]
        for g in range(G):
            start = pl.multiple_of(lax.rem(glob_ref[g], per) * BLOCK, BLOCK)
            cand_ref[pl.ds((c * G + g) * BLOCK, BLOCK)] = source[pl.ds(start, BLOCK)]


def pack(per, glob, k, v):
    columns = k.shape[1]
    edge = jax.ShapeDtypeStruct((2 * BLOCK, columns), BF16)
    return pl.pallas_call(
        functools.partial(pack_kernel, per),
        out_shape=(edge, edge, jax.ShapeDtypeStruct((2 * G * BLOCK, columns), BF16)),
        in_specs=[spec(SMEM), spec(), spec()],
        out_specs=(spec(), spec(), spec()),
        compiler_params=params(4),
        cost_estimate=LIGHT,
        name="pack",
    )(glob, k, v)


def merge_kernel(per, known, glob_ref, own_ref, got_ref, out_ref):
    me = lax.axis_index("seq")
    for g in range(G):
        differ = lax.bitwise_xor(me, lax.div(glob_ref[g], per))
        have = lax.bitwise_and(differ, jnp.int32(~known)) == 0
        for c in range(2):
            at = pl.ds((c * G + g) * BLOCK, BLOCK)
            out_ref[at] = jnp.where(have, own_ref[at], got_ref[at])


def spread(rows, glob, per, n):
    known = 0
    for step in (n // 2, n // 4):
        pairs = [(i, i ^ step) for i in range(n)]
        got = lax.ppermute(rows, "seq", pairs)
        rows = pl.pallas_call(
            functools.partial(merge_kernel, per, known),
            out_shape=jax.ShapeDtypeStruct(rows.shape, BF16),
            in_specs=[spec(SMEM), spec(), spec()],
            out_specs=spec(),
            compiler_params=params(4),
            cost_estimate=LIGHT,
            name="merge",
        )(glob, rows, got)
        known |= step
    return rows


def choose(n, cap, per, arrive_ref, d, got_refs, skip, held, keys, vals):
    half, plane = n // 2, n // 4
    me = lax.axis_index("seq")
    size = held.shape[1]
    for k, got_ref in enumerate(got_refs):
        held[k] = got_ref[pl.ds(skip if k < plane else 0, size)]
    biases = []
    for i in range(per):
        row = []
        for r in range(R):
            spot = arrive_ref[r, d * per + i]
            group = lax.div(spot, cap)
            differ = lax.bitwise_xor(group, me)
            here = differ < half
            slot = jnp.where(here, spot - group * cap, 0)
            k = jnp.where(here, differ, 0)
            at = pl.ds((i * R + r) * BLOCK, BLOCK)
            keys[at] = held[k, pl.ds(pl.multiple_of(slot * BLOCK, BLOCK), BLOCK), :]
            vals[at] = held[k, pl.ds(pl.multiple_of((cap + slot) * BLOCK, BLOCK), BLOCK), :]
            row.append(jnp.where(here, 0.0, NONE))
        biases.append(row)
    return biases


def flatten(columns, diagonal):
    return [jnp.sum(jnp.where(diagonal, x, 0.0), axis=0, keepdims=True) for x in columns]


def widen(biases):
    lane = lax.broadcasted_iota(I32, (1, R * BLOCK), 1)
    bias = jnp.full((1, R * BLOCK), biases[-1], F32)
    for r in reversed(range(R - 1)):
        bias = jnp.where(lane < (r + 1) * BLOCK, biases[r], bias)
    return bias


def batches(per, heads, step):
    for first in range(0, per, step):
        yield [(i, h) for i in range(first, min(per, first + step)) for h in range(heads)]


def rows_of(i):
    return pl.ds(i * BLOCK, BLOCK)


def picked_of(i):
    return pl.ds(i * R * BLOCK, R * BLOCK)


def cols_of(h):
    return pl.ds(h * DH, DH)


def dot_t(a, b):
    return lax.dot_general(a, b, (((1,), (1,)), ((), ())), preferred_element_type=F32)


def eye():
    shape = (BLOCK, BLOCK)
    return lax.broadcasted_iota(I32, shape, 0) == lax.broadcasted_iota(I32, shape, 1)


def far_kernel(n, cap, per, heads, arrive_ref, q_ref, *refs):
    half = n // 2
    got_refs, (out_ref, stat_ref, held, keys, vals) = refs[:half], refs[-5:]
    d = lax.bitwise_xor(lax.axis_index("seq"), half)
    scale = 1.0 / math.sqrt(DH)
    diagonal = eye()
    stat_ref[...] = jnp.zeros_like(stat_ref)
    biases = choose(n, cap, per, arrive_ref, d, got_refs, 0, held, keys, vals)
    for pairs in batches(per, heads, 4):
        s = [
            dot_t(q_ref[rows_of(i), cols_of(h)], keys[picked_of(i), cols_of(h)]) * scale
            + widen(biases[i])
            for i, h in pairs
        ]
        top = [jnp.max(x, axis=1, keepdims=True) for x in s]
        w = [jnp.exp(x - t) for x, t in zip(s, top)]
        total = [jnp.sum(x, axis=1, keepdims=True) for x in w]
        part = [
            jnp.dot(x.astype(BF16), vals[picked_of(i), cols_of(h)], preferred_element_type=F32)
            for x, (i, h) in zip(w, pairs)
        ]
        for x, t, (i, h) in zip(part, total, pairs):
            out_ref[rows_of(i), cols_of(h)] = (x / t).astype(BF16)
        for c, columns in enumerate((top, total)):
            for x, (i, h) in zip(flatten(columns, diagonal), pairs):
                stat_ref[pl.ds(i * heads + h, 1), pl.ds(c * BLOCK, BLOCK)] = x


def stat_shape(per, heads):
    return jax.ShapeDtypeStruct((-(-per * heads // 8) * 8, 2 * BLOCK), F32)


def far_part(n, cap, per, arrive, q, got, earlier):
    rows, columns = q.shape
    heads = columns // DH
    return pl.pallas_call(
        functools.partial(far_kernel, n, cap, per, heads),
        out_shape=(jax.ShapeDtypeStruct((rows, columns), BF16), stat_shape(per, heads)),
        in_specs=[spec(SMEM), spec()] + [spec()] * len(got) + [spec(pl.ANY)] * len(earlier),
        out_specs=(spec(), spec()),
        scratch_shapes=[pltpu.VMEM((n // 2, 2 * cap * BLOCK, columns), BF16)]
        + [pltpu.VMEM((rows * R, columns), BF16)] * 2,
        compiler_params=params(16),
        cost_estimate=LIGHT,
        name="far_part",
    )(arrive, q, *got, *earlier)


def own_kernel(
    n, cap, per, heads, arrive_ref, place_ref, q_ref, k_ref, v_ref, before_ref, after_ref, *refs
):
    half, plane = n // 2, n // 4
    got_refs = refs[:half]
    part_ref, stat_ref, keys, vals, glob, held, rand_keys, rand_vals = refs[-8:]
    me = lax.axis_index("seq")
    rows = per * BLOCK
    size = held.shape[1]
    for g in range(G):
        owner = lax.div(place_ref[g], per)
        k = lax.bitwise_and(lax.bitwise_xor(owner, me), plane - 1)
        for p in range(plane):
            @pl.when(k == p)
            def _(g=g, p=p):
                for c in range(2):
                    at = (c * G + g) * BLOCK
                    glob[pl.ds(at, BLOCK)] = got_refs[plane + p][pl.ds(size + at, BLOCK)]
    keys[:BLOCK] = before_ref[:BLOCK]
    vals[:BLOCK] = before_ref[BLOCK:]
    keys[pl.ds(BLOCK, rows)] = k_ref[...]
    vals[pl.ds(BLOCK, rows)] = v_ref[...]
    keys[pl.ds(BLOCK + rows, BLOCK)] = after_ref[:BLOCK]
    vals[pl.ds(BLOCK + rows, BLOCK)] = after_ref[BLOCK:]
    scale = 1.0 / math.sqrt(DH)
    diagonal = eye()
    stat_ref[...] = jnp.zeros_like(stat_ref)
    biases = choose(n, cap, per, arrive_ref, me, got_refs, size, held, rand_keys, rand_vals)
    for pairs in batches(per, heads, 2):
        sets = []
        for i, h in pairs:
            window, cols = pl.ds(i * BLOCK, 3 * BLOCK), cols_of(h)
            sets.append(
                (
                    (keys[window, cols], vals[window, cols]),
                    (glob[: G * BLOCK, cols], glob[G * BLOCK :, cols]),
                    (rand_keys[picked_of(i), cols], rand_vals[picked_of(i), cols]),
                )
            )
        s = [
            [dot_t(q_ref[rows_of(i), cols_of(h)], ks) * scale for ks, vs in three]
            for three, (i, h) in zip(sets, pairs)
        ]
        s = [[x, y, z + widen(biases[i])] for (x, y, z), (i, h) in zip(s, pairs)]
        top = [[jnp.max(x, axis=1, keepdims=True) for x in three] for three in s]
        top = [jnp.maximum(jnp.maximum(x, y), z) for x, y, z in top]
        w = [[jnp.exp(x - t) for x in three] for three, t in zip(s, top)]
        total = [[jnp.sum(x, axis=1, keepdims=True) for x in three] for three in w]
        total = [x + y + z for x, y, z in total]
        part = [
            [
                jnp.dot(x.astype(BF16), vs, preferred_element_type=F32)
                for x, (ks, vs) in zip(three, kv)
            ]
            for three, kv in zip(w, sets)
        ]
        for (x, y, z), (i, h) in zip(part, pairs):
            part_ref[rows_of(i), cols_of(h)] = x + y + z
        for c, columns in enumerate((top, total)):
            for x, (i, h) in zip(flatten(columns, diagonal), pairs):
                stat_ref[pl.ds(i * heads + h, 1), pl.ds(c * BLOCK, BLOCK)] = x


def own_part(n, cap, per, arrive, places, q, k, v, before, after, got):
    rows, columns = q.shape
    heads = columns // DH
    return pl.pallas_call(
        functools.partial(own_kernel, n, cap, per, heads),
        out_shape=(jax.ShapeDtypeStruct((rows, columns), F32), stat_shape(per, heads)),
        in_specs=[spec(SMEM)] * 2 + [spec()] * (5 + len(got)),
        out_specs=(spec(), spec()),
        scratch_shapes=[pltpu.VMEM((rows + 2 * BLOCK, columns), BF16)] * 2
        + [pltpu.VMEM((2 * G * BLOCK, columns), BF16)]
        + [pltpu.VMEM((n // 2, 2 * cap * BLOCK, columns), BF16)]
        + [pltpu.VMEM((rows * R, columns), BF16)] * 2,
        compiler_params=params(20),
        cost_estimate=LIGHT,
        name="own_part",
    )(arrive, places, q, k, v, before, after, *got)


def context_kernel(per, heads, part_ref, stat_ref, far_ref, far_stat_ref, out_ref):
    own, far = stat_ref[...], far_stat_ref[...]
    own_top, far_top = own[:, :BLOCK], far[:, :BLOCK]
    top = jnp.maximum(own_top, far_top)
    own_w = jnp.exp(own_top - top)
    far_w = jnp.exp(far_top - top) * far[:, BLOCK:]
    total = own_w * own[:, BLOCK:] + far_w
    used = lax.broadcasted_iota(I32, total.shape, 0) < per * heads
    total = jnp.where(used, total, 1.0)
    own_w = jnp.transpose(own_w / total)
    far_w = jnp.transpose(far_w / total)
    for i in range(per):
        for h in range(heads):
            j = i * heads + h
            out_ref[rows_of(i), cols_of(h)] = (
                part_ref[rows_of(i), cols_of(h)] * own_w[:, j : j + 1]
                + far_ref[rows_of(i), cols_of(h)].astype(F32) * far_w[:, j : j + 1]
            ).astype(BF16)


def contexts(per, part, stat, far, far_stat):
    rows, columns = part.shape
    heads = columns // DH
    return pl.pallas_call(
        functools.partial(context_kernel, per, heads),
        out_shape=jax.ShapeDtypeStruct((rows, columns), BF16),
        in_specs=[spec()] * 4,
        out_specs=spec(),
        compiler_params=params(8),
        cost_estimate=LIGHT,
        name="contexts",
    )(part, stat, far, far_stat)


def project_kernel(own_ref, other_refs, w_ref, out_ref):
    me = lax.axis_index("head")
    count = lax.axis_size("head")
    columns = own_ref.shape[1]
    total = None
    for step, rows_ref in enumerate([own_ref] + list(other_refs)):
        owner = lax.rem(me + step, count)
        at = pl.ds(pl.multiple_of(owner * columns, columns), columns)
        term = jnp.dot(rows_ref[...], w_ref[at, :], preferred_element_type=F32)
        total = term if total is None else total + term
    out_ref[...] = total.astype(BF16)


def project(own, others, w_out):
    rows, columns = own.shape
    wide = w_out.shape[1]
    tile = rows // 4
    block = pl.BlockSpec((tile, columns), lambda i: (i, 0))

    def kernel(own_ref, *refs):
        project_kernel(own_ref, refs[: len(others)], refs[-2], refs[-1])

    return pl.pallas_call(
        kernel,
        grid=(4,),
        out_shape=jax.ShapeDtypeStruct((rows, wide), BF16),
        in_specs=[block] * (1 + len(others)) + [spec()],
        out_specs=pl.BlockSpec((tile, wide), lambda i: (i, 0)),
        compiler_params=params(16),
        cost_estimate=LIGHT,
        name="project",
    )(own, *others, w_out)


def on_device(queries, keys, values, rand_group, rand_offset, glob_blocks, w_out):
    tokens_dev = queries.shape[0]
    per = tokens_dev // BLOCK
    n = lax.axis_size("seq")
    heads = lax.axis_size("head")
    cap = max(2, (rand_group.shape[0] // n * R + n - 1) // n)

    up = [(i, (i + 1) % n) for i in range(n)]
    down = [(j, i) for i, j in up]
    mates = [(i, i ^ (n // 4)) for i in range(n)]
    partners = [(i, i ^ (n // 2)) for i in range(n)]
    mate_k = lax.ppermute(keys, "seq", mates)
    mate_v = lax.ppermute(values, "seq", mates)
    far_q = lax.ppermute(queries, "seq", partners)
    first, last, cand = pack(per, glob_blocks, keys, values)
    glob = spread(cand, glob_blocks, per, n)
    before = lax.ppermute(last, "seq", up)
    after = lax.ppermute(first, "seq", down)

    spots, arrive = ranks(n, per, cap, rand_group.T, rand_offset.T)
    both = exchange(gather(n, cap, 0, (True, False), spots, keys, values), n)
    far_parts = gather(n, cap, 1, (True,), spots, mate_k, mate_v)
    own_parts = gather(n, cap, 1, (False,), spots, mate_k, mate_v, glob, [far_parts[0]])
    far_got = both + exchange(far_parts, n)
    own_got = both + exchange(own_parts, n)
    far, far_stat = far_part(n, cap, per, arrive, far_q, far_got, [own_parts[0]])
    far = lax.ppermute(far, "seq", partners)
    far_stat = lax.ppermute(far_stat, "seq", partners)
    part, stat = own_part(
        n, cap, per, arrive, glob_blocks, queries, keys, values, before, after, own_got
    )
    context = contexts(per, part, stat, far, far_stat)
    others = [
        lax.ppermute(context, "head", [((i + s) % heads, i) for i in range(heads)])
        for s in range(1, heads)
    ]
    return project(context, others, w_out)


def solution(mesh):
    return jax.shard_map(
        on_device,
        mesh=mesh,
        in_specs=(
            P("seq", "head"),
            P("seq", "head"),
            P("seq", "head"),
            P(),
            P(),
            P(),
            P(None, "head"),
        ),
        out_specs=P("seq", "head"),
        check_vma=False,
    )
```

```python
import functools
import math

import jax
import jax.numpy as jnp
from jax import lax
from jax.experimental import pallas as pl
from jax.experimental.pallas import tpu as pltpu
from jax.sharding import PartitionSpec as P

DH = 128
BLOCK = 64
R = 3
G = 2
VMEM = pltpu.MemorySpace.VMEM
SMEM = pltpu.MemorySpace.SMEM
BF16 = jnp.bfloat16
F32 = jnp.float32
I32 = jnp.int32
NONE = -1e30
PIECES = 3


def params(mib):
    return pltpu.CompilerParams(vmem_limit_bytes=mib * 1024 * 1024)


LIGHT = pl.CostEstimate(flops=1, bytes_accessed=1, transcendentals=0)


def spec(space=VMEM):
    return pl.BlockSpec(memory_space=space)


def rank_kernel(n, per, cap, g_ref, o_ref, spot_ref, arrive_ref, g_pad, o_pad):
    me = lax.axis_index("seq")
    nb = g_ref.shape[1]
    wide = g_pad.shape[1]
    tall = spot_ref.shape[0]
    g_pad[...] = jnp.full(g_pad.shape, -1, I32)
    o_pad[...] = jnp.zeros(o_pad.shape, I32)
    g_pad[:R, :nb] = g_ref[...]
    o_pad[:R, :nb] = o_ref[...]
    g = g_pad[...]
    lane = lax.broadcasted_iota(I32, g.shape, 1)
    place = lane
    for d in range(1, n):
        place = jnp.where(lane >= d * per, lane - d * per, place)
    rank = jnp.zeros(g.shape, I32)
    for s in range(1, per):
        back = pltpu.roll(g, s, axis=1)
        ahead = place >= s
        for r in range(R):
            same = jnp.broadcast_to(back[r : r + 1, :], g.shape) == g
            rank = rank + jnp.where(ahead & same, 1, 0)
    arrive_ref[...] = g * cap + rank
    row = lax.broadcasted_iota(I32, (tall, wide), 0)
    spots = jnp.zeros((tall, wide), F32)
    for side in range(2):
        named = jnp.where(g == lax.bitwise_xor(me, side * (n // 4)), o_pad[...], 0)
        for s in range(cap):
            picked = jnp.where(rank == s, named, 0).astype(F32)
            total = jnp.sum(picked, axis=0, keepdims=True)
            here = row == side * cap + s
            spots = spots + jnp.where(here, jnp.broadcast_to(total, (tall, wide)), 0.0)
    token = lax.broadcasted_iota(I32, (wide, 128), 0)
    first = lax.broadcasted_iota(I32, (wide, 128), 1) * per
    belongs = jnp.where((token >= first) & (token < first + per), 1.0, 0.0)
    spot_ref[...] = jnp.dot(
        spots.astype(BF16), belongs.astype(BF16), preferred_element_type=F32
    ).astype(I32)


def ranks(n, per, cap, groups, offsets):
    nb = groups.shape[1]
    wide = -(-nb // 128) * 128
    tall = -(-2 * cap // 8) * 8
    return pl.pallas_call(
        functools.partial(rank_kernel, n, per, cap),
        out_shape=(
            jax.ShapeDtypeStruct((tall, 128), I32),
            jax.ShapeDtypeStruct((8, wide), I32),
        ),
        in_specs=[spec(), spec()],
        out_specs=(spec(), spec()),
        scratch_shapes=[pltpu.VMEM((8, wide), I32), pltpu.VMEM((8, wide), I32)],
        compiler_params=params(4),
        cost_estimate=LIGHT,
        name="ranks",
    )(groups, offsets)


def gather_kernel(n, per, cap, side, users, glob, spot_ref, k_ref, v_ref, *refs):
    plane = n // 4
    me = lax.axis_index("seq")
    size = 2 * cap * BLOCK
    for k, out_ref in enumerate(refs[-plane:]):
        for u, far in enumerate(users):
            d = lax.bitwise_xor(me, k + (n // 2 if far else 0))
            for s in range(cap):
                start = spot_ref[side * cap + s, d] * BLOCK
                rows = pl.ds(pl.multiple_of(start, BLOCK), BLOCK)
                out_ref[pl.ds(u * size + s * BLOCK, BLOCK)] = k_ref[rows]
                out_ref[pl.ds(u * size + (cap + s) * BLOCK, BLOCK)] = v_ref[rows]
    if glob:
        shared_kernel(n, per, len(users) * size, *refs)


def shared_kernel(n, per, skip, place_ref, own_ref, got_ref, k_ref, v_ref, mk_ref, mv_ref, *refs):
    plane = n // 4
    me = lax.axis_index("seq")
    place = lax.bitwise_and(me, plane - 1)
    even = lax.bitwise_and(me, plane) == 0
    wide = 2 * G * BLOCK
    first, last = pl.ds(0, BLOCK), pl.ds((per - 1) * BLOCK, BLOCK)
    for k, out_ref in enumerate(refs[-plane:]):
        for g in range(G):
            owner = lax.div(place_ref[g], per)
            here = (owner >= n // 2) == (me >= n // 2)
            for c in range(2):
                at = (c * G + g) * BLOCK
                rows = pl.ds(at, BLOCK)
                out_ref[pl.ds(skip + at, BLOCK)] = jnp.where(here, own_ref[rows], got_ref[rows])
        target = lax.bitwise_xor(place, k)
        is_before = lax.rem(place + 1, plane) == target
        is_end = jnp.where(is_before, target == 0, target == plane - 1)
        far = is_end & (is_before == even)
        for c, (own, mate) in enumerate(((k_ref, mk_ref), (v_ref, mv_ref))):
            staged = got_ref[pl.ds(wide + c * BLOCK, BLOCK)]
            mates = jnp.where(is_before, mate[last], mate[first])
            owns = jnp.where(is_before, own[last], own[first])
            out_ref[pl.ds(skip + wide + c * BLOCK, BLOCK)] = jnp.where(
                far, staged, jnp.where(is_end, mates, owns)
            )


def gather(n, per, cap, side, users, spots, k, v, glob=(), earlier=()):
    plane = n // 4
    rows = 2 * cap * BLOCK * len(users) + (2 * (G + 1) * BLOCK if glob else 0)
    out = jax.ShapeDtypeStruct((rows, k.shape[1]), BF16)
    extra = [spec(SMEM)] + [spec()] * 6 if glob else []
    return pl.pallas_call(
        functools.partial(gather_kernel, n, per, cap, side, users, bool(glob)),
        out_shape=(out,) * plane,
        in_specs=[spec(SMEM), spec(), spec()] + extra + [spec(pl.ANY)] * len(earlier),
        out_specs=(spec(),) * plane,
        compiler_params=params(8),
        cost_estimate=LIGHT,
        name="gather_blocks",
    )(spots, k, v, *glob, *earlier)


def exchange(parts, n):
    got = [parts[0]]
    for k in range(1, n // 4):
        got.append(lax.ppermute(parts[k], "seq", [(i, i ^ k) for i in range(n)]))
    return got


def pick_kernel(n, per, place_ref, k_ref, v_ref, mate_k_ref, mate_v_ref, out_ref):
    me = lax.axis_index("seq")
    for g in range(G):
        owner = lax.div(place_ref[g], per)
        start = (place_ref[g] - owner * per) * BLOCK
        rows = pl.ds(pl.multiple_of(start, BLOCK), BLOCK)
        mine = lax.bitwise_and(lax.bitwise_xor(owner, me), n // 4) == 0
        for c, (own, mate) in enumerate(((k_ref, mate_k_ref), (v_ref, mate_v_ref))):
            at = pl.ds((c * G + g) * BLOCK, BLOCK)
            out_ref[at] = jnp.where(mine, own[rows], mate[rows])
    even = lax.bitwise_and(me, n // 4) == 0
    for c, mate in enumerate((mate_k_ref, mate_v_ref)):
        first, last = mate[:BLOCK], mate[(per - 1) * BLOCK :]
        out_ref[pl.ds((2 * G + c) * BLOCK, BLOCK)] = jnp.where(even, last, first)


def pick(n, per, places, k, v, mate_k, mate_v):
    return pl.pallas_call(
        functools.partial(pick_kernel, n, per),
        out_shape=jax.ShapeDtypeStruct((2 * (G + 1) * BLOCK, k.shape[1]), BF16),
        in_specs=[spec(SMEM)] + [spec()] * 4,
        out_specs=spec(),
        compiler_params=params(4),
        cost_estimate=LIGHT,
        name="pick",
    )(places, k, v, mate_k, mate_v)


def choose(n, cap, per, arrive_ref, d, got_refs, skip, held, keys, vals):
    half, plane = n // 2, n // 4
    me = lax.axis_index("seq")
    size = held.shape[1]
    for k, got_ref in enumerate(got_refs):
        held[k] = got_ref[pl.ds(skip if k < plane else 0, size)]
    biases = []
    for i in range(per):
        row = []
        for r in range(R):
            spot = arrive_ref[r, d * per + i]
            group = lax.div(spot, cap)
            differ = lax.bitwise_xor(group, me)
            here = differ < half
            slot = jnp.where(here, spot - group * cap, 0)
            k = jnp.where(here, differ, 0)
            at = pl.ds((i * R + r) * BLOCK, BLOCK)
            keys[at] = held[k, pl.ds(pl.multiple_of(slot * BLOCK, BLOCK), BLOCK), :]
            vals[at] = held[k, pl.ds(pl.multiple_of((cap + slot) * BLOCK, BLOCK), BLOCK), :]
            row.append(jnp.where(here, 0.0, NONE))
        biases.append(row)
    return biases


def flatten(columns, diagonal):
    return [jnp.sum(jnp.where(diagonal, x, 0.0), axis=0, keepdims=True) for x in columns]


def widen(biases):
    lane = lax.broadcasted_iota(I32, (1, R * BLOCK), 1)
    bias = jnp.full((1, R * BLOCK), biases[-1], F32)
    for r in reversed(range(R - 1)):
        bias = jnp.where(lane < (r + 1) * BLOCK, biases[r], bias)
    return bias


def batches(per, heads, step):
    for first in range(0, per, step):
        yield [(i, h) for i in range(first, min(per, first + step)) for h in range(heads)]


def rows_of(i):
    return pl.ds(i * BLOCK, BLOCK)


def picked_of(i):
    return pl.ds(i * R * BLOCK, R * BLOCK)


def cols_of(h):
    return pl.ds(h * DH, DH)


def dot_t(a, b):
    return lax.dot_general(a, b, (((1,), (1,)), ((), ())), preferred_element_type=F32)


def eye():
    shape = (BLOCK, BLOCK)
    return lax.broadcasted_iota(I32, shape, 0) == lax.broadcasted_iota(I32, shape, 1)


def far_kernel(n, cap, per, heads, arrive_ref, q_ref, *refs):
    half = n // 2
    got_refs, (out_ref, held, keys, vals, stat, pieces) = refs[:half], refs[-6:]
    d = lax.bitwise_xor(lax.axis_index("seq"), half)
    scale = 1.0 / math.sqrt(DH)
    diagonal = eye()
    stat[...] = jnp.zeros_like(stat)
    biases = choose(n, cap, per, arrive_ref, d, got_refs, 0, held, keys, vals)
    for pairs in batches(per, heads, 4):
        s = [
            dot_t(q_ref[rows_of(i), cols_of(h)], keys[picked_of(i), cols_of(h)]) * scale
            + widen(biases[i])
            for i, h in pairs
        ]
        top = [jnp.max(x, axis=1, keepdims=True) for x in s]
        w = [jnp.exp(x - t) for x, t in zip(s, top)]
        total = [jnp.sum(x, axis=1, keepdims=True) for x in w]
        part = [
            jnp.dot(x.astype(BF16), vals[picked_of(i), cols_of(h)], preferred_element_type=F32)
            for x, (i, h) in zip(w, pairs)
        ]
        for x, t, (i, h) in zip(part, total, pairs):
            out_ref[rows_of(i), cols_of(h)] = (x / t).astype(BF16)
        for c, columns in enumerate((top, total)):
            for x, (i, h) in zip(flatten(columns, diagonal), pairs):
                stat[i : i + 1, pl.ds(h * DH + c * BLOCK, BLOCK)] = x
    rest = stat[...]
    pieces[...] = jnp.zeros_like(pieces)
    for p in range(PIECES):
        piece = rest.astype(BF16).astype(F32)
        rest = rest - piece
        pieces[p * per : (p + 1) * per] = piece[:per]
    out_ref[pl.ds(per * BLOCK, pieces.shape[0])] = pieces[...].astype(BF16)


def stat_rows(per):
    return -(-per // 8) * 8


def piece_rows(per):
    return -(-PIECES * per // 16) * 16


def far_part(n, cap, per, arrive, q, got, earlier):
    rows, columns = q.shape
    heads = columns // DH
    return pl.pallas_call(
        functools.partial(far_kernel, n, cap, per, heads),
        out_shape=jax.ShapeDtypeStruct((rows + piece_rows(per), columns), BF16),
        in_specs=[spec(SMEM), spec()] + [spec()] * len(got) + [spec(pl.ANY)] * len(earlier),
        out_specs=spec(),
        scratch_shapes=[pltpu.VMEM((n // 2, 2 * cap * BLOCK, columns), BF16)]
        + [pltpu.VMEM((rows * R, columns), BF16)] * 2
        + [pltpu.VMEM((stat_rows(per), columns), F32)]
        + [pltpu.VMEM((piece_rows(per), columns), F32)],
        compiler_params=params(16),
        cost_estimate=LIGHT,
        name="far_part",
    )(arrive, q, *got, *earlier)


def own_kernel(
    n, cap, per, heads, arrive_ref, place_ref, q_ref, k_ref, v_ref, *refs
):
    half, plane = n // 2, n // 4
    got_refs = refs[:half]
    part_ref, stat_ref, keys, vals, glob, held, rand_keys, rand_vals = refs[-8:]
    me = lax.axis_index("seq")
    rows = per * BLOCK
    size = held.shape[1]
    for g in range(G):
        owner = lax.div(place_ref[g], per)
        k = lax.bitwise_and(lax.bitwise_xor(owner, me), plane - 1)
        for p in range(plane):
            @pl.when(k == p)
            def _(g=g, p=p):
                for c in range(2):
                    at = (c * G + g) * BLOCK
                    glob[pl.ds(at, BLOCK)] = got_refs[plane + p][pl.ds(size + at, BLOCK)]
    place = lax.bitwise_and(me, plane - 1)
    for start, neighbour in ((0, place + plane - 1), (BLOCK + rows, place + 1)):
        k = lax.bitwise_xor(place, lax.bitwise_and(neighbour, plane - 1))
        for p in range(1, plane):
            @pl.when(k == p)
            def _(start=start, p=p):
                at = size + 2 * G * BLOCK
                keys[pl.ds(start, BLOCK)] = got_refs[plane + p][pl.ds(at, BLOCK)]
                vals[pl.ds(start, BLOCK)] = got_refs[plane + p][pl.ds(at + BLOCK, BLOCK)]
    keys[pl.ds(BLOCK, rows)] = k_ref[...]
    vals[pl.ds(BLOCK, rows)] = v_ref[...]
    scale = 1.0 / math.sqrt(DH)
    diagonal = eye()
    stat_ref[...] = jnp.zeros_like(stat_ref)
    biases = choose(n, cap, per, arrive_ref, me, got_refs, size, held, rand_keys, rand_vals)
    for pairs in batches(per, heads, 2):
        sets = []
        for i, h in pairs:
            window, cols = pl.ds(i * BLOCK, 3 * BLOCK), cols_of(h)
            sets.append(
                (
                    (keys[window, cols], vals[window, cols]),
                    (glob[: G * BLOCK, cols], glob[G * BLOCK :, cols]),
                    (rand_keys[picked_of(i), cols], rand_vals[picked_of(i), cols]),
                )
            )
        s = [
            [dot_t(q_ref[rows_of(i), cols_of(h)], ks) * scale for ks, vs in three]
            for three, (i, h) in zip(sets, pairs)
        ]
        s = [[x, y, z + widen(biases[i])] for (x, y, z), (i, h) in zip(s, pairs)]
        top = [[jnp.max(x, axis=1, keepdims=True) for x in three] for three in s]
        top = [jnp.maximum(jnp.maximum(x, y), z) for x, y, z in top]
        w = [[jnp.exp(x - t) for x in three] for three, t in zip(s, top)]
        total = [[jnp.sum(x, axis=1, keepdims=True) for x in three] for three in w]
        total = [x + y + z for x, y, z in total]
        part = [
            [
                jnp.dot(x.astype(BF16), vs, preferred_element_type=F32)
                for x, (ks, vs) in zip(three, kv)
            ]
            for three, kv in zip(w, sets)
        ]
        for (x, y, z), (i, h) in zip(part, pairs):
            part_ref[rows_of(i), cols_of(h)] = x + y + z
        for c, columns in enumerate((top, total)):
            for x, (i, h) in zip(flatten(columns, diagonal), pairs):
                stat_ref[i : i + 1, pl.ds(h * DH + c * BLOCK, BLOCK)] = x


def own_part(n, cap, per, arrive, places, q, k, v, got):
    rows, columns = q.shape
    heads = columns // DH
    return pl.pallas_call(
        functools.partial(own_kernel, n, cap, per, heads),
        out_shape=(
            jax.ShapeDtypeStruct((rows, columns), F32),
            jax.ShapeDtypeStruct((stat_rows(per), columns), F32),
        ),
        in_specs=[spec(SMEM)] * 2 + [spec()] * (3 + len(got)),
        out_specs=(spec(), spec()),
        scratch_shapes=[pltpu.VMEM((rows + 2 * BLOCK, columns), BF16)] * 2
        + [pltpu.VMEM((2 * G * BLOCK, columns), BF16)]
        + [pltpu.VMEM((n // 2, 2 * cap * BLOCK, columns), BF16)]
        + [pltpu.VMEM((rows * R, columns), BF16)] * 2,
        compiler_params=params(20),
        cost_estimate=LIGHT,
        name="own_part",
    )(arrive, places, q, k, v, *got)


def context_kernel(per, heads, part_ref, stat_ref, far_ref, out_ref, pieces):
    pieces[...] = far_ref[pl.ds(per * BLOCK, pieces.shape[0])].astype(F32)
    far = sum(pieces[p * per : (p + 1) * per] for p in range(PIECES))
    own = stat_ref[:per]
    weights = []
    for h in range(heads):
        own_top, far_top = [x[:, h * DH : h * DH + BLOCK] for x in (own, far)]
        own_sum, far_sum = [x[:, h * DH + BLOCK : (h + 1) * DH] for x in (own, far)]
        top = jnp.maximum(own_top, far_top)
        own_w = jnp.exp(own_top - top)
        far_w = jnp.exp(far_top - top) * far_sum
        total = own_w * own_sum + far_w
        weights.append((jnp.transpose(own_w / total), jnp.transpose(far_w / total)))
    for i in range(per):
        for h, (own_w, far_w) in enumerate(weights):
            out_ref[rows_of(i), cols_of(h)] = (
                part_ref[rows_of(i), cols_of(h)] * own_w[:, i : i + 1]
                + far_ref[rows_of(i), cols_of(h)].astype(F32) * far_w[:, i : i + 1]
            ).astype(BF16)


def contexts(per, part, stat, far):
    rows, columns = part.shape
    heads = columns // DH
    return pl.pallas_call(
        functools.partial(context_kernel, per, heads),
        out_shape=jax.ShapeDtypeStruct((rows, columns), BF16),
        in_specs=[spec()] * 3,
        out_specs=spec(),
        scratch_shapes=[pltpu.VMEM((piece_rows(per), columns), F32)],
        compiler_params=params(8),
        cost_estimate=LIGHT,
        name="contexts",
    )(part, stat, far)


def project_kernel(own_ref, other_refs, w_ref, out_ref):
    me = lax.axis_index("head")
    count = lax.axis_size("head")
    columns = own_ref.shape[1]
    total = None
    for step, rows_ref in enumerate([own_ref] + list(other_refs)):
        owner = lax.rem(me + step, count)
        at = pl.ds(pl.multiple_of(owner * columns, columns), columns)
        term = jnp.dot(rows_ref[...], w_ref[at, :], preferred_element_type=F32)
        total = term if total is None else total + term
    out_ref[...] = total.astype(BF16)


def project(own, others, w_out):
    rows, columns = own.shape
    wide = w_out.shape[1]
    tile = rows // 4
    block = pl.BlockSpec((tile, columns), lambda i: (i, 0))

    def kernel(own_ref, *refs):
        project_kernel(own_ref, refs[: len(others)], refs[-2], refs[-1])

    return pl.pallas_call(
        kernel,
        grid=(4,),
        out_shape=jax.ShapeDtypeStruct((rows, wide), BF16),
        in_specs=[block] * (1 + len(others)) + [spec()],
        out_specs=pl.BlockSpec((tile, wide), lambda i: (i, 0)),
        compiler_params=params(16),
        cost_estimate=LIGHT,
        name="project",
    )(own, *others, w_out)


def on_device(queries, keys, values, rand_group, rand_offset, glob_blocks, w_out):
    tokens_dev = queries.shape[0]
    per = tokens_dev // BLOCK
    n = lax.axis_size("seq")
    heads = lax.axis_size("head")
    cap = max(2, (rand_group.shape[0] // n * R + n - 1) // n)

    mates = [(i, i ^ (n // 4)) for i in range(n)]
    partners = [(i, i ^ (n // 2)) for i in range(n)]
    mate_k = lax.ppermute(keys, "seq", mates)
    mate_v = lax.ppermute(values, "seq", mates)
    far_q = lax.ppermute(queries, "seq", partners)
    spots, arrive = ranks(n, per, cap, rand_group.T, rand_offset.T)
    both = exchange(gather(n, per, cap, 0, (True, False), spots, keys, values), n)
    far_parts = gather(n, per, cap, 1, (True,), spots, mate_k, mate_v)
    far_got = both + exchange(far_parts, n)
    cand = pick(n, per, glob_blocks, keys, values, mate_k, mate_v)
    shared = [glob_blocks, cand, lax.ppermute(cand, "seq", partners), keys, values]
    own_parts = gather(
        n, per, cap, 1, (False,), spots, mate_k, mate_v, shared + [mate_k, mate_v], [far_parts[0]]
    )
    own_got = both + exchange(own_parts, n)
    far = far_part(n, cap, per, arrive, far_q, far_got, [own_parts[0]])
    far = lax.ppermute(far, "seq", partners)
    part, stat = own_part(n, cap, per, arrive, glob_blocks, queries, keys, values, own_got)
    context = contexts(per, part, stat, far)
    others = [
        lax.ppermute(context, "head", [((i + s) % heads, i) for i in range(heads)])
        for s in range(1, heads)
    ]
    return project(context, others, w_out)


def solution(mesh):
    return jax.shard_map(
        on_device,
        mesh=mesh,
        in_specs=(
            P("seq", "head"),
            P("seq", "head"),
            P("seq", "head"),
            P(),
            P(),
            P(),
            P(None, "head"),
        ),
        out_specs=P("seq", "head"),
        check_vma=False,
    )
```

```python
import functools
import math

import jax
import jax.numpy as jnp
from jax import lax
from jax.experimental import pallas as pl
from jax.experimental.pallas import tpu as pltpu
from jax.sharding import PartitionSpec as P

DH = 128
BLOCK = 64
R = 3
G = 2
VMEM = pltpu.MemorySpace.VMEM
SMEM = pltpu.MemorySpace.SMEM
BF16 = jnp.bfloat16
F32 = jnp.float32
I32 = jnp.int32
NONE = -1e30
PIECES = 3


def params(mib):
    return pltpu.CompilerParams(vmem_limit_bytes=mib * 1024 * 1024)


LIGHT = pl.CostEstimate(flops=1, bytes_accessed=1, transcendentals=0)


def spec(space=VMEM):
    return pl.BlockSpec(memory_space=space)


def rank_kernel(n, per, cap, g_ref, o_ref, spot_ref, arrive_ref, g_pad, o_pad):
    me = lax.axis_index("seq")
    nb = g_ref.shape[1]
    wide = g_pad.shape[1]
    tall = spot_ref.shape[0]
    g_pad[...] = jnp.full(g_pad.shape, -1, I32)
    o_pad[...] = jnp.zeros(o_pad.shape, I32)
    g_pad[:R, :nb] = g_ref[...]
    o_pad[:R, :nb] = o_ref[...]
    g = g_pad[...]
    lane = lax.broadcasted_iota(I32, g.shape, 1)
    place = lane
    for d in range(1, n):
        place = jnp.where(lane >= d * per, lane - d * per, place)
    rank = jnp.zeros(g.shape, I32)
    for s in range(1, per):
        back = pltpu.roll(g, s, axis=1)
        ahead = place >= s
        for r in range(R):
            same = jnp.broadcast_to(back[r : r + 1, :], g.shape) == g
            rank = rank + jnp.where(ahead & same, 1, 0)
    arrive_ref[...] = g * cap + rank
    row = lax.broadcasted_iota(I32, (tall, wide), 0)
    spots = jnp.zeros((tall, wide), F32)
    for side in range(2):
        named = jnp.where(g == lax.bitwise_xor(me, side * (n // 4)), o_pad[...], 0)
        for s in range(cap):
            picked = jnp.where(rank == s, named, 0).astype(F32)
            total = jnp.sum(picked, axis=0, keepdims=True)
            here = row == side * cap + s
            spots = spots + jnp.where(here, jnp.broadcast_to(total, (tall, wide)), 0.0)
    token = lax.broadcasted_iota(I32, (wide, 128), 0)
    first = lax.broadcasted_iota(I32, (wide, 128), 1) * per
    belongs = jnp.where((token >= first) & (token < first + per), 1.0, 0.0)
    spot_ref[...] = jnp.dot(
        spots.astype(BF16), belongs.astype(BF16), preferred_element_type=F32
    ).astype(I32)


def ranks(n, per, cap, groups, offsets):
    nb = groups.shape[1]
    wide = -(-nb // 128) * 128
    tall = -(-2 * cap // 8) * 8
    return pl.pallas_call(
        functools.partial(rank_kernel, n, per, cap),
        out_shape=(
            jax.ShapeDtypeStruct((tall, 128), I32),
            jax.ShapeDtypeStruct((8, wide), I32),
        ),
        in_specs=[spec(), spec()],
        out_specs=(spec(), spec()),
        scratch_shapes=[pltpu.VMEM((8, wide), I32), pltpu.VMEM((8, wide), I32)],
        compiler_params=params(4),
        cost_estimate=LIGHT,
        name="ranks",
    )(groups, offsets)


def gather_kernel(n, per, cap, side, users, glob, spot_ref, kv_ref, *refs):
    plane = n // 4
    me = lax.axis_index("seq")
    size = 2 * cap * BLOCK
    for k, out_ref in enumerate(refs[-plane:]):
        for u, far in enumerate(users):
            d = lax.bitwise_xor(me, k + (n // 2 if far else 0))
            for s in range(cap):
                start = spot_ref[side * cap + s, d] * BLOCK
                for c in range(2):
                    rows = pl.ds(pl.multiple_of(start + c * per * BLOCK, BLOCK), BLOCK)
                    out_ref[pl.ds(u * size + (c * cap + s) * BLOCK, BLOCK)] = kv_ref[rows]
    if glob:
        shared_kernel(n, per, len(users) * size, *refs)


def shared_kernel(n, per, skip, place_ref, own_ref, got_ref, kv_ref, mate_ref, *refs):
    plane = n // 4
    me = lax.axis_index("seq")
    place = lax.bitwise_and(me, plane - 1)
    even = lax.bitwise_and(me, plane) == 0
    wide = 2 * G * BLOCK
    for k, out_ref in enumerate(refs[-plane:]):
        for g in range(G):
            owner = lax.div(place_ref[g], per)
            mine = lax.bitwise_and(lax.bitwise_xor(owner, me), plane) == 0
            for c in range(2):
                at = (c * G + g) * BLOCK
                rows = pl.ds(at, BLOCK)
                out_ref[pl.ds(skip + at, BLOCK)] = jnp.where(mine, own_ref[rows], got_ref[rows])
        target = lax.bitwise_xor(place, k)
        is_before = lax.rem(place + 1, plane) == target
        is_end = jnp.where(is_before, target == 0, target == plane - 1)
        far = is_end & (is_before == even)
        for c in range(2):
            first, last = pl.ds(c * per * BLOCK, BLOCK), pl.ds(((c + 1) * per - 1) * BLOCK, BLOCK)
            staged = got_ref[pl.ds(wide + c * BLOCK, BLOCK)]
            mates = jnp.where(is_before, mate_ref[last], mate_ref[first])
            owns = jnp.where(is_before, kv_ref[last], kv_ref[first])
            out_ref[pl.ds(skip + wide + c * BLOCK, BLOCK)] = jnp.where(
                far, staged, jnp.where(is_end, mates, owns)
            )


def gather(n, per, cap, side, users, spots, kv, glob=(), earlier=()):
    plane = n // 4
    rows = 2 * cap * BLOCK * len(users) + (2 * (G + 1) * BLOCK if glob else 0)
    out = jax.ShapeDtypeStruct((rows, kv.shape[1]), BF16)
    extra = [spec(SMEM)] + [spec()] * 4 if glob else []
    return pl.pallas_call(
        functools.partial(gather_kernel, n, per, cap, side, users, bool(glob)),
        out_shape=(out,) * plane,
        in_specs=[spec(SMEM), spec()] + extra + [spec(pl.ANY)] * len(earlier),
        out_specs=(spec(),) * plane,
        compiler_params=params(8),
        cost_estimate=LIGHT,
        name="gather_blocks",
    )(spots, kv, *glob, *earlier)


def exchange(parts, n):
    got = [parts[0]]
    for k in range(1, n // 4):
        got.append(lax.ppermute(parts[k], "seq", [(i, i ^ k) for i in range(n)]))
    return got


def stack_kernel(n, per, place_ref, k_ref, v_ref, kv_ref, out_ref):
    me = lax.axis_index("seq")
    even = lax.bitwise_and(me, n // 4) == 0
    for c, own in enumerate((k_ref, v_ref)):
        kv_ref[pl.ds(c * per * BLOCK, per * BLOCK)] = own[...]
        for g in range(G):
            start = lax.rem(place_ref[g], per) * BLOCK
            rows = pl.ds(pl.multiple_of(start, BLOCK), BLOCK)
            out_ref[pl.ds((c * G + g) * BLOCK, BLOCK)] = own[rows]
        first, last = own[:BLOCK], own[(per - 1) * BLOCK :]
        out_ref[pl.ds((2 * G + c) * BLOCK, BLOCK)] = jnp.where(even, first, last)


def stack(n, per, places, k, v):
    rows, columns = k.shape
    return pl.pallas_call(
        functools.partial(stack_kernel, n, per),
        out_shape=(
            jax.ShapeDtypeStruct((2 * rows, columns), BF16),
            jax.ShapeDtypeStruct((2 * (G + 1) * BLOCK, columns), BF16),
        ),
        in_specs=[spec(SMEM)] + [spec()] * 2,
        out_specs=(spec(), spec()),
        compiler_params=params(8),
        cost_estimate=LIGHT,
        name="stack",
    )(places, k, v)


def join_kernel(n, per, place_ref, own_ref, got_ref, out_ref):
    me = lax.axis_index("seq")
    for g in range(G):
        mine = lax.bitwise_and(lax.bitwise_xor(lax.div(place_ref[g], per), me), n // 2) == 0
        for c in range(2):
            rows = pl.ds((c * G + g) * BLOCK, BLOCK)
            out_ref[rows] = jnp.where(mine, own_ref[rows], got_ref[rows])
    rows = pl.ds(2 * G * BLOCK, 2 * BLOCK)
    out_ref[rows] = got_ref[rows]


def join(n, per, places, own, got):
    return pl.pallas_call(
        functools.partial(join_kernel, n, per),
        out_shape=jax.ShapeDtypeStruct(own.shape, BF16),
        in_specs=[spec(SMEM)] + [spec()] * 2,
        out_specs=spec(),
        compiler_params=params(4),
        cost_estimate=LIGHT,
        name="join",
    )(places, own, got)


def choose(n, cap, per, arrive_ref, d, got_refs, skip, held, keys, vals):
    half, plane = n // 2, n // 4
    me = lax.axis_index("seq")
    size = held.shape[1]
    for k, got_ref in enumerate(got_refs):
        held[k] = got_ref[pl.ds(skip if k < plane else 0, size)]
    biases = []
    for i in range(per):
        row = []
        for r in range(R):
            spot = arrive_ref[r, d * per + i]
            group = lax.div(spot, cap)
            differ = lax.bitwise_xor(group, me)
            here = differ < half
            slot = jnp.where(here, spot - group * cap, 0)
            k = jnp.where(here, differ, 0)
            at = pl.ds((i * R + r) * BLOCK, BLOCK)
            keys[at] = held[k, pl.ds(pl.multiple_of(slot * BLOCK, BLOCK), BLOCK), :]
            vals[at] = held[k, pl.ds(pl.multiple_of((cap + slot) * BLOCK, BLOCK), BLOCK), :]
            row.append(jnp.where(here, 0.0, NONE))
        biases.append(row)
    return biases


def flatten(columns, diagonal):
    return [jnp.sum(jnp.where(diagonal, x, 0.0), axis=0, keepdims=True) for x in columns]


def widen(biases):
    lane = lax.broadcasted_iota(I32, (1, R * BLOCK), 1)
    bias = jnp.full((1, R * BLOCK), biases[-1], F32)
    for r in reversed(range(R - 1)):
        bias = jnp.where(lane < (r + 1) * BLOCK, biases[r], bias)
    return bias


def batches(per, heads, step):
    for first in range(0, per, step):
        yield [(i, h) for i in range(first, min(per, first + step)) for h in range(heads)]


def rows_of(i):
    return pl.ds(i * BLOCK, BLOCK)


def picked_of(i):
    return pl.ds(i * R * BLOCK, R * BLOCK)


def cols_of(h):
    return pl.ds(h * DH, DH)


def dot_t(a, b):
    return lax.dot_general(a, b, (((1,), (1,)), ((), ())), preferred_element_type=F32)


def eye():
    shape = (BLOCK, BLOCK)
    return lax.broadcasted_iota(I32, shape, 0) == lax.broadcasted_iota(I32, shape, 1)


def far_kernel(n, cap, per, heads, arrive_ref, q_ref, *refs):
    half = n // 2
    got_refs, (out_ref, held, keys, vals, stat, pieces) = refs[:half], refs[-6:]
    d = lax.bitwise_xor(lax.axis_index("seq"), half)
    scale = 1.0 / math.sqrt(DH)
    diagonal = eye()
    stat[...] = jnp.zeros_like(stat)
    biases = choose(n, cap, per, arrive_ref, d, got_refs, 0, held, keys, vals)
    for pairs in batches(per, heads, 4):
        s = [
            dot_t(q_ref[rows_of(i), cols_of(h)], keys[picked_of(i), cols_of(h)]) * scale
            + widen(biases[i])
            for i, h in pairs
        ]
        top = [jnp.max(x, axis=1, keepdims=True) for x in s]
        w = [jnp.exp(x - t) for x, t in zip(s, top)]
        total = [jnp.sum(x, axis=1, keepdims=True) for x in w]
        part = [
            jnp.dot(x.astype(BF16), vals[picked_of(i), cols_of(h)], preferred_element_type=F32)
            for x, (i, h) in zip(w, pairs)
        ]
        for x, t, (i, h) in zip(part, total, pairs):
            out_ref[rows_of(i), cols_of(h)] = (x / t).astype(BF16)
        for c, columns in enumerate((top, total)):
            for x, (i, h) in zip(flatten(columns, diagonal), pairs):
                stat[i : i + 1, pl.ds(h * DH + c * BLOCK, BLOCK)] = x
    rest = stat[...]
    pieces[...] = jnp.zeros_like(pieces)
    for p in range(PIECES):
        piece = rest.astype(BF16).astype(F32)
        rest = rest - piece
        pieces[p * per : (p + 1) * per] = piece[:per]
    out_ref[pl.ds(per * BLOCK, pieces.shape[0])] = pieces[...].astype(BF16)


def stat_rows(per):
    return -(-per // 8) * 8


def piece_rows(per):
    return -(-PIECES * per // 16) * 16


def far_part(n, cap, per, arrive, q, got, earlier):
    rows, columns = q.shape
    heads = columns // DH
    return pl.pallas_call(
        functools.partial(far_kernel, n, cap, per, heads),
        out_shape=jax.ShapeDtypeStruct((rows + piece_rows(per), columns), BF16),
        in_specs=[spec(SMEM), spec()] + [spec()] * len(got) + [spec(pl.ANY)] * len(earlier),
        out_specs=spec(),
        scratch_shapes=[pltpu.VMEM((n // 2, 2 * cap * BLOCK, columns), BF16)]
        + [pltpu.VMEM((rows * R, columns), BF16)] * 2
        + [pltpu.VMEM((stat_rows(per), columns), F32)]
        + [pltpu.VMEM((piece_rows(per), columns), F32)],
        compiler_params=params(16),
        cost_estimate=LIGHT,
        name="far_part",
    )(arrive, q, *got, *earlier)


def own_kernel(
    n, cap, per, heads, arrive_ref, place_ref, q_ref, kv_ref, *refs
):
    half, plane = n // 2, n // 4
    got_refs = refs[:half]
    part_ref, stat_ref, keys, vals, glob, held, rand_keys, rand_vals = refs[-8:]
    me = lax.axis_index("seq")
    rows = per * BLOCK
    size = held.shape[1]
    for g in range(G):
        owner = lax.div(place_ref[g], per)
        k = lax.bitwise_and(lax.bitwise_xor(owner, me), plane - 1)
        for p in range(plane):
            @pl.when(k == p)
            def _(g=g, p=p):
                for c in range(2):
                    at = (c * G + g) * BLOCK
                    glob[pl.ds(at, BLOCK)] = got_refs[plane + p][pl.ds(size + at, BLOCK)]
    place = lax.bitwise_and(me, plane - 1)
    for start, neighbour in ((0, place + plane - 1), (BLOCK + rows, place + 1)):
        k = lax.bitwise_xor(place, lax.bitwise_and(neighbour, plane - 1))
        for p in range(1, plane):
            @pl.when(k == p)
            def _(start=start, p=p):
                at = size + 2 * G * BLOCK
                keys[pl.ds(start, BLOCK)] = got_refs[plane + p][pl.ds(at, BLOCK)]
                vals[pl.ds(start, BLOCK)] = got_refs[plane + p][pl.ds(at + BLOCK, BLOCK)]
    keys[pl.ds(BLOCK, rows)] = kv_ref[pl.ds(0, rows)]
    vals[pl.ds(BLOCK, rows)] = kv_ref[pl.ds(rows, rows)]
    scale = 1.0 / math.sqrt(DH)
    diagonal = eye()
    stat_ref[...] = jnp.zeros_like(stat_ref)
    biases = choose(n, cap, per, arrive_ref, me, got_refs, size, held, rand_keys, rand_vals)
    for pairs in batches(per, heads, 2):
        sets = []
        for i, h in pairs:
            window, cols = pl.ds(i * BLOCK, 3 * BLOCK), cols_of(h)
            sets.append(
                (
                    (keys[window, cols], vals[window, cols]),
                    (glob[: G * BLOCK, cols], glob[G * BLOCK :, cols]),
                    (rand_keys[picked_of(i), cols], rand_vals[picked_of(i), cols]),
                )
            )
        s = [
            [dot_t(q_ref[rows_of(i), cols_of(h)], ks) * scale for ks, vs in three]
            for three, (i, h) in zip(sets, pairs)
        ]
        s = [[x, y, z + widen(biases[i])] for (x, y, z), (i, h) in zip(s, pairs)]
        top = [[jnp.max(x, axis=1, keepdims=True) for x in three] for three in s]
        top = [jnp.maximum(jnp.maximum(x, y), z) for x, y, z in top]
        w = [[jnp.exp(x - t) for x in three] for three, t in zip(s, top)]
        total = [[jnp.sum(x, axis=1, keepdims=True) for x in three] for three in w]
        total = [x + y + z for x, y, z in total]
        part = [
            [
                jnp.dot(x.astype(BF16), vs, preferred_element_type=F32)
                for x, (ks, vs) in zip(three, kv)
            ]
            for three, kv in zip(w, sets)
        ]
        for (x, y, z), (i, h) in zip(part, pairs):
            part_ref[rows_of(i), cols_of(h)] = x + y + z
        for c, columns in enumerate((top, total)):
            for x, (i, h) in zip(flatten(columns, diagonal), pairs):
                stat_ref[i : i + 1, pl.ds(h * DH + c * BLOCK, BLOCK)] = x


def own_part(n, cap, per, arrive, places, q, kv, got):
    rows, columns = q.shape
    heads = columns // DH
    return pl.pallas_call(
        functools.partial(own_kernel, n, cap, per, heads),
        out_shape=(
            jax.ShapeDtypeStruct((rows, columns), F32),
            jax.ShapeDtypeStruct((stat_rows(per), columns), F32),
        ),
        in_specs=[spec(SMEM)] * 2 + [spec()] * (2 + len(got)),
        out_specs=(spec(), spec()),
        scratch_shapes=[pltpu.VMEM((rows + 2 * BLOCK, columns), BF16)] * 2
        + [pltpu.VMEM((2 * G * BLOCK, columns), BF16)]
        + [pltpu.VMEM((n // 2, 2 * cap * BLOCK, columns), BF16)]
        + [pltpu.VMEM((rows * R, columns), BF16)] * 2,
        compiler_params=params(20),
        cost_estimate=LIGHT,
        name="own_part",
    )(arrive, places, q, kv, *got)


def context_kernel(per, heads, part_ref, stat_ref, far_ref, out_ref, pieces):
    pieces[...] = far_ref[pl.ds(per * BLOCK, pieces.shape[0])].astype(F32)
    far = sum(pieces[p * per : (p + 1) * per] for p in range(PIECES))
    own = stat_ref[:per]
    weights = []
    for h in range(heads):
        own_top, far_top = [x[:, h * DH : h * DH + BLOCK] for x in (own, far)]
        own_sum, far_sum = [x[:, h * DH + BLOCK : (h + 1) * DH] for x in (own, far)]
        top = jnp.maximum(own_top, far_top)
        own_w = jnp.exp(own_top - top)
        far_w = jnp.exp(far_top - top) * far_sum
        total = own_w * own_sum + far_w
        weights.append((jnp.transpose(own_w / total), jnp.transpose(far_w / total)))
    for i in range(per):
        for h, (own_w, far_w) in enumerate(weights):
            out_ref[rows_of(i), cols_of(h)] = (
                part_ref[rows_of(i), cols_of(h)] * own_w[:, i : i + 1]
                + far_ref[rows_of(i), cols_of(h)].astype(F32) * far_w[:, i : i + 1]
            ).astype(BF16)


def contexts(per, part, stat, far):
    rows, columns = part.shape
    heads = columns // DH
    return pl.pallas_call(
        functools.partial(context_kernel, per, heads),
        out_shape=jax.ShapeDtypeStruct((rows, columns), BF16),
        in_specs=[spec()] * 3,
        out_specs=spec(),
        scratch_shapes=[pltpu.VMEM((piece_rows(per), columns), F32)],
        compiler_params=params(8),
        cost_estimate=LIGHT,
        name="contexts",
    )(part, stat, far)


def project_kernel(own_ref, other_refs, w_ref, out_ref):
    me = lax.axis_index("head")
    count = lax.axis_size("head")
    columns = own_ref.shape[1]
    total = None
    for step, rows_ref in enumerate([own_ref] + list(other_refs)):
        owner = lax.rem(me + step, count)
        at = pl.ds(pl.multiple_of(owner * columns, columns), columns)
        term = jnp.dot(rows_ref[...], w_ref[at, :], preferred_element_type=F32)
        total = term if total is None else total + term
    out_ref[...] = total.astype(BF16)


def project(own, others, w_out):
    rows, columns = own.shape
    wide = w_out.shape[1]
    tile = rows // 4
    block = pl.BlockSpec((tile, columns), lambda i: (i, 0))

    def kernel(own_ref, *refs):
        project_kernel(own_ref, refs[: len(others)], refs[-2], refs[-1])

    return pl.pallas_call(
        kernel,
        grid=(4,),
        out_shape=jax.ShapeDtypeStruct((rows, wide), BF16),
        in_specs=[block] * (1 + len(others)) + [spec()],
        out_specs=pl.BlockSpec((tile, wide), lambda i: (i, 0)),
        compiler_params=params(16),
        cost_estimate=LIGHT,
        name="project",
    )(own, *others, w_out)


def on_device(queries, keys, values, rand_group, rand_offset, glob_blocks, w_out):
    tokens_dev = queries.shape[0]
    per = tokens_dev // BLOCK
    n = lax.axis_size("seq")
    heads = lax.axis_size("head")
    cap = max(2, (rand_group.shape[0] // n * R + n - 1) // n)

    mates = [(i, i ^ (n // 4)) for i in range(n)]
    partners = [(i, i ^ (n // 2)) for i in range(n)]
    kv, cand = stack(n, per, glob_blocks, keys, values)
    mate_kv = lax.ppermute(kv, "seq", mates)
    got = lax.ppermute(cand, "seq", partners)
    later_q, _ = lax.optimization_barrier((queries, got))
    far_q = lax.ppermute(later_q, "seq", partners)
    spots, arrive = ranks(n, per, cap, rand_group.T, rand_offset.T)
    both = exchange(gather(n, per, cap, 0, (True, False), spots, kv), n)
    far_parts = gather(n, per, cap, 1, (True,), spots, mate_kv, (), both[1:3])
    far_got = both + exchange(far_parts, n)
    cand = join(n, per, glob_blocks, cand, got)
    shared = [glob_blocks, cand, lax.ppermute(cand, "seq", mates), kv, mate_kv]
    own_parts = gather(n, per, cap, 1, (False,), spots, mate_kv, shared, [far_parts[0]])
    own_got = both + exchange(own_parts, n)
    far = far_part(n, cap, per, arrive, far_q, far_got, [own_parts[0]])
    far = lax.ppermute(far, "seq", partners)
    part, stat = own_part(n, cap, per, arrive, glob_blocks, queries, kv, own_got)
    context = contexts(per, part, stat, far)
    others = [
        lax.ppermute(context, "head", [((i + s) % heads, i) for i in range(heads)])
        for s in range(1, heads)
    ]
    return project(context, others, w_out)


def solution(mesh):
    return jax.shard_map(
        on_device,
        mesh=mesh,
        in_specs=(
            P("seq", "head"),
            P("seq", "head"),
            P("seq", "head"),
            P(),
            P(),
            P(),
            P(None, "head"),
        ),
        out_specs=P("seq", "head"),
        check_vma=False,
    )
```

```python
import functools
import math

import jax
import jax.numpy as jnp
from jax import lax
from jax.experimental import pallas as pl
from jax.experimental.pallas import tpu as pltpu
from jax.sharding import PartitionSpec as P

DH = 128
BLOCK = 64
R = 3
G = 2
VMEM = pltpu.MemorySpace.VMEM
SMEM = pltpu.MemorySpace.SMEM
BF16 = jnp.bfloat16
F32 = jnp.float32
I32 = jnp.int32
NONE = -1e30
PIECES = 3


def params(mib):
    return pltpu.CompilerParams(vmem_limit_bytes=mib * 1024 * 1024)


LIGHT = pl.CostEstimate(flops=1, bytes_accessed=1, transcendentals=0)


def spec(space=VMEM):
    return pl.BlockSpec(memory_space=space)


def rank_kernel(n, per, cap, g_ref, o_ref, spot_ref, arrive_ref, g_pad, o_pad):
    me = lax.axis_index("seq")
    nb = g_ref.shape[1]
    wide = g_pad.shape[1]
    tall = spot_ref.shape[0]
    g_pad[...] = jnp.full(g_pad.shape, -1, I32)
    o_pad[...] = jnp.zeros(o_pad.shape, I32)
    g_pad[:R, :nb] = g_ref[...]
    o_pad[:R, :nb] = o_ref[...]
    g = g_pad[...]
    lane = lax.broadcasted_iota(I32, g.shape, 1)
    place = lane
    for d in range(1, n):
        place = jnp.where(lane >= d * per, lane - d * per, place)
    rank = jnp.zeros(g.shape, I32)
    for s in range(1, per):
        back = pltpu.roll(g, s, axis=1)
        ahead = place >= s
        for r in range(R):
            same = jnp.broadcast_to(back[r : r + 1, :], g.shape) == g
            rank = rank + jnp.where(ahead & same, 1, 0)
    arrive_ref[...] = g * cap + rank
    row = lax.broadcasted_iota(I32, (tall, wide), 0)
    spots = jnp.zeros((tall, wide), F32)
    for side in range(2):
        named = jnp.where(g == lax.bitwise_xor(me, side * (n // 4)), o_pad[...], 0)
        for s in range(cap):
            picked = jnp.where(rank == s, named, 0).astype(F32)
            total = jnp.sum(picked, axis=0, keepdims=True)
            here = row == side * cap + s
            spots = spots + jnp.where(here, jnp.broadcast_to(total, (tall, wide)), 0.0)
    token = lax.broadcasted_iota(I32, (wide, 128), 0)
    first = lax.broadcasted_iota(I32, (wide, 128), 1) * per
    belongs = jnp.where((token >= first) & (token < first + per), 1.0, 0.0)
    spot_ref[...] = jnp.dot(
        spots.astype(BF16), belongs.astype(BF16), preferred_element_type=F32
    ).astype(I32)


def ranks(n, per, cap, groups, offsets):
    nb = groups.shape[1]
    wide = -(-nb // 128) * 128
    tall = -(-2 * cap // 8) * 8
    return pl.pallas_call(
        functools.partial(rank_kernel, n, per, cap),
        out_shape=(
            jax.ShapeDtypeStruct((tall, 128), I32),
            jax.ShapeDtypeStruct((8, wide), I32),
        ),
        in_specs=[spec(), spec()],
        out_specs=(spec(), spec()),
        scratch_shapes=[pltpu.VMEM((8, wide), I32), pltpu.VMEM((8, wide), I32)],
        compiler_params=params(4),
        cost_estimate=LIGHT,
        name="ranks",
    )(groups, offsets)


def gather_kernel(n, per, cap, side, users, glob, count, spot_ref, *refs):
    sources, refs = refs[:count], refs[count:]
    plane = n // 4
    me = lax.axis_index("seq")
    size = 2 * cap * BLOCK
    for k, out_ref in enumerate(refs[-plane:]):
        for u, far in enumerate(users):
            d = lax.bitwise_xor(me, k + (n // 2 if far else 0))
            for s in range(cap):
                start = spot_ref[side * cap + s, d] * BLOCK
                for c in range(2):
                    skip = c * per * BLOCK if count == 1 else 0
                    rows = pl.ds(pl.multiple_of(start + skip, BLOCK), BLOCK)
                    out_ref[pl.ds(u * size + (c * cap + s) * BLOCK, BLOCK)] = sources[c % count][rows]
    if glob:
        shared_kernel(n, per, len(users) * size, *refs)


def shared_kernel(n, per, skip, place_ref, own_ref, got_ref, kv_ref, mate_ref, *refs):
    plane = n // 4
    me = lax.axis_index("seq")
    place = lax.bitwise_and(me, plane - 1)
    even = lax.bitwise_and(me, plane) == 0
    wide = 2 * G * BLOCK
    for k, out_ref in enumerate(refs[-plane:]):
        for g in range(G):
            owner = lax.div(place_ref[g], per)
            mine = lax.bitwise_and(lax.bitwise_xor(owner, me), plane) == 0
            for c in range(2):
                at = (c * G + g) * BLOCK
                rows = pl.ds(at, BLOCK)
                out_ref[pl.ds(skip + at, BLOCK)] = jnp.where(mine, own_ref[rows], got_ref[rows])
        target = lax.bitwise_xor(place, k)
        is_before = lax.rem(place + 1, plane) == target
        is_end = jnp.where(is_before, target == 0, target == plane - 1)
        far = is_end & (is_before == even)
        for c in range(2):
            first, last = pl.ds(c * per * BLOCK, BLOCK), pl.ds(((c + 1) * per - 1) * BLOCK, BLOCK)
            staged = got_ref[pl.ds(wide + c * BLOCK, BLOCK)]
            mates = jnp.where(is_before, mate_ref[last], mate_ref[first])
            owns = jnp.where(is_before, kv_ref[last], kv_ref[first])
            out_ref[pl.ds(skip + wide + c * BLOCK, BLOCK)] = jnp.where(
                far, staged, jnp.where(is_end, mates, owns)
            )


def gather(n, per, cap, side, users, spots, sources, glob=(), earlier=()):
    plane = n // 4
    rows = 2 * cap * BLOCK * len(users) + (2 * (G + 1) * BLOCK if glob else 0)
    out = jax.ShapeDtypeStruct((rows, sources[0].shape[1]), BF16)
    extra = [spec(SMEM)] + [spec()] * 4 if glob else []
    return pl.pallas_call(
        functools.partial(gather_kernel, n, per, cap, side, users, bool(glob), len(sources)),
        out_shape=(out,) * plane,
        in_specs=[spec(SMEM)] + [spec()] * len(sources) + extra + [spec(pl.ANY)] * len(earlier),
        out_specs=(spec(),) * plane,
        compiler_params=params(8),
        cost_estimate=LIGHT,
        name="gather_blocks",
    )(spots, *sources, *glob, *earlier)


def exchange(parts, n):
    got = [parts[0]]
    for k in range(1, n // 4):
        got.append(lax.ppermute(parts[k], "seq", [(i, i ^ k) for i in range(n)]))
    return got


def stack_kernel(n, per, place_ref, k_ref, v_ref, earlier_ref, kv_ref, out_ref):
    me = lax.axis_index("seq")
    even = lax.bitwise_and(me, n // 4) == 0
    for c, own in enumerate((k_ref, v_ref)):
        kv_ref[pl.ds(c * per * BLOCK, per * BLOCK)] = own[...]
        for g in range(G):
            start = lax.rem(place_ref[g], per) * BLOCK
            rows = pl.ds(pl.multiple_of(start, BLOCK), BLOCK)
            out_ref[pl.ds((c * G + g) * BLOCK, BLOCK)] = own[rows]
        first, last = own[:BLOCK], own[(per - 1) * BLOCK :]
        out_ref[pl.ds((2 * G + c) * BLOCK, BLOCK)] = jnp.where(even, first, last)


def stack(n, per, places, k, v, earlier):
    rows, columns = k.shape
    return pl.pallas_call(
        functools.partial(stack_kernel, n, per),
        out_shape=(
            jax.ShapeDtypeStruct((2 * rows, columns), BF16),
            jax.ShapeDtypeStruct((2 * (G + 1) * BLOCK, columns), BF16),
        ),
        in_specs=[spec(SMEM), spec(), spec(), spec(pl.ANY)],
        out_specs=(spec(), spec()),
        compiler_params=params(8),
        cost_estimate=LIGHT,
        name="stack",
    )(places, k, v, earlier)


def join_kernel(n, per, place_ref, own_ref, got_ref, out_ref):
    me = lax.axis_index("seq")
    for g in range(G):
        mine = lax.bitwise_and(lax.bitwise_xor(lax.div(place_ref[g], per), me), n // 2) == 0
        for c in range(2):
            rows = pl.ds((c * G + g) * BLOCK, BLOCK)
            out_ref[rows] = jnp.where(mine, own_ref[rows], got_ref[rows])
    rows = pl.ds(2 * G * BLOCK, 2 * BLOCK)
    out_ref[rows] = got_ref[rows]


def join(n, per, places, own, got):
    return pl.pallas_call(
        functools.partial(join_kernel, n, per),
        out_shape=jax.ShapeDtypeStruct(own.shape, BF16),
        in_specs=[spec(SMEM)] + [spec()] * 2,
        out_specs=spec(),
        compiler_params=params(4),
        cost_estimate=LIGHT,
        name="join",
    )(places, own, got)


def choose(n, cap, per, arrive_ref, d, got_refs, skip, held, keys, vals):
    half, plane = n // 2, n // 4
    me = lax.axis_index("seq")
    size = held.shape[1]
    for k, got_ref in enumerate(got_refs):
        held[k] = got_ref[pl.ds(skip if k < plane else 0, size)]
    biases = []
    for i in range(per):
        row = []
        for r in range(R):
            spot = arrive_ref[r, d * per + i]
            group = lax.div(spot, cap)
            differ = lax.bitwise_xor(group, me)
            here = differ < half
            slot = jnp.where(here, spot - group * cap, 0)
            k = jnp.where(here, differ, 0)
            at = pl.ds((i * R + r) * BLOCK, BLOCK)
            keys[at] = held[k, pl.ds(pl.multiple_of(slot * BLOCK, BLOCK), BLOCK), :]
            vals[at] = held[k, pl.ds(pl.multiple_of((cap + slot) * BLOCK, BLOCK), BLOCK), :]
            row.append(jnp.where(here, 0.0, NONE))
        biases.append(row)
    return biases


def flatten(columns, diagonal):
    return [jnp.sum(jnp.where(diagonal, x, 0.0), axis=0, keepdims=True) for x in columns]


def widen(biases):
    lane = lax.broadcasted_iota(I32, (1, R * BLOCK), 1)
    bias = jnp.full((1, R * BLOCK), biases[-1], F32)
    for r in reversed(range(R - 1)):
        bias = jnp.where(lane < (r + 1) * BLOCK, biases[r], bias)
    return bias


def batches(per, heads, step):
    for first in range(0, per, step):
        yield [(i, h) for i in range(first, min(per, first + step)) for h in range(heads)]


def rows_of(i):
    return pl.ds(i * BLOCK, BLOCK)


def picked_of(i):
    return pl.ds(i * R * BLOCK, R * BLOCK)


def cols_of(h):
    return pl.ds(h * DH, DH)


def dot_t(a, b):
    return lax.dot_general(a, b, (((1,), (1,)), ((), ())), preferred_element_type=F32)


def eye():
    shape = (BLOCK, BLOCK)
    return lax.broadcasted_iota(I32, shape, 0) == lax.broadcasted_iota(I32, shape, 1)


def far_kernel(n, cap, per, heads, arrive_ref, q_ref, *refs):
    half = n // 2
    got_refs, (out_ref, held, keys, vals, stat, pieces) = refs[:half], refs[-6:]
    d = lax.bitwise_xor(lax.axis_index("seq"), half)
    scale = 1.0 / math.sqrt(DH)
    diagonal = eye()
    stat[...] = jnp.zeros_like(stat)
    biases = choose(n, cap, per, arrive_ref, d, got_refs, 0, held, keys, vals)
    for pairs in batches(per, heads, 4):
        s = [
            dot_t(q_ref[rows_of(i), cols_of(h)], keys[picked_of(i), cols_of(h)]) * scale
            + widen(biases[i])
            for i, h in pairs
        ]
        top = [jnp.max(x, axis=1, keepdims=True) for x in s]
        w = [jnp.exp(x - t) for x, t in zip(s, top)]
        total = [jnp.sum(x, axis=1, keepdims=True) for x in w]
        part = [
            jnp.dot(x.astype(BF16), vals[picked_of(i), cols_of(h)], preferred_element_type=F32)
            for x, (i, h) in zip(w, pairs)
        ]
        for x, t, (i, h) in zip(part, total, pairs):
            out_ref[rows_of(i), cols_of(h)] = (x / t).astype(BF16)
        for c, columns in enumerate((top, total)):
            for x, (i, h) in zip(flatten(columns, diagonal), pairs):
                stat[i : i + 1, pl.ds(h * DH + c * BLOCK, BLOCK)] = x
    rest = stat[...]
    pieces[...] = jnp.zeros_like(pieces)
    for p in range(PIECES):
        piece = rest.astype(BF16).astype(F32)
        rest = rest - piece
        pieces[p * per : (p + 1) * per] = piece[:per]
    out_ref[pl.ds(per * BLOCK, pieces.shape[0])] = pieces[...].astype(BF16)


def stat_rows(per):
    return -(-per // 8) * 8


def piece_rows(per):
    return -(-PIECES * per // 16) * 16


def far_part(n, cap, per, arrive, q, got, earlier):
    rows, columns = q.shape
    heads = columns // DH
    return pl.pallas_call(
        functools.partial(far_kernel, n, cap, per, heads),
        out_shape=jax.ShapeDtypeStruct((rows + piece_rows(per), columns), BF16),
        in_specs=[spec(SMEM), spec()] + [spec()] * len(got) + [spec(pl.ANY)] * len(earlier),
        out_specs=spec(),
        scratch_shapes=[pltpu.VMEM((n // 2, 2 * cap * BLOCK, columns), BF16)]
        + [pltpu.VMEM((rows * R, columns), BF16)] * 2
        + [pltpu.VMEM((stat_rows(per), columns), F32)]
        + [pltpu.VMEM((piece_rows(per), columns), F32)],
        compiler_params=params(16),
        cost_estimate=LIGHT,
        name="far_part",
    )(arrive, q, *got, *earlier)


def own_kernel(
    n, cap, per, heads, arrive_ref, place_ref, q_hbm, kv_ref, *refs
):
    half, plane = n // 2, n // 4
    got_refs = refs[:half]
    part_ref, stat_ref, keys, vals, glob, held, rand_keys, rand_vals, q_ref, sem = refs[-10:]
    fetch = pltpu.make_async_copy(q_hbm, q_ref, sem)
    fetch.start()
    me = lax.axis_index("seq")
    rows = per * BLOCK
    size = held.shape[1]
    for g in range(G):
        owner = lax.div(place_ref[g], per)
        k = lax.bitwise_and(lax.bitwise_xor(owner, me), plane - 1)
        for p in range(plane):
            @pl.when(k == p)
            def _(g=g, p=p):
                for c in range(2):
                    at = (c * G + g) * BLOCK
                    glob[pl.ds(at, BLOCK)] = got_refs[plane + p][pl.ds(size + at, BLOCK)]
    place = lax.bitwise_and(me, plane - 1)
    for start, neighbour in ((0, place + plane - 1), (BLOCK + rows, place + 1)):
        k = lax.bitwise_xor(place, lax.bitwise_and(neighbour, plane - 1))
        for p in range(1, plane):
            @pl.when(k == p)
            def _(start=start, p=p):
                at = size + 2 * G * BLOCK
                keys[pl.ds(start, BLOCK)] = got_refs[plane + p][pl.ds(at, BLOCK)]
                vals[pl.ds(start, BLOCK)] = got_refs[plane + p][pl.ds(at + BLOCK, BLOCK)]
    keys[pl.ds(BLOCK, rows)] = kv_ref[pl.ds(0, rows)]
    vals[pl.ds(BLOCK, rows)] = kv_ref[pl.ds(rows, rows)]
    scale = 1.0 / math.sqrt(DH)
    diagonal = eye()
    stat_ref[...] = jnp.zeros_like(stat_ref)
    biases = choose(n, cap, per, arrive_ref, me, got_refs, size, held, rand_keys, rand_vals)
    fetch.wait()
    for pairs in batches(per, heads, 2):
        sets = []
        for i, h in pairs:
            window, cols = pl.ds(i * BLOCK, 3 * BLOCK), cols_of(h)
            sets.append(
                (
                    (keys[window, cols], vals[window, cols]),
                    (glob[: G * BLOCK, cols], glob[G * BLOCK :, cols]),
                    (rand_keys[picked_of(i), cols], rand_vals[picked_of(i), cols]),
                )
            )
        s = [
            [dot_t(q_ref[rows_of(i), cols_of(h)], ks) * scale for ks, vs in three]
            for three, (i, h) in zip(sets, pairs)
        ]
        s = [[x, y, z + widen(biases[i])] for (x, y, z), (i, h) in zip(s, pairs)]
        top = [[jnp.max(x, axis=1, keepdims=True) for x in three] for three in s]
        top = [jnp.maximum(jnp.maximum(x, y), z) for x, y, z in top]
        w = [[jnp.exp(x - t) for x in three] for three, t in zip(s, top)]
        total = [[jnp.sum(x, axis=1, keepdims=True) for x in three] for three in w]
        total = [x + y + z for x, y, z in total]
        part = [
            [
                jnp.dot(x.astype(BF16), vs, preferred_element_type=F32)
                for x, (ks, vs) in zip(three, kv)
            ]
            for three, kv in zip(w, sets)
        ]
        for (x, y, z), (i, h) in zip(part, pairs):
            part_ref[rows_of(i), cols_of(h)] = x + y + z
        for c, columns in enumerate((top, total)):
            for x, (i, h) in zip(flatten(columns, diagonal), pairs):
                stat_ref[i : i + 1, pl.ds(h * DH + c * BLOCK, BLOCK)] = x


def own_part(n, cap, per, arrive, places, q, kv, got):
    rows, columns = q.shape
    heads = columns // DH
    return pl.pallas_call(
        functools.partial(own_kernel, n, cap, per, heads),
        out_shape=(
            jax.ShapeDtypeStruct((rows, columns), F32),
            jax.ShapeDtypeStruct((stat_rows(per), columns), F32),
        ),
        in_specs=[spec(SMEM)] * 2 + [spec(pl.ANY)] + [spec()] * (1 + len(got)),
        out_specs=(spec(), spec()),
        scratch_shapes=[pltpu.VMEM((rows + 2 * BLOCK, columns), BF16)] * 2
        + [pltpu.VMEM((2 * G * BLOCK, columns), BF16)]
        + [pltpu.VMEM((n // 2, 2 * cap * BLOCK, columns), BF16)]
        + [pltpu.VMEM((rows * R, columns), BF16)] * 2
        + [pltpu.VMEM((rows, columns), BF16), pltpu.SemaphoreType.DMA],
        compiler_params=params(20),
        cost_estimate=LIGHT,
        name="own_part",
    )(arrive, places, q, kv, *got)


def context_kernel(per, heads, part_ref, stat_ref, far_ref, out_ref, pieces):
    pieces[...] = far_ref[pl.ds(per * BLOCK, pieces.shape[0])].astype(F32)
    far = sum(pieces[p * per : (p + 1) * per] for p in range(PIECES))
    own = stat_ref[:per]
    weights = []
    for h in range(heads):
        own_top, far_top = [x[:, h * DH : h * DH + BLOCK] for x in (own, far)]
        own_sum, far_sum = [x[:, h * DH + BLOCK : (h + 1) * DH] for x in (own, far)]
        top = jnp.maximum(own_top, far_top)
        own_w = jnp.exp(own_top - top)
        far_w = jnp.exp(far_top - top) * far_sum
        total = own_w * own_sum + far_w
        weights.append((jnp.transpose(own_w / total), jnp.transpose(far_w / total)))
    for i in range(per):
        for h, (own_w, far_w) in enumerate(weights):
            out_ref[rows_of(i), cols_of(h)] = (
                part_ref[rows_of(i), cols_of(h)] * own_w[:, i : i + 1]
                + far_ref[rows_of(i), cols_of(h)].astype(F32) * far_w[:, i : i + 1]
            ).astype(BF16)


def contexts(per, part, stat, far):
    rows, columns = part.shape
    heads = columns // DH
    return pl.pallas_call(
        functools.partial(context_kernel, per, heads),
        out_shape=jax.ShapeDtypeStruct((rows, columns), BF16),
        in_specs=[spec()] * 3,
        out_specs=spec(),
        scratch_shapes=[pltpu.VMEM((piece_rows(per), columns), F32)],
        compiler_params=params(8),
        cost_estimate=LIGHT,
        name="contexts",
    )(part, stat, far)


def project_kernel(own_ref, other_refs, w_ref, out_ref):
    me = lax.axis_index("head")
    count = lax.axis_size("head")
    columns = own_ref.shape[1]
    total = None
    for step, rows_ref in enumerate([own_ref] + list(other_refs)):
        owner = lax.rem(me + step, count)
        at = pl.ds(pl.multiple_of(owner * columns, columns), columns)
        term = jnp.dot(rows_ref[...], w_ref[at, :], preferred_element_type=F32)
        total = term if total is None else total + term
    out_ref[...] = total.astype(BF16)


def project(own, others, w_out):
    rows, columns = own.shape
    wide = w_out.shape[1]
    tile = rows // 4
    block = pl.BlockSpec((tile, columns), lambda i: (i, 0))

    def kernel(own_ref, *refs):
        project_kernel(own_ref, refs[: len(others)], refs[-2], refs[-1])

    return pl.pallas_call(
        kernel,
        grid=(4,),
        out_shape=jax.ShapeDtypeStruct((rows, wide), BF16),
        in_specs=[block] * (1 + len(others)) + [spec()],
        out_specs=pl.BlockSpec((tile, wide), lambda i: (i, 0)),
        compiler_params=params(16),
        cost_estimate=LIGHT,
        name="project",
    )(own, *others, w_out)


def on_device(queries, keys, values, rand_group, rand_offset, glob_blocks, w_out):
    tokens_dev = queries.shape[0]
    per = tokens_dev // BLOCK
    n = lax.axis_size("seq")
    heads = lax.axis_size("head")
    cap = max(2, (rand_group.shape[0] // n * R + n - 1) // n)

    mates = [(i, i ^ (n // 4)) for i in range(n)]
    partners = [(i, i ^ (n // 2)) for i in range(n)]
    far_q = lax.ppermute(queries, "seq", partners)
    spots, arrive = ranks(n, per, cap, rand_group.T, rand_offset.T)
    both = gather(n, per, cap, 0, (True, False), spots, [keys, values])
    kv, cand = stack(n, per, glob_blocks, keys, values, both[0])
    both = exchange(both, n)
    mate_kv = lax.ppermute(kv, "seq", mates)
    later, _ = lax.optimization_barrier((cand, far_q))
    got = lax.ppermute(later, "seq", partners)
    far_parts = gather(n, per, cap, 1, (True,), spots, [mate_kv], (), both[1:3])
    far_got = both + exchange(far_parts, n)
    cand = join(n, per, glob_blocks, cand, got)
    shared = [glob_blocks, cand, lax.ppermute(cand, "seq", mates), kv, mate_kv]
    own_parts = gather(n, per, cap, 1, (False,), spots, [mate_kv], shared, [far_parts[0]])
    own_got = both + exchange(own_parts, n)
    far = far_part(n, cap, per, arrive, far_q, far_got, [own_parts[0]])
    far = lax.ppermute(far, "seq", partners)
    part, stat = own_part(n, cap, per, arrive, glob_blocks, queries, kv, own_got)
    context = contexts(per, part, stat, far)
    others = [
        lax.ppermute(context, "head", [((i + s) % heads, i) for i in range(heads)])
        for s in range(1, heads)
    ]
    return project(context, others, w_out)


def solution(mesh):
    return jax.shard_map(
        on_device,
        mesh=mesh,
        in_specs=(
            P("seq", "head"),
            P("seq", "head"),
            P("seq", "head"),
            P(),
            P(),
            P(),
            P(None, "head"),
        ),
        out_specs=P("seq", "head"),
        check_vma=False,
    )
```

```python
import functools
import math

import jax
import jax.numpy as jnp
from jax import lax
from jax.experimental import pallas as pl
from jax.experimental.pallas import tpu as pltpu
from jax.sharding import PartitionSpec as P

DH = 128
BLOCK = 64
R = 3
G = 2
VMEM = pltpu.MemorySpace.VMEM
SMEM = pltpu.MemorySpace.SMEM
BF16 = jnp.bfloat16
F32 = jnp.float32
I32 = jnp.int32
NONE = -1e30
PIECES = 3


def params(mib):
    return pltpu.CompilerParams(vmem_limit_bytes=mib * 1024 * 1024)


LIGHT = pl.CostEstimate(flops=1, bytes_accessed=1, transcendentals=0)


def spec(space=VMEM):
    return pl.BlockSpec(memory_space=space)


def rank_kernel(n, per, cap, g_ref, o_ref, spot_ref, arrive_ref, g_pad, o_pad):
    me = lax.axis_index("seq")
    nb = g_ref.shape[1]
    wide = g_pad.shape[1]
    tall = spot_ref.shape[0]
    g_pad[...] = jnp.full(g_pad.shape, -1, I32)
    o_pad[...] = jnp.zeros(o_pad.shape, I32)
    g_pad[:R, :nb] = g_ref[...]
    o_pad[:R, :nb] = o_ref[...]
    g = g_pad[...]
    lane = lax.broadcasted_iota(I32, g.shape, 1)
    place = lane
    for d in range(1, n):
        place = jnp.where(lane >= d * per, lane - d * per, place)
    rank = jnp.zeros(g.shape, I32)
    for s in range(1, per):
        back = pltpu.roll(g, s, axis=1)
        ahead = place >= s
        for r in range(R):
            same = jnp.broadcast_to(back[r : r + 1, :], g.shape) == g
            rank = rank + jnp.where(ahead & same, 1, 0)
    arrive_ref[...] = g * cap + rank
    row = lax.broadcasted_iota(I32, (tall, wide), 0)
    spots = jnp.zeros((tall, wide), F32)
    for side in range(2):
        named = jnp.where(g == lax.bitwise_xor(me, side * (n // 4)), o_pad[...], 0)
        for s in range(cap):
            picked = jnp.where(rank == s, named, 0).astype(F32)
            total = jnp.sum(picked, axis=0, keepdims=True)
            here = row == side * cap + s
            spots = spots + jnp.where(here, jnp.broadcast_to(total, (tall, wide)), 0.0)
    token = lax.broadcasted_iota(I32, (wide, 128), 0)
    first = lax.broadcasted_iota(I32, (wide, 128), 1) * per
    belongs = jnp.where((token >= first) & (token < first + per), 1.0, 0.0)
    spot_ref[...] = jnp.dot(
        spots.astype(BF16), belongs.astype(BF16), preferred_element_type=F32
    ).astype(I32)


def ranks(n, per, cap, groups, offsets):
    nb = groups.shape[1]
    wide = -(-nb // 128) * 128
    tall = -(-2 * cap // 8) * 8
    return pl.pallas_call(
        functools.partial(rank_kernel, n, per, cap),
        out_shape=(
            jax.ShapeDtypeStruct((tall, 128), I32),
            jax.ShapeDtypeStruct((8, wide), I32),
        ),
        in_specs=[spec(), spec()],
        out_specs=(spec(), spec()),
        scratch_shapes=[pltpu.VMEM((8, wide), I32), pltpu.VMEM((8, wide), I32)],
        compiler_params=params(4),
        cost_estimate=LIGHT,
        name="ranks",
    )(groups, offsets)


def gather_kernel(n, per, cap, lists, shared, count, spot_ref, *refs):
    plane = n // 4
    me = lax.axis_index("seq")
    size = 2 * cap * BLOCK
    sources, outs = refs[:count], refs[-plane:]
    for k, out_ref in enumerate(outs):
        for u, (side, far) in enumerate(lists):
            d = lax.bitwise_xor(me, k + (n // 2 if far else 0))
            for s in range(cap):
                start = spot_ref[side * cap + s, d] * BLOCK
                for c in range(2):
                    rows = pl.ds(pl.multiple_of(start + c * per * BLOCK, BLOCK), BLOCK)
                    out_ref[pl.ds(u * size + (c * cap + s) * BLOCK, BLOCK)] = sources[side][rows]
        if shared:
            shared_rows(n, per, k, len(lists) * size, refs[count], sources, out_ref)


def shared_rows(n, per, k, skip, place_ref, sources, out_ref):
    plane = n // 4
    me = lax.axis_index("seq")
    place = lax.bitwise_and(me, plane - 1)
    own_ref, mate_ref = sources
    for g in range(G):
        owner = lax.div(place_ref[g], per)
        start = (place_ref[g] - owner * per) * BLOCK
        mine = lax.bitwise_and(lax.bitwise_xor(owner, me), plane) == 0
        for c in range(2):
            rows = pl.ds(pl.multiple_of(start + c * per * BLOCK, BLOCK), BLOCK)
            out_ref[pl.ds(skip + (c * G + g) * BLOCK, BLOCK)] = jnp.where(
                mine, own_ref[rows], mate_ref[rows]
            )
    target = lax.bitwise_xor(place, k)
    is_before = lax.rem(place + 1, plane) == target
    is_end = jnp.where(is_before, target == 0, target == plane - 1)
    for c in range(2):
        first, last = pl.ds(c * per * BLOCK, BLOCK), pl.ds(((c + 1) * per - 1) * BLOCK, BLOCK)
        mates = jnp.where(is_before, mate_ref[last], mate_ref[first])
        owns = jnp.where(is_before, own_ref[last], own_ref[first])
        out_ref[pl.ds(skip + (2 * G + c) * BLOCK, BLOCK)] = jnp.where(is_end, mates, owns)


def gather(n, per, cap, lists, spots, sources, places=None, earlier=()):
    plane, shared = n // 4, places is not None
    rows = 2 * cap * BLOCK * len(lists) + (2 * (G + 1) * BLOCK if shared else 0)
    out = jax.ShapeDtypeStruct((rows, sources[0].shape[1]), BF16)
    extra = [places] if shared else []
    return pl.pallas_call(
        functools.partial(gather_kernel, n, per, cap, lists, shared, len(sources)),
        out_shape=(out,) * plane,
        in_specs=[spec(SMEM)]
        + [spec()] * len(sources)
        + [spec(SMEM)] * len(extra)
        + [spec(pl.ANY)] * len(earlier),
        out_specs=(spec(),) * plane,
        compiler_params=params(8),
        cost_estimate=LIGHT,
        name="gather_blocks",
    )(spots, *sources, *extra, *earlier)


def exchange(parts, n):
    got = [parts[0]]
    for k in range(1, n // 4):
        got.append(lax.ppermute(parts[k], "seq", [(i, i ^ k) for i in range(n)]))
    return got


def stack_kernel(k_ref, v_ref, kv_ref):
    rows = k_ref.shape[0]
    kv_ref[pl.ds(0, rows)] = k_ref[...]
    kv_ref[pl.ds(rows, rows)] = v_ref[...]


def stack(k, v):
    rows, columns = k.shape
    return pl.pallas_call(
        stack_kernel,
        out_shape=jax.ShapeDtypeStruct((2 * rows, columns), BF16),
        in_specs=[spec(), spec()],
        out_specs=spec(),
        compiler_params=params(8),
        cost_estimate=LIGHT,
        name="stack",
    )(k, v)


def choose(n, cap, per, arrive_ref, d, got_refs, skips, held, keys, vals):
    half, plane = n // 2, n // 4
    me = lax.axis_index("seq")
    size = held.shape[1]
    for k, got_ref in enumerate(got_refs):
        held[k] = got_ref[pl.ds(skips[k // plane], size)]
    biases = []
    for i in range(per):
        row = []
        for r in range(R):
            spot = arrive_ref[r, d * per + i]
            group = lax.div(spot, cap)
            differ = lax.bitwise_xor(group, me)
            here = differ < half
            slot = jnp.where(here, spot - group * cap, 0)
            k = jnp.where(here, differ, 0)
            at = pl.ds((i * R + r) * BLOCK, BLOCK)
            keys[at] = held[k, pl.ds(pl.multiple_of(slot * BLOCK, BLOCK), BLOCK), :]
            vals[at] = held[k, pl.ds(pl.multiple_of((cap + slot) * BLOCK, BLOCK), BLOCK), :]
            row.append(jnp.where(here, 0.0, NONE))
        biases.append(row)
    return biases


def shared_blocks(n, per, place_ref, got_refs, skip, glob, ends):
    plane = n // 4
    me = lax.axis_index("seq")
    place = lax.bitwise_and(me, plane - 1)
    biases = []
    for g in range(G):
        differ = lax.bitwise_xor(lax.div(place_ref[g], per), me)
        for p, got_ref in enumerate(got_refs):
            @pl.when(lax.bitwise_and(differ, plane - 1) == p)
            def _(g=g, got_ref=got_ref):
                for c in range(2):
                    at = (c * G + g) * BLOCK
                    glob[pl.ds(at, BLOCK)] = got_ref[pl.ds(skip + at, BLOCK)]
        biases.append(jnp.where(differ < n // 2, 0.0, NONE))
    for e, neighbour in enumerate((place + plane - 1, place + 1)):
        k = lax.bitwise_xor(place, lax.bitwise_and(neighbour, plane - 1))
        for p, got_ref in enumerate(got_refs):
            @pl.when(k == p)
            def _(e=e, got_ref=got_ref):
                ends[pl.ds(e * 2 * BLOCK, 2 * BLOCK)] = got_ref[
                    pl.ds(skip + 2 * G * BLOCK, 2 * BLOCK)
                ]
    return biases


def widen(biases):
    count = len(biases)
    lane = lax.broadcasted_iota(I32, (1, count * BLOCK), 1)
    bias = jnp.full((1, count * BLOCK), biases[-1], F32)
    for r in reversed(range(count - 1)):
        bias = jnp.where(lane < (r + 1) * BLOCK, biases[r], bias)
    return bias


def batches(per, heads, step):
    for first in range(0, per, step):
        yield [(i, h) for i in range(first, min(per, first + step)) for h in range(heads)]


def rows_of(i):
    return pl.ds(i * BLOCK, BLOCK)


def picked_of(i):
    return pl.ds(i * R * BLOCK, R * BLOCK)


def cols_of(h):
    return pl.ds(h * DH, DH)


def dot_t(a, b):
    return lax.dot_general(a, b, (((1,), (1,)), ((), ())), preferred_element_type=F32)


def eye():
    shape = (BLOCK, BLOCK)
    return lax.broadcasted_iota(I32, shape, 0) == lax.broadcasted_iota(I32, shape, 1)


def flatten(columns, diagonal):
    return [jnp.sum(jnp.where(diagonal, x, 0.0), axis=0, keepdims=True) for x in columns]


def attend(queries, sets):
    scale = 1.0 / math.sqrt(DH)
    s = [
        [dot_t(q, ks) * scale + bias if bias is not None else dot_t(q, ks) * scale
         for ks, vs, bias in group]
        for q, group in zip(queries, sets)
    ]
    top = [[jnp.max(x, axis=1, keepdims=True) for x in group] for group in s]
    top = [functools.reduce(jnp.maximum, group) for group in top]
    w = [[jnp.exp(x - t) for x in group] for group, t in zip(s, top)]
    total = [sum(jnp.sum(x, axis=1, keepdims=True) for x in group) for group in w]
    part = [
        sum(
            jnp.dot(x.astype(BF16), vs, preferred_element_type=F32)
            for x, (ks, vs, bias) in zip(ws, group)
        )
        for ws, group in zip(w, sets)
    ]
    return part, top, total


def far_kernel(n, cap, per, heads, arrive_ref, place_ref, q_ref, *refs):
    half, plane = n // 2, n // 4
    got_refs = refs[:half]
    out_ref, held, keys, vals, glob, ends, stat, pieces = refs[half:]
    me = lax.axis_index("seq")
    d = lax.bitwise_xor(me, half)
    diagonal = eye()
    stat[...] = jnp.zeros_like(stat)
    size = held.shape[1]
    biases = choose(n, cap, per, arrive_ref, d, got_refs, (0, 0), held, keys, vals)
    glob_bias = widen(shared_blocks(n, per, place_ref, got_refs[plane:], size, glob, ends))
    inside = lax.bitwise_and(me, half - 1)
    end_bias = [jnp.where(inside == x, 0.0, NONE) for x in (0, half - 1)]
    for pairs in batches(per, heads, 3):
        sets = []
        for i, h in pairs:
            cols = cols_of(h)
            group = [
                (keys[picked_of(i), cols], vals[picked_of(i), cols], widen(biases[i])),
                (glob[: G * BLOCK, cols], glob[G * BLOCK :, cols], glob_bias),
            ]
            for e, edge in enumerate((0, per - 1)):
                if i == edge:
                    at = e * 2 * BLOCK
                    group.append(
                        (ends[at : at + BLOCK, cols], ends[at + BLOCK : at + 2 * BLOCK, cols],
                         end_bias[e])
                    )
            sets.append(group)
        part, top, total = attend([q_ref[rows_of(i), cols_of(h)] for i, h in pairs], sets)
        for x, t, (i, h) in zip(part, total, pairs):
            out_ref[rows_of(i), cols_of(h)] = (x / t).astype(BF16)
        for c, columns in enumerate((top, total)):
            for x, (i, h) in zip(flatten(columns, diagonal), pairs):
                stat[i : i + 1, pl.ds(h * DH + c * BLOCK, BLOCK)] = x
    rest = stat[...]
    pieces[...] = jnp.zeros_like(pieces)
    for p in range(PIECES):
        piece = rest.astype(BF16).astype(F32)
        rest = rest - piece
        pieces[p * per : (p + 1) * per] = piece[:per]
    out_ref[pl.ds(per * BLOCK, pieces.shape[0])] = pieces[...].astype(BF16)


def stat_rows(per):
    return -(-per // 8) * 8


def piece_rows(per):
    return -(-PIECES * per // 16) * 16


def scratches(n, cap, per, columns):
    return (
        [pltpu.VMEM((n // 2, 2 * cap * BLOCK, columns), BF16)]
        + [pltpu.VMEM((per * R * BLOCK, columns), BF16)] * 2
        + [pltpu.VMEM((2 * G * BLOCK, columns), BF16), pltpu.VMEM((4 * BLOCK, columns), BF16)]
    )


def far_part(n, cap, per, arrive, places, q, got):
    rows, columns = q.shape
    heads = columns // DH
    return pl.pallas_call(
        functools.partial(far_kernel, n, cap, per, heads),
        out_shape=jax.ShapeDtypeStruct((rows + piece_rows(per), columns), BF16),
        in_specs=[spec(SMEM)] * 2 + [spec()] * (1 + len(got)),
        out_specs=spec(),
        scratch_shapes=scratches(n, cap, per, columns)
        + [pltpu.VMEM((stat_rows(per), columns), F32)]
        + [pltpu.VMEM((piece_rows(per), columns), F32)],
        compiler_params=params(16),
        cost_estimate=LIGHT,
        name="far_part",
    )(arrive, places, q, *got)


def own_kernel(n, cap, per, heads, arrive_ref, place_ref, q_hbm, kv_ref, *refs):
    half, plane = n // 2, n // 4
    got_refs, shared_refs = refs[:half], refs[half : half + plane]
    part_ref, stat_ref, held, rand_keys, rand_vals, glob, ends, keys, vals, q_ref, sem = refs[
        half + plane :
    ]
    fetch = pltpu.make_async_copy(q_hbm, q_ref, sem)
    fetch.start()
    me = lax.axis_index("seq")
    rows = per * BLOCK
    size = held.shape[1]
    diagonal = eye()
    stat_ref[...] = jnp.zeros_like(stat_ref)
    glob_bias = widen(shared_blocks(n, per, place_ref, shared_refs, size, glob, ends))
    keys[:BLOCK] = ends[:BLOCK]
    vals[:BLOCK] = ends[BLOCK : 2 * BLOCK]
    keys[pl.ds(BLOCK, rows)] = kv_ref[pl.ds(0, rows)]
    vals[pl.ds(BLOCK, rows)] = kv_ref[pl.ds(rows, rows)]
    keys[pl.ds(BLOCK + rows, BLOCK)] = ends[2 * BLOCK : 3 * BLOCK]
    vals[pl.ds(BLOCK + rows, BLOCK)] = ends[3 * BLOCK :]
    biases = choose(
        n, cap, per, arrive_ref, me, got_refs, (0, size), held, rand_keys, rand_vals
    )
    inside = lax.bitwise_and(me, half - 1)
    first_bias, last_bias = [jnp.where(inside == x, NONE, 0.0) for x in (0, half - 1)]
    fetch.wait()
    for pairs in batches(per, heads, 2):
        sets = []
        for i, h in pairs:
            window, cols = pl.ds(i * BLOCK, 3 * BLOCK), cols_of(h)
            bias = None
            if i in (0, per - 1):
                bias = widen([first_bias if i == 0 else 0.0, 0.0, last_bias if i else 0.0])
            sets.append(
                [
                    (keys[window, cols], vals[window, cols], bias),
                    (glob[: G * BLOCK, cols], glob[G * BLOCK :, cols], glob_bias),
                    (rand_keys[picked_of(i), cols], rand_vals[picked_of(i), cols], widen(biases[i])),
                ]
            )
        part, top, total = attend([q_ref[rows_of(i), cols_of(h)] for i, h in pairs], sets)
        for x, (i, h) in zip(part, pairs):
            part_ref[rows_of(i), cols_of(h)] = x
        for c, columns in enumerate((top, total)):
            for x, (i, h) in zip(flatten(columns, diagonal), pairs):
                stat_ref[i : i + 1, pl.ds(h * DH + c * BLOCK, BLOCK)] = x


def own_part(n, cap, per, arrive, places, q, kv, got, shared):
    rows, columns = q.shape
    heads = columns // DH
    return pl.pallas_call(
        functools.partial(own_kernel, n, cap, per, heads),
        out_shape=(
            jax.ShapeDtypeStruct((rows, columns), F32),
            jax.ShapeDtypeStruct((stat_rows(per), columns), F32),
        ),
        in_specs=[spec(SMEM)] * 2 + [spec(pl.ANY)] + [spec()] * (1 + len(got) + len(shared)),
        out_specs=(spec(), spec()),
        scratch_shapes=scratches(n, cap, per, columns)
        + [pltpu.VMEM((rows + 2 * BLOCK, columns), BF16)] * 2
        + [pltpu.VMEM((rows, columns), BF16), pltpu.SemaphoreType.DMA],
        compiler_params=params(20),
        cost_estimate=LIGHT,
        name="own_part",
    )(arrive, places, q, kv, *got, *shared)


def context_kernel(per, heads, part_ref, stat_ref, far_ref, out_ref, pieces):
    pieces[...] = far_ref[pl.ds(per * BLOCK, pieces.shape[0])].astype(F32)
    far = sum(pieces[p * per : (p + 1) * per] for p in range(PIECES))
    own = stat_ref[:per]
    weights = []
    for h in range(heads):
        own_top, far_top = [x[:, h * DH : h * DH + BLOCK] for x in (own, far)]
        own_sum, far_sum = [x[:, h * DH + BLOCK : (h + 1) * DH] for x in (own, far)]
        top = jnp.maximum(own_top, far_top)
        own_w = jnp.exp(own_top - top)
        far_w = jnp.exp(far_top - top) * far_sum
        total = own_w * own_sum + far_w
        weights.append((jnp.transpose(own_w / total), jnp.transpose(far_w / total)))
    for i in range(per):
        for h, (own_w, far_w) in enumerate(weights):
            out_ref[rows_of(i), cols_of(h)] = (
                part_ref[rows_of(i), cols_of(h)] * own_w[:, i : i + 1]
                + far_ref[rows_of(i), cols_of(h)].astype(F32) * far_w[:, i : i + 1]
            ).astype(BF16)


def contexts(per, part, stat, far):
    rows, columns = part.shape
    heads = columns // DH
    return pl.pallas_call(
        functools.partial(context_kernel, per, heads),
        out_shape=jax.ShapeDtypeStruct((rows, columns), BF16),
        in_specs=[spec()] * 3,
        out_specs=spec(),
        scratch_shapes=[pltpu.VMEM((piece_rows(per), columns), F32)],
        compiler_params=params(8),
        cost_estimate=LIGHT,
        name="contexts",
    )(part, stat, far)


def project_kernel(own_ref, other_refs, w_ref, out_ref):
    me = lax.axis_index("head")
    count = lax.axis_size("head")
    columns = own_ref.shape[1]
    total = None
    for step, rows_ref in enumerate([own_ref] + list(other_refs)):
        owner = lax.rem(me + step, count)
        at = pl.ds(pl.multiple_of(owner * columns, columns), columns)
        term = jnp.dot(rows_ref[...], w_ref[at, :], preferred_element_type=F32)
        total = term if total is None else total + term
    out_ref[...] = total.astype(BF16)


def project(own, others, w_out):
    rows, columns = own.shape
    wide = w_out.shape[1]
    tile = rows // 4
    block = pl.BlockSpec((tile, columns), lambda i: (i, 0))

    def kernel(own_ref, *refs):
        project_kernel(own_ref, refs[: len(others)], refs[-2], refs[-1])

    return pl.pallas_call(
        kernel,
        grid=(4,),
        out_shape=jax.ShapeDtypeStruct((rows, wide), BF16),
        in_specs=[block] * (1 + len(others)) + [spec()],
        out_specs=pl.BlockSpec((tile, wide), lambda i: (i, 0)),
        compiler_params=params(16),
        cost_estimate=LIGHT,
        name="project",
    )(own, *others, w_out)


def on_device(queries, keys, values, rand_group, rand_offset, glob_blocks, w_out):
    tokens_dev = queries.shape[0]
    per = tokens_dev // BLOCK
    n = lax.axis_size("seq")
    heads = lax.axis_size("head")
    cap = max(2, (rand_group.shape[0] // n * R + n - 1) // n)

    mates = [(i, i ^ (n // 4)) for i in range(n)]
    partners = [(i, i ^ (n // 2)) for i in range(n)]
    kv = stack(keys, values)
    mate_kv = lax.ppermute(kv, "seq", mates)
    far_q = lax.ppermute(queries, "seq", partners)
    spots, arrive = ranks(n, per, cap, rand_group.T, rand_offset.T)
    near_far = exchange(gather(n, per, cap, ((0, True),), spots, [kv]), n)
    both = [kv, mate_kv]
    mate_far = gather(n, per, cap, ((1, True),), spots, both, glob_blocks, near_far[1:4])
    mate_far = exchange(mate_far, n)
    far = far_part(n, cap, per, arrive, glob_blocks, far_q, near_far + mate_far)
    own = exchange(gather(n, per, cap, ((0, False), (1, False)), spots, both, None, [far]), n)
    far = lax.ppermute(far, "seq", partners)
    part, stat = own_part(n, cap, per, arrive, glob_blocks, queries, kv, own + own, mate_far)
    context = contexts(per, part, stat, far)
    others = [
        lax.ppermute(context, "head", [((i + s) % heads, i) for i in range(heads)])
        for s in range(1, heads)
    ]
    return project(context, others, w_out)


def solution(mesh):
    return jax.shard_map(
        on_device,
        mesh=mesh,
        in_specs=(
            P("seq", "head"),
            P("seq", "head"),
            P("seq", "head"),
            P(),
            P(),
            P(),
            P(None, "head"),
        ),
        out_specs=P("seq", "head"),
        check_vma=False,
    )
```

```python
import functools
import math

import jax
import jax.numpy as jnp
from jax import lax
from jax.experimental import pallas as pl
from jax.experimental.pallas import tpu as pltpu
from jax.sharding import PartitionSpec as P

DH = 128
BLOCK = 64
R = 3
G = 2
VMEM = pltpu.MemorySpace.VMEM
SMEM = pltpu.MemorySpace.SMEM
BF16 = jnp.bfloat16
F32 = jnp.float32
I32 = jnp.int32
NONE = -1e30
PIECES = 3


def params(mib):
    return pltpu.CompilerParams(vmem_limit_bytes=mib * 1024 * 1024)


LIGHT = pl.CostEstimate(flops=1, bytes_accessed=1, transcendentals=0)


def spec(space=VMEM):
    return pl.BlockSpec(memory_space=space)


def rank_kernel(n, per, cap, g_ref, o_ref, spot_ref, arrive_ref, g_pad, o_pad):
    me = lax.axis_index("seq")
    nb = g_ref.shape[1]
    wide = g_pad.shape[1]
    tall = spot_ref.shape[0]
    g_pad[...] = jnp.full(g_pad.shape, -1, I32)
    o_pad[...] = jnp.zeros(o_pad.shape, I32)
    g_pad[:R, :nb] = g_ref[...]
    o_pad[:R, :nb] = o_ref[...]
    g = g_pad[...]
    lane = lax.broadcasted_iota(I32, g.shape, 1)
    place = lane
    for d in range(1, n):
        place = jnp.where(lane >= d * per, lane - d * per, place)
    rank = jnp.zeros(g.shape, I32)
    for s in range(1, per):
        back = pltpu.roll(g, s, axis=1)
        ahead = place >= s
        for r in range(R):
            same = jnp.broadcast_to(back[r : r + 1, :], g.shape) == g
            rank = rank + jnp.where(ahead & same, 1, 0)
    arrive_ref[...] = g * cap + rank
    row = lax.broadcasted_iota(I32, (tall, wide), 0)
    spots = jnp.zeros((tall, wide), F32)
    for side in range(2):
        named = jnp.where(g == lax.bitwise_xor(me, side * (n // 4)), o_pad[...], 0)
        for s in range(cap):
            picked = jnp.where(rank == s, named, 0).astype(F32)
            total = jnp.sum(picked, axis=0, keepdims=True)
            here = row == side * cap + s
            spots = spots + jnp.where(here, jnp.broadcast_to(total, (tall, wide)), 0.0)
    token = lax.broadcasted_iota(I32, (wide, 128), 0)
    first = lax.broadcasted_iota(I32, (wide, 128), 1) * per
    belongs = jnp.where((token >= first) & (token < first + per), 1.0, 0.0)
    spot_ref[...] = jnp.dot(
        spots.astype(BF16), belongs.astype(BF16), preferred_element_type=F32
    ).astype(I32)


def ranks(n, per, cap, groups, offsets):
    nb = groups.shape[1]
    wide = -(-nb // 128) * 128
    tall = -(-2 * cap // 8) * 8
    return pl.pallas_call(
        functools.partial(rank_kernel, n, per, cap),
        out_shape=(
            jax.ShapeDtypeStruct((tall, 128), I32),
            jax.ShapeDtypeStruct((8, wide), I32),
        ),
        in_specs=[spec(), spec()],
        out_specs=(spec(), spec()),
        scratch_shapes=[pltpu.VMEM((8, wide), I32), pltpu.VMEM((8, wide), I32)],
        compiler_params=params(4),
        cost_estimate=LIGHT,
        name="ranks",
    )(groups, offsets)


def gather_kernel(n, per, cap, lists, shared, count, spot_ref, *refs):
    plane = n // 4
    me = lax.axis_index("seq")
    size = 2 * cap * BLOCK
    sources, outs = refs[:count], refs[-plane:]
    place_ref, shared_refs = refs[count], refs[count + 1 : count + 3]
    for k, out_ref in enumerate(outs):
        for u, (side, far) in enumerate(lists):
            d = lax.bitwise_xor(me, k + (n // 2 if far else 0))
            for s in range(cap):
                start = spot_ref[side * cap + s, d] * BLOCK
                for c in range(2):
                    rows = pl.ds(pl.multiple_of(start + c * per * BLOCK, BLOCK), BLOCK)
                    out_ref[pl.ds(u * size + (c * cap + s) * BLOCK, BLOCK)] = sources[side][rows]
        if shared:
            shared_rows(
                n, per, k, len(lists) * size, place_ref, sources[0], shared_refs, out_ref
            )


def shared_rows(n, per, k, skip, place_ref, kv_ref, shared_refs, out_ref):
    plane = n // 4
    me = lax.axis_index("seq")
    place = lax.bitwise_and(me, plane - 1)
    own_ref, mate_ref = shared_refs
    for g in range(G):
        mine = lax.bitwise_and(lax.bitwise_xor(lax.div(place_ref[g], per), me), plane) == 0
        for c in range(2):
            rows = pl.ds((c * G + g) * BLOCK, BLOCK)
            out_ref[pl.ds(skip + (c * G + g) * BLOCK, BLOCK)] = jnp.where(
                mine, own_ref[rows], mate_ref[rows]
            )
    target = lax.bitwise_xor(place, k)
    is_before = lax.rem(place + 1, plane) == target
    is_end = jnp.where(is_before, target == 0, target == plane - 1)
    for c in range(2):
        first, last = pl.ds(c * per * BLOCK, BLOCK), pl.ds(((c + 1) * per - 1) * BLOCK, BLOCK)
        rows = pl.ds((2 * G + c) * BLOCK, BLOCK)
        owns = jnp.where(is_before, kv_ref[last], kv_ref[first])
        out_ref[pl.ds(skip + (2 * G + c) * BLOCK, BLOCK)] = jnp.where(
            is_end, mate_ref[rows], owns
        )


def gather(n, per, cap, lists, spots, sources, shared=(), earlier=()):
    plane = n // 4
    rows = 2 * cap * BLOCK * len(lists) + (2 * (G + 1) * BLOCK if shared else 0)
    out = jax.ShapeDtypeStruct((rows, sources[0].shape[1]), BF16)
    return pl.pallas_call(
        functools.partial(gather_kernel, n, per, cap, lists, bool(shared), len(sources)),
        out_shape=(out,) * plane,
        in_specs=[spec(SMEM)]
        + [spec()] * len(sources)
        + ([spec(SMEM), spec(), spec()] if shared else [])
        + [spec(pl.ANY)] * len(earlier),
        out_specs=(spec(),) * plane,
        compiler_params=params(8),
        cost_estimate=LIGHT,
        name="gather_blocks",
    )(spots, *sources, *shared, *earlier)


def exchange(parts, n):
    got = [parts[0]]
    for k in range(1, n // 4):
        got.append(lax.ppermute(parts[k], "seq", [(i, i ^ k) for i in range(n)]))
    return got


def stack_kernel(n, per, place_ref, k_ref, v_ref, kv_ref, out_ref):
    rows, plane = per * BLOCK, n // 4
    at_end = lax.bitwise_and(lax.axis_index("seq"), plane - 1) == plane - 1
    for c, own in enumerate((k_ref, v_ref)):
        kv_ref[pl.ds(c * rows, rows)] = own[...]
        for g in range(G):
            start = pl.multiple_of(lax.rem(place_ref[g], per) * BLOCK, BLOCK)
            out_ref[pl.ds((c * G + g) * BLOCK, BLOCK)] = own[pl.ds(start, BLOCK)]
        first, last = own[:BLOCK], own[rows - BLOCK :]
        out_ref[pl.ds((2 * G + c) * BLOCK, BLOCK)] = jnp.where(at_end, last, first)


def stack(n, per, places, k, v):
    rows, columns = k.shape
    return pl.pallas_call(
        functools.partial(stack_kernel, n, per),
        out_shape=(
            jax.ShapeDtypeStruct((2 * rows, columns), BF16),
            jax.ShapeDtypeStruct((2 * (G + 1) * BLOCK, columns), BF16),
        ),
        in_specs=[spec(SMEM), spec(), spec()],
        out_specs=(spec(), spec()),
        compiler_params=params(8),
        cost_estimate=LIGHT,
        name="stack",
    )(places, k, v)


def choose(n, cap, per, arrive_ref, d, got_refs, skips, held, keys, vals):
    half, plane = n // 2, n // 4
    me = lax.axis_index("seq")
    size = held.shape[1]
    for k, got_ref in enumerate(got_refs):
        held[k] = got_ref[pl.ds(skips[k // plane], size)]
    biases = []
    for i in range(per):
        row = []
        for r in range(R):
            spot = arrive_ref[r, d * per + i]
            group = lax.div(spot, cap)
            differ = lax.bitwise_xor(group, me)
            here = differ < half
            slot = jnp.where(here, spot - group * cap, 0)
            k = jnp.where(here, differ, 0)
            at = pl.ds((i * R + r) * BLOCK, BLOCK)
            keys[at] = held[k, pl.ds(pl.multiple_of(slot * BLOCK, BLOCK), BLOCK), :]
            vals[at] = held[k, pl.ds(pl.multiple_of((cap + slot) * BLOCK, BLOCK), BLOCK), :]
            row.append(jnp.where(here, 0.0, NONE))
        biases.append(row)
    return biases


def shared_blocks(n, per, place_ref, got_refs, skip, glob, ends):
    plane = n // 4
    me = lax.axis_index("seq")
    place = lax.bitwise_and(me, plane - 1)
    biases = []
    for g in range(G):
        differ = lax.bitwise_xor(lax.div(place_ref[g], per), me)
        for p, got_ref in enumerate(got_refs):
            @pl.when(lax.bitwise_and(differ, plane - 1) == p)
            def _(g=g, got_ref=got_ref):
                for c in range(2):
                    at = (c * G + g) * BLOCK
                    glob[pl.ds(at, BLOCK)] = got_ref[pl.ds(skip + at, BLOCK)]
        biases.append(jnp.where(differ < n // 2, 0.0, NONE))
    for e, neighbour in enumerate((place + plane - 1, place + 1)):
        k = lax.bitwise_xor(place, lax.bitwise_and(neighbour, plane - 1))
        for p, got_ref in enumerate(got_refs):
            @pl.when(k == p)
            def _(e=e, got_ref=got_ref):
                ends[pl.ds(e * 2 * BLOCK, 2 * BLOCK)] = got_ref[
                    pl.ds(skip + 2 * G * BLOCK, 2 * BLOCK)
                ]
    return biases


def widen(biases):
    count = len(biases)
    lane = lax.broadcasted_iota(I32, (1, count * BLOCK), 1)
    bias = jnp.full((1, count * BLOCK), biases[-1], F32)
    for r in reversed(range(count - 1)):
        bias = jnp.where(lane < (r + 1) * BLOCK, biases[r], bias)
    return bias


def batches(per, heads, step):
    for first in range(0, per, step):
        yield [(i, h) for i in range(first, min(per, first + step)) for h in range(heads)]


def rows_of(i):
    return pl.ds(i * BLOCK, BLOCK)


def picked_of(i):
    return pl.ds(i * R * BLOCK, R * BLOCK)


def cols_of(h):
    return pl.ds(h * DH, DH)


def dot_t(a, b):
    return lax.dot_general(a, b, (((1,), (1,)), ((), ())), preferred_element_type=F32)


def eye():
    shape = (BLOCK, BLOCK)
    return lax.broadcasted_iota(I32, shape, 0) == lax.broadcasted_iota(I32, shape, 1)


def flatten(columns, diagonal):
    return [jnp.sum(jnp.where(diagonal, x, 0.0), axis=0, keepdims=True) for x in columns]


def attend(queries, sets):
    scale = 1.0 / math.sqrt(DH)
    s = [
        [dot_t(q, ks) * scale + bias if bias is not None else dot_t(q, ks) * scale
         for ks, vs, bias in group]
        for q, group in zip(queries, sets)
    ]
    top = [[jnp.max(x, axis=1, keepdims=True) for x in group] for group in s]
    top = [functools.reduce(jnp.maximum, group) for group in top]
    w = [[jnp.exp(x - t) for x in group] for group, t in zip(s, top)]
    total = [sum(jnp.sum(x, axis=1, keepdims=True) for x in group) for group in w]
    part = [
        sum(
            jnp.dot(x.astype(BF16), vs, preferred_element_type=F32)
            for x, (ks, vs, bias) in zip(ws, group)
        )
        for ws, group in zip(w, sets)
    ]
    return part, top, total


def far_kernel(n, cap, per, heads, arrive_ref, place_ref, q_ref, *refs):
    half, plane = n // 2, n // 4
    got_refs = refs[:half]
    out_ref, held, keys, vals, glob, ends, stat, pieces = refs[half:]
    me = lax.axis_index("seq")
    d = lax.bitwise_xor(me, half)
    diagonal = eye()
    stat[...] = jnp.zeros_like(stat)
    size = held.shape[1]
    biases = choose(n, cap, per, arrive_ref, d, got_refs, (0, 0), held, keys, vals)
    glob_bias = widen(shared_blocks(n, per, place_ref, got_refs[:plane], size, glob, ends))
    inside = lax.bitwise_and(me, half - 1)
    end_bias = [jnp.where(inside == x, 0.0, NONE) for x in (0, half - 1)]
    for pairs in batches(per, heads, 3):
        sets = []
        for i, h in pairs:
            cols = cols_of(h)
            group = [
                (keys[picked_of(i), cols], vals[picked_of(i), cols], widen(biases[i])),
                (glob[: G * BLOCK, cols], glob[G * BLOCK :, cols], glob_bias),
            ]
            for e, edge in enumerate((0, per - 1)):
                if i == edge:
                    at = e * 2 * BLOCK
                    group.append(
                        (ends[at : at + BLOCK, cols], ends[at + BLOCK : at + 2 * BLOCK, cols],
                         end_bias[e])
                    )
            sets.append(group)
        part, top, total = attend([q_ref[rows_of(i), cols_of(h)] for i, h in pairs], sets)
        for x, t, (i, h) in zip(part, total, pairs):
            out_ref[rows_of(i), cols_of(h)] = (x / t).astype(BF16)
        for c, columns in enumerate((top, total)):
            for x, (i, h) in zip(flatten(columns, diagonal), pairs):
                stat[i : i + 1, pl.ds(h * DH + c * BLOCK, BLOCK)] = x
    rest = stat[...]
    pieces[...] = jnp.zeros_like(pieces)
    for p in range(PIECES):
        piece = rest.astype(BF16).astype(F32)
        rest = rest - piece
        pieces[p * per : (p + 1) * per] = piece[:per]
    out_ref[pl.ds(per * BLOCK, pieces.shape[0])] = pieces[...].astype(BF16)


def stat_rows(per):
    return -(-per // 8) * 8


def piece_rows(per):
    return -(-PIECES * per // 16) * 16


def scratches(n, cap, per, columns):
    return (
        [pltpu.VMEM((n // 2, 2 * cap * BLOCK, columns), BF16)]
        + [pltpu.VMEM((per * R * BLOCK, columns), BF16)] * 2
        + [pltpu.VMEM((2 * G * BLOCK, columns), BF16), pltpu.VMEM((4 * BLOCK, columns), BF16)]
    )


def far_part(n, cap, per, arrive, places, q, got):
    rows, columns = q.shape
    heads = columns // DH
    return pl.pallas_call(
        functools.partial(far_kernel, n, cap, per, heads),
        out_shape=jax.ShapeDtypeStruct((rows + piece_rows(per), columns), BF16),
        in_specs=[spec(SMEM)] * 2 + [spec()] * (1 + len(got)),
        out_specs=spec(),
        scratch_shapes=scratches(n, cap, per, columns)
        + [pltpu.VMEM((stat_rows(per), columns), F32)]
        + [pltpu.VMEM((piece_rows(per), columns), F32)],
        compiler_params=params(16),
        cost_estimate=LIGHT,
        name="far_part",
    )(arrive, places, q, *got)


def store_part(heads, pairs, part, top, total, part_ref, stat_ref, diagonal):
    for x, (i, h) in zip(part, pairs):
        part_ref[rows_of(i), cols_of(h)] = x
    for c, columns in enumerate((top, total)):
        for x, (i, h) in zip(flatten(columns, diagonal), pairs):
            stat_ref[i : i + 1, pl.ds(h * DH + c * BLOCK, BLOCK)] = x


def near_kernel(n, cap, per, heads, place_ref, q_ref, kv_ref, *refs):
    half, plane = n // 2, n // 4
    shared_refs = refs[:plane]
    part_ref, stat_ref, glob, ends, keys, vals = refs[plane:]
    me = lax.axis_index("seq")
    rows = per * BLOCK
    diagonal = eye()
    stat_ref[...] = jnp.zeros_like(stat_ref)
    size = 2 * cap * BLOCK
    glob_bias = widen(shared_blocks(n, per, place_ref, shared_refs, size, glob, ends))
    keys[:BLOCK] = ends[:BLOCK]
    vals[:BLOCK] = ends[BLOCK : 2 * BLOCK]
    keys[pl.ds(BLOCK, rows)] = kv_ref[pl.ds(0, rows)]
    vals[pl.ds(BLOCK, rows)] = kv_ref[pl.ds(rows, rows)]
    keys[pl.ds(BLOCK + rows, BLOCK)] = ends[2 * BLOCK : 3 * BLOCK]
    vals[pl.ds(BLOCK + rows, BLOCK)] = ends[3 * BLOCK :]
    inside = lax.bitwise_and(me, half - 1)
    first_bias, last_bias = [jnp.where(inside == x, NONE, 0.0) for x in (0, half - 1)]
    for pairs in batches(per, heads, 2):
        sets = []
        for i, h in pairs:
            window, cols = pl.ds(i * BLOCK, 3 * BLOCK), cols_of(h)
            bias = None
            if i in (0, per - 1):
                bias = widen([first_bias if i == 0 else 0.0, 0.0, last_bias if i else 0.0])
            sets.append(
                [
                    (keys[window, cols], vals[window, cols], bias),
                    (glob[: G * BLOCK, cols], glob[G * BLOCK :, cols], glob_bias),
                ]
            )
        parts = attend([q_ref[rows_of(i), cols_of(h)] for i, h in pairs], sets)
        store_part(heads, pairs, *parts, part_ref, stat_ref, diagonal)


def part_shapes(per, columns):
    return (
        jax.ShapeDtypeStruct((per * BLOCK, columns), F32),
        jax.ShapeDtypeStruct((stat_rows(per), columns), F32),
    )


def near_part(n, cap, per, places, q, kv, shared):
    rows, columns = q.shape
    heads = columns // DH
    return pl.pallas_call(
        functools.partial(near_kernel, n, cap, per, heads),
        out_shape=part_shapes(per, columns),
        in_specs=[spec(SMEM)] + [spec()] * (2 + len(shared)),
        out_specs=(spec(), spec()),
        scratch_shapes=scratches(n, cap, per, columns)[3:]
        + [pltpu.VMEM((rows + 2 * BLOCK, columns), BF16)] * 2,
        compiler_params=params(16),
        cost_estimate=LIGHT,
        name="near_part",
    )(places, q, kv, *shared)


def rand_kernel(n, cap, per, heads, arrive_ref, q_ref, *refs):
    got_refs = refs[: n // 4] * 2
    part_ref, stat_ref, held, keys, vals = refs[n // 4 :]
    diagonal = eye()
    stat_ref[...] = jnp.zeros_like(stat_ref)
    skips = (0, held.shape[1])
    me = lax.axis_index("seq")
    biases = choose(n, cap, per, arrive_ref, me, got_refs, skips, held, keys, vals)
    for pairs in batches(per, heads, 4):
        sets = [
            [(keys[picked_of(i), cols_of(h)], vals[picked_of(i), cols_of(h)], widen(biases[i]))]
            for i, h in pairs
        ]
        parts = attend([q_ref[rows_of(i), cols_of(h)] for i, h in pairs], sets)
        store_part(heads, pairs, *parts, part_ref, stat_ref, diagonal)


def rand_part(n, cap, per, arrive, q, got):
    columns = q.shape[1]
    return pl.pallas_call(
        functools.partial(rand_kernel, n, cap, per, columns // DH),
        out_shape=part_shapes(per, columns),
        in_specs=[spec(SMEM), spec()] + [spec()] * len(got),
        out_specs=(spec(), spec()),
        scratch_shapes=scratches(n, cap, per, columns)[:3],
        compiler_params=params(16),
        cost_estimate=LIGHT,
        name="rand_part",
    )(arrive, q, *got)


def context_kernel(
    per, heads, near_ref, near_stat_ref, rand_ref, rand_stat_ref, far_ref, out_ref, pieces
):
    pieces[...] = far_ref[pl.ds(per * BLOCK, pieces.shape[0])].astype(F32)
    far = sum(pieces[p * per : (p + 1) * per] for p in range(PIECES))
    stats = (near_stat_ref[:per], rand_stat_ref[:per], far)
    weights = []
    for h in range(heads):
        tops = [x[:, h * DH : h * DH + BLOCK] for x in stats]
        sums = [x[:, h * DH + BLOCK : (h + 1) * DH] for x in stats]
        top = functools.reduce(jnp.maximum, tops)
        w = [jnp.exp(x - top) for x in tops]
        total = sum(x * y for x, y in zip(w, sums))
        w[2] = w[2] * sums[2]
        weights.append([jnp.transpose(x / total) for x in w])
    for i in range(per):
        for h, ws in enumerate(weights):
            rows, cols = rows_of(i), cols_of(h)
            parts = (near_ref[rows, cols], rand_ref[rows, cols], far_ref[rows, cols].astype(F32))
            out_ref[rows, cols] = sum(x * w[:, i : i + 1] for x, w in zip(parts, ws)).astype(BF16)


def contexts(per, near, near_stat, rand, rand_stat, far):
    rows, columns = near.shape
    heads = columns // DH
    return pl.pallas_call(
        functools.partial(context_kernel, per, heads),
        out_shape=jax.ShapeDtypeStruct((rows, columns), BF16),
        in_specs=[spec()] * 5,
        out_specs=spec(),
        scratch_shapes=[pltpu.VMEM((piece_rows(per), columns), F32)],
        compiler_params=params(8),
        cost_estimate=LIGHT,
        name="contexts",
    )(near, near_stat, rand, rand_stat, far)


def project_kernel(own_ref, other_refs, w_ref, out_ref):
    me = lax.axis_index("head")
    count = lax.axis_size("head")
    columns = own_ref.shape[1]
    total = None
    for step, rows_ref in enumerate([own_ref] + list(other_refs)):
        owner = lax.rem(me + step, count)
        at = pl.ds(pl.multiple_of(owner * columns, columns), columns)
        term = jnp.dot(rows_ref[...], w_ref[at, :], preferred_element_type=F32)
        total = term if total is None else total + term
    out_ref[...] = total.astype(BF16)


def project(own, others, w_out):
    rows, columns = own.shape
    wide = w_out.shape[1]
    tile = rows // 4
    block = pl.BlockSpec((tile, columns), lambda i: (i, 0))

    def kernel(own_ref, *refs):
        project_kernel(own_ref, refs[: len(others)], refs[-2], refs[-1])

    return pl.pallas_call(
        kernel,
        grid=(4,),
        out_shape=jax.ShapeDtypeStruct((rows, wide), BF16),
        in_specs=[block] * (1 + len(others)) + [spec()],
        out_specs=pl.BlockSpec((tile, wide), lambda i: (i, 0)),
        compiler_params=params(16),
        cost_estimate=LIGHT,
        name="project",
    )(own, *others, w_out)


def on_device(queries, keys, values, rand_group, rand_offset, glob_blocks, w_out):
    tokens_dev = queries.shape[0]
    per = tokens_dev // BLOCK
    n = lax.axis_size("seq")
    heads = lax.axis_size("head")
    cap = max(2, (rand_group.shape[0] // n * R + n - 1) // n)

    mates = [(i, i ^ (n // 4)) for i in range(n)]
    partners = [(i, i ^ (n // 2)) for i in range(n)]
    kv, packed = stack(n, per, glob_blocks, keys, values)
    mate_packed = lax.ppermute(packed, "seq", mates)
    mate_kv = lax.ppermute(kv, "seq", mates)
    later_q, _ = lax.optimization_barrier((queries, mate_packed))
    far_q = lax.ppermute(later_q, "seq", partners)
    spots, arrive = ranks(n, per, cap, rand_group.T, rand_offset.T)
    shared = [glob_blocks, packed, mate_packed]
    near_far = exchange(gather(n, per, cap, ((0, True),), spots, [kv], shared), n)
    both = [kv, mate_kv]
    mate_far = gather(n, per, cap, ((1, True),), spots, both, (), near_far[1:4])
    mate_far = exchange(mate_far, n)
    far = far_part(n, cap, per, arrive, glob_blocks, far_q, near_far + mate_far)
    own = exchange(gather(n, per, cap, ((0, False), (1, False)), spots, both, (), [far]), n)
    far = lax.ppermute(far, "seq", partners)
    near, near_stat = near_part(n, cap, per, glob_blocks, queries, kv, near_far)
    rand, rand_stat = rand_part(n, cap, per, arrive, queries, own)
    context = contexts(per, near, near_stat, rand, rand_stat, far)
    others = [
        lax.ppermute(context, "head", [((i + s) % heads, i) for i in range(heads)])
        for s in range(1, heads)
    ]
    return project(context, others, w_out)


def solution(mesh):
    return jax.shard_map(
        on_device,
        mesh=mesh,
        in_specs=(
            P("seq", "head"),
            P("seq", "head"),
            P("seq", "head"),
            P(),
            P(),
            P(),
            P(None, "head"),
        ),
        out_specs=P("seq", "head"),
        check_vma=False,
    )
```

```python
import functools
import math

import jax
import jax.numpy as jnp
from jax import lax
from jax.experimental import pallas as pl
from jax.experimental.pallas import tpu as pltpu
from jax.sharding import PartitionSpec as P

DH = 128
BLOCK = 64
R = 3
G = 2
VMEM = pltpu.MemorySpace.VMEM
SMEM = pltpu.MemorySpace.SMEM
BF16 = jnp.bfloat16
F32 = jnp.float32
I32 = jnp.int32
NONE = -1e30
PIECES = 3


def params(mib):
    return pltpu.CompilerParams(vmem_limit_bytes=mib * 1024 * 1024)


LIGHT = pl.CostEstimate(flops=1, bytes_accessed=1, transcendentals=0)


def spec(space=VMEM):
    return pl.BlockSpec(memory_space=space)


def rank_kernel(n, per, cap, g_ref, o_ref, spot_ref, arrive_ref, g_pad, o_pad):
    me = lax.axis_index("seq")
    nb = g_ref.shape[1]
    wide = g_pad.shape[1]
    tall = spot_ref.shape[0]
    g_pad[...] = jnp.full(g_pad.shape, -1, I32)
    o_pad[...] = jnp.zeros(o_pad.shape, I32)
    g_pad[:R, :nb] = g_ref[...]
    o_pad[:R, :nb] = o_ref[...]
    g = g_pad[...]
    lane = lax.broadcasted_iota(I32, g.shape, 1)
    place = lane
    for d in range(1, n):
        place = jnp.where(lane >= d * per, lane - d * per, place)
    rank = jnp.zeros(g.shape, I32)
    for s in range(1, per):
        back = pltpu.roll(g, s, axis=1)
        ahead = place >= s
        for r in range(R):
            same = jnp.broadcast_to(back[r : r + 1, :], g.shape) == g
            rank = rank + jnp.where(ahead & same, 1, 0)
    arrive_ref[...] = g * cap + rank
    row = lax.broadcasted_iota(I32, (tall, wide), 0)
    spots = jnp.zeros((tall, wide), F32)
    for side in range(2):
        named = jnp.where(g == lax.bitwise_xor(me, side * (n // 4)), o_pad[...], 0)
        for s in range(cap):
            picked = jnp.where(rank == s, named, 0).astype(F32)
            total = jnp.sum(picked, axis=0, keepdims=True)
            here = row == side * cap + s
            spots = spots + jnp.where(here, jnp.broadcast_to(total, (tall, wide)), 0.0)
    token = lax.broadcasted_iota(I32, (wide, 128), 0)
    first = lax.broadcasted_iota(I32, (wide, 128), 1) * per
    belongs = jnp.where((token >= first) & (token < first + per), 1.0, 0.0)
    spot_ref[...] = jnp.dot(
        spots.astype(BF16), belongs.astype(BF16), preferred_element_type=F32
    ).astype(I32)


def ranks(n, per, cap, groups, offsets):
    nb = groups.shape[1]
    wide = -(-nb // 128) * 128
    tall = -(-2 * cap // 8) * 8
    return pl.pallas_call(
        functools.partial(rank_kernel, n, per, cap),
        out_shape=(
            jax.ShapeDtypeStruct((tall, 128), I32),
            jax.ShapeDtypeStruct((8, wide), I32),
        ),
        in_specs=[spec(), spec()],
        out_specs=(spec(), spec()),
        scratch_shapes=[pltpu.VMEM((8, wide), I32), pltpu.VMEM((8, wide), I32)],
        compiler_params=params(4),
        cost_estimate=LIGHT,
        name="ranks",
    )(groups, offsets)


def gather_kernel(n, per, cap, lists, shared, count, spot_ref, *refs):
    plane = n // 4
    me = lax.axis_index("seq")
    size = 2 * cap * BLOCK
    sources, outs = refs[:count], refs[-plane:]
    for k, out_ref in enumerate(outs):
        for u, (side, far) in enumerate(lists):
            d = lax.bitwise_xor(me, k + (n // 2 if far else 0))
            for s in range(cap):
                start = spot_ref[side * cap + s, d] * BLOCK
                rows = pl.ds(pl.multiple_of(start, BLOCK), BLOCK)
                for c in range(2):
                    at = pl.ds(u * size + (c * cap + s) * BLOCK, BLOCK)
                    out_ref[at] = sources[2 * side + c][rows]
        if shared:
            shared_rows(n, per, k, len(lists) * size, refs[count], sources, out_ref)


def shared_rows(n, per, k, skip, place_ref, sources, out_ref):
    plane = n // 4
    me = lax.axis_index("seq")
    place = lax.bitwise_and(me, plane - 1)
    target = lax.bitwise_xor(place, k)
    is_before = lax.rem(place + 1, plane) == target
    is_end = jnp.where(is_before, target == 0, target == plane - 1)
    edge = pl.multiple_of(jnp.where(is_before, (per - 1) * BLOCK, 0), BLOCK)
    for c in range(2):
        own_ref, mate_ref = sources[c], sources[2 + c]
        for g in range(G):
            owner = lax.div(place_ref[g], per)
            start = pl.multiple_of((place_ref[g] - owner * per) * BLOCK, BLOCK)
            rows = pl.ds(start, BLOCK)
            mine = lax.bitwise_and(lax.bitwise_xor(owner, me), plane) == 0
            out_ref[pl.ds(skip + (c * G + g) * BLOCK, BLOCK)] = jnp.where(
                mine, own_ref[rows], mate_ref[rows]
            )
        rows = pl.ds(edge, BLOCK)
        out_ref[pl.ds(skip + (2 * G + c) * BLOCK, BLOCK)] = jnp.where(
            is_end, mate_ref[rows], own_ref[rows]
        )


def gather(n, per, cap, lists, spots, sources, shared=(), earlier=()):
    plane = n // 4
    rows = 2 * cap * BLOCK * len(lists) + (2 * (G + 1) * BLOCK if shared else 0)
    out = jax.ShapeDtypeStruct((rows, sources[0].shape[1]), BF16)
    return pl.pallas_call(
        functools.partial(gather_kernel, n, per, cap, lists, bool(shared), len(sources)),
        out_shape=(out,) * plane,
        in_specs=[spec(SMEM)]
        + [spec()] * len(sources)
        + [spec(SMEM)] * len(shared)
        + [spec(pl.ANY)] * len(earlier),
        out_specs=(spec(),) * plane,
        compiler_params=params(8),
        cost_estimate=LIGHT,
        name="gather_blocks",
    )(spots, *sources, *shared, *earlier)


def exchange(parts, n):
    got = [parts[0]]
    for k in range(1, n // 4):
        got.append(lax.ppermute(parts[k], "seq", [(i, i ^ k) for i in range(n)]))
    return got


def choose(n, cap, per, arrive_ref, d, got_refs, skips, held, keys, vals):
    half, plane = n // 2, n // 4
    me = lax.axis_index("seq")
    size = held.shape[1]
    for k, got_ref in enumerate(got_refs):
        held[k] = got_ref[pl.ds(skips[k // plane], size)]
    biases = []
    for i in range(per):
        row = []
        for r in range(R):
            spot = arrive_ref[r, d * per + i]
            group = lax.div(spot, cap)
            differ = lax.bitwise_xor(group, me)
            here = differ < half
            slot = jnp.where(here, spot - group * cap, 0)
            k = jnp.where(here, differ, 0)
            at = pl.ds((i * R + r) * BLOCK, BLOCK)
            keys[at] = held[k, pl.ds(pl.multiple_of(slot * BLOCK, BLOCK), BLOCK), :]
            vals[at] = held[k, pl.ds(pl.multiple_of((cap + slot) * BLOCK, BLOCK), BLOCK), :]
            row.append(jnp.where(here, 0.0, NONE))
        biases.append(row)
    return biases


def shared_blocks(n, per, place_ref, got_refs, skip, glob, ends):
    plane = n // 4
    me = lax.axis_index("seq")
    place = lax.bitwise_and(me, plane - 1)
    biases = []
    for g in range(G):
        differ = lax.bitwise_xor(lax.div(place_ref[g], per), me)
        for p, got_ref in enumerate(got_refs):
            @pl.when(lax.bitwise_and(differ, plane - 1) == p)
            def _(g=g, got_ref=got_ref):
                for c in range(2):
                    at = (c * G + g) * BLOCK
                    glob[pl.ds(at, BLOCK)] = got_ref[pl.ds(skip + at, BLOCK)]
        biases.append(jnp.where(differ < n // 2, 0.0, NONE))
    for e, neighbour in enumerate((place + plane - 1, place + 1)):
        k = lax.bitwise_xor(place, lax.bitwise_and(neighbour, plane - 1))
        for p, got_ref in enumerate(got_refs):
            @pl.when(k == p)
            def _(e=e, got_ref=got_ref):
                ends[pl.ds(e * 2 * BLOCK, 2 * BLOCK)] = got_ref[
                    pl.ds(skip + 2 * G * BLOCK, 2 * BLOCK)
                ]
    return biases


def widen(biases):
    count = len(biases)
    lane = lax.broadcasted_iota(I32, (1, count * BLOCK), 1)
    bias = jnp.full((1, count * BLOCK), biases[-1], F32)
    for r in reversed(range(count - 1)):
        bias = jnp.where(lane < (r + 1) * BLOCK, biases[r], bias)
    return bias


def batches(per, heads, step):
    for first in range(0, per, step):
        yield [(i, h) for i in range(first, min(per, first + step)) for h in range(heads)]


def rows_of(i):
    return pl.ds(i * BLOCK, BLOCK)


def picked_of(i):
    return pl.ds(i * R * BLOCK, R * BLOCK)


def cols_of(h):
    return pl.ds(h * DH, DH)


def dot_t(a, b):
    return lax.dot_general(a, b, (((1,), (1,)), ((), ())), preferred_element_type=F32)


def eye():
    shape = (BLOCK, BLOCK)
    return lax.broadcasted_iota(I32, shape, 0) == lax.broadcasted_iota(I32, shape, 1)


def flatten(columns, diagonal):
    return [jnp.sum(jnp.where(diagonal, x, 0.0), axis=0, keepdims=True) for x in columns]


def attend(queries, sets):
    scale = 1.0 / math.sqrt(DH)
    s = [
        [dot_t(q, ks) * scale + bias if bias is not None else dot_t(q, ks) * scale
         for ks, vs, bias in group]
        for q, group in zip(queries, sets)
    ]
    top = [[jnp.max(x, axis=1, keepdims=True) for x in group] for group in s]
    top = [functools.reduce(jnp.maximum, group) for group in top]
    w = [[jnp.exp(x - t) for x in group] for group, t in zip(s, top)]
    total = [sum(jnp.sum(x, axis=1, keepdims=True) for x in group) for group in w]
    part = [
        sum(
            jnp.dot(x.astype(BF16), vs, preferred_element_type=F32)
            for x, (ks, vs, bias) in zip(ws, group)
        )
        for ws, group in zip(w, sets)
    ]
    return part, top, total


def far_kernel(n, cap, per, heads, arrive_ref, place_ref, q_ref, *refs):
    half, plane = n // 2, n // 4
    got_refs = refs[:half]
    out_ref, held, keys, vals, glob, ends, stat, pieces = refs[half:]
    me = lax.axis_index("seq")
    d = lax.bitwise_xor(me, half)
    diagonal = eye()
    stat[...] = jnp.zeros_like(stat)
    size = held.shape[1]
    biases = choose(n, cap, per, arrive_ref, d, got_refs, (0, 0), held, keys, vals)
    glob_bias = widen(shared_blocks(n, per, place_ref, got_refs[plane:], size, glob, ends))
    inside = lax.bitwise_and(me, half - 1)
    end_bias = [jnp.where(inside == x, 0.0, NONE) for x in (0, half - 1)]
    for pairs in batches(per, heads, 3):
        sets = []
        for i, h in pairs:
            cols = cols_of(h)
            group = [
                (keys[picked_of(i), cols], vals[picked_of(i), cols], widen(biases[i])),
                (glob[: G * BLOCK, cols], glob[G * BLOCK :, cols], glob_bias),
            ]
            for e, edge in enumerate((0, per - 1)):
                if i == edge:
                    at = e * 2 * BLOCK
                    group.append(
                        (ends[at : at + BLOCK, cols], ends[at + BLOCK : at + 2 * BLOCK, cols],
                         end_bias[e])
                    )
            sets.append(group)
        part, top, total = attend([q_ref[rows_of(i), cols_of(h)] for i, h in pairs], sets)
        for x, t, (i, h) in zip(part, total, pairs):
            out_ref[rows_of(i), cols_of(h)] = (x / t).astype(BF16)
        for c, columns in enumerate((top, total)):
            for x, (i, h) in zip(flatten(columns, diagonal), pairs):
                stat[i : i + 1, pl.ds(h * DH + c * BLOCK, BLOCK)] = x
    rest = stat[...]
    pieces[...] = jnp.zeros_like(pieces)
    for p in range(PIECES):
        piece = rest.astype(BF16).astype(F32)
        rest = rest - piece
        pieces[p * per : (p + 1) * per] = piece[:per]
    out_ref[pl.ds(per * BLOCK, pieces.shape[0])] = pieces[...].astype(BF16)


def stat_rows(per):
    return -(-per // 8) * 8


def piece_rows(per):
    return -(-PIECES * per // 16) * 16


def scratches(n, cap, per, columns):
    return (
        [pltpu.VMEM((n // 2, 2 * cap * BLOCK, columns), BF16)]
        + [pltpu.VMEM((per * R * BLOCK, columns), BF16)] * 2
        + [pltpu.VMEM((2 * G * BLOCK, columns), BF16), pltpu.VMEM((4 * BLOCK, columns), BF16)]
    )


def far_part(n, cap, per, arrive, places, q, got):
    rows, columns = q.shape
    heads = columns // DH
    return pl.pallas_call(
        functools.partial(far_kernel, n, cap, per, heads),
        out_shape=jax.ShapeDtypeStruct((rows + piece_rows(per), columns), BF16),
        in_specs=[spec(SMEM)] * 2 + [spec()] * (1 + len(got)),
        out_specs=spec(),
        scratch_shapes=scratches(n, cap, per, columns)
        + [pltpu.VMEM((stat_rows(per), columns), F32)]
        + [pltpu.VMEM((piece_rows(per), columns), F32)],
        compiler_params=params(16),
        cost_estimate=LIGHT,
        name="far_part",
    )(arrive, places, q, *got)


def store_part(heads, pairs, part, top, total, part_ref, stat_ref, diagonal):
    for x, (i, h) in zip(part, pairs):
        part_ref[rows_of(i), cols_of(h)] = x
    for c, columns in enumerate((top, total)):
        for x, (i, h) in zip(flatten(columns, diagonal), pairs):
            stat_ref[i : i + 1, pl.ds(h * DH + c * BLOCK, BLOCK)] = x


def near_kernel(n, cap, per, heads, place_ref, q_ref, k_ref, v_ref, *refs):
    half, plane = n // 2, n // 4
    shared_refs = refs[:plane]
    part_ref, stat_ref, glob, ends, keys, vals = refs[plane:]
    me = lax.axis_index("seq")
    rows = per * BLOCK
    diagonal = eye()
    stat_ref[...] = jnp.zeros_like(stat_ref)
    size = 2 * cap * BLOCK
    glob_bias = widen(shared_blocks(n, per, place_ref, shared_refs, size, glob, ends))
    keys[:BLOCK] = ends[:BLOCK]
    vals[:BLOCK] = ends[BLOCK : 2 * BLOCK]
    keys[pl.ds(BLOCK, rows)] = k_ref[...]
    vals[pl.ds(BLOCK, rows)] = v_ref[...]
    keys[pl.ds(BLOCK + rows, BLOCK)] = ends[2 * BLOCK : 3 * BLOCK]
    vals[pl.ds(BLOCK + rows, BLOCK)] = ends[3 * BLOCK :]
    inside = lax.bitwise_and(me, half - 1)
    first_bias, last_bias = [jnp.where(inside == x, NONE, 0.0) for x in (0, half - 1)]
    for pairs in batches(per, heads, 2):
        sets = []
        for i, h in pairs:
            window, cols = pl.ds(i * BLOCK, 3 * BLOCK), cols_of(h)
            bias = None
            if i in (0, per - 1):
                bias = widen([first_bias if i == 0 else 0.0, 0.0, last_bias if i else 0.0])
            sets.append(
                [
                    (keys[window, cols], vals[window, cols], bias),
                    (glob[: G * BLOCK, cols], glob[G * BLOCK :, cols], glob_bias),
                ]
            )
        parts = attend([q_ref[rows_of(i), cols_of(h)] for i, h in pairs], sets)
        store_part(heads, pairs, *parts, part_ref, stat_ref, diagonal)


def part_shapes(per, columns):
    return (
        jax.ShapeDtypeStruct((per * BLOCK, columns), F32),
        jax.ShapeDtypeStruct((stat_rows(per), columns), F32),
    )


def near_part(n, cap, per, places, q, k, v, shared):
    rows, columns = q.shape
    heads = columns // DH
    return pl.pallas_call(
        functools.partial(near_kernel, n, cap, per, heads),
        out_shape=part_shapes(per, columns),
        in_specs=[spec(SMEM)] + [spec()] * (3 + len(shared)),
        out_specs=(spec(), spec()),
        scratch_shapes=scratches(n, cap, per, columns)[3:]
        + [pltpu.VMEM((rows + 2 * BLOCK, columns), BF16)] * 2,
        compiler_params=params(16),
        cost_estimate=LIGHT,
        name="near_part",
    )(places, q, k, v, *shared)


def rand_kernel(n, cap, per, heads, arrive_ref, q_ref, *refs):
    got_refs = refs[: n // 4] * 2
    part_ref, stat_ref, held, keys, vals = refs[n // 4 :]
    diagonal = eye()
    stat_ref[...] = jnp.zeros_like(stat_ref)
    skips = (0, held.shape[1])
    me = lax.axis_index("seq")
    biases = choose(n, cap, per, arrive_ref, me, got_refs, skips, held, keys, vals)
    for pairs in batches(per, heads, 4):
        sets = [
            [(keys[picked_of(i), cols_of(h)], vals[picked_of(i), cols_of(h)], widen(biases[i]))]
            for i, h in pairs
        ]
        parts = attend([q_ref[rows_of(i), cols_of(h)] for i, h in pairs], sets)
        store_part(heads, pairs, *parts, part_ref, stat_ref, diagonal)


def rand_part(n, cap, per, arrive, q, got):
    columns = q.shape[1]
    return pl.pallas_call(
        functools.partial(rand_kernel, n, cap, per, columns // DH),
        out_shape=part_shapes(per, columns),
        in_specs=[spec(SMEM), spec()] + [spec()] * len(got),
        out_specs=(spec(), spec()),
        scratch_shapes=scratches(n, cap, per, columns)[:3],
        compiler_params=params(16),
        cost_estimate=LIGHT,
        name="rand_part",
    )(arrive, q, *got)


def context_kernel(
    per, heads, near_ref, near_stat_ref, rand_ref, rand_stat_ref, far_ref, out_ref, pieces
):
    pieces[...] = far_ref[pl.ds(per * BLOCK, pieces.shape[0])].astype(F32)
    far = sum(pieces[p * per : (p + 1) * per] for p in range(PIECES))
    stats = (near_stat_ref[:per], rand_stat_ref[:per], far)
    weights = []
    for h in range(heads):
        tops = [x[:, h * DH : h * DH + BLOCK] for x in stats]
        sums = [x[:, h * DH + BLOCK : (h + 1) * DH] for x in stats]
        top = functools.reduce(jnp.maximum, tops)
        w = [jnp.exp(x - top) for x in tops]
        total = sum(x * y for x, y in zip(w, sums))
        w[2] = w[2] * sums[2]
        weights.append([jnp.transpose(x / total) for x in w])
    for i in range(per):
        for h, ws in enumerate(weights):
            rows, cols = rows_of(i), cols_of(h)
            parts = (near_ref[rows, cols], rand_ref[rows, cols], far_ref[rows, cols].astype(F32))
            out_ref[rows, cols] = sum(x * w[:, i : i + 1] for x, w in zip(parts, ws)).astype(BF16)


def contexts(per, near, near_stat, rand, rand_stat, far):
    rows, columns = near.shape
    heads = columns // DH
    return pl.pallas_call(
        functools.partial(context_kernel, per, heads),
        out_shape=jax.ShapeDtypeStruct((rows, columns), BF16),
        in_specs=[spec()] * 5,
        out_specs=spec(),
        scratch_shapes=[pltpu.VMEM((piece_rows(per), columns), F32)],
        compiler_params=params(8),
        cost_estimate=LIGHT,
        name="contexts",
    )(near, near_stat, rand, rand_stat, far)


def project_kernel(own_ref, other_refs, w_ref, out_ref):
    me = lax.axis_index("head")
    count = lax.axis_size("head")
    columns = own_ref.shape[1]
    total = None
    for step, rows_ref in enumerate([own_ref] + list(other_refs)):
        owner = lax.rem(me + step, count)
        at = pl.ds(pl.multiple_of(owner * columns, columns), columns)
        term = jnp.dot(rows_ref[...], w_ref[at, :], preferred_element_type=F32)
        total = term if total is None else total + term
    out_ref[...] = total.astype(BF16)


def project(own, others, w_out):
    rows, columns = own.shape
    wide = w_out.shape[1]
    tile = rows // 4
    block = pl.BlockSpec((tile, columns), lambda i: (i, 0))

    def kernel(own_ref, *refs):
        project_kernel(own_ref, refs[: len(others)], refs[-2], refs[-1])

    return pl.pallas_call(
        kernel,
        grid=(4,),
        out_shape=jax.ShapeDtypeStruct((rows, wide), BF16),
        in_specs=[block] * (1 + len(others)) + [spec()],
        out_specs=pl.BlockSpec((tile, wide), lambda i: (i, 0)),
        compiler_params=params(16),
        cost_estimate=LIGHT,
        name="project",
    )(own, *others, w_out)


def on_device(queries, keys, values, rand_group, rand_offset, glob_blocks, w_out):
    tokens_dev = queries.shape[0]
    per = tokens_dev // BLOCK
    n = lax.axis_size("seq")
    heads = lax.axis_size("head")
    cap = max(2, (rand_group.shape[0] // n * R + n - 1) // n)

    mates = [(i, i ^ (n // 4)) for i in range(n)]
    partners = [(i, i ^ (n // 2)) for i in range(n)]
    mate_k = lax.ppermute(keys, "seq", mates)
    mate_v = lax.ppermute(values, "seq", mates)
    later_q, _ = lax.optimization_barrier((queries, mate_k))
    far_q = lax.ppermute(later_q, "seq", partners)
    spots, arrive = ranks(n, per, cap, rand_group.T, rand_offset.T)
    near_far = exchange(gather(n, per, cap, ((0, True),), spots, [keys, values]), n)
    both = [keys, values, mate_k, mate_v]
    mate_far = gather(n, per, cap, ((1, True),), spots, both, [glob_blocks], near_far[1:4])
    mate_far = exchange(mate_far, n)
    far = far_part(n, cap, per, arrive, glob_blocks, far_q, near_far + mate_far)
    own = exchange(gather(n, per, cap, ((0, False), (1, False)), spots, both, (), [far]), n)
    far = lax.ppermute(far, "seq", partners)
    near, near_stat = near_part(n, cap, per, glob_blocks, queries, keys, values, mate_far)
    rand, rand_stat = rand_part(n, cap, per, arrive, queries, own)
    context = contexts(per, near, near_stat, rand, rand_stat, far)
    others = [
        lax.ppermute(context, "head", [((i + s) % heads, i) for i in range(heads)])
        for s in range(1, heads)
    ]
    return project(context, others, w_out)


def solution(mesh):
    return jax.shard_map(
        on_device,
        mesh=mesh,
        in_specs=(
            P("seq", "head"),
            P("seq", "head"),
            P("seq", "head"),
            P(),
            P(),
            P(),
            P(None, "head"),
        ),
        out_specs=P("seq", "head"),
        check_vma=False,
    )
```

```python
import functools
import math

import jax
import jax.numpy as jnp
from jax import lax
from jax.experimental import pallas as pl
from jax.experimental.pallas import tpu as pltpu
from jax.sharding import PartitionSpec as P

DH = 128
BLOCK = 64
R = 3
G = 2
VMEM = pltpu.MemorySpace.VMEM
SMEM = pltpu.MemorySpace.SMEM
BF16 = jnp.bfloat16
F32 = jnp.float32
I32 = jnp.int32
NONE = -1e30
PIECES = 3


def params(mib):
    return pltpu.CompilerParams(vmem_limit_bytes=mib * 1024 * 1024)


LIGHT = pl.CostEstimate(flops=1, bytes_accessed=1, transcendentals=0)


def spec(space=VMEM):
    return pl.BlockSpec(memory_space=space)


def rank_kernel(n, per, cap, g_ref, o_ref, spot_ref, arrive_ref, g_pad, o_pad):
    me = lax.axis_index("seq")
    nb = g_ref.shape[1]
    wide = g_pad.shape[1]
    tall = spot_ref.shape[0]
    g_pad[...] = jnp.full(g_pad.shape, -1, I32)
    o_pad[...] = jnp.zeros(o_pad.shape, I32)
    g_pad[:R, :nb] = g_ref[...]
    o_pad[:R, :nb] = o_ref[...]
    g = g_pad[...]
    lane = lax.broadcasted_iota(I32, g.shape, 1)
    place = lane
    for d in range(1, n):
        place = jnp.where(lane >= d * per, lane - d * per, place)
    rank = jnp.zeros(g.shape, I32)
    for s in range(1, per):
        back = pltpu.roll(g, s, axis=1)
        ahead = place >= s
        for r in range(R):
            same = jnp.broadcast_to(back[r : r + 1, :], g.shape) == g
            rank = rank + jnp.where(ahead & same, 1, 0)
    arrive_ref[...] = g * cap + rank
    row = lax.broadcasted_iota(I32, (tall, wide), 0)
    spots = jnp.zeros((tall, wide), F32)
    for side in range(2):
        named = jnp.where(g == lax.bitwise_xor(me, side * (n // 4)), o_pad[...], 0)
        for s in range(cap):
            picked = jnp.where(rank == s, named, 0).astype(F32)
            total = jnp.sum(picked, axis=0, keepdims=True)
            here = row == side * cap + s
            spots = spots + jnp.where(here, jnp.broadcast_to(total, (tall, wide)), 0.0)
    token = lax.broadcasted_iota(I32, (wide, 128), 0)
    first = lax.broadcasted_iota(I32, (wide, 128), 1) * per
    belongs = jnp.where((token >= first) & (token < first + per), 1.0, 0.0)
    spot_ref[...] = jnp.dot(
        spots.astype(BF16), belongs.astype(BF16), preferred_element_type=F32
    ).astype(I32)


def ranks(n, per, cap, groups, offsets):
    nb = groups.shape[1]
    wide = -(-nb // 128) * 128
    tall = -(-2 * cap // 8) * 8
    return pl.pallas_call(
        functools.partial(rank_kernel, n, per, cap),
        out_shape=(
            jax.ShapeDtypeStruct((tall, 128), I32),
            jax.ShapeDtypeStruct((8, wide), I32),
        ),
        in_specs=[spec(), spec()],
        out_specs=(spec(), spec()),
        scratch_shapes=[pltpu.VMEM((8, wide), I32), pltpu.VMEM((8, wide), I32)],
        compiler_params=params(4),
        cost_estimate=LIGHT,
        name="ranks",
    )(groups, offsets)


def gather_kernel(n, per, cap, lists, shared, count, spot_ref, *refs):
    plane = n // 4
    me = lax.axis_index("seq")
    sources, outs = refs[:count], refs[-plane:]
    for k, out_ref in enumerate(outs):
        at = 0
        for side, far, parts in lists:
            d = lax.bitwise_xor(me, k + (n // 2 if far else 0))
            for c in parts:
                for s in range(cap):
                    start = spot_ref[side * cap + s, d] * BLOCK
                    rows = pl.ds(pl.multiple_of(start, BLOCK), BLOCK)
                    out_ref[pl.ds(at, BLOCK)] = sources[2 * side + c][rows]
                    at += BLOCK
        if shared:
            shared_rows(n, per, k, at, refs[count], sources, out_ref)


def shared_rows(n, per, k, skip, place_ref, sources, out_ref):
    plane = n // 4
    me = lax.axis_index("seq")
    place = lax.bitwise_and(me, plane - 1)
    target = lax.bitwise_xor(place, k)
    is_before = lax.rem(place + 1, plane) == target
    is_end = jnp.where(is_before, target == 0, target == plane - 1)
    edge = pl.multiple_of(jnp.where(is_before, (per - 1) * BLOCK, 0), BLOCK)
    for c in range(2):
        own_ref, mate_ref = sources[c], sources[2 + c]
        for g in range(G):
            owner = lax.div(place_ref[g], per)
            start = pl.multiple_of((place_ref[g] - owner * per) * BLOCK, BLOCK)
            rows = pl.ds(start, BLOCK)
            mine = lax.bitwise_and(lax.bitwise_xor(owner, me), plane) == 0
            out_ref[pl.ds(skip + (c * G + g) * BLOCK, BLOCK)] = jnp.where(
                mine, own_ref[rows], mate_ref[rows]
            )
        rows = pl.ds(edge, BLOCK)
        out_ref[pl.ds(skip + (2 * G + c) * BLOCK, BLOCK)] = jnp.where(
            is_end, mate_ref[rows], own_ref[rows]
        )


def gather(n, per, cap, lists, spots, sources, shared=(), earlier=()):
    plane = n // 4
    rows = sum(len(parts) for _, _, parts in lists) * cap * BLOCK
    rows += 2 * (G + 1) * BLOCK if shared else 0
    out = jax.ShapeDtypeStruct((rows, sources[0].shape[1]), BF16)
    return pl.pallas_call(
        functools.partial(gather_kernel, n, per, cap, lists, bool(shared), len(sources)),
        out_shape=(out,) * plane,
        in_specs=[spec(SMEM)]
        + [spec()] * len(sources)
        + [spec(SMEM)] * len(shared)
        + [spec(pl.ANY)] * len(earlier),
        out_specs=(spec(),) * plane,
        compiler_params=params(8),
        cost_estimate=LIGHT,
        name="gather_blocks",
    )(spots, *sources, *shared, *earlier)


def exchange(parts, n):
    got = [parts[0]]
    for k in range(1, n // 4):
        got.append(lax.ppermute(parts[k], "seq", [(i, i ^ k) for i in range(n)]))
    return got


def choose(n, cap, per, arrive_ref, d, sources, held, keys, vals):
    half = n // 2
    me = lax.axis_index("seq")
    for k, pair in enumerate(sources):
        for c, (ref, row) in enumerate(pair):
            held[k, pl.ds(c * cap * BLOCK, cap * BLOCK)] = ref[pl.ds(row, cap * BLOCK)]
    biases = []
    for i in range(per):
        row = []
        for r in range(R):
            spot = arrive_ref[r, d * per + i]
            group = lax.div(spot, cap)
            differ = lax.bitwise_xor(group, me)
            here = differ < half
            slot = jnp.where(here, spot - group * cap, 0)
            k = jnp.where(here, differ, 0)
            at = pl.ds((i * R + r) * BLOCK, BLOCK)
            keys[at] = held[k, pl.ds(pl.multiple_of(slot * BLOCK, BLOCK), BLOCK), :]
            vals[at] = held[k, pl.ds(pl.multiple_of((cap + slot) * BLOCK, BLOCK), BLOCK), :]
            row.append(jnp.where(here, 0.0, NONE))
        biases.append(row)
    return biases


def shared_blocks(n, per, place_ref, got_refs, skip, glob, ends):
    plane = n // 4
    me = lax.axis_index("seq")
    place = lax.bitwise_and(me, plane - 1)
    biases = []
    for g in range(G):
        differ = lax.bitwise_xor(lax.div(place_ref[g], per), me)
        for p, got_ref in enumerate(got_refs):
            @pl.when(lax.bitwise_and(differ, plane - 1) == p)
            def _(g=g, got_ref=got_ref):
                for c in range(2):
                    at = (c * G + g) * BLOCK
                    glob[pl.ds(at, BLOCK)] = got_ref[pl.ds(skip + at, BLOCK)]
        biases.append(jnp.where(differ < n // 2, 0.0, NONE))
    for e, neighbour in enumerate((place + plane - 1, place + 1)):
        k = lax.bitwise_xor(place, lax.bitwise_and(neighbour, plane - 1))
        for p, got_ref in enumerate(got_refs):
            @pl.when(k == p)
            def _(e=e, got_ref=got_ref):
                ends[pl.ds(e * 2 * BLOCK, 2 * BLOCK)] = got_ref[
                    pl.ds(skip + 2 * G * BLOCK, 2 * BLOCK)
                ]
    return biases


def widen(biases):
    count = len(biases)
    lane = lax.broadcasted_iota(I32, (1, count * BLOCK), 1)
    bias = jnp.full((1, count * BLOCK), biases[-1], F32)
    for r in reversed(range(count - 1)):
        bias = jnp.where(lane < (r + 1) * BLOCK, biases[r], bias)
    return bias


def batches(per, heads, step):
    for first in range(0, per, step):
        yield [(i, h) for i in range(first, min(per, first + step)) for h in range(heads)]


def rows_of(i):
    return pl.ds(i * BLOCK, BLOCK)


def picked_of(i):
    return pl.ds(i * R * BLOCK, R * BLOCK)


def cols_of(h):
    return pl.ds(h * DH, DH)


def dot_t(a, b):
    return lax.dot_general(a, b, (((1,), (1,)), ((), ())), preferred_element_type=F32)


def eye():
    shape = (BLOCK, BLOCK)
    return lax.broadcasted_iota(I32, shape, 0) == lax.broadcasted_iota(I32, shape, 1)


def flatten(columns, diagonal):
    return [jnp.sum(jnp.where(diagonal, x, 0.0), axis=0, keepdims=True) for x in columns]


def attend(queries, sets):
    scale = 1.0 / math.sqrt(DH)
    s = [
        [dot_t(q, ks) * scale + bias if bias is not None else dot_t(q, ks) * scale
         for ks, vs, bias in group]
        for q, group in zip(queries, sets)
    ]
    top = [[jnp.max(x, axis=1, keepdims=True) for x in group] for group in s]
    top = [functools.reduce(jnp.maximum, group) for group in top]
    w = [[jnp.exp(x - t) for x in group] for group, t in zip(s, top)]
    total = [sum(jnp.sum(x, axis=1, keepdims=True) for x in group) for group in w]
    part = [
        sum(
            jnp.dot(x.astype(BF16), vs, preferred_element_type=F32)
            for x, (ks, vs, bias) in zip(ws, group)
        )
        for ws, group in zip(w, sets)
    ]
    return part, top, total


def far_kernel(n, cap, per, heads, arrive_ref, place_ref, q_ref, *refs):
    half, plane = n // 2, n // 4
    got_refs = refs[:half]
    out_ref, held, keys, vals, glob, ends, stat, pieces = refs[half + 1 :]
    me = lax.axis_index("seq")
    d = lax.bitwise_xor(me, half)
    diagonal = eye()
    stat[...] = jnp.zeros_like(stat)
    size = held.shape[1]
    sources = [((ref, 0), (ref, cap * BLOCK)) for ref in got_refs]
    biases = choose(n, cap, per, arrive_ref, d, sources, held, keys, vals)
    glob_bias = widen(shared_blocks(n, per, place_ref, got_refs[plane:], size, glob, ends))
    inside = lax.bitwise_and(me, half - 1)
    end_bias = [jnp.where(inside == x, 0.0, NONE) for x in (0, half - 1)]
    for pairs in batches(per, heads, 3):
        sets = []
        for i, h in pairs:
            cols = cols_of(h)
            group = [
                (keys[picked_of(i), cols], vals[picked_of(i), cols], widen(biases[i])),
                (glob[: G * BLOCK, cols], glob[G * BLOCK :, cols], glob_bias),
            ]
            for e, edge in enumerate((0, per - 1)):
                if i == edge:
                    at = e * 2 * BLOCK
                    group.append(
                        (ends[at : at + BLOCK, cols], ends[at + BLOCK : at + 2 * BLOCK, cols],
                         end_bias[e])
                    )
            sets.append(group)
        part, top, total = attend([q_ref[rows_of(i), cols_of(h)] for i, h in pairs], sets)
        for x, t, (i, h) in zip(part, total, pairs):
            out_ref[rows_of(i), cols_of(h)] = (x / t).astype(BF16)
        for c, columns in enumerate((top, total)):
            for x, (i, h) in zip(flatten(columns, diagonal), pairs):
                stat[i : i + 1, pl.ds(h * DH + c * BLOCK, BLOCK)] = x
    rest = stat[...]
    pieces[...] = jnp.zeros_like(pieces)
    for p in range(PIECES):
        piece = rest.astype(BF16).astype(F32)
        rest = rest - piece
        pieces[p * per : (p + 1) * per] = piece[:per]
    out_ref[pl.ds(per * BLOCK, pieces.shape[0])] = pieces[...].astype(BF16)


def stat_rows(per):
    return -(-per // 8) * 8


def piece_rows(per):
    return -(-PIECES * per // 16) * 16


def scratches(n, cap, per, columns):
    return (
        [pltpu.VMEM((n // 2, 2 * cap * BLOCK, columns), BF16)]
        + [pltpu.VMEM((per * R * BLOCK, columns), BF16)] * 2
        + [pltpu.VMEM((2 * G * BLOCK, columns), BF16), pltpu.VMEM((4 * BLOCK, columns), BF16)]
    )


def far_part(n, cap, per, arrive, places, q, got, earlier):
    rows, columns = q.shape
    heads = columns // DH
    return pl.pallas_call(
        functools.partial(far_kernel, n, cap, per, heads),
        out_shape=jax.ShapeDtypeStruct((rows + piece_rows(per), columns), BF16),
        in_specs=[spec(SMEM)] * 2 + [spec()] * (1 + len(got)) + [spec(pl.ANY)],
        out_specs=spec(),
        scratch_shapes=scratches(n, cap, per, columns)
        + [pltpu.VMEM((stat_rows(per), columns), F32)]
        + [pltpu.VMEM((piece_rows(per), columns), F32)],
        compiler_params=params(16),
        cost_estimate=LIGHT,
        name="far_part",
    )(arrive, places, q, *got, earlier)


def store_part(heads, pairs, part, top, total, part_ref, stat_ref, diagonal):
    for x, (i, h) in zip(part, pairs):
        part_ref[rows_of(i), cols_of(h)] = x
    for c, columns in enumerate((top, total)):
        for x, (i, h) in zip(flatten(columns, diagonal), pairs):
            stat_ref[i : i + 1, pl.ds(h * DH + c * BLOCK, BLOCK)] = x


def near_kernel(n, cap, per, heads, place_ref, q_ref, k_ref, v_ref, *refs):
    half, plane = n // 2, n // 4
    shared_refs = refs[:plane]
    part_ref, stat_ref, glob, ends, keys, vals = refs[plane:]
    me = lax.axis_index("seq")
    rows = per * BLOCK
    diagonal = eye()
    stat_ref[...] = jnp.zeros_like(stat_ref)
    size = 2 * cap * BLOCK
    glob_bias = widen(shared_blocks(n, per, place_ref, shared_refs, size, glob, ends))
    keys[:BLOCK] = ends[:BLOCK]
    vals[:BLOCK] = ends[BLOCK : 2 * BLOCK]
    keys[pl.ds(BLOCK, rows)] = k_ref[...]
    vals[pl.ds(BLOCK, rows)] = v_ref[...]
    keys[pl.ds(BLOCK + rows, BLOCK)] = ends[2 * BLOCK : 3 * BLOCK]
    vals[pl.ds(BLOCK + rows, BLOCK)] = ends[3 * BLOCK :]
    inside = lax.bitwise_and(me, half - 1)
    first_bias, last_bias = [jnp.where(inside == x, NONE, 0.0) for x in (0, half - 1)]
    for pairs in batches(per, heads, 2):
        sets = []
        for i, h in pairs:
            window, cols = pl.ds(i * BLOCK, 3 * BLOCK), cols_of(h)
            bias = None
            if i in (0, per - 1):
                bias = widen([first_bias if i == 0 else 0.0, 0.0, last_bias if i else 0.0])
            sets.append(
                [
                    (keys[window, cols], vals[window, cols], bias),
                    (glob[: G * BLOCK, cols], glob[G * BLOCK :, cols], glob_bias),
                ]
            )
        parts = attend([q_ref[rows_of(i), cols_of(h)] for i, h in pairs], sets)
        store_part(heads, pairs, *parts, part_ref, stat_ref, diagonal)


def part_shapes(per, columns):
    return (
        jax.ShapeDtypeStruct((per * BLOCK, columns), F32),
        jax.ShapeDtypeStruct((stat_rows(per), columns), F32),
    )


def near_part(n, cap, per, places, q, k, v, shared):
    rows, columns = q.shape
    heads = columns // DH
    return pl.pallas_call(
        functools.partial(near_kernel, n, cap, per, heads),
        out_shape=part_shapes(per, columns),
        in_specs=[spec(SMEM)] + [spec()] * (3 + len(shared)),
        out_specs=(spec(), spec()),
        scratch_shapes=scratches(n, cap, per, columns)[3:]
        + [pltpu.VMEM((rows + 2 * BLOCK, columns), BF16)] * 2,
        compiler_params=params(16),
        cost_estimate=LIGHT,
        name="near_part",
    )(places, q, k, v, *shared)


def rand_kernel(n, cap, per, heads, arrive_ref, q_ref, *refs):
    plane = n // 4
    early, late = refs[:plane], refs[plane : 2 * plane]
    part_ref, stat_ref, held, keys, vals = refs[2 * plane :]
    diagonal = eye()
    stat_ref[...] = jnp.zeros_like(stat_ref)
    me = lax.axis_index("seq")
    size = cap * BLOCK
    sources = [((x, 2 * size), (y, 0)) for x, y in zip(early, late)]
    sources += [((y, size), (y, 2 * size)) for y in late]
    biases = choose(n, cap, per, arrive_ref, me, sources, held, keys, vals)
    for pairs in batches(per, heads, 4):
        sets = [
            [(keys[picked_of(i), cols_of(h)], vals[picked_of(i), cols_of(h)], widen(biases[i]))]
            for i, h in pairs
        ]
        parts = attend([q_ref[rows_of(i), cols_of(h)] for i, h in pairs], sets)
        store_part(heads, pairs, *parts, part_ref, stat_ref, diagonal)


def rand_part(n, cap, per, arrive, q, early, late):
    columns = q.shape[1]
    return pl.pallas_call(
        functools.partial(rand_kernel, n, cap, per, columns // DH),
        out_shape=part_shapes(per, columns),
        in_specs=[spec(SMEM), spec()] + [spec()] * (len(early) + len(late)),
        out_specs=(spec(), spec()),
        scratch_shapes=scratches(n, cap, per, columns)[:3],
        compiler_params=params(16),
        cost_estimate=LIGHT,
        name="rand_part",
    )(arrive, q, *early, *late)


def context_kernel(
    per, heads, near_ref, near_stat_ref, rand_ref, rand_stat_ref, far_ref, out_ref, pieces
):
    pieces[...] = far_ref[pl.ds(per * BLOCK, pieces.shape[0])].astype(F32)
    far = sum(pieces[p * per : (p + 1) * per] for p in range(PIECES))
    stats = (near_stat_ref[:per], rand_stat_ref[:per], far)
    weights = []
    for h in range(heads):
        tops = [x[:, h * DH : h * DH + BLOCK] for x in stats]
        sums = [x[:, h * DH + BLOCK : (h + 1) * DH] for x in stats]
        top = functools.reduce(jnp.maximum, tops)
        w = [jnp.exp(x - top) for x in tops]
        total = sum(x * y for x, y in zip(w, sums))
        w[2] = w[2] * sums[2]
        weights.append([jnp.transpose(x / total) for x in w])
    for i in range(per):
        for h, ws in enumerate(weights):
            rows, cols = rows_of(i), cols_of(h)
            parts = (near_ref[rows, cols], rand_ref[rows, cols], far_ref[rows, cols].astype(F32))
            out_ref[rows, cols] = sum(x * w[:, i : i + 1] for x, w in zip(parts, ws)).astype(BF16)


def contexts(per, near, near_stat, rand, rand_stat, far):
    rows, columns = near.shape
    heads = columns // DH
    return pl.pallas_call(
        functools.partial(context_kernel, per, heads),
        out_shape=jax.ShapeDtypeStruct((rows, columns), BF16),
        in_specs=[spec()] * 5,
        out_specs=spec(),
        scratch_shapes=[pltpu.VMEM((piece_rows(per), columns), F32)],
        compiler_params=params(8),
        cost_estimate=LIGHT,
        name="contexts",
    )(near, near_stat, rand, rand_stat, far)


def project_kernel(rows_refs, w_ref, out_ref, joined):
    me = lax.axis_index("head")
    count = len(rows_refs)
    columns = rows_refs[0].shape[1]
    for step, rows_ref in enumerate(rows_refs):
        owner = lax.rem(me + step, count)
        for h in range(count):
            @pl.when(owner == h)
            def _(h=h, rows_ref=rows_ref):
                joined[:, pl.ds(h * columns, columns)] = rows_ref[...]
    out_ref[...] = jnp.dot(
        joined[...], w_ref[...], preferred_element_type=F32
    ).astype(BF16)


def project(parts, w_out):
    rows, columns = parts[0].shape
    wide = w_out.shape[1]
    tile = rows // 4
    block = pl.BlockSpec((tile, columns), lambda i: (i, 0))

    def kernel(*refs):
        project_kernel(refs[: len(parts)], *refs[len(parts) :])

    return pl.pallas_call(
        kernel,
        grid=(4,),
        out_shape=jax.ShapeDtypeStruct((rows, wide), BF16),
        in_specs=[block] * len(parts) + [spec()],
        out_specs=pl.BlockSpec((tile, wide), lambda i: (i, 0)),
        scratch_shapes=[pltpu.VMEM((tile, w_out.shape[0]), BF16)],
        compiler_params=params(16),
        cost_estimate=LIGHT,
        name="project",
    )(*parts, w_out)


def on_device(queries, keys, values, rand_group, rand_offset, glob_blocks, w_out):
    tokens_dev = queries.shape[0]
    per = tokens_dev // BLOCK
    n = lax.axis_size("seq")
    heads = lax.axis_size("head")
    cap = max(2, (rand_group.shape[0] // n * R + n - 1) // n)

    mates = [(i, i ^ (n // 4)) for i in range(n)]
    partners = [(i, i ^ (n // 2)) for i in range(n)]
    mate_k = lax.ppermute(keys, "seq", mates)
    mate_v = lax.ppermute(values, "seq", mates)
    later_q, _, _ = lax.optimization_barrier((queries, mate_k, mate_v))
    far_q = lax.ppermute(later_q, "seq", partners)
    spots, arrive = ranks(n, per, cap, rand_group.T, rand_offset.T)
    lists = ((0, True, (0, 1)), (0, False, (0,)))
    first = exchange(gather(n, per, cap, lists, spots, [keys, values]), n)
    both = [keys, values, mate_k, mate_v]
    lists = ((1, True, (0, 1)),)
    second = exchange(gather(n, per, cap, lists, spots, both, [glob_blocks], first[1:4]), n)
    lists = ((0, False, (1,)), (1, False, (0, 1)))
    third = gather(n, per, cap, lists, spots, both, (), second[1:2])
    far = far_part(n, cap, per, arrive, glob_blocks, far_q, first + second, third[0])
    far = lax.ppermute(far, "seq", partners)
    third = exchange(third, n)
    near, near_stat = near_part(n, cap, per, glob_blocks, queries, keys, values, second)
    rand, rand_stat = rand_part(n, cap, per, arrive, queries, first, third)
    context = contexts(per, near, near_stat, rand, rand_stat, far)
    others = [
        lax.ppermute(context, "head", [((i + s) % heads, i) for i in range(heads)])
        for s in range(1, heads)
    ]
    return project([context] + others, w_out)


def solution(mesh):
    return jax.shard_map(
        on_device,
        mesh=mesh,
        in_specs=(
            P("seq", "head"),
            P("seq", "head"),
            P("seq", "head"),
            P(),
            P(),
            P(),
            P(None, "head"),
        ),
        out_specs=P("seq", "head"),
        check_vma=False,
    )
```

```python
import functools
import math

import jax
import jax.numpy as jnp
from jax import lax
from jax.experimental import pallas as pl
from jax.experimental.pallas import tpu as pltpu
from jax.sharding import PartitionSpec as P

DH = 128
BLOCK = 64
R = 3
G = 2
VMEM = pltpu.MemorySpace.VMEM
SMEM = pltpu.MemorySpace.SMEM
BF16 = jnp.bfloat16
F32 = jnp.float32
I32 = jnp.int32
NONE = -1e30
PIECES = 3


def params(mib):
    return pltpu.CompilerParams(vmem_limit_bytes=mib * 1024 * 1024)


LIGHT = pl.CostEstimate(flops=1, bytes_accessed=1, transcendentals=0)


def spec(space=VMEM):
    return pl.BlockSpec(memory_space=space)


def rank_kernel(n, per, cap, g_ref, o_ref, spot_ref, arrive_ref, g_pad, o_pad):
    me = lax.axis_index("seq")
    nb = g_ref.shape[1]
    wide = g_pad.shape[1]
    tall = spot_ref.shape[0]
    g_pad[...] = jnp.full(g_pad.shape, -1, I32)
    o_pad[...] = jnp.zeros(o_pad.shape, I32)
    g_pad[:R, :nb] = g_ref[...]
    o_pad[:R, :nb] = o_ref[...]
    g = g_pad[...]
    lane = lax.broadcasted_iota(I32, g.shape, 1)
    place = lane
    for d in range(1, n):
        place = jnp.where(lane >= d * per, lane - d * per, place)
    rank = jnp.zeros(g.shape, I32)
    for s in range(1, per):
        back = pltpu.roll(g, s, axis=1)
        ahead = place >= s
        for r in range(R):
            same = jnp.broadcast_to(back[r : r + 1, :], g.shape) == g
            rank = rank + jnp.where(ahead & same, 1, 0)
    arrive_ref[...] = g * cap + rank
    row = lax.broadcasted_iota(I32, (tall, wide), 0)
    spots = jnp.zeros((tall, wide), F32)
    for side in range(2):
        named = jnp.where(g == lax.bitwise_xor(me, side * (n // 4)), o_pad[...], 0)
        for s in range(cap):
            picked = jnp.where(rank == s, named, 0).astype(F32)
            total = jnp.sum(picked, axis=0, keepdims=True)
            here = row == side * cap + s
            spots = spots + jnp.where(here, jnp.broadcast_to(total, (tall, wide)), 0.0)
    token = lax.broadcasted_iota(I32, (wide, 128), 0)
    first = lax.broadcasted_iota(I32, (wide, 128), 1) * per
    belongs = jnp.where((token >= first) & (token < first + per), 1.0, 0.0)
    spot_ref[...] = jnp.dot(
        spots.astype(BF16), belongs.astype(BF16), preferred_element_type=F32
    ).astype(I32)


def ranks(n, per, cap, groups, offsets):
    nb = groups.shape[1]
    wide = -(-nb // 128) * 128
    tall = -(-2 * cap // 8) * 8
    return pl.pallas_call(
        functools.partial(rank_kernel, n, per, cap),
        out_shape=(
            jax.ShapeDtypeStruct((tall, 128), I32),
            jax.ShapeDtypeStruct((8, wide), I32),
        ),
        in_specs=[spec(), spec()],
        out_specs=(spec(), spec()),
        scratch_shapes=[pltpu.VMEM((8, wide), I32), pltpu.VMEM((8, wide), I32)],
        compiler_params=params(4),
        cost_estimate=LIGHT,
        name="ranks",
    )(groups, offsets)


def gather_kernel(n, per, cap, lists, shared, names, spot_ref, *refs):
    plane = n // 4
    me = lax.axis_index("seq")
    sources, outs = dict(zip(names, refs)), refs[-plane:]
    for k, out_ref in enumerate(outs):
        at = 0
        for side, far, parts in lists:
            d = lax.bitwise_xor(me, k + (n // 2 if far else 0))
            for c in parts:
                for s in range(cap):
                    start = spot_ref[side * cap + s, d] * BLOCK
                    rows = pl.ds(pl.multiple_of(start, BLOCK), BLOCK)
                    out_ref[pl.ds(at, BLOCK)] = sources[side, c][rows]
                    at += BLOCK
        if shared:
            (c,) = lists[0][2]
            place_ref = refs[len(names)]
            shared_rows(n, per, k, at, place_ref, sources[0, c], sources[1, c], out_ref)


def shared_rows(n, per, k, at, place_ref, own_ref, mate_ref, out_ref):
    plane = n // 4
    me = lax.axis_index("seq")
    for g in range(G):
        owner = lax.div(place_ref[g], per)
        start = pl.multiple_of((place_ref[g] - owner * per) * BLOCK, BLOCK)
        rows = pl.ds(start, BLOCK)
        mine = lax.bitwise_and(lax.bitwise_xor(owner, me), plane) == 0
        out_ref[pl.ds(at + g * BLOCK, BLOCK)] = jnp.where(mine, own_ref[rows], mate_ref[rows])
    place = lax.bitwise_and(me, plane - 1)
    target = lax.bitwise_xor(place, k)
    is_before = lax.rem(place + 1, plane) == target
    is_end = jnp.where(is_before, target == 0, target == plane - 1)
    rows = pl.ds(pl.multiple_of(jnp.where(is_before, (per - 1) * BLOCK, 0), BLOCK), BLOCK)
    out_ref[pl.ds(at + G * BLOCK, BLOCK)] = jnp.where(is_end, mate_ref[rows], own_ref[rows])


def gather(n, per, cap, lists, spots, sources, shared=(), earlier=()):
    plane = n // 4
    names, arrays = tuple(sources), list(sources.values())
    rows = sum(len(parts) for _, _, parts in lists) * cap * BLOCK
    rows += (G + 1) * BLOCK if shared else 0
    out = jax.ShapeDtypeStruct((rows, arrays[0].shape[1]), BF16)
    return pl.pallas_call(
        functools.partial(gather_kernel, n, per, cap, lists, bool(shared), names),
        out_shape=(out,) * plane,
        in_specs=[spec(SMEM)]
        + [spec()] * len(arrays)
        + [spec(SMEM)] * len(shared)
        + [spec(pl.ANY)] * len(earlier),
        out_specs=(spec(),) * plane,
        compiler_params=params(8),
        cost_estimate=LIGHT,
        name="gather_blocks",
    )(spots, *arrays, *shared, *earlier)


def exchange(parts, n):
    got = [parts[0]]
    for k in range(1, n // 4):
        got.append(lax.ppermute(parts[k], "seq", [(i, i ^ k) for i in range(n)]))
    return got


def choose(n, cap, per, arrive_ref, d, sources, held, keys, vals):
    half = n // 2
    me = lax.axis_index("seq")
    for k, pair in enumerate(sources):
        for c, (ref, row) in enumerate(pair):
            held[k, pl.ds(c * cap * BLOCK, cap * BLOCK)] = ref[pl.ds(row, cap * BLOCK)]
    biases = []
    for i in range(per):
        row = []
        for r in range(R):
            spot = arrive_ref[r, d * per + i]
            group = lax.div(spot, cap)
            differ = lax.bitwise_xor(group, me)
            here = differ < half
            slot = jnp.where(here, spot - group * cap, 0)
            k = jnp.where(here, differ, 0)
            at = pl.ds((i * R + r) * BLOCK, BLOCK)
            keys[at] = held[k, pl.ds(pl.multiple_of(slot * BLOCK, BLOCK), BLOCK), :]
            vals[at] = held[k, pl.ds(pl.multiple_of((cap + slot) * BLOCK, BLOCK), BLOCK), :]
            row.append(jnp.where(here, 0.0, NONE))
        biases.append(row)
    return biases


def shared_blocks(n, per, place_ref, key_refs, val_refs, skip, glob, ends):
    plane = n // 4
    me = lax.axis_index("seq")
    place = lax.bitwise_and(me, plane - 1)
    biases = []
    for g in range(G):
        differ = lax.bitwise_xor(lax.div(place_ref[g], per), me)
        for p, pair in enumerate(zip(key_refs, val_refs)):
            @pl.when(lax.bitwise_and(differ, plane - 1) == p)
            def _(g=g, pair=pair):
                for c, ref in enumerate(pair):
                    at = pl.ds((c * G + g) * BLOCK, BLOCK)
                    glob[at] = ref[pl.ds(skip + g * BLOCK, BLOCK)]
        biases.append(jnp.where(differ < n // 2, 0.0, NONE))
    for e, neighbour in enumerate((place + plane - 1, place + 1)):
        k = lax.bitwise_xor(place, lax.bitwise_and(neighbour, plane - 1))
        for p, pair in enumerate(zip(key_refs, val_refs)):
            @pl.when(k == p)
            def _(e=e, pair=pair):
                for c, ref in enumerate(pair):
                    at = pl.ds((2 * e + c) * BLOCK, BLOCK)
                    ends[at] = ref[pl.ds(skip + G * BLOCK, BLOCK)]
    return biases


def widen(biases):
    count = len(biases)
    lane = lax.broadcasted_iota(I32, (1, count * BLOCK), 1)
    bias = jnp.full((1, count * BLOCK), biases[-1], F32)
    for r in reversed(range(count - 1)):
        bias = jnp.where(lane < (r + 1) * BLOCK, biases[r], bias)
    return bias


def batches(per, heads, step):
    for first in range(0, per, step):
        yield [(i, h) for i in range(first, min(per, first + step)) for h in range(heads)]


def rows_of(i):
    return pl.ds(i * BLOCK, BLOCK)


def picked_of(i):
    return pl.ds(i * R * BLOCK, R * BLOCK)


def cols_of(h):
    return pl.ds(h * DH, DH)


def dot_t(a, b):
    return lax.dot_general(a, b, (((1,), (1,)), ((), ())), preferred_element_type=F32)


def eye():
    shape = (BLOCK, BLOCK)
    return lax.broadcasted_iota(I32, shape, 0) == lax.broadcasted_iota(I32, shape, 1)


def flatten(columns, diagonal):
    return [jnp.sum(jnp.where(diagonal, x, 0.0), axis=0, keepdims=True) for x in columns]


def attend(queries, sets):
    scale = 1.0 / math.sqrt(DH)
    s = [
        [dot_t(q, ks) * scale + bias if bias is not None else dot_t(q, ks) * scale
         for ks, vs, bias in group]
        for q, group in zip(queries, sets)
    ]
    top = [[jnp.max(x, axis=1, keepdims=True) for x in group] for group in s]
    top = [functools.reduce(jnp.maximum, group) for group in top]
    w = [[jnp.exp(x - t) for x in group] for group, t in zip(s, top)]
    total = [sum(jnp.sum(x, axis=1, keepdims=True) for x in group) for group in w]
    part = [
        sum(
            jnp.dot(x.astype(BF16), vs, preferred_element_type=F32)
            for x, (ks, vs, bias) in zip(ws, group)
        )
        for ws, group in zip(w, sets)
    ]
    return part, top, total


def far_kernel(n, cap, per, heads, arrive_ref, place_ref, q_ref, *refs):
    half, plane = n // 2, n // 4
    first, second = refs[:plane], (refs[plane:half], refs[half : half + plane])
    out_ref, held, keys, vals, glob, ends, stat, pieces = refs[half + plane + 1 :]
    me = lax.axis_index("seq")
    d = lax.bitwise_xor(me, half)
    diagonal = eye()
    stat[...] = jnp.zeros_like(stat)
    size = cap * BLOCK
    sources = [((ref, 0), (ref, size)) for ref in first]
    sources += [((x, 0), (y, 0)) for x, y in zip(*second)]
    biases = choose(n, cap, per, arrive_ref, d, sources, held, keys, vals)
    glob_bias = widen(shared_blocks(n, per, place_ref, *second, size, glob, ends))
    inside = lax.bitwise_and(me, half - 1)
    end_bias = [jnp.where(inside == x, 0.0, NONE) for x in (0, half - 1)]
    for pairs in batches(per, heads, 3):
        sets = []
        for i, h in pairs:
            cols = cols_of(h)
            group = [
                (keys[picked_of(i), cols], vals[picked_of(i), cols], widen(biases[i])),
                (glob[: G * BLOCK, cols], glob[G * BLOCK :, cols], glob_bias),
            ]
            for e, edge in enumerate((0, per - 1)):
                if i == edge:
                    at = e * 2 * BLOCK
                    group.append(
                        (ends[at : at + BLOCK, cols], ends[at + BLOCK : at + 2 * BLOCK, cols],
                         end_bias[e])
                    )
            sets.append(group)
        part, top, total = attend([q_ref[rows_of(i), cols_of(h)] for i, h in pairs], sets)
        for x, t, (i, h) in zip(part, total, pairs):
            out_ref[rows_of(i), cols_of(h)] = (x / t).astype(BF16)
        for c, columns in enumerate((top, total)):
            for x, (i, h) in zip(flatten(columns, diagonal), pairs):
                stat[i : i + 1, pl.ds(h * DH + c * BLOCK, BLOCK)] = x
    rest = stat[...]
    pieces[...] = jnp.zeros_like(pieces)
    for p in range(PIECES):
        piece = rest.astype(BF16).astype(F32)
        rest = rest - piece
        pieces[p * per : (p + 1) * per] = piece[:per]
    out_ref[pl.ds(per * BLOCK, pieces.shape[0])] = pieces[...].astype(BF16)


def stat_rows(per):
    return -(-per // 8) * 8


def piece_rows(per):
    return -(-PIECES * per // 16) * 16


def scratches(n, cap, per, columns):
    return (
        [pltpu.VMEM((n // 2, 2 * cap * BLOCK, columns), BF16)]
        + [pltpu.VMEM((per * R * BLOCK, columns), BF16)] * 2
        + [pltpu.VMEM((2 * G * BLOCK, columns), BF16), pltpu.VMEM((4 * BLOCK, columns), BF16)]
    )


def far_part(n, cap, per, arrive, places, q, got, earlier):
    rows, columns = q.shape
    heads = columns // DH
    return pl.pallas_call(
        functools.partial(far_kernel, n, cap, per, heads),
        out_shape=jax.ShapeDtypeStruct((rows + piece_rows(per), columns), BF16),
        in_specs=[spec(SMEM)] * 2 + [spec()] * (1 + len(got)) + [spec(pl.ANY)],
        out_specs=spec(),
        scratch_shapes=scratches(n, cap, per, columns)
        + [pltpu.VMEM((stat_rows(per), columns), F32)]
        + [pltpu.VMEM((piece_rows(per), columns), F32)],
        compiler_params=params(16),
        cost_estimate=LIGHT,
        name="far_part",
    )(arrive, places, q, *got, earlier)


def store_part(heads, pairs, part, top, total, part_ref, stat_ref, diagonal):
    for x, (i, h) in zip(part, pairs):
        part_ref[rows_of(i), cols_of(h)] = x
    for c, columns in enumerate((top, total)):
        for x, (i, h) in zip(flatten(columns, diagonal), pairs):
            stat_ref[i : i + 1, pl.ds(h * DH + c * BLOCK, BLOCK)] = x


def near_kernel(n, cap, per, heads, place_ref, q_ref, k_ref, v_ref, *refs):
    half, plane = n // 2, n // 4
    second = refs[:plane], refs[plane:half]
    part_ref, stat_ref, glob, ends, keys, vals = refs[half:]
    me = lax.axis_index("seq")
    rows = per * BLOCK
    diagonal = eye()
    stat_ref[...] = jnp.zeros_like(stat_ref)
    size = cap * BLOCK
    glob_bias = widen(shared_blocks(n, per, place_ref, *second, size, glob, ends))
    keys[:BLOCK] = ends[:BLOCK]
    vals[:BLOCK] = ends[BLOCK : 2 * BLOCK]
    keys[pl.ds(BLOCK, rows)] = k_ref[...]
    vals[pl.ds(BLOCK, rows)] = v_ref[...]
    keys[pl.ds(BLOCK + rows, BLOCK)] = ends[2 * BLOCK : 3 * BLOCK]
    vals[pl.ds(BLOCK + rows, BLOCK)] = ends[3 * BLOCK :]
    inside = lax.bitwise_and(me, half - 1)
    first_bias, last_bias = [jnp.where(inside == x, NONE, 0.0) for x in (0, half - 1)]
    for pairs in batches(per, heads, 2):
        sets = []
        for i, h in pairs:
            window, cols = pl.ds(i * BLOCK, 3 * BLOCK), cols_of(h)
            bias = None
            if i in (0, per - 1):
                bias = widen([first_bias if i == 0 else 0.0, 0.0, last_bias if i else 0.0])
            sets.append(
                [
                    (keys[window, cols], vals[window, cols], bias),
                    (glob[: G * BLOCK, cols], glob[G * BLOCK :, cols], glob_bias),
                ]
            )
        parts = attend([q_ref[rows_of(i), cols_of(h)] for i, h in pairs], sets)
        store_part(heads, pairs, *parts, part_ref, stat_ref, diagonal)


def part_shapes(per, columns):
    return (
        jax.ShapeDtypeStruct((per * BLOCK, columns), F32),
        jax.ShapeDtypeStruct((stat_rows(per), columns), F32),
    )


def near_part(n, cap, per, places, q, k, v, shared):
    rows, columns = q.shape
    heads = columns // DH
    return pl.pallas_call(
        functools.partial(near_kernel, n, cap, per, heads),
        out_shape=part_shapes(per, columns),
        in_specs=[spec(SMEM)] + [spec()] * (3 + len(shared)),
        out_specs=(spec(), spec()),
        scratch_shapes=scratches(n, cap, per, columns)[3:]
        + [pltpu.VMEM((rows + 2 * BLOCK, columns), BF16)] * 2,
        compiler_params=params(16),
        cost_estimate=LIGHT,
        name="near_part",
    )(places, q, k, v, *shared)


def rand_kernel(n, cap, per, heads, arrive_ref, q_ref, *refs):
    plane = n // 4
    part_ref, stat_ref, held, keys, vals = refs[plane:]
    diagonal = eye()
    stat_ref[...] = jnp.zeros_like(stat_ref)
    me = lax.axis_index("seq")
    size = cap * BLOCK
    sources = [
        ((ref, 2 * side * size), (ref, (2 * side + 1) * size))
        for side in range(2)
        for ref in refs[:plane]
    ]
    biases = choose(n, cap, per, arrive_ref, me, sources, held, keys, vals)
    for pairs in batches(per, heads, 4):
        sets = [
            [(keys[picked_of(i), cols_of(h)], vals[picked_of(i), cols_of(h)], widen(biases[i]))]
            for i, h in pairs
        ]
        parts = attend([q_ref[rows_of(i), cols_of(h)] for i, h in pairs], sets)
        store_part(heads, pairs, *parts, part_ref, stat_ref, diagonal)


def rand_part(n, cap, per, arrive, q, got):
    columns = q.shape[1]
    return pl.pallas_call(
        functools.partial(rand_kernel, n, cap, per, columns // DH),
        out_shape=part_shapes(per, columns),
        in_specs=[spec(SMEM), spec()] + [spec()] * len(got),
        out_specs=(spec(), spec()),
        scratch_shapes=scratches(n, cap, per, columns)[:3],
        compiler_params=params(16),
        cost_estimate=LIGHT,
        name="rand_part",
    )(arrive, q, *got)


def context_kernel(
    per, heads, near_ref, near_stat_ref, rand_ref, rand_stat_ref, far_ref, out_ref, pieces
):
    pieces[...] = far_ref[pl.ds(per * BLOCK, pieces.shape[0])].astype(F32)
    far = sum(pieces[p * per : (p + 1) * per] for p in range(PIECES))
    stats = (near_stat_ref[:per], rand_stat_ref[:per], far)
    weights = []
    for h in range(heads):
        tops = [x[:, h * DH : h * DH + BLOCK] for x in stats]
        sums = [x[:, h * DH + BLOCK : (h + 1) * DH] for x in stats]
        top = functools.reduce(jnp.maximum, tops)
        w = [jnp.exp(x - top) for x in tops]
        total = sum(x * y for x, y in zip(w, sums))
        w[2] = w[2] * sums[2]
        weights.append([jnp.transpose(x / total) for x in w])
    for i in range(per):
        for h, ws in enumerate(weights):
            rows, cols = rows_of(i), cols_of(h)
            parts = (near_ref[rows, cols], rand_ref[rows, cols], far_ref[rows, cols].astype(F32))
            out_ref[rows, cols] = sum(x * w[:, i : i + 1] for x, w in zip(parts, ws)).astype(BF16)


def contexts(per, near, near_stat, rand, rand_stat, far):
    rows, columns = near.shape
    heads = columns // DH
    return pl.pallas_call(
        functools.partial(context_kernel, per, heads),
        out_shape=jax.ShapeDtypeStruct((rows, columns), BF16),
        in_specs=[spec()] * 5,
        out_specs=spec(),
        scratch_shapes=[pltpu.VMEM((piece_rows(per), columns), F32)],
        compiler_params=params(8),
        cost_estimate=LIGHT,
        name="contexts",
    )(near, near_stat, rand, rand_stat, far)


def project_kernel(rows_refs, w_ref, out_ref, joined):
    me = lax.axis_index("head")
    count = len(rows_refs)
    columns = rows_refs[0].shape[1]
    for step, rows_ref in enumerate(rows_refs):
        owner = lax.rem(me + step, count)
        for h in range(count):
            @pl.when(owner == h)
            def _(h=h, rows_ref=rows_ref):
                joined[:, pl.ds(h * columns, columns)] = rows_ref[...]
    out_ref[...] = jnp.dot(
        joined[...], w_ref[...], preferred_element_type=F32
    ).astype(BF16)


def project(parts, w_out):
    rows, columns = parts[0].shape
    wide = w_out.shape[1]
    tile = rows // 4
    block = pl.BlockSpec((tile, columns), lambda i: (i, 0))

    def kernel(*refs):
        project_kernel(refs[: len(parts)], *refs[len(parts) :])

    return pl.pallas_call(
        kernel,
        grid=(4,),
        out_shape=jax.ShapeDtypeStruct((rows, wide), BF16),
        in_specs=[block] * len(parts) + [spec()],
        out_specs=pl.BlockSpec((tile, wide), lambda i: (i, 0)),
        scratch_shapes=[pltpu.VMEM((tile, w_out.shape[0]), BF16)],
        compiler_params=params(16),
        cost_estimate=LIGHT,
        name="project",
    )(*parts, w_out)


def on_device(queries, keys, values, rand_group, rand_offset, glob_blocks, w_out):
    tokens_dev = queries.shape[0]
    per = tokens_dev // BLOCK
    n = lax.axis_size("seq")
    heads = lax.axis_size("head")
    cap = max(2, (rand_group.shape[0] // n * R + n - 1) // n)

    mates = [(i, i ^ (n // 4)) for i in range(n)]
    partners = [(i, i ^ (n // 2)) for i in range(n)]
    mate_k = lax.ppermute(keys, "seq", mates)
    mate_v = lax.ppermute(values, "seq", mates)
    later_q, _ = lax.optimization_barrier((queries, mate_k))
    far_q = lax.ppermute(later_q, "seq", partners)
    spots, arrive = ranks(n, per, cap, rand_group.T, rand_offset.T)
    rows = {(0, 0): keys, (0, 1): values}
    lists = ((0, True, (0, 1)),)
    first = exchange(gather(n, per, cap, lists, spots, rows), n)
    rows = {(0, 0): keys, (1, 0): mate_k}
    lists = ((1, True, (0,)),)
    second_k = exchange(gather(n, per, cap, lists, spots, rows, [glob_blocks], first[1:4]), n)
    rows = {(0, 1): values, (1, 1): mate_v}
    lists = ((1, True, (1,)),)
    sent = gather(n, per, cap, lists, spots, rows, [glob_blocks], second_k[1:2])
    second = second_k + exchange(sent, n)
    rows = {(0, 0): keys, (0, 1): values, (1, 0): mate_k, (1, 1): mate_v}
    lists = ((0, False, (0, 1)), (1, False, (0, 1)))
    third = gather(n, per, cap, lists, spots, rows, (), sent[:1])
    far = far_part(n, cap, per, arrive, glob_blocks, far_q, first + second, third[0])
    far = lax.ppermute(far, "seq", partners)
    third = exchange(third, n)
    near, near_stat = near_part(n, cap, per, glob_blocks, queries, keys, values, second)
    rand, rand_stat = rand_part(n, cap, per, arrive, queries, third)
    context = contexts(per, near, near_stat, rand, rand_stat, far)
    others = [
        lax.ppermute(context, "head", [((i + s) % heads, i) for i in range(heads)])
        for s in range(1, heads)
    ]
    return project([context] + others, w_out)


def solution(mesh):
    return jax.shard_map(
        on_device,
        mesh=mesh,
        in_specs=(
            P("seq", "head"),
            P("seq", "head"),
            P("seq", "head"),
            P(),
            P(),
            P(),
            P(None, "head"),
        ),
        out_specs=P("seq", "head"),
        check_vma=False,
    )
```

```python
import functools
import math

import jax
import jax.numpy as jnp
from jax import lax
from jax.experimental import pallas as pl
from jax.experimental.pallas import tpu as pltpu
from jax.sharding import PartitionSpec as P

DH = 128
BLOCK = 64
R = 3
G = 2
VMEM = pltpu.MemorySpace.VMEM
SMEM = pltpu.MemorySpace.SMEM
BF16 = jnp.bfloat16
F32 = jnp.float32
I32 = jnp.int32
NONE = -1e30
PIECES = 3


def params(mib):
    return pltpu.CompilerParams(vmem_limit_bytes=mib * 1024 * 1024)


LIGHT = pl.CostEstimate(flops=1, bytes_accessed=1, transcendentals=0)
HEAVY = pl.CostEstimate(flops=4 * 10**9, bytes_accessed=1, transcendentals=0)


def spec(space=VMEM):
    return pl.BlockSpec(memory_space=space)


def rank_kernel(n, per, cap, g_ref, o_ref, spot_ref, arrive_ref, g_pad, o_pad):
    me = lax.axis_index("seq")
    nb = g_ref.shape[1]
    wide = g_pad.shape[1]
    tall = spot_ref.shape[0]
    g_pad[...] = jnp.full(g_pad.shape, -1, I32)
    o_pad[...] = jnp.zeros(o_pad.shape, I32)
    g_pad[:R, :nb] = g_ref[...]
    o_pad[:R, :nb] = o_ref[...]
    g = g_pad[...]
    lane = lax.broadcasted_iota(I32, g.shape, 1)
    place = lane
    for d in range(1, n):
        place = jnp.where(lane >= d * per, lane - d * per, place)
    rank = jnp.zeros(g.shape, I32)
    for s in range(1, per):
        back = pltpu.roll(g, s, axis=1)
        ahead = place >= s
        for r in range(R):
            same = jnp.broadcast_to(back[r : r + 1, :], g.shape) == g
            rank = rank + jnp.where(ahead & same, 1, 0)
    arrive_ref[...] = g * cap + rank
    row = lax.broadcasted_iota(I32, (tall, wide), 0)
    spots = jnp.zeros((tall, wide), F32)
    for side in range(2):
        named = jnp.where(g == lax.bitwise_xor(me, side * (n // 4)), o_pad[...], 0)
        for s in range(cap):
            picked = jnp.where(rank == s, named, 0).astype(F32)
            total = jnp.sum(picked, axis=0, keepdims=True)
            here = row == side * cap + s
            spots = spots + jnp.where(here, jnp.broadcast_to(total, (tall, wide)), 0.0)
    token = lax.broadcasted_iota(I32, (wide, 128), 0)
    first = lax.broadcasted_iota(I32, (wide, 128), 1) * per
    belongs = jnp.where((token >= first) & (token < first + per), 1.0, 0.0)
    spot_ref[...] = jnp.dot(
        spots.astype(BF16), belongs.astype(BF16), preferred_element_type=F32
    ).astype(I32)


def ranks(n, per, cap, groups, offsets):
    nb = groups.shape[1]
    wide = -(-nb // 128) * 128
    tall = -(-2 * cap // 8) * 8
    return pl.pallas_call(
        functools.partial(rank_kernel, n, per, cap),
        out_shape=(
            jax.ShapeDtypeStruct((tall, 128), I32),
            jax.ShapeDtypeStruct((8, wide), I32),
        ),
        in_specs=[spec(), spec()],
        out_specs=(spec(), spec()),
        scratch_shapes=[pltpu.VMEM((8, wide), I32), pltpu.VMEM((8, wide), I32)],
        compiler_params=params(4),
        cost_estimate=LIGHT,
        name="ranks",
    )(groups, offsets)


def gather_kernel(n, per, cap, lists, shared, names, spot_ref, *refs):
    plane = n // 4
    me = lax.axis_index("seq")
    sources, outs = dict(zip(names, refs)), refs[-plane:]
    for k, out_ref in enumerate(outs):
        at = 0
        for side, far, parts in lists:
            d = lax.bitwise_xor(me, k + (n // 2 if far else 0))
            for c in parts:
                for s in range(cap):
                    start = spot_ref[side * cap + s, d] * BLOCK
                    rows = pl.ds(pl.multiple_of(start, BLOCK), BLOCK)
                    out_ref[pl.ds(at, BLOCK)] = sources[side, c][rows]
                    at += BLOCK
        if shared:
            (c,) = lists[0][2]
            place_ref = refs[len(names)]
            shared_rows(n, per, k, at, place_ref, sources[0, c], sources[1, c], out_ref)


def shared_rows(n, per, k, at, place_ref, own_ref, mate_ref, out_ref):
    plane = n // 4
    me = lax.axis_index("seq")
    for g in range(G):
        owner = lax.div(place_ref[g], per)
        start = pl.multiple_of((place_ref[g] - owner * per) * BLOCK, BLOCK)
        rows = pl.ds(start, BLOCK)
        mine = lax.bitwise_and(lax.bitwise_xor(owner, me), plane) == 0
        out_ref[pl.ds(at + g * BLOCK, BLOCK)] = jnp.where(mine, own_ref[rows], mate_ref[rows])
    place = lax.bitwise_and(me, plane - 1)
    target = lax.bitwise_xor(place, k)
    is_before = lax.rem(place + 1, plane) == target
    is_end = jnp.where(is_before, target == 0, target == plane - 1)
    rows = pl.ds(pl.multiple_of(jnp.where(is_before, (per - 1) * BLOCK, 0), BLOCK), BLOCK)
    out_ref[pl.ds(at + G * BLOCK, BLOCK)] = jnp.where(is_end, mate_ref[rows], own_ref[rows])


def gather(n, per, cap, lists, spots, sources, shared=(), earlier=()):
    plane = n // 4
    names, arrays = tuple(sources), list(sources.values())
    rows = sum(len(parts) for _, _, parts in lists) * cap * BLOCK
    rows += (G + 1) * BLOCK if shared else 0
    out = jax.ShapeDtypeStruct((rows, arrays[0].shape[1]), BF16)
    return pl.pallas_call(
        functools.partial(gather_kernel, n, per, cap, lists, bool(shared), names),
        out_shape=(out,) * plane,
        in_specs=[spec(SMEM)]
        + [spec()] * len(arrays)
        + [spec(SMEM)] * len(shared)
        + [spec(pl.ANY)] * len(earlier),
        out_specs=(spec(),) * plane,
        compiler_params=params(8),
        cost_estimate=LIGHT,
        name="gather_blocks",
    )(spots, *arrays, *shared, *earlier)


def exchange(parts, n):
    got = [parts[0]]
    for k in range(1, n // 4):
        got.append(lax.ppermute(parts[k], "seq", [(i, i ^ k) for i in range(n)]))
    return got


def choose(n, cap, per, arrive_ref, d, sources, held, keys, vals):
    half = n // 2
    me = lax.axis_index("seq")
    for k, pair in enumerate(sources):
        for c, (ref, row) in enumerate(pair):
            held[k, pl.ds(c * cap * BLOCK, cap * BLOCK)] = ref[pl.ds(row, cap * BLOCK)]
    biases = []
    for i in range(per):
        row = []
        for r in range(R):
            spot = arrive_ref[r, d * per + i]
            group = lax.div(spot, cap)
            differ = lax.bitwise_xor(group, me)
            here = differ < half
            slot = jnp.where(here, spot - group * cap, 0)
            k = jnp.where(here, differ, 0)
            at = pl.ds((i * R + r) * BLOCK, BLOCK)
            keys[at] = held[k, pl.ds(pl.multiple_of(slot * BLOCK, BLOCK), BLOCK), :]
            vals[at] = held[k, pl.ds(pl.multiple_of((cap + slot) * BLOCK, BLOCK), BLOCK), :]
            row.append(jnp.where(here, 0.0, NONE))
        biases.append(row)
    return biases


def shared_blocks(n, per, place_ref, key_refs, val_refs, skip, glob, ends):
    plane = n // 4
    me = lax.axis_index("seq")
    place = lax.bitwise_and(me, plane - 1)
    biases = []
    for g in range(G):
        differ = lax.bitwise_xor(lax.div(place_ref[g], per), me)
        for p, pair in enumerate(zip(key_refs, val_refs)):
            @pl.when(lax.bitwise_and(differ, plane - 1) == p)
            def _(g=g, pair=pair):
                for c, ref in enumerate(pair):
                    at = pl.ds((c * G + g) * BLOCK, BLOCK)
                    glob[at] = ref[pl.ds(skip + g * BLOCK, BLOCK)]
        biases.append(jnp.where(differ < n // 2, 0.0, NONE))
    for e, neighbour in enumerate((place + plane - 1, place + 1)):
        k = lax.bitwise_xor(place, lax.bitwise_and(neighbour, plane - 1))
        for p, pair in enumerate(zip(key_refs, val_refs)):
            @pl.when(k == p)
            def _(e=e, pair=pair):
                for c, ref in enumerate(pair):
                    at = pl.ds((2 * e + c) * BLOCK, BLOCK)
                    ends[at] = ref[pl.ds(skip + G * BLOCK, BLOCK)]
    return biases


def widen(biases):
    count = len(biases)
    lane = lax.broadcasted_iota(I32, (1, count * BLOCK), 1)
    bias = jnp.full((1, count * BLOCK), biases[-1], F32)
    for r in reversed(range(count - 1)):
        bias = jnp.where(lane < (r + 1) * BLOCK, biases[r], bias)
    return bias


def batches(per, heads, step):
    for first in range(0, per, step):
        yield [(i, h) for i in range(first, min(per, first + step)) for h in range(heads)]


def rows_of(i):
    return pl.ds(i * BLOCK, BLOCK)


def picked_of(i):
    return pl.ds(i * R * BLOCK, R * BLOCK)


def cols_of(h):
    return pl.ds(h * DH, DH)


def dot_t(a, b):
    return lax.dot_general(a, b, (((1,), (1,)), ((), ())), preferred_element_type=F32)


def eye():
    shape = (BLOCK, BLOCK)
    return lax.broadcasted_iota(I32, shape, 0) == lax.broadcasted_iota(I32, shape, 1)


def flatten(columns, diagonal):
    return [jnp.sum(jnp.where(diagonal, x, 0.0), axis=0, keepdims=True) for x in columns]


def attend(queries, sets):
    scale = 1.0 / math.sqrt(DH)
    s = [
        [dot_t(q, ks) * scale + bias if bias is not None else dot_t(q, ks) * scale
         for ks, vs, bias in group]
        for q, group in zip(queries, sets)
    ]
    top = [[jnp.max(x, axis=1, keepdims=True) for x in group] for group in s]
    top = [functools.reduce(jnp.maximum, group) for group in top]
    w = [[jnp.exp(x - t) for x in group] for group, t in zip(s, top)]
    total = [sum(jnp.sum(x, axis=1, keepdims=True) for x in group) for group in w]
    part = [
        sum(
            jnp.dot(x.astype(BF16), vs, preferred_element_type=F32)
            for x, (ks, vs, bias) in zip(ws, group)
        )
        for ws, group in zip(w, sets)
    ]
    return part, top, total


def far_kernel(n, cap, per, heads, arrive_ref, place_ref, q_ref, *refs):
    half, plane = n // 2, n // 4
    first, second = refs[:plane], (refs[plane:half], refs[half : half + plane])
    out_ref, held, keys, vals, glob, ends, stat, pieces = refs[half + plane + 1 :]
    me = lax.axis_index("seq")
    d = lax.bitwise_xor(me, half)
    diagonal = eye()
    stat[...] = jnp.zeros_like(stat)
    size = cap * BLOCK
    sources = [((ref, 0), (ref, size)) for ref in first]
    sources += [((x, 0), (y, 0)) for x, y in zip(*second)]
    biases = choose(n, cap, per, arrive_ref, d, sources, held, keys, vals)
    glob_bias = widen(shared_blocks(n, per, place_ref, *second, size, glob, ends))
    inside = lax.bitwise_and(me, half - 1)
    end_bias = [jnp.where(inside == x, 0.0, NONE) for x in (0, half - 1)]
    for pairs in batches(per, heads, 3):
        sets = []
        for i, h in pairs:
            cols = cols_of(h)
            group = [
                (keys[picked_of(i), cols], vals[picked_of(i), cols], widen(biases[i])),
                (glob[: G * BLOCK, cols], glob[G * BLOCK :, cols], glob_bias),
            ]
            for e, edge in enumerate((0, per - 1)):
                if i == edge:
                    at = e * 2 * BLOCK
                    group.append(
                        (ends[at : at + BLOCK, cols], ends[at + BLOCK : at + 2 * BLOCK, cols],
                         end_bias[e])
                    )
            sets.append(group)
        part, top, total = attend([q_ref[rows_of(i), cols_of(h)] for i, h in pairs], sets)
        for x, t, (i, h) in zip(part, total, pairs):
            out_ref[rows_of(i), cols_of(h)] = (x / t).astype(BF16)
        for c, columns in enumerate((top, total)):
            for x, (i, h) in zip(flatten(columns, diagonal), pairs):
                stat[i : i + 1, pl.ds(h * DH + c * BLOCK, BLOCK)] = x
    rest = stat[...]
    pieces[...] = jnp.zeros_like(pieces)
    for p in range(PIECES):
        piece = rest.astype(BF16).astype(F32)
        rest = rest - piece
        pieces[p * per : (p + 1) * per] = piece[:per]
    out_ref[pl.ds(per * BLOCK, pieces.shape[0])] = pieces[...].astype(BF16)


def stat_rows(per):
    return -(-per // 8) * 8


def piece_rows(per):
    return -(-PIECES * per // 16) * 16


def scratches(n, cap, per, columns):
    return (
        [pltpu.VMEM((n // 2, 2 * cap * BLOCK, columns), BF16)]
        + [pltpu.VMEM((per * R * BLOCK, columns), BF16)] * 2
        + [pltpu.VMEM((2 * G * BLOCK, columns), BF16), pltpu.VMEM((4 * BLOCK, columns), BF16)]
    )


def far_part(n, cap, per, arrive, places, q, got, earlier):
    rows, columns = q.shape
    heads = columns // DH
    return pl.pallas_call(
        functools.partial(far_kernel, n, cap, per, heads),
        out_shape=jax.ShapeDtypeStruct((rows + piece_rows(per), columns), BF16),
        in_specs=[spec(SMEM)] * 2 + [spec()] * (1 + len(got)) + [spec(pl.ANY)],
        out_specs=spec(),
        scratch_shapes=scratches(n, cap, per, columns)
        + [pltpu.VMEM((stat_rows(per), columns), F32)]
        + [pltpu.VMEM((piece_rows(per), columns), F32)],
        compiler_params=params(16),
        cost_estimate=HEAVY,
        name="far_part",
    )(arrive, places, q, *got, earlier)


def store_part(heads, pairs, part, top, total, part_ref, stat_ref, diagonal):
    for x, (i, h) in zip(part, pairs):
        part_ref[rows_of(i), cols_of(h)] = x
    for c, columns in enumerate((top, total)):
        for x, (i, h) in zip(flatten(columns, diagonal), pairs):
            stat_ref[i : i + 1, pl.ds(h * DH + c * BLOCK, BLOCK)] = x


def near_kernel(n, cap, per, heads, place_ref, q_ref, k_ref, v_ref, *refs):
    half, plane = n // 2, n // 4
    second = refs[:plane], refs[plane:half]
    part_ref, stat_ref, glob, ends, keys, vals = refs[half:]
    me = lax.axis_index("seq")
    rows = per * BLOCK
    diagonal = eye()
    stat_ref[...] = jnp.zeros_like(stat_ref)
    size = cap * BLOCK
    glob_bias = widen(shared_blocks(n, per, place_ref, *second, size, glob, ends))
    keys[:BLOCK] = ends[:BLOCK]
    vals[:BLOCK] = ends[BLOCK : 2 * BLOCK]
    keys[pl.ds(BLOCK, rows)] = k_ref[...]
    vals[pl.ds(BLOCK, rows)] = v_ref[...]
    keys[pl.ds(BLOCK + rows, BLOCK)] = ends[2 * BLOCK : 3 * BLOCK]
    vals[pl.ds(BLOCK + rows, BLOCK)] = ends[3 * BLOCK :]
    inside = lax.bitwise_and(me, half - 1)
    first_bias, last_bias = [jnp.where(inside == x, NONE, 0.0) for x in (0, half - 1)]
    for pairs in batches(per, heads, 2):
        sets = []
        for i, h in pairs:
            window, cols = pl.ds(i * BLOCK, 3 * BLOCK), cols_of(h)
            bias = None
            if i in (0, per - 1):
                bias = widen([first_bias if i == 0 else 0.0, 0.0, last_bias if i else 0.0])
            sets.append(
                [
                    (keys[window, cols], vals[window, cols], bias),
                    (glob[: G * BLOCK, cols], glob[G * BLOCK :, cols], glob_bias),
                ]
            )
        parts = attend([q_ref[rows_of(i), cols_of(h)] for i, h in pairs], sets)
        store_part(heads, pairs, *parts, part_ref, stat_ref, diagonal)


def part_shapes(per, columns):
    return (
        jax.ShapeDtypeStruct((per * BLOCK, columns), F32),
        jax.ShapeDtypeStruct((stat_rows(per), columns), F32),
    )


def near_part(n, cap, per, places, q, k, v, shared):
    rows, columns = q.shape
    heads = columns // DH
    return pl.pallas_call(
        functools.partial(near_kernel, n, cap, per, heads),
        out_shape=part_shapes(per, columns),
        in_specs=[spec(SMEM)] + [spec()] * (3 + len(shared)),
        out_specs=(spec(), spec()),
        scratch_shapes=scratches(n, cap, per, columns)[3:]
        + [pltpu.VMEM((rows + 2 * BLOCK, columns), BF16)] * 2,
        compiler_params=params(16),
        cost_estimate=LIGHT,
        name="near_part",
    )(places, q, k, v, *shared)


def rand_kernel(n, cap, per, heads, arrive_ref, q_ref, *refs):
    plane = n // 4
    early, late = refs[:plane], refs[plane : 2 * plane]
    part_ref, stat_ref, held, keys, vals = refs[2 * plane :]
    diagonal = eye()
    stat_ref[...] = jnp.zeros_like(stat_ref)
    me = lax.axis_index("seq")
    size = cap * BLOCK
    sources = [((x, 2 * size), (y, 0)) for x, y in zip(early, late)]
    sources += [((y, size), (y, 2 * size)) for y in late]
    biases = choose(n, cap, per, arrive_ref, me, sources, held, keys, vals)
    for pairs in batches(per, heads, 4):
        sets = [
            [(keys[picked_of(i), cols_of(h)], vals[picked_of(i), cols_of(h)], widen(biases[i]))]
            for i, h in pairs
        ]
        parts = attend([q_ref[rows_of(i), cols_of(h)] for i, h in pairs], sets)
        store_part(heads, pairs, *parts, part_ref, stat_ref, diagonal)


def rand_part(n, cap, per, arrive, q, early, late):
    columns = q.shape[1]
    return pl.pallas_call(
        functools.partial(rand_kernel, n, cap, per, columns // DH),
        out_shape=part_shapes(per, columns),
        in_specs=[spec(SMEM), spec()] + [spec()] * (len(early) + len(late)),
        out_specs=(spec(), spec()),
        scratch_shapes=scratches(n, cap, per, columns)[:3],
        compiler_params=params(16),
        cost_estimate=HEAVY,
        name="rand_part",
    )(arrive, q, *early, *late)


def context_kernel(
    per, heads, near_ref, near_stat_ref, rand_ref, rand_stat_ref, far_ref, out_ref, pieces
):
    pieces[...] = far_ref[pl.ds(per * BLOCK, pieces.shape[0])].astype(F32)
    far = sum(pieces[p * per : (p + 1) * per] for p in range(PIECES))
    stats = (near_stat_ref[:per], rand_stat_ref[:per], far)
    weights = []
    for h in range(heads):
        tops = [x[:, h * DH : h * DH + BLOCK] for x in stats]
        sums = [x[:, h * DH + BLOCK : (h + 1) * DH] for x in stats]
        top = functools.reduce(jnp.maximum, tops)
        w = [jnp.exp(x - top) for x in tops]
        total = sum(x * y for x, y in zip(w, sums))
        w[2] = w[2] * sums[2]
        weights.append([jnp.transpose(x / total) for x in w])
    for i in range(per):
        for h, ws in enumerate(weights):
            rows, cols = rows_of(i), cols_of(h)
            parts = (near_ref[rows, cols], rand_ref[rows, cols], far_ref[rows, cols].astype(F32))
            out_ref[rows, cols] = sum(x * w[:, i : i + 1] for x, w in zip(parts, ws)).astype(BF16)


def contexts(per, near, near_stat, rand, rand_stat, far):
    rows, columns = near.shape
    heads = columns // DH
    return pl.pallas_call(
        functools.partial(context_kernel, per, heads),
        out_shape=jax.ShapeDtypeStruct((rows, columns), BF16),
        in_specs=[spec()] * 5,
        out_specs=spec(),
        scratch_shapes=[pltpu.VMEM((piece_rows(per), columns), F32)],
        compiler_params=params(8),
        cost_estimate=LIGHT,
        name="contexts",
    )(near, near_stat, rand, rand_stat, far)


def project_kernel(rows_refs, w_ref, out_ref, joined):
    me = lax.axis_index("head")
    count = len(rows_refs)
    columns = rows_refs[0].shape[1]
    for step, rows_ref in enumerate(rows_refs):
        owner = lax.rem(me + step, count)
        for h in range(count):
            @pl.when(owner == h)
            def _(h=h, rows_ref=rows_ref):
                joined[:, pl.ds(h * columns, columns)] = rows_ref[...]
    out_ref[...] = jnp.dot(
        joined[...], w_ref[...], preferred_element_type=F32
    ).astype(BF16)


def project(parts, w_out):
    rows, columns = parts[0].shape
    wide = w_out.shape[1]
    tile = rows // 4
    block = pl.BlockSpec((tile, columns), lambda i: (i, 0))

    def kernel(*refs):
        project_kernel(refs[: len(parts)], *refs[len(parts) :])

    return pl.pallas_call(
        kernel,
        grid=(4,),
        out_shape=jax.ShapeDtypeStruct((rows, wide), BF16),
        in_specs=[block] * len(parts) + [spec()],
        out_specs=pl.BlockSpec((tile, wide), lambda i: (i, 0)),
        scratch_shapes=[pltpu.VMEM((tile, w_out.shape[0]), BF16)],
        compiler_params=params(16),
        cost_estimate=LIGHT,
        name="project",
    )(*parts, w_out)


def on_device(queries, keys, values, rand_group, rand_offset, glob_blocks, w_out):
    tokens_dev = queries.shape[0]
    per = tokens_dev // BLOCK
    n = lax.axis_size("seq")
    heads = lax.axis_size("head")
    cap = max(2, (rand_group.shape[0] // n * R + n - 1) // n)

    mates = [(i, i ^ (n // 4)) for i in range(n)]
    partners = [(i, i ^ (n // 2)) for i in range(n)]
    mate_k = lax.ppermute(keys, "seq", mates)
    mate_v = lax.ppermute(values, "seq", mates)
    later_q, _ = lax.optimization_barrier((queries, mate_k))
    far_q = lax.ppermute(later_q, "seq", partners)
    spots, arrive = ranks(n, per, cap, rand_group.T, rand_offset.T)
    rows = {(0, 0): keys, (0, 1): values}
    lists = ((0, True, (0, 1)), (0, False, (0,)))
    first = exchange(gather(n, per, cap, lists, spots, rows), n)
    rows = {(0, 0): keys, (1, 0): mate_k}
    lists = ((1, True, (0,)),)
    second_k = exchange(gather(n, per, cap, lists, spots, rows, [glob_blocks], first[1:4]), n)
    rows = {(0, 1): values, (1, 1): mate_v}
    lists = ((1, True, (1,)),)
    sent = gather(n, per, cap, lists, spots, rows, [glob_blocks], second_k[1:2])
    second = second_k + exchange(sent, n)
    rows = {(0, 0): keys, (0, 1): values, (1, 0): mate_k, (1, 1): mate_v}
    lists = ((0, False, (1,)), (1, False, (0, 1)))
    third = gather(n, per, cap, lists, spots, rows, (), sent[:1])
    far = far_part(n, cap, per, arrive, glob_blocks, far_q, first + second, third[0])
    far = lax.ppermute(far, "seq", partners)
    third = exchange(third, n)
    near, near_stat = near_part(n, cap, per, glob_blocks, queries, keys, values, second)
    rand, rand_stat = rand_part(n, cap, per, arrive, queries, first, third)
    context = contexts(per, near, near_stat, rand, rand_stat, far)
    others = [
        lax.ppermute(context, "head", [((i + s) % heads, i) for i in range(heads)])
        for s in range(1, heads)
    ]
    return project([context] + others, w_out)


def solution(mesh):
    return jax.shard_map(
        on_device,
        mesh=mesh,
        in_specs=(
            P("seq", "head"),
            P("seq", "head"),
            P("seq", "head"),
            P(),
            P(),
            P(),
            P(None, "head"),
        ),
        out_specs=P("seq", "head"),
        check_vma=False,
    )
```

```python
import functools
import math

import jax
import jax.numpy as jnp
from jax import lax
from jax.experimental import pallas as pl
from jax.experimental.pallas import tpu as pltpu
from jax.sharding import PartitionSpec as P

DH = 128
BLOCK = 64
R = 3
G = 2
VMEM = pltpu.MemorySpace.VMEM
SMEM = pltpu.MemorySpace.SMEM
BF16 = jnp.bfloat16
F32 = jnp.float32
I32 = jnp.int32
NONE = -1e30
PIECES = 3


def params(mib):
    return pltpu.CompilerParams(vmem_limit_bytes=mib * 1024 * 1024)


LIGHT = pl.CostEstimate(flops=1, bytes_accessed=1, transcendentals=0)
HEAVY = pl.CostEstimate(flops=4 * 10**9, bytes_accessed=1, transcendentals=0)


def spec(space=VMEM):
    return pl.BlockSpec(memory_space=space)


def rank_kernel(n, per, cap, g_ref, o_ref, spot_ref, arrive_ref, g_pad, o_pad):
    me = lax.axis_index("seq")
    nb = g_ref.shape[1]
    wide = g_pad.shape[1]
    tall = spot_ref.shape[0]
    g_pad[...] = jnp.full(g_pad.shape, -1, I32)
    o_pad[...] = jnp.zeros(o_pad.shape, I32)
    g_pad[:R, :nb] = g_ref[...]
    o_pad[:R, :nb] = o_ref[...]
    g = g_pad[...]
    lane = lax.broadcasted_iota(I32, g.shape, 1)
    place = lane
    for d in range(1, n):
        place = jnp.where(lane >= d * per, lane - d * per, place)
    rank = jnp.zeros(g.shape, I32)
    for s in range(1, per):
        back = pltpu.roll(g, s, axis=1)
        ahead = place >= s
        for r in range(R):
            same = jnp.broadcast_to(back[r : r + 1, :], g.shape) == g
            rank = rank + jnp.where(ahead & same, 1, 0)
    arrive_ref[...] = g * cap + rank
    row = lax.broadcasted_iota(I32, (tall, wide), 0)
    spots = jnp.zeros((tall, wide), F32)
    for side in range(2):
        named = jnp.where(g == lax.bitwise_xor(me, side * (n // 4)), o_pad[...], 0)
        for s in range(cap):
            picked = jnp.where(rank == s, named, 0).astype(F32)
            total = jnp.sum(picked, axis=0, keepdims=True)
            here = row == side * cap + s
            spots = spots + jnp.where(here, jnp.broadcast_to(total, (tall, wide)), 0.0)
    token = lax.broadcasted_iota(I32, (wide, 128), 0)
    first = lax.broadcasted_iota(I32, (wide, 128), 1) * per
    belongs = jnp.where((token >= first) & (token < first + per), 1.0, 0.0)
    spot_ref[...] = jnp.dot(
        spots.astype(BF16), belongs.astype(BF16), preferred_element_type=F32
    ).astype(I32)


def ranks(n, per, cap, groups, offsets):
    nb = groups.shape[1]
    wide = -(-nb // 128) * 128
    tall = -(-2 * cap // 8) * 8
    return pl.pallas_call(
        functools.partial(rank_kernel, n, per, cap),
        out_shape=(
            jax.ShapeDtypeStruct((tall, 128), I32),
            jax.ShapeDtypeStruct((8, wide), I32),
        ),
        in_specs=[spec(), spec()],
        out_specs=(spec(), spec()),
        scratch_shapes=[pltpu.VMEM((8, wide), I32), pltpu.VMEM((8, wide), I32)],
        compiler_params=params(4),
        cost_estimate=LIGHT,
        name="ranks",
    )(groups, offsets)


def gather_kernel(n, per, cap, lists, shared, names, spot_ref, *refs):
    plane = n // 4
    me = lax.axis_index("seq")
    sources, outs = dict(zip(names, refs)), refs[-plane:]
    for k, out_ref in enumerate(outs):
        at = 0
        for side, far, parts in lists:
            d = lax.bitwise_xor(me, k + (n // 2 if far else 0))
            for c in parts:
                for s in range(cap):
                    start = spot_ref[side * cap + s, d] * BLOCK
                    rows = pl.ds(pl.multiple_of(start, BLOCK), BLOCK)
                    out_ref[pl.ds(at, BLOCK)] = sources[side, c][rows]
                    at += BLOCK
        if shared:
            (c,) = lists[0][2]
            place_ref = refs[len(names)]
            shared_rows(n, per, k, at, place_ref, sources[0, c], sources[1, c], out_ref)


def shared_rows(n, per, k, at, place_ref, own_ref, mate_ref, out_ref):
    plane = n // 4
    me = lax.axis_index("seq")
    for g in range(G):
        owner = lax.div(place_ref[g], per)
        start = pl.multiple_of((place_ref[g] - owner * per) * BLOCK, BLOCK)
        rows = pl.ds(start, BLOCK)
        mine = lax.bitwise_and(lax.bitwise_xor(owner, me), plane) == 0
        out_ref[pl.ds(at + g * BLOCK, BLOCK)] = jnp.where(mine, own_ref[rows], mate_ref[rows])
    place = lax.bitwise_and(me, plane - 1)
    target = lax.bitwise_xor(place, k)
    is_before = lax.rem(place + 1, plane) == target
    is_end = jnp.where(is_before, target == 0, target == plane - 1)
    rows = pl.ds(pl.multiple_of(jnp.where(is_before, (per - 1) * BLOCK, 0), BLOCK), BLOCK)
    out_ref[pl.ds(at + G * BLOCK, BLOCK)] = jnp.where(is_end, mate_ref[rows], own_ref[rows])


def gather(n, per, cap, lists, spots, sources, shared=(), earlier=()):
    plane = n // 4
    names, arrays = tuple(sources), list(sources.values())
    rows = sum(len(parts) for _, _, parts in lists) * cap * BLOCK
    rows += (G + 1) * BLOCK if shared else 0
    out = jax.ShapeDtypeStruct((rows, arrays[0].shape[1]), BF16)
    return pl.pallas_call(
        functools.partial(gather_kernel, n, per, cap, lists, bool(shared), names),
        out_shape=(out,) * plane,
        in_specs=[spec(SMEM)]
        + [spec()] * len(arrays)
        + [spec(SMEM)] * len(shared)
        + [spec(pl.ANY)] * len(earlier),
        out_specs=(spec(),) * plane,
        compiler_params=params(8),
        cost_estimate=LIGHT,
        name="gather_blocks",
    )(spots, *arrays, *shared, *earlier)


def exchange(parts, n):
    got = [parts[0]]
    for k in range(1, n // 4):
        got.append(lax.ppermute(parts[k], "seq", [(i, i ^ k) for i in range(n)]))
    return got


def choose(n, cap, per, span, arrive_ref, d, sources, held, keys, vals):
    half = n // 2
    me = lax.axis_index("seq")
    for k, pair in enumerate(sources):
        for c, (ref, row) in enumerate(pair):
            held[k, pl.ds(c * cap * BLOCK, cap * BLOCK)] = ref[pl.ds(row, cap * BLOCK)]
    biases = {}
    for i in range(*span):
        row = []
        for r in range(R):
            spot = arrive_ref[r, d * per + i]
            group = lax.div(spot, cap)
            differ = lax.bitwise_xor(group, me)
            here = differ < half
            slot = jnp.where(here, spot - group * cap, 0)
            k = jnp.where(here, differ, 0)
            at = pl.ds((i * R + r) * BLOCK, BLOCK)
            keys[at] = held[k, pl.ds(pl.multiple_of(slot * BLOCK, BLOCK), BLOCK), :]
            vals[at] = held[k, pl.ds(pl.multiple_of((cap + slot) * BLOCK, BLOCK), BLOCK), :]
            row.append(jnp.where(here, 0.0, NONE))
        biases[i] = row
    return biases


def shared_blocks(n, per, place_ref, key_refs, val_refs, skip, glob, ends):
    plane = n // 4
    me = lax.axis_index("seq")
    place = lax.bitwise_and(me, plane - 1)
    biases = []
    for g in range(G):
        differ = lax.bitwise_xor(lax.div(place_ref[g], per), me)
        for p, pair in enumerate(zip(key_refs, val_refs)):
            @pl.when(lax.bitwise_and(differ, plane - 1) == p)
            def _(g=g, pair=pair):
                for c, ref in enumerate(pair):
                    at = pl.ds((c * G + g) * BLOCK, BLOCK)
                    glob[at] = ref[pl.ds(skip + g * BLOCK, BLOCK)]
        biases.append(jnp.where(differ < n // 2, 0.0, NONE))
    for e, neighbour in enumerate((place + plane - 1, place + 1)):
        k = lax.bitwise_xor(place, lax.bitwise_and(neighbour, plane - 1))
        for p, pair in enumerate(zip(key_refs, val_refs)):
            @pl.when(k == p)
            def _(e=e, pair=pair):
                for c, ref in enumerate(pair):
                    at = pl.ds((2 * e + c) * BLOCK, BLOCK)
                    ends[at] = ref[pl.ds(skip + G * BLOCK, BLOCK)]
    return biases


def widen(biases):
    count = len(biases)
    lane = lax.broadcasted_iota(I32, (1, count * BLOCK), 1)
    bias = jnp.full((1, count * BLOCK), biases[-1], F32)
    for r in reversed(range(count - 1)):
        bias = jnp.where(lane < (r + 1) * BLOCK, biases[r], bias)
    return bias


def batches(span, heads, step):
    for first in range(*span, step):
        yield [(i, h) for i in range(first, min(span[1], first + step)) for h in range(heads)]


def rows_of(i):
    return pl.ds(i * BLOCK, BLOCK)


def picked_of(i):
    return pl.ds(i * R * BLOCK, R * BLOCK)


def cols_of(h):
    return pl.ds(h * DH, DH)


def dot_t(a, b):
    return lax.dot_general(a, b, (((1,), (1,)), ((), ())), preferred_element_type=F32)


def eye():
    shape = (BLOCK, BLOCK)
    return lax.broadcasted_iota(I32, shape, 0) == lax.broadcasted_iota(I32, shape, 1)


def flatten(columns, diagonal):
    return [jnp.sum(jnp.where(diagonal, x, 0.0), axis=0, keepdims=True) for x in columns]


def attend(queries, sets):
    scale = 1.0 / math.sqrt(DH)
    s = [
        [dot_t(q, ks) * scale + bias if bias is not None else dot_t(q, ks) * scale
         for ks, vs, bias in group]
        for q, group in zip(queries, sets)
    ]
    top = [[jnp.max(x, axis=1, keepdims=True) for x in group] for group in s]
    top = [functools.reduce(jnp.maximum, group) for group in top]
    w = [[jnp.exp(x - t) for x in group] for group, t in zip(s, top)]
    total = [sum(jnp.sum(x, axis=1, keepdims=True) for x in group) for group in w]
    part = [
        sum(
            jnp.dot(x.astype(BF16), vs, preferred_element_type=F32)
            for x, (ks, vs, bias) in zip(ws, group)
        )
        for ws, group in zip(w, sets)
    ]
    return part, top, total


def far_kernel(n, cap, per, heads, span, arrive_ref, place_ref, q_ref, *refs):
    half, plane = n // 2, n // 4
    first, second = refs[:plane], (refs[plane:half], refs[half : half + plane])
    out_ref, held, keys, vals, glob, ends, stat, pieces = refs[half + plane + 1 :]
    me = lax.axis_index("seq")
    d = lax.bitwise_xor(me, half)
    diagonal = eye()
    stat[...] = jnp.zeros_like(stat)
    size = cap * BLOCK
    sources = [((ref, 0), (ref, size)) for ref in first]
    sources += [((x, 0), (y, 0)) for x, y in zip(*second)]
    biases = choose(n, cap, per, span, arrive_ref, d, sources, held, keys, vals)
    glob_bias = widen(shared_blocks(n, per, place_ref, *second, size, glob, ends))
    inside = lax.bitwise_and(me, half - 1)
    end_bias = [jnp.where(inside == x, 0.0, NONE) for x in (0, half - 1)]
    low, high = span
    count = high - low
    for pairs in batches(span, heads, 3):
        sets = []
        for i, h in pairs:
            cols = cols_of(h)
            group = [
                (keys[picked_of(i), cols], vals[picked_of(i), cols], widen(biases[i])),
                (glob[: G * BLOCK, cols], glob[G * BLOCK :, cols], glob_bias),
            ]
            for e, edge in enumerate((0, per - 1)):
                if i == edge:
                    at = e * 2 * BLOCK
                    group.append(
                        (ends[at : at + BLOCK, cols], ends[at + BLOCK : at + 2 * BLOCK, cols],
                         end_bias[e])
                    )
            sets.append(group)
        part, top, total = attend([q_ref[rows_of(i), cols_of(h)] for i, h in pairs], sets)
        for x, t, (i, h) in zip(part, total, pairs):
            out_ref[rows_of(i - low), cols_of(h)] = (x / t).astype(BF16)
        for c, columns in enumerate((top, total)):
            for x, (i, h) in zip(flatten(columns, diagonal), pairs):
                stat[i - low : i - low + 1, pl.ds(h * DH + c * BLOCK, BLOCK)] = x
    rest = stat[...]
    pieces[...] = jnp.zeros_like(pieces)
    for p in range(PIECES):
        piece = rest.astype(BF16).astype(F32)
        rest = rest - piece
        pieces[p * count : (p + 1) * count] = piece[:count]
    out_ref[pl.ds(count * BLOCK, pieces.shape[0])] = pieces[...].astype(BF16)


def stat_rows(per):
    return -(-per // 8) * 8


def piece_rows(per):
    return -(-PIECES * per // 16) * 16


def scratches(n, cap, per, columns):
    return (
        [pltpu.VMEM((n // 2, 2 * cap * BLOCK, columns), BF16)]
        + [pltpu.VMEM((per * R * BLOCK, columns), BF16)] * 2
        + [pltpu.VMEM((2 * G * BLOCK, columns), BF16), pltpu.VMEM((4 * BLOCK, columns), BF16)]
    )


def far_part(n, cap, per, span, arrive, places, q, got, earlier):
    columns = q.shape[1]
    count = span[1] - span[0]
    heads = columns // DH
    return pl.pallas_call(
        functools.partial(far_kernel, n, cap, per, heads, span),
        out_shape=jax.ShapeDtypeStruct((count * BLOCK + piece_rows(count), columns), BF16),
        in_specs=[spec(SMEM)] * 2 + [spec()] * (1 + len(got)) + [spec(pl.ANY)],
        out_specs=spec(),
        scratch_shapes=scratches(n, cap, per, columns)
        + [pltpu.VMEM((stat_rows(count), columns), F32)]
        + [pltpu.VMEM((piece_rows(count), columns), F32)],
        compiler_params=params(16),
        cost_estimate=HEAVY,
        name="far_part",
    )(arrive, places, q, *got, earlier)


def store_part(heads, pairs, part, top, total, part_ref, stat_ref, diagonal):
    for x, (i, h) in zip(part, pairs):
        part_ref[rows_of(i), cols_of(h)] = x
    for c, columns in enumerate((top, total)):
        for x, (i, h) in zip(flatten(columns, diagonal), pairs):
            stat_ref[i : i + 1, pl.ds(h * DH + c * BLOCK, BLOCK)] = x


def near_kernel(n, cap, per, heads, place_ref, q_ref, k_ref, v_ref, *refs):
    half, plane = n // 2, n // 4
    second = refs[:plane], refs[plane:half]
    part_ref, stat_ref, glob, ends, keys, vals = refs[half + 1 :]
    me = lax.axis_index("seq")
    rows = per * BLOCK
    diagonal = eye()
    stat_ref[...] = jnp.zeros_like(stat_ref)
    size = cap * BLOCK
    glob_bias = widen(shared_blocks(n, per, place_ref, *second, size, glob, ends))
    keys[:BLOCK] = ends[:BLOCK]
    vals[:BLOCK] = ends[BLOCK : 2 * BLOCK]
    keys[pl.ds(BLOCK, rows)] = k_ref[...]
    vals[pl.ds(BLOCK, rows)] = v_ref[...]
    keys[pl.ds(BLOCK + rows, BLOCK)] = ends[2 * BLOCK : 3 * BLOCK]
    vals[pl.ds(BLOCK + rows, BLOCK)] = ends[3 * BLOCK :]
    inside = lax.bitwise_and(me, half - 1)
    first_bias, last_bias = [jnp.where(inside == x, NONE, 0.0) for x in (0, half - 1)]
    for pairs in batches((0, per), heads, 2):
        sets = []
        for i, h in pairs:
            window, cols = pl.ds(i * BLOCK, 3 * BLOCK), cols_of(h)
            bias = None
            if i in (0, per - 1):
                bias = widen([first_bias if i == 0 else 0.0, 0.0, last_bias if i else 0.0])
            sets.append(
                [
                    (keys[window, cols], vals[window, cols], bias),
                    (glob[: G * BLOCK, cols], glob[G * BLOCK :, cols], glob_bias),
                ]
            )
        parts = attend([q_ref[rows_of(i), cols_of(h)] for i, h in pairs], sets)
        store_part(heads, pairs, *parts, part_ref, stat_ref, diagonal)


def part_shapes(per, columns):
    return (
        jax.ShapeDtypeStruct((per * BLOCK, columns), F32),
        jax.ShapeDtypeStruct((stat_rows(per), columns), F32),
    )


def near_part(n, cap, per, places, q, k, v, shared, earlier):
    rows, columns = q.shape
    heads = columns // DH
    return pl.pallas_call(
        functools.partial(near_kernel, n, cap, per, heads),
        out_shape=part_shapes(per, columns),
        in_specs=[spec(SMEM)] + [spec()] * (3 + len(shared)) + [spec(pl.ANY)],
        out_specs=(spec(), spec()),
        scratch_shapes=scratches(n, cap, per, columns)[3:]
        + [pltpu.VMEM((rows + 2 * BLOCK, columns), BF16)] * 2,
        compiler_params=params(16),
        cost_estimate=LIGHT,
        name="near_part",
    )(places, q, k, v, *shared, earlier)


def rand_kernel(n, cap, per, heads, arrive_ref, q_ref, *refs):
    plane = n // 4
    early, late = refs[:plane], refs[plane : 2 * plane]
    part_ref, stat_ref, held, keys, vals = refs[2 * plane :]
    diagonal = eye()
    stat_ref[...] = jnp.zeros_like(stat_ref)
    me = lax.axis_index("seq")
    size = cap * BLOCK
    sources = [((x, 2 * size), (y, 0)) for x, y in zip(early, late)]
    sources += [((y, size), (y, 2 * size)) for y in late]
    biases = choose(n, cap, per, (0, per), arrive_ref, me, sources, held, keys, vals)
    for pairs in batches((0, per), heads, 4):
        sets = [
            [(keys[picked_of(i), cols_of(h)], vals[picked_of(i), cols_of(h)], widen(biases[i]))]
            for i, h in pairs
        ]
        parts = attend([q_ref[rows_of(i), cols_of(h)] for i, h in pairs], sets)
        store_part(heads, pairs, *parts, part_ref, stat_ref, diagonal)


def rand_part(n, cap, per, arrive, q, early, late):
    columns = q.shape[1]
    return pl.pallas_call(
        functools.partial(rand_kernel, n, cap, per, columns // DH),
        out_shape=part_shapes(per, columns),
        in_specs=[spec(SMEM), spec()] + [spec()] * (len(early) + len(late)),
        out_specs=(spec(), spec()),
        scratch_shapes=scratches(n, cap, per, columns)[:3],
        compiler_params=params(16),
        cost_estimate=HEAVY,
        name="rand_part",
    )(arrive, q, *early, *late)


def context_kernel(
    span, heads, near_ref, near_stat_ref, rand_ref, rand_stat_ref, far_ref, out_ref, pieces
):
    low, high = span
    count = high - low
    pieces[...] = far_ref[pl.ds(count * BLOCK, pieces.shape[0])].astype(F32)
    far = sum(pieces[p * count : (p + 1) * count] for p in range(PIECES))
    stats = (near_stat_ref[low:high], rand_stat_ref[low:high], far)
    weights = []
    for h in range(heads):
        tops = [x[:, h * DH : h * DH + BLOCK] for x in stats]
        sums = [x[:, h * DH + BLOCK : (h + 1) * DH] for x in stats]
        top = functools.reduce(jnp.maximum, tops)
        w = [jnp.exp(x - top) for x in tops]
        total = sum(x * y for x, y in zip(w, sums))
        w[2] = w[2] * sums[2]
        weights.append([jnp.transpose(x / total) for x in w])
    for i in range(count):
        for h, ws in enumerate(weights):
            rows, here, cols = rows_of(low + i), rows_of(i), cols_of(h)
            parts = (near_ref[rows, cols], rand_ref[rows, cols], far_ref[here, cols].astype(F32))
            out_ref[here, cols] = sum(x * w[:, i : i + 1] for x, w in zip(parts, ws)).astype(BF16)


def contexts(span, near, near_stat, rand, rand_stat, far):
    columns = near.shape[1]
    count = span[1] - span[0]
    return pl.pallas_call(
        functools.partial(context_kernel, span, columns // DH),
        out_shape=jax.ShapeDtypeStruct((count * BLOCK, columns), BF16),
        in_specs=[spec()] * 5,
        out_specs=spec(),
        scratch_shapes=[pltpu.VMEM((piece_rows(count), columns), F32)],
        compiler_params=params(8),
        cost_estimate=LIGHT,
        name="contexts",
    )(near, near_stat, rand, rand_stat, far)


def project_kernel(span, count, steps, *refs):
    parts, w_ref, (out_ref, joined, product, sems) = refs[:count], refs[count], refs[-4:]
    me = lax.axis_index("head")
    columns = parts[0].shape[1]
    for step, rows_ref in enumerate(parts):
        owner = lax.rem(me + step, count)
        for h in range(count):
            @pl.when(owner == h)
            def _(h=h, rows_ref=rows_ref):
                joined[:, pl.ds(h * columns, columns)] = rows_ref[...]
    size = joined.shape[0] // steps
    copies = []
    for step in range(steps):
        rows = pl.ds(step * size, size)
        product[rows] = jnp.dot(
            joined[rows], w_ref[...], preferred_element_type=F32
        ).astype(BF16)
        target = out_ref.at[pl.ds(span[0] * BLOCK + step * size, size)]
        copies.append(pltpu.make_async_copy(product.at[rows], target, sems.at[step]))
        copies[-1].start()
    for copy in copies:
        copy.wait()


def project(span, tokens, parts, w_out, done=None):
    rows = parts[0].shape[0]
    wide = w_out.shape[1]
    steps = 4
    before = [] if done is None else [done]
    return pl.pallas_call(
        functools.partial(project_kernel, span, len(parts), steps),
        out_shape=jax.ShapeDtypeStruct((tokens, wide), BF16),
        in_specs=[spec()] * (len(parts) + 1) + [spec(pl.ANY)] * len(before),
        out_specs=spec(pl.ANY),
        scratch_shapes=[
            pltpu.VMEM((rows, w_out.shape[0]), BF16),
            pltpu.VMEM((rows, wide), BF16),
            pltpu.SemaphoreType.DMA((steps,)),
        ],
        input_output_aliases={len(parts) + 1: 0} if before else {},
        compiler_params=params(16),
        cost_estimate=LIGHT,
        name="project",
    )(*parts, w_out, *before)


def on_device(queries, keys, values, rand_group, rand_offset, glob_blocks, w_out):
    tokens_dev = queries.shape[0]
    per = tokens_dev // BLOCK
    n = lax.axis_size("seq")
    heads = lax.axis_size("head")
    cap = max(2, (rand_group.shape[0] // n * R + n - 1) // n)

    mates = [(i, i ^ (n // 4)) for i in range(n)]
    partners = [(i, i ^ (n // 2)) for i in range(n)]
    mate_k = lax.ppermute(keys, "seq", mates)
    mate_v = lax.ppermute(values, "seq", mates)
    later_q, _ = lax.optimization_barrier((queries, mate_k))
    far_q = lax.ppermute(later_q, "seq", partners)
    spots, arrive = ranks(n, per, cap, rand_group.T, rand_offset.T)
    rows = {(0, 0): keys, (0, 1): values}
    lists = ((0, True, (0, 1)), (0, False, (0,)))
    first = exchange(gather(n, per, cap, lists, spots, rows), n)
    rows = {(0, 0): keys, (1, 0): mate_k}
    lists = ((1, True, (0,)),)
    second_k = exchange(gather(n, per, cap, lists, spots, rows, [glob_blocks], first[1:4]), n)
    rows = {(0, 1): values, (1, 1): mate_v}
    lists = ((1, True, (1,)),)
    sent = gather(n, per, cap, lists, spots, rows, [glob_blocks], second_k[1:2])
    second = second_k + exchange(sent, n)
    rows = {(0, 0): keys, (0, 1): values, (1, 0): mate_k, (1, 1): mate_v}
    lists = ((0, False, (1,)), (1, False, (0, 1)))
    third = gather(n, per, cap, lists, spots, rows, (), sent[:1])
    middle = (per + 1) // 2
    spans = ((0, middle), (middle, per))
    fars = []
    earlier = third[0]
    for span in spans:
        earlier = far_part(
            n, cap, per, span, arrive, glob_blocks, far_q, first + second, earlier
        )
        fars.append(lax.ppermute(earlier, "seq", partners))
    third = exchange(third, n)
    near, near_stat = near_part(n, cap, per, glob_blocks, queries, keys, values, second, earlier)
    rand, rand_stat = rand_part(n, cap, per, arrive, queries, first, third)
    out = None
    for span, far in zip(spans, fars):
        context = contexts(span, near, near_stat, rand, rand_stat, far)
        others = [
            lax.ppermute(context, "head", [((i + s) % heads, i) for i in range(heads)])
            for s in range(1, heads)
        ]
        out = project(span, tokens_dev, [context] + others, w_out, out)
    return out


def solution(mesh):
    return jax.shard_map(
        on_device,
        mesh=mesh,
        in_specs=(
            P("seq", "head"),
            P("seq", "head"),
            P("seq", "head"),
            P(),
            P(),
            P(),
            P(None, "head"),
        ),
        out_specs=P("seq", "head"),
        check_vma=False,
    )
```

```python
import functools
import math

import jax
import jax.numpy as jnp
from jax import lax
from jax.experimental import pallas as pl
from jax.experimental.pallas import tpu as pltpu
from jax.sharding import PartitionSpec as P

DH = 128
BLOCK = 64
R = 3
G = 2
VMEM = pltpu.MemorySpace.VMEM
SMEM = pltpu.MemorySpace.SMEM
BF16 = jnp.bfloat16
F32 = jnp.float32
I32 = jnp.int32
NONE = -1e30
PIECES = 3


def params(mib):
    return pltpu.CompilerParams(vmem_limit_bytes=mib * 1024 * 1024)


LIGHT = pl.CostEstimate(flops=1, bytes_accessed=1, transcendentals=0)
HEAVY = pl.CostEstimate(flops=4 * 10**9, bytes_accessed=1, transcendentals=0)


def spec(space=VMEM):
    return pl.BlockSpec(memory_space=space)


def rank_kernel(n, per, cap, g_ref, o_ref, spot_ref, arrive_ref, g_pad, o_pad):
    me = lax.axis_index("seq")
    nb = g_ref.shape[1]
    wide = g_pad.shape[1]
    tall = spot_ref.shape[0]
    g_pad[...] = jnp.full(g_pad.shape, -1, I32)
    o_pad[...] = jnp.zeros(o_pad.shape, I32)
    g_pad[:R, :nb] = g_ref[...]
    o_pad[:R, :nb] = o_ref[...]
    g = g_pad[...]
    lane = lax.broadcasted_iota(I32, g.shape, 1)
    place = lane
    for d in range(1, n):
        place = jnp.where(lane >= d * per, lane - d * per, place)
    rank = jnp.zeros(g.shape, I32)
    for s in range(1, per):
        back = pltpu.roll(g, s, axis=1)
        ahead = place >= s
        for r in range(R):
            same = jnp.broadcast_to(back[r : r + 1, :], g.shape) == g
            rank = rank + jnp.where(ahead & same, 1, 0)
    arrive_ref[...] = g * cap + rank
    row = lax.broadcasted_iota(I32, (tall, wide), 0)
    spots = jnp.zeros((tall, wide), F32)
    for side in range(2):
        named = jnp.where(g == lax.bitwise_xor(me, side * (n // 4)), o_pad[...], 0)
        for s in range(cap):
            picked = jnp.where(rank == s, named, 0).astype(F32)
            total = jnp.sum(picked, axis=0, keepdims=True)
            here = row == side * cap + s
            spots = spots + jnp.where(here, jnp.broadcast_to(total, (tall, wide)), 0.0)
    token = lax.broadcasted_iota(I32, (wide, 128), 0)
    first = lax.broadcasted_iota(I32, (wide, 128), 1) * per
    belongs = jnp.where((token >= first) & (token < first + per), 1.0, 0.0)
    spot_ref[...] = jnp.dot(
        spots.astype(BF16), belongs.astype(BF16), preferred_element_type=F32
    ).astype(I32)


def ranks(n, per, cap, groups, offsets):
    nb = groups.shape[1]
    wide = -(-nb // 128) * 128
    tall = -(-2 * cap // 8) * 8
    return pl.pallas_call(
        functools.partial(rank_kernel, n, per, cap),
        out_shape=(
            jax.ShapeDtypeStruct((tall, 128), I32),
            jax.ShapeDtypeStruct((8, wide), I32),
        ),
        in_specs=[spec(), spec()],
        out_specs=(spec(), spec()),
        scratch_shapes=[pltpu.VMEM((8, wide), I32), pltpu.VMEM((8, wide), I32)],
        compiler_params=params(4),
        cost_estimate=LIGHT,
        name="ranks",
    )(groups, offsets)


def gather_kernel(n, per, cap, lists, shared, names, spot_ref, *refs):
    plane = n // 4
    me = lax.axis_index("seq")
    sources, outs = dict(zip(names, refs)), refs[-plane:]
    for k, out_ref in enumerate(outs):
        at = 0
        for side, far, parts in lists:
            d = lax.bitwise_xor(me, k + (n // 2 if far else 0))
            for c in parts:
                for s in range(cap):
                    start = spot_ref[side * cap + s, d] * BLOCK
                    rows = pl.ds(pl.multiple_of(start, BLOCK), BLOCK)
                    out_ref[pl.ds(at, BLOCK)] = sources[side, c][rows]
                    at += BLOCK
        if shared:
            (c,) = lists[0][2]
            place_ref = refs[len(names)]
            shared_rows(n, per, k, at, place_ref, sources[0, c], sources[1, c], out_ref)


def shared_rows(n, per, k, at, place_ref, own_ref, mate_ref, out_ref):
    plane = n // 4
    me = lax.axis_index("seq")
    for g in range(G):
        owner = lax.div(place_ref[g], per)
        start = pl.multiple_of((place_ref[g] - owner * per) * BLOCK, BLOCK)
        rows = pl.ds(start, BLOCK)
        mine = lax.bitwise_and(lax.bitwise_xor(owner, me), plane) == 0
        out_ref[pl.ds(at + g * BLOCK, BLOCK)] = jnp.where(mine, own_ref[rows], mate_ref[rows])
    place = lax.bitwise_and(me, plane - 1)
    target = lax.bitwise_xor(place, k)
    is_before = lax.rem(place + 1, plane) == target
    is_end = jnp.where(is_before, target == 0, target == plane - 1)
    rows = pl.ds(pl.multiple_of(jnp.where(is_before, (per - 1) * BLOCK, 0), BLOCK), BLOCK)
    out_ref[pl.ds(at + G * BLOCK, BLOCK)] = jnp.where(is_end, mate_ref[rows], own_ref[rows])


def gather(n, per, cap, lists, spots, sources, shared=(), earlier=()):
    plane = n // 4
    names, arrays = tuple(sources), list(sources.values())
    rows = sum(len(parts) for _, _, parts in lists) * cap * BLOCK
    rows += (G + 1) * BLOCK if shared else 0
    out = jax.ShapeDtypeStruct((rows, arrays[0].shape[1]), BF16)
    return pl.pallas_call(
        functools.partial(gather_kernel, n, per, cap, lists, bool(shared), names),
        out_shape=(out,) * plane,
        in_specs=[spec(SMEM)]
        + [spec()] * len(arrays)
        + [spec(SMEM)] * len(shared)
        + [spec(pl.ANY)] * len(earlier),
        out_specs=(spec(),) * plane,
        compiler_params=params(8),
        cost_estimate=LIGHT,
        name="gather_blocks",
    )(spots, *arrays, *shared, *earlier)


def exchange(parts, n):
    got = [parts[0]]
    for k in range(1, n // 4):
        got.append(lax.ppermute(parts[k], "seq", [(i, i ^ k) for i in range(n)]))
    return got


def choose(n, cap, per, span, arrive_ref, d, sources, held, keys, vals):
    half = n // 2
    me = lax.axis_index("seq")
    for k, pair in enumerate(sources):
        for c, (ref, row) in enumerate(pair):
            held[k, pl.ds(c * cap * BLOCK, cap * BLOCK)] = ref[pl.ds(row, cap * BLOCK)]
    biases = {}
    for i in range(*span):
        row = []
        for r in range(R):
            spot = arrive_ref[r, d * per + i]
            group = lax.div(spot, cap)
            differ = lax.bitwise_xor(group, me)
            here = differ < half
            slot = jnp.where(here, spot - group * cap, 0)
            k = jnp.where(here, differ, 0)
            at = pl.ds((i * R + r) * BLOCK, BLOCK)
            keys[at] = held[k, pl.ds(pl.multiple_of(slot * BLOCK, BLOCK), BLOCK), :]
            vals[at] = held[k, pl.ds(pl.multiple_of((cap + slot) * BLOCK, BLOCK), BLOCK), :]
            row.append(jnp.where(here, 0.0, NONE))
        biases[i] = row
    return biases


def shared_blocks(n, per, place_ref, key_refs, val_refs, skip, glob, ends):
    plane = n // 4
    me = lax.axis_index("seq")
    place = lax.bitwise_and(me, plane - 1)
    biases = []
    for g in range(G):
        differ = lax.bitwise_xor(lax.div(place_ref[g], per), me)
        for p, pair in enumerate(zip(key_refs, val_refs)):
            @pl.when(lax.bitwise_and(differ, plane - 1) == p)
            def _(g=g, pair=pair):
                for c, ref in enumerate(pair):
                    at = pl.ds((c * G + g) * BLOCK, BLOCK)
                    glob[at] = ref[pl.ds(skip + g * BLOCK, BLOCK)]
        biases.append(jnp.where(differ < n // 2, 0.0, NONE))
    for e, neighbour in enumerate((place + plane - 1, place + 1)):
        k = lax.bitwise_xor(place, lax.bitwise_and(neighbour, plane - 1))
        for p, pair in enumerate(zip(key_refs, val_refs)):
            @pl.when(k == p)
            def _(e=e, pair=pair):
                for c, ref in enumerate(pair):
                    at = pl.ds((2 * e + c) * BLOCK, BLOCK)
                    ends[at] = ref[pl.ds(skip + G * BLOCK, BLOCK)]
    return biases


def widen(biases):
    count = len(biases)
    lane = lax.broadcasted_iota(I32, (1, count * BLOCK), 1)
    bias = jnp.full((1, count * BLOCK), biases[-1], F32)
    for r in reversed(range(count - 1)):
        bias = jnp.where(lane < (r + 1) * BLOCK, biases[r], bias)
    return bias


def batches(span, heads, step):
    for first in range(*span, step):
        yield [(i, h) for i in range(first, min(span[1], first + step)) for h in range(heads)]


def rows_of(i):
    return pl.ds(i * BLOCK, BLOCK)


def picked_of(i):
    return pl.ds(i * R * BLOCK, R * BLOCK)


def cols_of(h):
    return pl.ds(h * DH, DH)


def dot_t(a, b):
    return lax.dot_general(a, b, (((1,), (1,)), ((), ())), preferred_element_type=F32)


def eye():
    shape = (BLOCK, BLOCK)
    return lax.broadcasted_iota(I32, shape, 0) == lax.broadcasted_iota(I32, shape, 1)


def flatten(columns, diagonal):
    return [jnp.sum(jnp.where(diagonal, x, 0.0), axis=0, keepdims=True) for x in columns]


def attend(queries, sets):
    scale = 1.0 / math.sqrt(DH)
    s = [
        [dot_t(q, ks) * scale + bias if bias is not None else dot_t(q, ks) * scale
         for ks, vs, bias in group]
        for q, group in zip(queries, sets)
    ]
    top = [[jnp.max(x, axis=1, keepdims=True) for x in group] for group in s]
    top = [functools.reduce(jnp.maximum, group) for group in top]
    w = [[jnp.exp(x - t) for x in group] for group, t in zip(s, top)]
    total = [sum(jnp.sum(x, axis=1, keepdims=True) for x in group) for group in w]
    part = [
        sum(
            jnp.dot(x.astype(BF16), vs, preferred_element_type=F32)
            for x, (ks, vs, bias) in zip(ws, group)
        )
        for ws, group in zip(w, sets)
    ]
    return part, top, total


def far_kernel(n, cap, per, heads, span, arrive_ref, place_ref, q_ref, *refs):
    half, plane = n // 2, n // 4
    first, second = refs[:plane], (refs[plane:half], refs[half : half + plane])
    out_ref, held, keys, vals, glob, ends, stat, pieces = refs[half + plane + 1 :]
    me = lax.axis_index("seq")
    d = lax.bitwise_xor(me, half)
    diagonal = eye()
    stat[...] = jnp.zeros_like(stat)
    size = cap * BLOCK
    sources = [((ref, 0), (ref, size)) for ref in first]
    sources += [((x, 0), (y, 0)) for x, y in zip(*second)]
    biases = choose(n, cap, per, span, arrive_ref, d, sources, held, keys, vals)
    glob_bias = widen(shared_blocks(n, per, place_ref, *second, size, glob, ends))
    inside = lax.bitwise_and(me, half - 1)
    end_bias = [jnp.where(inside == x, 0.0, NONE) for x in (0, half - 1)]
    low, high = span
    count = high - low
    for pairs in batches(span, heads, 3):
        sets = []
        for i, h in pairs:
            cols = cols_of(h)
            group = [
                (keys[picked_of(i), cols], vals[picked_of(i), cols], widen(biases[i])),
                (glob[: G * BLOCK, cols], glob[G * BLOCK :, cols], glob_bias),
            ]
            for e, edge in enumerate((0, per - 1)):
                if i == edge:
                    at = e * 2 * BLOCK
                    group.append(
                        (ends[at : at + BLOCK, cols], ends[at + BLOCK : at + 2 * BLOCK, cols],
                         end_bias[e])
                    )
            sets.append(group)
        part, top, total = attend([q_ref[rows_of(i), cols_of(h)] for i, h in pairs], sets)
        for x, t, (i, h) in zip(part, total, pairs):
            out_ref[rows_of(i - low), cols_of(h)] = (x / t).astype(BF16)
        for c, columns in enumerate((top, total)):
            for x, (i, h) in zip(flatten(columns, diagonal), pairs):
                stat[i - low : i - low + 1, pl.ds(h * DH + c * BLOCK, BLOCK)] = x
    rest = stat[...]
    pieces[...] = jnp.zeros_like(pieces)
    for p in range(PIECES):
        piece = rest.astype(BF16).astype(F32)
        rest = rest - piece
        pieces[p * count : (p + 1) * count] = piece[:count]
    out_ref[pl.ds(count * BLOCK, pieces.shape[0])] = pieces[...].astype(BF16)


def stat_rows(per):
    return -(-per // 8) * 8


def piece_rows(per):
    return -(-PIECES * per // 16) * 16


def scratches(n, cap, per, columns):
    return (
        [pltpu.VMEM((n // 2, 2 * cap * BLOCK, columns), BF16)]
        + [pltpu.VMEM((per * R * BLOCK, columns), BF16)] * 2
        + [pltpu.VMEM((2 * G * BLOCK, columns), BF16), pltpu.VMEM((4 * BLOCK, columns), BF16)]
    )


def far_part(n, cap, per, span, arrive, places, q, got, earlier):
    columns = q.shape[1]
    count = span[1] - span[0]
    heads = columns // DH
    return pl.pallas_call(
        functools.partial(far_kernel, n, cap, per, heads, span),
        out_shape=jax.ShapeDtypeStruct((count * BLOCK + piece_rows(count), columns), BF16),
        in_specs=[spec(SMEM)] * 2 + [spec()] * (1 + len(got)) + [spec(pl.ANY)],
        out_specs=spec(),
        scratch_shapes=scratches(n, cap, per, columns)
        + [pltpu.VMEM((stat_rows(count), columns), F32)]
        + [pltpu.VMEM((piece_rows(count), columns), F32)],
        compiler_params=params(16),
        cost_estimate=HEAVY,
        name="far_part",
    )(arrive, places, q, *got, earlier)


def store_part(heads, pairs, part, top, total, part_ref, stat_ref, diagonal):
    for x, (i, h) in zip(part, pairs):
        part_ref[rows_of(i), cols_of(h)] = x
    for c, columns in enumerate((top, total)):
        for x, (i, h) in zip(flatten(columns, diagonal), pairs):
            stat_ref[i : i + 1, pl.ds(h * DH + c * BLOCK, BLOCK)] = x


def near_kernel(n, cap, per, heads, place_ref, q_ref, k_ref, v_ref, *refs):
    half, plane = n // 2, n // 4
    second = refs[:plane], refs[plane:half]
    part_ref, stat_ref, glob, ends, keys, vals = refs[half + 1 :]
    me = lax.axis_index("seq")
    rows = per * BLOCK
    diagonal = eye()
    stat_ref[...] = jnp.zeros_like(stat_ref)
    size = cap * BLOCK
    glob_bias = widen(shared_blocks(n, per, place_ref, *second, size, glob, ends))
    keys[:BLOCK] = ends[:BLOCK]
    vals[:BLOCK] = ends[BLOCK : 2 * BLOCK]
    keys[pl.ds(BLOCK, rows)] = k_ref[...]
    vals[pl.ds(BLOCK, rows)] = v_ref[...]
    keys[pl.ds(BLOCK + rows, BLOCK)] = ends[2 * BLOCK : 3 * BLOCK]
    vals[pl.ds(BLOCK + rows, BLOCK)] = ends[3 * BLOCK :]
    inside = lax.bitwise_and(me, half - 1)
    first_bias, last_bias = [jnp.where(inside == x, NONE, 0.0) for x in (0, half - 1)]
    for pairs in batches((0, per), heads, 2):
        sets = []
        for i, h in pairs:
            window, cols = pl.ds(i * BLOCK, 3 * BLOCK), cols_of(h)
            bias = None
            if i in (0, per - 1):
                bias = widen([first_bias if i == 0 else 0.0, 0.0, last_bias if i else 0.0])
            sets.append(
                [
                    (keys[window, cols], vals[window, cols], bias),
                    (glob[: G * BLOCK, cols], glob[G * BLOCK :, cols], glob_bias),
                ]
            )
        parts = attend([q_ref[rows_of(i), cols_of(h)] for i, h in pairs], sets)
        store_part(heads, pairs, *parts, part_ref, stat_ref, diagonal)


def part_shapes(per, columns):
    return (
        jax.ShapeDtypeStruct((per * BLOCK, columns), F32),
        jax.ShapeDtypeStruct((stat_rows(per), columns), F32),
    )


def near_part(n, cap, per, places, q, k, v, shared, earlier):
    rows, columns = q.shape
    heads = columns // DH
    return pl.pallas_call(
        functools.partial(near_kernel, n, cap, per, heads),
        out_shape=part_shapes(per, columns),
        in_specs=[spec(SMEM)] + [spec()] * (3 + len(shared)) + [spec(pl.ANY)],
        out_specs=(spec(), spec()),
        scratch_shapes=scratches(n, cap, per, columns)[3:]
        + [pltpu.VMEM((rows + 2 * BLOCK, columns), BF16)] * 2,
        compiler_params=params(16),
        cost_estimate=LIGHT,
        name="near_part",
    )(places, q, k, v, *shared, earlier)


def rand_kernel(n, cap, per, heads, arrive_ref, q_ref, *refs):
    plane = n // 4
    part_ref, stat_ref, held, keys, vals = refs[plane:]
    diagonal = eye()
    stat_ref[...] = jnp.zeros_like(stat_ref)
    me = lax.axis_index("seq")
    size = cap * BLOCK
    sources = [
        ((ref, 2 * side * size), (ref, (2 * side + 1) * size))
        for side in range(2)
        for ref in refs[:plane]
    ]
    biases = choose(n, cap, per, (0, per), arrive_ref, me, sources, held, keys, vals)
    for pairs in batches((0, per), heads, 4):
        sets = [
            [(keys[picked_of(i), cols_of(h)], vals[picked_of(i), cols_of(h)], widen(biases[i]))]
            for i, h in pairs
        ]
        parts = attend([q_ref[rows_of(i), cols_of(h)] for i, h in pairs], sets)
        store_part(heads, pairs, *parts, part_ref, stat_ref, diagonal)


def rand_part(n, cap, per, arrive, q, got):
    columns = q.shape[1]
    return pl.pallas_call(
        functools.partial(rand_kernel, n, cap, per, columns // DH),
        out_shape=part_shapes(per, columns),
        in_specs=[spec(SMEM), spec()] + [spec()] * len(got),
        out_specs=(spec(), spec()),
        scratch_shapes=scratches(n, cap, per, columns)[:3],
        compiler_params=params(16),
        cost_estimate=HEAVY,
        name="rand_part",
    )(arrive, q, *got)


def context_kernel(
    span, heads, near_ref, near_stat_ref, rand_ref, rand_stat_ref, far_ref, out_ref, pieces
):
    low, high = span
    count = high - low
    pieces[...] = far_ref[pl.ds(count * BLOCK, pieces.shape[0])].astype(F32)
    far = sum(pieces[p * count : (p + 1) * count] for p in range(PIECES))
    stats = (near_stat_ref[low:high], rand_stat_ref[low:high], far)
    weights = []
    for h in range(heads):
        tops = [x[:, h * DH : h * DH + BLOCK] for x in stats]
        sums = [x[:, h * DH + BLOCK : (h + 1) * DH] for x in stats]
        top = functools.reduce(jnp.maximum, tops)
        w = [jnp.exp(x - top) for x in tops]
        total = sum(x * y for x, y in zip(w, sums))
        w[2] = w[2] * sums[2]
        weights.append([jnp.transpose(x / total) for x in w])
    for i in range(count):
        for h, ws in enumerate(weights):
            rows, here, cols = rows_of(low + i), rows_of(i), cols_of(h)
            parts = (near_ref[rows, cols], rand_ref[rows, cols], far_ref[here, cols].astype(F32))
            out_ref[here, cols] = sum(x * w[:, i : i + 1] for x, w in zip(parts, ws)).astype(BF16)


def contexts(span, near, near_stat, rand, rand_stat, far):
    columns = near.shape[1]
    count = span[1] - span[0]
    return pl.pallas_call(
        functools.partial(context_kernel, span, columns // DH),
        out_shape=jax.ShapeDtypeStruct((count * BLOCK, columns), BF16),
        in_specs=[spec()] * 5,
        out_specs=spec(),
        scratch_shapes=[pltpu.VMEM((piece_rows(count), columns), F32)],
        compiler_params=params(8),
        cost_estimate=LIGHT,
        name="contexts",
    )(near, near_stat, rand, rand_stat, far)


def project_kernel(span, count, steps, *refs):
    parts, w_ref, (out_ref, joined, product, sems) = refs[:count], refs[count], refs[-4:]
    me = lax.axis_index("head")
    columns = parts[0].shape[1]
    for step, rows_ref in enumerate(parts):
        owner = lax.rem(me + step, count)
        for h in range(count):
            @pl.when(owner == h)
            def _(h=h, rows_ref=rows_ref):
                joined[:, pl.ds(h * columns, columns)] = rows_ref[...]
    size = joined.shape[0] // steps
    copies = []
    for step in range(steps):
        rows = pl.ds(step * size, size)
        product[rows] = jnp.dot(
            joined[rows], w_ref[...], preferred_element_type=F32
        ).astype(BF16)
        target = out_ref.at[pl.ds(span[0] * BLOCK + step * size, size)]
        copies.append(pltpu.make_async_copy(product.at[rows], target, sems.at[step]))
        copies[-1].start()
    for copy in copies:
        copy.wait()


def project(span, tokens, parts, w_out, done=None):
    rows = parts[0].shape[0]
    wide = w_out.shape[1]
    steps = 4
    before = [] if done is None else [done]
    return pl.pallas_call(
        functools.partial(project_kernel, span, len(parts), steps),
        out_shape=jax.ShapeDtypeStruct((tokens, wide), BF16),
        in_specs=[spec()] * (len(parts) + 1) + [spec(pl.ANY)] * len(before),
        out_specs=spec(pl.ANY),
        scratch_shapes=[
            pltpu.VMEM((rows, w_out.shape[0]), BF16),
            pltpu.VMEM((rows, wide), BF16),
            pltpu.SemaphoreType.DMA((steps,)),
        ],
        input_output_aliases={len(parts) + 1: 0} if before else {},
        compiler_params=params(16),
        cost_estimate=LIGHT,
        name="project",
    )(*parts, w_out, *before)


def on_device(queries, keys, values, rand_group, rand_offset, glob_blocks, w_out):
    tokens_dev = queries.shape[0]
    per = tokens_dev // BLOCK
    n = lax.axis_size("seq")
    heads = lax.axis_size("head")
    cap = max(2, (rand_group.shape[0] // n * R + n - 1) // n)

    mates = [(i, i ^ (n // 4)) for i in range(n)]
    partners = [(i, i ^ (n // 2)) for i in range(n)]
    mate_k = lax.ppermute(keys, "seq", mates)
    mate_v = lax.ppermute(values, "seq", mates)
    spots, arrive = ranks(n, per, cap, rand_group.T, rand_offset.T)
    rows = {(0, 0): keys, (0, 1): values}
    lists = ((0, True, (0, 1)),)
    first = exchange(gather(n, per, cap, lists, spots, rows), n)
    later_q = lax.optimization_barrier((queries, *first[1:4]))[0]
    far_q = lax.ppermute(later_q, "seq", partners)
    rows = {(0, 0): keys, (1, 0): mate_k}
    lists = ((1, True, (0,)),)
    second_k = exchange(gather(n, per, cap, lists, spots, rows, [glob_blocks], first[1:4]), n)
    rows = {(0, 1): values, (1, 1): mate_v}
    lists = ((1, True, (1,)),)
    sent = gather(n, per, cap, lists, spots, rows, [glob_blocks], second_k[1:2])
    second = second_k + exchange(sent, n)
    rows = {(0, 0): keys, (0, 1): values, (1, 0): mate_k, (1, 1): mate_v}
    lists = ((0, False, (0, 1)), (1, False, (0, 1)))
    third = gather(n, per, cap, lists, spots, rows, (), sent[:1])
    middle = (per + 1) // 2
    spans = ((0, middle), (middle, per))
    fars = []
    earlier = third[0]
    for span in spans:
        earlier = far_part(
            n, cap, per, span, arrive, glob_blocks, far_q, first + second, earlier
        )
        fars.append(lax.ppermute(earlier, "seq", partners))
    third = exchange(third, n)
    near, near_stat = near_part(n, cap, per, glob_blocks, queries, keys, values, second, earlier)
    rand, rand_stat = rand_part(n, cap, per, arrive, queries, third)
    out = None
    for span, far in zip(spans, fars):
        context = contexts(span, near, near_stat, rand, rand_stat, far)
        others = [
            lax.ppermute(context, "head", [((i + s) % heads, i) for i in range(heads)])
            for s in range(1, heads)
        ]
        out = project(span, tokens_dev, [context] + others, w_out, out)
    return out


def solution(mesh):
    return jax.shard_map(
        on_device,
        mesh=mesh,
        in_specs=(
            P("seq", "head"),
            P("seq", "head"),
            P("seq", "head"),
            P(),
            P(),
            P(),
            P(None, "head"),
        ),
        out_specs=P("seq", "head"),
        check_vma=False,
    )
```

```python
import functools
import math

import jax
import jax.numpy as jnp
from jax import lax
from jax.experimental import pallas as pl
from jax.experimental.pallas import tpu as pltpu
from jax.sharding import PartitionSpec as P

DH = 128
BLOCK = 64
R = 3
G = 2
VMEM = pltpu.MemorySpace.VMEM
SMEM = pltpu.MemorySpace.SMEM
BF16 = jnp.bfloat16
F32 = jnp.float32
I32 = jnp.int32
NONE = -1e30
PIECES = 3


def params(mib):
    return pltpu.CompilerParams(vmem_limit_bytes=mib * 1024 * 1024)


LIGHT = pl.CostEstimate(flops=1, bytes_accessed=1, transcendentals=0)
HEAVY = pl.CostEstimate(flops=4 * 10**9, bytes_accessed=1, transcendentals=0)


def spec(space=VMEM):
    return pl.BlockSpec(memory_space=space)


def rank_kernel(n, per, cap, g_ref, o_ref, spot_ref, arrive_ref, g_pad, o_pad):
    me = lax.axis_index("seq")
    nb = g_ref.shape[1]
    wide = g_pad.shape[1]
    tall = spot_ref.shape[0]
    g_pad[...] = jnp.full(g_pad.shape, -1, I32)
    o_pad[...] = jnp.zeros(o_pad.shape, I32)
    g_pad[:R, :nb] = g_ref[...]
    o_pad[:R, :nb] = o_ref[...]
    g = g_pad[...]
    lane = lax.broadcasted_iota(I32, g.shape, 1)
    place = lane
    for d in range(1, n):
        place = jnp.where(lane >= d * per, lane - d * per, place)
    rank = jnp.zeros(g.shape, I32)
    for s in range(1, per):
        back = pltpu.roll(g, s, axis=1)
        ahead = place >= s
        for r in range(R):
            same = jnp.broadcast_to(back[r : r + 1, :], g.shape) == g
            rank = rank + jnp.where(ahead & same, 1, 0)
    arrive_ref[...] = g * cap + rank
    row = lax.broadcasted_iota(I32, (tall, wide), 0)
    spots = jnp.zeros((tall, wide), F32)
    for side in range(2):
        named = jnp.where(g == lax.bitwise_xor(me, side * (n // 4)), o_pad[...], 0)
        for s in range(cap):
            picked = jnp.where(rank == s, named, 0).astype(F32)
            total = jnp.sum(picked, axis=0, keepdims=True)
            here = row == side * cap + s
            spots = spots + jnp.where(here, jnp.broadcast_to(total, (tall, wide)), 0.0)
    token = lax.broadcasted_iota(I32, (wide, 128), 0)
    first = lax.broadcasted_iota(I32, (wide, 128), 1) * per
    belongs = jnp.where((token >= first) & (token < first + per), 1.0, 0.0)
    spot_ref[...] = jnp.dot(
        spots.astype(BF16), belongs.astype(BF16), preferred_element_type=F32
    ).astype(I32)


def ranks(n, per, cap, groups, offsets):
    nb = groups.shape[1]
    wide = -(-nb // 128) * 128
    tall = -(-2 * cap // 8) * 8
    return pl.pallas_call(
        functools.partial(rank_kernel, n, per, cap),
        out_shape=(
            jax.ShapeDtypeStruct((tall, 128), I32),
            jax.ShapeDtypeStruct((8, wide), I32),
        ),
        in_specs=[spec(), spec()],
        out_specs=(spec(), spec()),
        scratch_shapes=[pltpu.VMEM((8, wide), I32), pltpu.VMEM((8, wide), I32)],
        compiler_params=params(4),
        cost_estimate=LIGHT,
        name="ranks",
    )(groups, offsets)


def gather_kernel(n, per, cap, lists, shared, names, spot_ref, *refs):
    plane = n // 4
    me = lax.axis_index("seq")
    sources, outs = dict(zip(names, refs)), refs[-plane:]
    for k, out_ref in enumerate(outs):
        at = 0
        for side, far, parts in lists:
            d = lax.bitwise_xor(me, k + (n // 2 if far else 0))
            for c in parts:
                for s in range(cap):
                    start = spot_ref[side * cap + s, d] * BLOCK
                    rows = pl.ds(pl.multiple_of(start, BLOCK), BLOCK)
                    out_ref[pl.ds(at, BLOCK)] = sources[side, c][rows]
                    at += BLOCK
        if shared:
            (c,) = lists[0][2]
            place_ref = refs[len(names)]
            shared_rows(n, per, k, at, place_ref, sources[0, c], sources[1, c], out_ref)


def shared_rows(n, per, k, at, place_ref, own_ref, mate_ref, out_ref):
    plane = n // 4
    me = lax.axis_index("seq")
    for g in range(G):
        owner = lax.div(place_ref[g], per)
        start = pl.multiple_of((place_ref[g] - owner * per) * BLOCK, BLOCK)
        rows = pl.ds(start, BLOCK)
        mine = lax.bitwise_and(lax.bitwise_xor(owner, me), plane) == 0
        out_ref[pl.ds(at + g * BLOCK, BLOCK)] = jnp.where(mine, own_ref[rows], mate_ref[rows])
    place = lax.bitwise_and(me, plane - 1)
    target = lax.bitwise_xor(place, k)
    is_before = lax.rem(place + 1, plane) == target
    is_end = jnp.where(is_before, target == 0, target == plane - 1)
    rows = pl.ds(pl.multiple_of(jnp.where(is_before, (per - 1) * BLOCK, 0), BLOCK), BLOCK)
    out_ref[pl.ds(at + G * BLOCK, BLOCK)] = jnp.where(is_end, mate_ref[rows], own_ref[rows])


def gather(n, per, cap, lists, spots, sources, shared=(), earlier=()):
    plane = n // 4
    names, arrays = tuple(sources), list(sources.values())
    rows = sum(len(parts) for _, _, parts in lists) * cap * BLOCK
    rows += (G + 1) * BLOCK if shared else 0
    out = jax.ShapeDtypeStruct((rows, arrays[0].shape[1]), BF16)
    return pl.pallas_call(
        functools.partial(gather_kernel, n, per, cap, lists, bool(shared), names),
        out_shape=(out,) * plane,
        in_specs=[spec(SMEM)]
        + [spec()] * len(arrays)
        + [spec(SMEM)] * len(shared)
        + [spec(pl.ANY)] * len(earlier),
        out_specs=(spec(),) * plane,
        compiler_params=params(8),
        cost_estimate=LIGHT,
        name="gather_blocks",
    )(spots, *arrays, *shared, *earlier)


def exchange(parts, n):
    got = [parts[0]]
    for k in range(1, n // 4):
        got.append(lax.ppermute(parts[k], "seq", [(i, i ^ k) for i in range(n)]))
    return got


def choose(n, cap, per, span, arrive_ref, d, sources, held, keys, vals):
    half = n // 2
    me = lax.axis_index("seq")
    for k, pair in enumerate(sources):
        for c, (ref, row) in enumerate(pair):
            held[k, pl.ds(c * cap * BLOCK, cap * BLOCK)] = ref[pl.ds(row, cap * BLOCK)]
    biases = {}
    for i in range(*span):
        row = []
        for r in range(R):
            spot = arrive_ref[r, d * per + i]
            group = lax.div(spot, cap)
            differ = lax.bitwise_xor(group, me)
            here = differ < half
            slot = jnp.where(here, spot - group * cap, 0)
            k = jnp.where(here, differ, 0)
            at = pl.ds((i * R + r) * BLOCK, BLOCK)
            keys[at] = held[k, pl.ds(pl.multiple_of(slot * BLOCK, BLOCK), BLOCK), :]
            vals[at] = held[k, pl.ds(pl.multiple_of((cap + slot) * BLOCK, BLOCK), BLOCK), :]
            row.append(jnp.where(here, 0.0, NONE))
        biases[i] = row
    return biases


def shared_blocks(n, per, place_ref, key_refs, val_refs, skip, glob, ends):
    plane = n // 4
    me = lax.axis_index("seq")
    place = lax.bitwise_and(me, plane - 1)
    biases = []
    for g in range(G):
        differ = lax.bitwise_xor(lax.div(place_ref[g], per), me)
        for p, pair in enumerate(zip(key_refs, val_refs)):
            @pl.when(lax.bitwise_and(differ, plane - 1) == p)
            def _(g=g, pair=pair):
                for c, ref in enumerate(pair):
                    at = pl.ds((c * G + g) * BLOCK, BLOCK)
                    glob[at] = ref[pl.ds(skip + g * BLOCK, BLOCK)]
        biases.append(jnp.where(differ < n // 2, 0.0, NONE))
    for e, neighbour in enumerate((place + plane - 1, place + 1)):
        k = lax.bitwise_xor(place, lax.bitwise_and(neighbour, plane - 1))
        for p, pair in enumerate(zip(key_refs, val_refs)):
            @pl.when(k == p)
            def _(e=e, pair=pair):
                for c, ref in enumerate(pair):
                    at = pl.ds((2 * e + c) * BLOCK, BLOCK)
                    ends[at] = ref[pl.ds(skip + G * BLOCK, BLOCK)]
    return biases


def widen(biases):
    count = len(biases)
    lane = lax.broadcasted_iota(I32, (1, count * BLOCK), 1)
    bias = jnp.full((1, count * BLOCK), biases[-1], F32)
    for r in reversed(range(count - 1)):
        bias = jnp.where(lane < (r + 1) * BLOCK, biases[r], bias)
    return bias


def batches(span, heads, step):
    for first in range(*span, step):
        yield [(i, h) for i in range(first, min(span[1], first + step)) for h in range(heads)]


def rows_of(i):
    return pl.ds(i * BLOCK, BLOCK)


def picked_of(i):
    return pl.ds(i * R * BLOCK, R * BLOCK)


def cols_of(h):
    return pl.ds(h * DH, DH)


def dot_t(a, b):
    return lax.dot_general(a, b, (((1,), (1,)), ((), ())), preferred_element_type=F32)


def eye():
    shape = (BLOCK, BLOCK)
    return lax.broadcasted_iota(I32, shape, 0) == lax.broadcasted_iota(I32, shape, 1)


def flatten(columns, diagonal):
    return [jnp.sum(jnp.where(diagonal, x, 0.0), axis=0, keepdims=True) for x in columns]


def attend(queries, sets):
    scale = 1.0 / math.sqrt(DH)
    s = [
        [dot_t(q, ks) * scale + bias if bias is not None else dot_t(q, ks) * scale
         for ks, vs, bias in group]
        for q, group in zip(queries, sets)
    ]
    top = [[jnp.max(x, axis=1, keepdims=True) for x in group] for group in s]
    top = [functools.reduce(jnp.maximum, group) for group in top]
    w = [[jnp.exp(x - t) for x in group] for group, t in zip(s, top)]
    total = [sum(jnp.sum(x, axis=1, keepdims=True) for x in group) for group in w]
    part = [
        sum(
            jnp.dot(x.astype(BF16), vs, preferred_element_type=F32)
            for x, (ks, vs, bias) in zip(ws, group)
        )
        for ws, group in zip(w, sets)
    ]
    return part, top, total


def far_kernel(n, cap, per, heads, span, arrive_ref, place_ref, q_ref, *refs):
    half, plane = n // 2, n // 4
    first, second = refs[:plane], (refs[plane:half], refs[half : half + plane])
    out_ref, held, keys, vals, glob, ends, stat, pieces = refs[half + plane + 1 :]
    me = lax.axis_index("seq")
    d = lax.bitwise_xor(me, half)
    diagonal = eye()
    stat[...] = jnp.zeros_like(stat)
    size = cap * BLOCK
    sources = [((ref, 0), (ref, size)) for ref in first]
    sources += [((x, 0), (y, 0)) for x, y in zip(*second)]
    biases = choose(n, cap, per, span, arrive_ref, d, sources, held, keys, vals)
    glob_bias = widen(shared_blocks(n, per, place_ref, *second, size, glob, ends))
    inside = lax.bitwise_and(me, half - 1)
    end_bias = [jnp.where(inside == x, 0.0, NONE) for x in (0, half - 1)]
    low, high = span
    count = high - low
    for pairs in batches(span, heads, 3):
        sets = []
        for i, h in pairs:
            cols = cols_of(h)
            group = [
                (keys[picked_of(i), cols], vals[picked_of(i), cols], widen(biases[i])),
                (glob[: G * BLOCK, cols], glob[G * BLOCK :, cols], glob_bias),
            ]
            for e, edge in enumerate((0, per - 1)):
                if i == edge:
                    at = e * 2 * BLOCK
                    group.append(
                        (ends[at : at + BLOCK, cols], ends[at + BLOCK : at + 2 * BLOCK, cols],
                         end_bias[e])
                    )
            sets.append(group)
        part, top, total = attend([q_ref[rows_of(i), cols_of(h)] for i, h in pairs], sets)
        for x, t, (i, h) in zip(part, total, pairs):
            out_ref[rows_of(i - low), cols_of(h)] = (x / t).astype(BF16)
        for c, columns in enumerate((top, total)):
            for x, (i, h) in zip(flatten(columns, diagonal), pairs):
                stat[i - low : i - low + 1, pl.ds(h * DH + c * BLOCK, BLOCK)] = x
    rest = stat[...]
    pieces[...] = jnp.zeros_like(pieces)
    for p in range(PIECES):
        piece = rest.astype(BF16).astype(F32)
        rest = rest - piece
        pieces[p * count : (p + 1) * count] = piece[:count]
    out_ref[pl.ds(count * BLOCK, pieces.shape[0])] = pieces[...].astype(BF16)


def stat_rows(per):
    return -(-per // 8) * 8


def piece_rows(per):
    return -(-PIECES * per // 16) * 16


def scratches(n, cap, per, columns):
    return (
        [pltpu.VMEM((n // 2, 2 * cap * BLOCK, columns), BF16)]
        + [pltpu.VMEM((per * R * BLOCK, columns), BF16)] * 2
        + [pltpu.VMEM((2 * G * BLOCK, columns), BF16), pltpu.VMEM((4 * BLOCK, columns), BF16)]
    )


def far_part(n, cap, per, span, arrive, places, q, got, earlier):
    columns = q.shape[1]
    count = span[1] - span[0]
    heads = columns // DH
    return pl.pallas_call(
        functools.partial(far_kernel, n, cap, per, heads, span),
        out_shape=jax.ShapeDtypeStruct((count * BLOCK + piece_rows(count), columns), BF16),
        in_specs=[spec(SMEM)] * 2 + [spec()] * (1 + len(got)) + [spec(pl.ANY)],
        out_specs=spec(),
        scratch_shapes=scratches(n, cap, per, columns)
        + [pltpu.VMEM((stat_rows(count), columns), F32)]
        + [pltpu.VMEM((piece_rows(count), columns), F32)],
        compiler_params=params(16),
        cost_estimate=HEAVY,
        name="far_part",
    )(arrive, places, q, *got, earlier)


def store_part(heads, pairs, part, top, total, part_ref, stat_ref, diagonal):
    for x, (i, h) in zip(part, pairs):
        part_ref[rows_of(i), cols_of(h)] = x
    for c, columns in enumerate((top, total)):
        for x, (i, h) in zip(flatten(columns, diagonal), pairs):
            stat_ref[i : i + 1, pl.ds(h * DH + c * BLOCK, BLOCK)] = x


def near_kernel(n, cap, per, heads, place_ref, q_ref, k_ref, v_ref, *refs):
    half, plane = n // 2, n // 4
    second = refs[:plane], refs[plane:half]
    part_ref, stat_ref, glob, ends, keys, vals = refs[half + 1 :]
    me = lax.axis_index("seq")
    rows = per * BLOCK
    diagonal = eye()
    stat_ref[...] = jnp.zeros_like(stat_ref)
    size = cap * BLOCK
    glob_bias = widen(shared_blocks(n, per, place_ref, *second, size, glob, ends))
    keys[:BLOCK] = ends[:BLOCK]
    vals[:BLOCK] = ends[BLOCK : 2 * BLOCK]
    keys[pl.ds(BLOCK, rows)] = k_ref[...]
    vals[pl.ds(BLOCK, rows)] = v_ref[...]
    keys[pl.ds(BLOCK + rows, BLOCK)] = ends[2 * BLOCK : 3 * BLOCK]
    vals[pl.ds(BLOCK + rows, BLOCK)] = ends[3 * BLOCK :]
    inside = lax.bitwise_and(me, half - 1)
    first_bias, last_bias = [jnp.where(inside == x, NONE, 0.0) for x in (0, half - 1)]
    for pairs in batches((0, per), heads, 2):
        sets = []
        for i, h in pairs:
            window, cols = pl.ds(i * BLOCK, 3 * BLOCK), cols_of(h)
            bias = None
            if i in (0, per - 1):
                bias = widen([first_bias if i == 0 else 0.0, 0.0, last_bias if i else 0.0])
            sets.append(
                [
                    (keys[window, cols], vals[window, cols], bias),
                    (glob[: G * BLOCK, cols], glob[G * BLOCK :, cols], glob_bias),
                ]
            )
        parts = attend([q_ref[rows_of(i), cols_of(h)] for i, h in pairs], sets)
        store_part(heads, pairs, *parts, part_ref, stat_ref, diagonal)


def part_shapes(per, columns):
    return (
        jax.ShapeDtypeStruct((per * BLOCK, columns), F32),
        jax.ShapeDtypeStruct((stat_rows(per), columns), F32),
    )


def near_part(n, cap, per, places, q, k, v, shared, earlier):
    rows, columns = q.shape
    heads = columns // DH
    return pl.pallas_call(
        functools.partial(near_kernel, n, cap, per, heads),
        out_shape=part_shapes(per, columns),
        in_specs=[spec(SMEM)] + [spec()] * (3 + len(shared)) + [spec(pl.ANY)],
        out_specs=(spec(), spec()),
        scratch_shapes=scratches(n, cap, per, columns)[3:]
        + [pltpu.VMEM((rows + 2 * BLOCK, columns), BF16)] * 2,
        compiler_params=params(16),
        cost_estimate=LIGHT,
        name="near_part",
    )(places, q, k, v, *shared, earlier)


def rand_kernel(n, cap, per, heads, arrive_ref, q_ref, *refs):
    plane = n // 4
    part_ref, stat_ref, held, keys, vals = refs[plane:]
    diagonal = eye()
    stat_ref[...] = jnp.zeros_like(stat_ref)
    me = lax.axis_index("seq")
    size = cap * BLOCK
    sources = [
        ((ref, 2 * side * size), (ref, (2 * side + 1) * size))
        for side in range(2)
        for ref in refs[:plane]
    ]
    biases = choose(n, cap, per, (0, per), arrive_ref, me, sources, held, keys, vals)
    for pairs in batches((0, per), heads, 4):
        sets = [
            [(keys[picked_of(i), cols_of(h)], vals[picked_of(i), cols_of(h)], widen(biases[i]))]
            for i, h in pairs
        ]
        parts = attend([q_ref[rows_of(i), cols_of(h)] for i, h in pairs], sets)
        store_part(heads, pairs, *parts, part_ref, stat_ref, diagonal)


def rand_part(n, cap, per, arrive, q, got):
    columns = q.shape[1]
    return pl.pallas_call(
        functools.partial(rand_kernel, n, cap, per, columns // DH),
        out_shape=part_shapes(per, columns),
        in_specs=[spec(SMEM), spec()] + [spec()] * len(got),
        out_specs=(spec(), spec()),
        scratch_shapes=scratches(n, cap, per, columns)[:3],
        compiler_params=params(16),
        cost_estimate=HEAVY,
        name="rand_part",
    )(arrive, q, *got)


def context_kernel(
    span, heads, near_ref, near_stat_ref, rand_ref, rand_stat_ref, far_ref, out_ref, pieces
):
    low, high = span
    count = high - low
    pieces[...] = far_ref[pl.ds(count * BLOCK, pieces.shape[0])].astype(F32)
    far = sum(pieces[p * count : (p + 1) * count] for p in range(PIECES))
    stats = (near_stat_ref[low:high], rand_stat_ref[low:high], far)
    weights = []
    for h in range(heads):
        tops = [x[:, h * DH : h * DH + BLOCK] for x in stats]
        sums = [x[:, h * DH + BLOCK : (h + 1) * DH] for x in stats]
        top = functools.reduce(jnp.maximum, tops)
        w = [jnp.exp(x - top) for x in tops]
        total = sum(x * y for x, y in zip(w, sums))
        w[2] = w[2] * sums[2]
        weights.append([jnp.transpose(x / total) for x in w])
    for i in range(count):
        for h, ws in enumerate(weights):
            rows, here, cols = rows_of(low + i), rows_of(i), cols_of(h)
            parts = (near_ref[rows, cols], rand_ref[rows, cols], far_ref[here, cols].astype(F32))
            out_ref[here, cols] = sum(x * w[:, i : i + 1] for x, w in zip(parts, ws)).astype(BF16)


def contexts(span, near, near_stat, rand, rand_stat, far):
    columns = near.shape[1]
    count = span[1] - span[0]
    return pl.pallas_call(
        functools.partial(context_kernel, span, columns // DH),
        out_shape=jax.ShapeDtypeStruct((count * BLOCK, columns), BF16),
        in_specs=[spec()] * 5,
        out_specs=spec(),
        scratch_shapes=[pltpu.VMEM((piece_rows(count), columns), F32)],
        compiler_params=params(8),
        cost_estimate=LIGHT,
        name="contexts",
    )(near, near_stat, rand, rand_stat, far)


def project_kernel(span, count, steps, *refs):
    parts, w_ref, (out_ref, joined, product, sems) = refs[:count], refs[count], refs[-4:]
    me = lax.axis_index("head")
    columns = parts[0].shape[1]
    for step, rows_ref in enumerate(parts):
        owner = lax.rem(me + step, count)
        for h in range(count):
            @pl.when(owner == h)
            def _(h=h, rows_ref=rows_ref):
                joined[:, pl.ds(h * columns, columns)] = rows_ref[...]
    size = joined.shape[0] // steps
    copies = []
    for step in range(steps):
        rows = pl.ds(step * size, size)
        product[rows] = jnp.dot(
            joined[rows], w_ref[...], preferred_element_type=F32
        ).astype(BF16)
        target = out_ref.at[pl.ds(span[0] * BLOCK + step * size, size)]
        copies.append(pltpu.make_async_copy(product.at[rows], target, sems.at[step]))
        copies[-1].start()
    for copy in copies:
        copy.wait()


def project(span, tokens, parts, w_out, done=None):
    rows = parts[0].shape[0]
    wide = w_out.shape[1]
    steps = 4
    before = [] if done is None else [done]
    return pl.pallas_call(
        functools.partial(project_kernel, span, len(parts), steps),
        out_shape=jax.ShapeDtypeStruct((tokens, wide), BF16),
        in_specs=[spec()] * (len(parts) + 1) + [spec(pl.ANY)] * len(before),
        out_specs=spec(pl.ANY),
        scratch_shapes=[
            pltpu.VMEM((rows, w_out.shape[0]), BF16),
            pltpu.VMEM((rows, wide), BF16),
            pltpu.SemaphoreType.DMA((steps,)),
        ],
        input_output_aliases={len(parts) + 1: 0} if before else {},
        compiler_params=params(16),
        cost_estimate=LIGHT,
        name="project",
    )(*parts, w_out, *before)


def on_device(queries, keys, values, rand_group, rand_offset, glob_blocks, w_out):
    tokens_dev = queries.shape[0]
    per = tokens_dev // BLOCK
    n = lax.axis_size("seq")
    heads = lax.axis_size("head")
    cap = max(2, (rand_group.shape[0] // n * R + n - 1) // n)

    mates = [(i, i ^ (n // 4)) for i in range(n)]
    partners = [(i, i ^ (n // 2)) for i in range(n)]
    mate_k = lax.ppermute(keys, "seq", mates)
    mate_v = lax.ppermute(values, "seq", mates)
    spots, arrive = ranks(n, per, cap, rand_group.T, rand_offset.T)
    rows = {(0, 0): keys, (0, 1): values}
    lists = ((0, True, (0, 1)),)
    first = exchange(gather(n, per, cap, lists, spots, rows), n)
    later_q = lax.optimization_barrier((queries, *first[1:4]))[0]
    far_q = lax.ppermute(later_q, "seq", partners)
    rows = {(0, 0): keys, (1, 0): mate_k}
    lists = ((1, True, (0,)),)
    second_k = exchange(gather(n, per, cap, lists, spots, rows, [glob_blocks], first[1:4]), n)
    rows = {(0, 1): values, (1, 1): mate_v}
    lists = ((1, True, (1,)),)
    sent = gather(n, per, cap, lists, spots, rows, [glob_blocks], second_k[1:2])
    second = second_k + exchange(sent, n)
    rows = {(0, 0): keys, (0, 1): values, (1, 0): mate_k, (1, 1): mate_v}
    lists = ((0, False, (0, 1)), (1, False, (0, 1)))
    third = gather(n, per, cap, lists, spots, rows, (), sent[:1])
    middle = (per + 1) // 2
    spans = ((0, middle), (middle, per))
    fars = []
    earlier = third[0]
    for span in spans:
        earlier = far_part(
            n, cap, per, span, arrive, glob_blocks, far_q, first + second, earlier
        )
        fars.append(earlier)
    last, _ = lax.optimization_barrier((third[-1], fars[1]))
    third = exchange([*third[:-1], last], n)
    fars = [lax.ppermute(far, "seq", partners) for far in fars]
    near, near_stat = near_part(n, cap, per, glob_blocks, queries, keys, values, second, earlier)
    rand, rand_stat = rand_part(n, cap, per, arrive, queries, third)
    out = None
    for span, far in zip(spans, fars):
        context = contexts(span, near, near_stat, rand, rand_stat, far)
        others = [
            lax.ppermute(context, "head", [((i + s) % heads, i) for i in range(heads)])
            for s in range(1, heads)
        ]
        out = project(span, tokens_dev, [context] + others, w_out, out)
    return out


def solution(mesh):
    return jax.shard_map(
        on_device,
        mesh=mesh,
        in_specs=(
            P("seq", "head"),
            P("seq", "head"),
            P("seq", "head"),
            P(),
            P(),
            P(),
            P(None, "head"),
        ),
        out_specs=P("seq", "head"),
        check_vma=False,
    )
```

```python
import functools
import math

import jax
import jax.numpy as jnp
from jax import lax
from jax.experimental import pallas as pl
from jax.experimental.pallas import tpu as pltpu
from jax.sharding import PartitionSpec as P

DH = 128
BLOCK = 64
R = 3
G = 2
VMEM = pltpu.MemorySpace.VMEM
SMEM = pltpu.MemorySpace.SMEM
BF16 = jnp.bfloat16
F32 = jnp.float32
I32 = jnp.int32
NONE = -1e30
PIECES = 3


def params(mib):
    return pltpu.CompilerParams(vmem_limit_bytes=mib * 1024 * 1024)


LIGHT = pl.CostEstimate(flops=1, bytes_accessed=1, transcendentals=0)
HEAVY = pl.CostEstimate(flops=4 * 10**9, bytes_accessed=1, transcendentals=0)


def spec(space=VMEM):
    return pl.BlockSpec(memory_space=space)


def rank_kernel(n, per, cap, g_ref, o_ref, spot_ref, arrive_ref, g_pad, o_pad):
    me = lax.axis_index("seq")
    nb = g_ref.shape[1]
    wide = g_pad.shape[1]
    tall = spot_ref.shape[0]
    g_pad[...] = jnp.full(g_pad.shape, -1, I32)
    o_pad[...] = jnp.zeros(o_pad.shape, I32)
    g_pad[:R, :nb] = g_ref[...]
    o_pad[:R, :nb] = o_ref[...]
    g = g_pad[...]
    lane = lax.broadcasted_iota(I32, g.shape, 1)
    place = lane
    for d in range(1, n):
        place = jnp.where(lane >= d * per, lane - d * per, place)
    rank = jnp.zeros(g.shape, I32)
    for s in range(1, per):
        back = pltpu.roll(g, s, axis=1)
        ahead = place >= s
        for r in range(R):
            same = jnp.broadcast_to(back[r : r + 1, :], g.shape) == g
            rank = rank + jnp.where(ahead & same, 1, 0)
    arrive_ref[...] = g * cap + rank
    row = lax.broadcasted_iota(I32, (tall, wide), 0)
    spots = jnp.zeros((tall, wide), F32)
    for side in range(2):
        named = jnp.where(g == lax.bitwise_xor(me, side * (n // 4)), o_pad[...], 0)
        for s in range(cap):
            picked = jnp.where(rank == s, named, 0).astype(F32)
            total = jnp.sum(picked, axis=0, keepdims=True)
            here = row == side * cap + s
            spots = spots + jnp.where(here, jnp.broadcast_to(total, (tall, wide)), 0.0)
    token = lax.broadcasted_iota(I32, (wide, 128), 0)
    first = lax.broadcasted_iota(I32, (wide, 128), 1) * per
    belongs = jnp.where((token >= first) & (token < first + per), 1.0, 0.0)
    spot_ref[...] = jnp.dot(
        spots.astype(BF16), belongs.astype(BF16), preferred_element_type=F32
    ).astype(I32)


def ranks(n, per, cap, groups, offsets):
    nb = groups.shape[1]
    wide = -(-nb // 128) * 128
    tall = -(-2 * cap // 8) * 8
    return pl.pallas_call(
        functools.partial(rank_kernel, n, per, cap),
        out_shape=(
            jax.ShapeDtypeStruct((tall, 128), I32),
            jax.ShapeDtypeStruct((8, wide), I32),
        ),
        in_specs=[spec(), spec()],
        out_specs=(spec(), spec()),
        scratch_shapes=[pltpu.VMEM((8, wide), I32), pltpu.VMEM((8, wide), I32)],
        compiler_params=params(4),
        cost_estimate=LIGHT,
        name="ranks",
    )(groups, offsets)


def gather_kernel(n, per, cap, lists, shared, names, spot_ref, *refs):
    plane = n // 4
    me = lax.axis_index("seq")
    sources, outs = dict(zip(names, refs)), refs[-plane:]
    for k, out_ref in enumerate(outs):
        at = 0
        for side, far, parts in lists:
            d = lax.bitwise_xor(me, k + (n // 2 if far else 0))
            for c in parts:
                for s in range(cap):
                    start = spot_ref[side * cap + s, d] * BLOCK
                    rows = pl.ds(pl.multiple_of(start, BLOCK), BLOCK)
                    out_ref[pl.ds(at, BLOCK)] = sources[side, c][rows]
                    at += BLOCK
        if shared:
            (c,) = lists[0][2]
            place_ref = refs[len(names)]
            shared_rows(n, per, k, at, place_ref, sources[0, c], sources[1, c], out_ref)


def shared_rows(n, per, k, at, place_ref, own_ref, mate_ref, out_ref):
    plane = n // 4
    me = lax.axis_index("seq")
    for g in range(G):
        owner = lax.div(place_ref[g], per)
        start = pl.multiple_of((place_ref[g] - owner * per) * BLOCK, BLOCK)
        rows = pl.ds(start, BLOCK)
        mine = lax.bitwise_and(lax.bitwise_xor(owner, me), plane) == 0
        out_ref[pl.ds(at + g * BLOCK, BLOCK)] = jnp.where(mine, own_ref[rows], mate_ref[rows])
    place = lax.bitwise_and(me, plane - 1)
    target = lax.bitwise_xor(place, k)
    is_before = lax.rem(place + 1, plane) == target
    is_end = jnp.where(is_before, target == 0, target == plane - 1)
    rows = pl.ds(pl.multiple_of(jnp.where(is_before, (per - 1) * BLOCK, 0), BLOCK), BLOCK)
    out_ref[pl.ds(at + G * BLOCK, BLOCK)] = jnp.where(is_end, mate_ref[rows], own_ref[rows])


def gather(n, per, cap, lists, spots, sources, shared=(), earlier=()):
    plane = n // 4
    names, arrays = tuple(sources), list(sources.values())
    rows = sum(len(parts) for _, _, parts in lists) * cap * BLOCK
    rows += (G + 1) * BLOCK if shared else 0
    out = jax.ShapeDtypeStruct((rows, arrays[0].shape[1]), BF16)
    return pl.pallas_call(
        functools.partial(gather_kernel, n, per, cap, lists, bool(shared), names),
        out_shape=(out,) * plane,
        in_specs=[spec(SMEM)]
        + [spec()] * len(arrays)
        + [spec(SMEM)] * len(shared)
        + [spec(pl.ANY)] * len(earlier),
        out_specs=(spec(),) * plane,
        compiler_params=params(8),
        cost_estimate=LIGHT,
        name="gather_blocks",
    )(spots, *arrays, *shared, *earlier)


def exchange(parts, n):
    got = [parts[0]]
    for k in range(1, n // 4):
        got.append(lax.ppermute(parts[k], "seq", [(i, i ^ k) for i in range(n)]))
    return got


def choose(n, cap, per, span, arrive_ref, d, sources, held, keys, vals):
    half = n // 2
    me = lax.axis_index("seq")
    for k, pair in enumerate(sources):
        for c, (ref, row) in enumerate(pair):
            held[k, pl.ds(c * cap * BLOCK, cap * BLOCK)] = ref[pl.ds(row, cap * BLOCK)]
    biases = {}
    for i in range(*span):
        row = []
        for r in range(R):
            spot = arrive_ref[r, d * per + i]
            group = lax.div(spot, cap)
            differ = lax.bitwise_xor(group, me)
            here = differ < half
            slot = jnp.where(here, spot - group * cap, 0)
            k = jnp.where(here, differ, 0)
            at = pl.ds((i * R + r) * BLOCK, BLOCK)
            keys[at] = held[k, pl.ds(pl.multiple_of(slot * BLOCK, BLOCK), BLOCK), :]
            vals[at] = held[k, pl.ds(pl.multiple_of((cap + slot) * BLOCK, BLOCK), BLOCK), :]
            row.append(jnp.where(here, 0.0, NONE))
        biases[i] = row
    return biases


def shared_blocks(n, per, place_ref, key_refs, val_refs, skip, glob, ends):
    plane = n // 4
    me = lax.axis_index("seq")
    place = lax.bitwise_and(me, plane - 1)
    biases = []
    for g in range(G):
        differ = lax.bitwise_xor(lax.div(place_ref[g], per), me)
        for p, pair in enumerate(zip(key_refs, val_refs)):
            @pl.when(lax.bitwise_and(differ, plane - 1) == p)
            def _(g=g, pair=pair):
                for c, ref in enumerate(pair):
                    at = pl.ds((c * G + g) * BLOCK, BLOCK)
                    glob[at] = ref[pl.ds(skip + g * BLOCK, BLOCK)]
        biases.append(jnp.where(differ < n // 2, 0.0, NONE))
    for e, neighbour in enumerate((place + plane - 1, place + 1)):
        k = lax.bitwise_xor(place, lax.bitwise_and(neighbour, plane - 1))
        for p, pair in enumerate(zip(key_refs, val_refs)):
            @pl.when(k == p)
            def _(e=e, pair=pair):
                for c, ref in enumerate(pair):
                    at = pl.ds((2 * e + c) * BLOCK, BLOCK)
                    ends[at] = ref[pl.ds(skip + G * BLOCK, BLOCK)]
    return biases


def widen(biases):
    count = len(biases)
    lane = lax.broadcasted_iota(I32, (1, count * BLOCK), 1)
    bias = jnp.full((1, count * BLOCK), biases[-1], F32)
    for r in reversed(range(count - 1)):
        bias = jnp.where(lane < (r + 1) * BLOCK, biases[r], bias)
    return bias


def batches(span, heads, step):
    for first in range(*span, step):
        yield [(i, h) for i in range(first, min(span[1], first + step)) for h in range(heads)]


def rows_of(i):
    return pl.ds(i * BLOCK, BLOCK)


def picked_of(i):
    return pl.ds(i * R * BLOCK, R * BLOCK)


def cols_of(h):
    return pl.ds(h * DH, DH)


def dot_t(a, b):
    return lax.dot_general(a, b, (((1,), (1,)), ((), ())), preferred_element_type=F32)


def eye():
    shape = (BLOCK, BLOCK)
    return lax.broadcasted_iota(I32, shape, 0) == lax.broadcasted_iota(I32, shape, 1)


def flatten(columns, diagonal):
    return [jnp.sum(jnp.where(diagonal, x, 0.0), axis=0, keepdims=True) for x in columns]


def attend(queries, sets):
    scale = 1.0 / math.sqrt(DH)
    s = [
        [dot_t(q, ks) * scale + bias if bias is not None else dot_t(q, ks) * scale
         for ks, vs, bias in group]
        for q, group in zip(queries, sets)
    ]
    top = [[jnp.max(x, axis=1, keepdims=True) for x in group] for group in s]
    top = [functools.reduce(jnp.maximum, group) for group in top]
    w = [[jnp.exp(x - t) for x in group] for group, t in zip(s, top)]
    total = [sum(jnp.sum(x, axis=1, keepdims=True) for x in group) for group in w]
    part = [
        sum(
            jnp.dot(x.astype(BF16), vs, preferred_element_type=F32)
            for x, (ks, vs, bias) in zip(ws, group)
        )
        for ws, group in zip(w, sets)
    ]
    return part, top, total


def far_kernel(n, cap, per, heads, span, arrive_ref, place_ref, q_ref, *refs):
    half, plane = n // 2, n // 4
    first, second = refs[:plane], (refs[plane:half], refs[half : half + plane])
    out_ref, held, keys, vals, glob, ends, stat, pieces = refs[half + plane + 1 :]
    me = lax.axis_index("seq")
    d = lax.bitwise_xor(me, half)
    diagonal = eye()
    stat[...] = jnp.zeros_like(stat)
    size = cap * BLOCK
    sources = [((ref, 0), (ref, size)) for ref in first]
    sources += [((x, 0), (y, 0)) for x, y in zip(*second)]
    biases = choose(n, cap, per, span, arrive_ref, d, sources, held, keys, vals)
    glob_bias = widen(shared_blocks(n, per, place_ref, *second, size, glob, ends))
    inside = lax.bitwise_and(me, half - 1)
    end_bias = [jnp.where(inside == x, 0.0, NONE) for x in (0, half - 1)]
    low, high = span
    count = high - low
    for pairs in batches(span, heads, 3):
        sets = []
        for i, h in pairs:
            cols = cols_of(h)
            group = [
                (keys[picked_of(i), cols], vals[picked_of(i), cols], widen(biases[i])),
                (glob[: G * BLOCK, cols], glob[G * BLOCK :, cols], glob_bias),
            ]
            for e, edge in enumerate((0, per - 1)):
                if i == edge:
                    at = e * 2 * BLOCK
                    group.append(
                        (ends[at : at + BLOCK, cols], ends[at + BLOCK : at + 2 * BLOCK, cols],
                         end_bias[e])
                    )
            sets.append(group)
        part, top, total = attend([q_ref[rows_of(i), cols_of(h)] for i, h in pairs], sets)
        for x, t, (i, h) in zip(part, total, pairs):
            out_ref[rows_of(i - low), cols_of(h)] = (x / t).astype(BF16)
        for c, columns in enumerate((top, total)):
            for x, (i, h) in zip(flatten(columns, diagonal), pairs):
                stat[i - low : i - low + 1, pl.ds(h * DH + c * BLOCK, BLOCK)] = x
    rest = stat[...]
    pieces[...] = jnp.zeros_like(pieces)
    for p in range(PIECES):
        piece = rest.astype(BF16).astype(F32)
        rest = rest - piece
        pieces[p * count : (p + 1) * count] = piece[:count]
    out_ref[pl.ds(count * BLOCK, pieces.shape[0])] = pieces[...].astype(BF16)


def stat_rows(per):
    return -(-per // 8) * 8


def piece_rows(per):
    return -(-PIECES * per // 16) * 16


def scratches(n, cap, per, columns):
    return (
        [pltpu.VMEM((n // 2, 2 * cap * BLOCK, columns), BF16)]
        + [pltpu.VMEM((per * R * BLOCK, columns), BF16)] * 2
        + [pltpu.VMEM((2 * G * BLOCK, columns), BF16), pltpu.VMEM((4 * BLOCK, columns), BF16)]
    )


def far_part(n, cap, per, span, arrive, places, q, got, earlier):
    columns = q.shape[1]
    count = span[1] - span[0]
    heads = columns // DH
    return pl.pallas_call(
        functools.partial(far_kernel, n, cap, per, heads, span),
        out_shape=jax.ShapeDtypeStruct((count * BLOCK + piece_rows(count), columns), BF16),
        in_specs=[spec(SMEM)] * 2 + [spec()] * (1 + len(got)) + [spec(pl.ANY)],
        out_specs=spec(),
        scratch_shapes=scratches(n, cap, per, columns)
        + [pltpu.VMEM((stat_rows(count), columns), F32)]
        + [pltpu.VMEM((piece_rows(count), columns), F32)],
        compiler_params=params(16),
        cost_estimate=HEAVY,
        name="far_part",
    )(arrive, places, q, *got, earlier)


def store_part(heads, pairs, part, top, total, part_ref, stat_ref, diagonal):
    for x, (i, h) in zip(part, pairs):
        part_ref[rows_of(i), cols_of(h)] = x
    for c, columns in enumerate((top, total)):
        for x, (i, h) in zip(flatten(columns, diagonal), pairs):
            stat_ref[i : i + 1, pl.ds(h * DH + c * BLOCK, BLOCK)] = x


def near_kernel(n, cap, per, heads, place_ref, q_ref, k_ref, v_ref, *refs):
    half, plane = n // 2, n // 4
    second = refs[:plane], refs[plane:half]
    part_ref, stat_ref, glob, ends, keys, vals = refs[half + 1 :]
    me = lax.axis_index("seq")
    rows = per * BLOCK
    diagonal = eye()
    stat_ref[...] = jnp.zeros_like(stat_ref)
    size = cap * BLOCK
    glob_bias = widen(shared_blocks(n, per, place_ref, *second, size, glob, ends))
    keys[:BLOCK] = ends[:BLOCK]
    vals[:BLOCK] = ends[BLOCK : 2 * BLOCK]
    keys[pl.ds(BLOCK, rows)] = k_ref[...]
    vals[pl.ds(BLOCK, rows)] = v_ref[...]
    keys[pl.ds(BLOCK + rows, BLOCK)] = ends[2 * BLOCK : 3 * BLOCK]
    vals[pl.ds(BLOCK + rows, BLOCK)] = ends[3 * BLOCK :]
    inside = lax.bitwise_and(me, half - 1)
    first_bias, last_bias = [jnp.where(inside == x, NONE, 0.0) for x in (0, half - 1)]
    for pairs in batches((0, per), heads, 2):
        sets = []
        for i, h in pairs:
            window, cols = pl.ds(i * BLOCK, 3 * BLOCK), cols_of(h)
            bias = None
            if i in (0, per - 1):
                bias = widen([first_bias if i == 0 else 0.0, 0.0, last_bias if i else 0.0])
            sets.append(
                [
                    (keys[window, cols], vals[window, cols], bias),
                    (glob[: G * BLOCK, cols], glob[G * BLOCK :, cols], glob_bias),
                ]
            )
        parts = attend([q_ref[rows_of(i), cols_of(h)] for i, h in pairs], sets)
        store_part(heads, pairs, *parts, part_ref, stat_ref, diagonal)


def part_shapes(per, columns):
    return (
        jax.ShapeDtypeStruct((per * BLOCK, columns), F32),
        jax.ShapeDtypeStruct((stat_rows(per), columns), F32),
    )


def near_part(n, cap, per, places, q, k, v, shared, earlier):
    rows, columns = q.shape
    heads = columns // DH
    return pl.pallas_call(
        functools.partial(near_kernel, n, cap, per, heads),
        out_shape=part_shapes(per, columns),
        in_specs=[spec(SMEM)] + [spec()] * (3 + len(shared)) + [spec(pl.ANY)],
        out_specs=(spec(), spec()),
        scratch_shapes=scratches(n, cap, per, columns)[3:]
        + [pltpu.VMEM((rows + 2 * BLOCK, columns), BF16)] * 2,
        compiler_params=params(16),
        cost_estimate=LIGHT,
        name="near_part",
    )(places, q, k, v, *shared, earlier)


def rand_kernel(n, cap, per, heads, arrive_ref, q_ref, *refs):
    plane = n // 4
    part_ref, stat_ref, held, keys, vals = refs[plane:]
    diagonal = eye()
    stat_ref[...] = jnp.zeros_like(stat_ref)
    me = lax.axis_index("seq")
    size = cap * BLOCK
    sources = [
        ((ref, 2 * side * size), (ref, (2 * side + 1) * size))
        for side in range(2)
        for ref in refs[:plane]
    ]
    biases = choose(n, cap, per, (0, per), arrive_ref, me, sources, held, keys, vals)
    for pairs in batches((0, per), heads, 4):
        sets = [
            [(keys[picked_of(i), cols_of(h)], vals[picked_of(i), cols_of(h)], widen(biases[i]))]
            for i, h in pairs
        ]
        parts = attend([q_ref[rows_of(i), cols_of(h)] for i, h in pairs], sets)
        store_part(heads, pairs, *parts, part_ref, stat_ref, diagonal)


def rand_part(n, cap, per, arrive, q, got):
    columns = q.shape[1]
    return pl.pallas_call(
        functools.partial(rand_kernel, n, cap, per, columns // DH),
        out_shape=part_shapes(per, columns),
        in_specs=[spec(SMEM), spec()] + [spec()] * len(got),
        out_specs=(spec(), spec()),
        scratch_shapes=scratches(n, cap, per, columns)[:3],
        compiler_params=params(16),
        cost_estimate=HEAVY,
        name="rand_part",
    )(arrive, q, *got)


def context_kernel(
    span, heads, near_ref, near_stat_ref, rand_ref, rand_stat_ref, far_ref, out_ref, pieces
):
    low, high = span
    count = high - low
    pieces[...] = far_ref[pl.ds(count * BLOCK, pieces.shape[0])].astype(F32)
    far = sum(pieces[p * count : (p + 1) * count] for p in range(PIECES))
    stats = (near_stat_ref[low:high], rand_stat_ref[low:high], far)
    weights = []
    for h in range(heads):
        tops = [x[:, h * DH : h * DH + BLOCK] for x in stats]
        sums = [x[:, h * DH + BLOCK : (h + 1) * DH] for x in stats]
        top = functools.reduce(jnp.maximum, tops)
        w = [jnp.exp(x - top) for x in tops]
        total = sum(x * y for x, y in zip(w, sums))
        w[2] = w[2] * sums[2]
        weights.append([jnp.transpose(x / total) for x in w])
    for i in range(count):
        for h, ws in enumerate(weights):
            rows, here, cols = rows_of(low + i), rows_of(i), cols_of(h)
            parts = (near_ref[rows, cols], rand_ref[rows, cols], far_ref[here, cols].astype(F32))
            out_ref[here, cols] = sum(x * w[:, i : i + 1] for x, w in zip(parts, ws)).astype(BF16)


def contexts(span, near, near_stat, rand, rand_stat, far):
    columns = near.shape[1]
    count = span[1] - span[0]
    return pl.pallas_call(
        functools.partial(context_kernel, span, columns // DH),
        out_shape=jax.ShapeDtypeStruct((count * BLOCK, columns), BF16),
        in_specs=[spec()] * 5,
        out_specs=spec(),
        scratch_shapes=[pltpu.VMEM((piece_rows(count), columns), F32)],
        compiler_params=params(8),
        cost_estimate=LIGHT,
        name="contexts",
    )(near, near_stat, rand, rand_stat, far)


def project_kernel(span, count, steps, *refs):
    parts, w_ref, (out_ref, joined, product, sems) = refs[:count], refs[count], refs[-4:]
    me = lax.axis_index("head")
    columns = parts[0].shape[1]
    for step, rows_ref in enumerate(parts):
        owner = lax.rem(me + step, count)
        for h in range(count):
            @pl.when(owner == h)
            def _(h=h, rows_ref=rows_ref):
                joined[:, pl.ds(h * columns, columns)] = rows_ref[...]
    size = joined.shape[0] // steps
    copies = []
    for step in range(steps):
        rows = pl.ds(step * size, size)
        product[rows] = jnp.dot(
            joined[rows], w_ref[...], preferred_element_type=F32
        ).astype(BF16)
        target = out_ref.at[pl.ds(span[0] * BLOCK + step * size, size)]
        copies.append(pltpu.make_async_copy(product.at[rows], target, sems.at[step]))
        copies[-1].start()
    for copy in copies:
        copy.wait()


def project(span, tokens, parts, w_out, done=None):
    rows = parts[0].shape[0]
    wide = w_out.shape[1]
    steps = 4
    before = [] if done is None else [done]
    return pl.pallas_call(
        functools.partial(project_kernel, span, len(parts), steps),
        out_shape=jax.ShapeDtypeStruct((tokens, wide), BF16),
        in_specs=[spec()] * (len(parts) + 1) + [spec(pl.ANY)] * len(before),
        out_specs=spec(pl.ANY),
        scratch_shapes=[
            pltpu.VMEM((rows, w_out.shape[0]), BF16),
            pltpu.VMEM((rows, wide), BF16),
            pltpu.SemaphoreType.DMA((steps,)),
        ],
        input_output_aliases={len(parts) + 1: 0} if before else {},
        compiler_params=params(16),
        cost_estimate=LIGHT,
        name="project",
    )(*parts, w_out, *before)


def on_device(queries, keys, values, rand_group, rand_offset, glob_blocks, w_out):
    tokens_dev = queries.shape[0]
    per = tokens_dev // BLOCK
    n = lax.axis_size("seq")
    heads = lax.axis_size("head")
    cap = max(2, (rand_group.shape[0] // n * R + n - 1) // n)

    mates = [(i, i ^ (n // 4)) for i in range(n)]
    partners = [(i, i ^ (n // 2)) for i in range(n)]
    mate_k = lax.ppermute(keys, "seq", mates)
    mate_v = lax.ppermute(values, "seq", mates)
    spots, arrive = ranks(n, per, cap, rand_group.T, rand_offset.T)
    rows = {(0, 0): keys, (0, 1): values}
    lists = ((0, True, (0, 1)),)
    first = exchange(gather(n, per, cap, lists, spots, rows), n)
    later_q = lax.optimization_barrier((queries, first[1]))[0]
    far_q = lax.ppermute(later_q, "seq", partners)
    rows = {(0, 0): keys, (1, 0): mate_k}
    lists = ((1, True, (0,)),)
    second_k = exchange(gather(n, per, cap, lists, spots, rows, [glob_blocks], first[1:4]), n)
    rows = {(0, 1): values, (1, 1): mate_v}
    lists = ((1, True, (1,)),)
    sent = gather(n, per, cap, lists, spots, rows, [glob_blocks], second_k[1:2])
    second = second_k + exchange(sent, n)
    rows = {(0, 0): keys, (0, 1): values, (1, 0): mate_k, (1, 1): mate_v}
    lists = ((0, False, (0, 1)), (1, False, (0, 1)))
    third = gather(n, per, cap, lists, spots, rows, (), sent[:1])
    middle = (per + 1) // 2
    spans = ((0, middle), (middle, per))
    fars = []
    earlier = third[0]
    for span in spans:
        earlier = far_part(
            n, cap, per, span, arrive, glob_blocks, far_q, first + second, earlier
        )
        fars.append(lax.ppermute(earlier, "seq", partners))
    third = exchange(third, n)
    near, near_stat = near_part(n, cap, per, glob_blocks, queries, keys, values, second, earlier)
    rand, rand_stat = rand_part(n, cap, per, arrive, queries, third)
    out = None
    for span, far in zip(spans, fars):
        context = contexts(span, near, near_stat, rand, rand_stat, far)
        others = [
            lax.ppermute(context, "head", [((i + s) % heads, i) for i in range(heads)])
            for s in range(1, heads)
        ]
        out = project(span, tokens_dev, [context] + others, w_out, out)
    return out


def solution(mesh):
    return jax.shard_map(
        on_device,
        mesh=mesh,
        in_specs=(
            P("seq", "head"),
            P("seq", "head"),
            P("seq", "head"),
            P(),
            P(),
            P(),
            P(None, "head"),
        ),
        out_specs=P("seq", "head"),
        check_vma=False,
    )
```

```python
import functools
import math

import jax
import jax.numpy as jnp
from jax import lax
from jax.experimental import pallas as pl
from jax.experimental.pallas import tpu as pltpu
from jax.sharding import PartitionSpec as P

DH = 128
BLOCK = 64
R = 3
G = 2
VMEM = pltpu.MemorySpace.VMEM
SMEM = pltpu.MemorySpace.SMEM
BF16 = jnp.bfloat16
F32 = jnp.float32
I32 = jnp.int32
NONE = -1e30
PIECES = 3


def params(mib):
    return pltpu.CompilerParams(vmem_limit_bytes=mib * 1024 * 1024)


LIGHT = pl.CostEstimate(flops=1, bytes_accessed=1, transcendentals=0)
HEAVY = pl.CostEstimate(flops=4 * 10**9, bytes_accessed=1, transcendentals=0)


def spec(space=VMEM):
    return pl.BlockSpec(memory_space=space)


def rank_kernel(n, per, cap, g_ref, o_ref, spot_ref, arrive_ref, g_pad, o_pad):
    me = lax.axis_index("seq")
    nb = g_ref.shape[1]
    wide = g_pad.shape[1]
    tall = spot_ref.shape[0]
    g_pad[...] = jnp.full(g_pad.shape, -1, I32)
    o_pad[...] = jnp.zeros(o_pad.shape, I32)
    g_pad[:R, :nb] = g_ref[...]
    o_pad[:R, :nb] = o_ref[...]
    g = g_pad[...]
    lane = lax.broadcasted_iota(I32, g.shape, 1)
    place = lane
    for d in range(1, n):
        place = jnp.where(lane >= d * per, lane - d * per, place)
    rank = jnp.zeros(g.shape, I32)
    for s in range(1, per):
        back = pltpu.roll(g, s, axis=1)
        ahead = place >= s
        for r in range(R):
            same = jnp.broadcast_to(back[r : r + 1, :], g.shape) == g
            rank = rank + jnp.where(ahead & same, 1, 0)
    arrive_ref[...] = g * cap + rank
    row = lax.broadcasted_iota(I32, (tall, wide), 0)
    spots = jnp.zeros((tall, wide), F32)
    for side in range(2):
        named = jnp.where(g == lax.bitwise_xor(me, side * (n // 4)), o_pad[...], 0)
        for s in range(cap):
            picked = jnp.where(rank == s, named, 0).astype(F32)
            total = jnp.sum(picked, axis=0, keepdims=True)
            here = row == side * cap + s
            spots = spots + jnp.where(here, jnp.broadcast_to(total, (tall, wide)), 0.0)
    token = lax.broadcasted_iota(I32, (wide, 128), 0)
    first = lax.broadcasted_iota(I32, (wide, 128), 1) * per
    belongs = jnp.where((token >= first) & (token < first + per), 1.0, 0.0)
    spot_ref[...] = jnp.dot(
        spots.astype(BF16), belongs.astype(BF16), preferred_element_type=F32
    ).astype(I32)


def ranks(n, per, cap, groups, offsets):
    nb = groups.shape[1]
    wide = -(-nb // 128) * 128
    tall = -(-2 * cap // 8) * 8
    return pl.pallas_call(
        functools.partial(rank_kernel, n, per, cap),
        out_shape=(
            jax.ShapeDtypeStruct((tall, 128), I32),
            jax.ShapeDtypeStruct((8, wide), I32),
        ),
        in_specs=[spec(), spec()],
        out_specs=(spec(), spec()),
        scratch_shapes=[pltpu.VMEM((8, wide), I32), pltpu.VMEM((8, wide), I32)],
        compiler_params=params(4),
        cost_estimate=LIGHT,
        name="ranks",
    )(groups, offsets)


def gather_kernel(n, per, cap, lists, shared, names, spot_ref, *refs):
    plane = n // 4
    me = lax.axis_index("seq")
    sources, outs = dict(zip(names, refs)), refs[-plane:]
    for k, out_ref in enumerate(outs):
        at = 0
        for side, far, parts in lists:
            d = lax.bitwise_xor(me, k + (n // 2 if far else 0))
            for c in parts:
                for s in range(cap):
                    start = spot_ref[side * cap + s, d] * BLOCK
                    rows = pl.ds(pl.multiple_of(start, BLOCK), BLOCK)
                    out_ref[pl.ds(at, BLOCK)] = sources[side, c][rows]
                    at += BLOCK
        if shared:
            (c,) = lists[0][2]
            place_ref = refs[len(names)]
            shared_rows(n, per, k, at, place_ref, sources[0, c], sources[1, c], out_ref)


def shared_rows(n, per, k, at, place_ref, own_ref, mate_ref, out_ref):
    plane = n // 4
    me = lax.axis_index("seq")
    for g in range(G):
        owner = lax.div(place_ref[g], per)
        start = pl.multiple_of((place_ref[g] - owner * per) * BLOCK, BLOCK)
        rows = pl.ds(start, BLOCK)
        mine = lax.bitwise_and(lax.bitwise_xor(owner, me), plane) == 0
        out_ref[pl.ds(at + g * BLOCK, BLOCK)] = jnp.where(mine, own_ref[rows], mate_ref[rows])
    place = lax.bitwise_and(me, plane - 1)
    target = lax.bitwise_xor(place, k)
    is_before = lax.rem(place + 1, plane) == target
    is_end = jnp.where(is_before, target == 0, target == plane - 1)
    rows = pl.ds(pl.multiple_of(jnp.where(is_before, (per - 1) * BLOCK, 0), BLOCK), BLOCK)
    out_ref[pl.ds(at + G * BLOCK, BLOCK)] = jnp.where(is_end, mate_ref[rows], own_ref[rows])


def gather(n, per, cap, lists, spots, sources, shared=(), earlier=()):
    plane = n // 4
    names, arrays = tuple(sources), list(sources.values())
    rows = sum(len(parts) for _, _, parts in lists) * cap * BLOCK
    rows += (G + 1) * BLOCK if shared else 0
    out = jax.ShapeDtypeStruct((rows, arrays[0].shape[1]), BF16)
    return pl.pallas_call(
        functools.partial(gather_kernel, n, per, cap, lists, bool(shared), names),
        out_shape=(out,) * plane,
        in_specs=[spec(SMEM)]
        + [spec()] * len(arrays)
        + [spec(SMEM)] * len(shared)
        + [spec(pl.ANY)] * len(earlier),
        out_specs=(spec(),) * plane,
        compiler_params=params(8),
        cost_estimate=LIGHT,
        name="gather_blocks",
    )(spots, *arrays, *shared, *earlier)


def exchange(parts, n):
    got = [parts[0]]
    for k in range(1, n // 4):
        got.append(lax.ppermute(parts[k], "seq", [(i, i ^ k) for i in range(n)]))
    return got


def choose(n, cap, per, span, arrive_ref, d, sources, held, keys, vals):
    half = n // 2
    me = lax.axis_index("seq")
    for k, pair in enumerate(sources):
        for c, (ref, row) in enumerate(pair):
            held[k, pl.ds(c * cap * BLOCK, cap * BLOCK)] = ref[pl.ds(row, cap * BLOCK)]
    biases = {}
    for i in range(*span):
        row = []
        for r in range(R):
            spot = arrive_ref[r, d * per + i]
            group = lax.div(spot, cap)
            differ = lax.bitwise_xor(group, me)
            here = differ < half
            slot = jnp.where(here, spot - group * cap, 0)
            k = jnp.where(here, differ, 0)
            at = pl.ds((i * R + r) * BLOCK, BLOCK)
            keys[at] = held[k, pl.ds(pl.multiple_of(slot * BLOCK, BLOCK), BLOCK), :]
            vals[at] = held[k, pl.ds(pl.multiple_of((cap + slot) * BLOCK, BLOCK), BLOCK), :]
            row.append(jnp.where(here, 0.0, NONE))
        biases[i] = row
    return biases


def shared_blocks(n, per, place_ref, key_refs, val_refs, skip, glob, ends):
    plane = n // 4
    me = lax.axis_index("seq")
    place = lax.bitwise_and(me, plane - 1)
    biases = []
    for g in range(G):
        differ = lax.bitwise_xor(lax.div(place_ref[g], per), me)
        for p, pair in enumerate(zip(key_refs, val_refs)):
            @pl.when(lax.bitwise_and(differ, plane - 1) == p)
            def _(g=g, pair=pair):
                for c, ref in enumerate(pair):
                    at = pl.ds((c * G + g) * BLOCK, BLOCK)
                    glob[at] = ref[pl.ds(skip + g * BLOCK, BLOCK)]
        biases.append(jnp.where(differ < n // 2, 0.0, NONE))
    for e, neighbour in enumerate((place + plane - 1, place + 1)):
        k = lax.bitwise_xor(place, lax.bitwise_and(neighbour, plane - 1))
        for p, pair in enumerate(zip(key_refs, val_refs)):
            @pl.when(k == p)
            def _(e=e, pair=pair):
                for c, ref in enumerate(pair):
                    at = pl.ds((2 * e + c) * BLOCK, BLOCK)
                    ends[at] = ref[pl.ds(skip + G * BLOCK, BLOCK)]
    return biases


def widen(biases):
    count = len(biases)
    lane = lax.broadcasted_iota(I32, (1, count * BLOCK), 1)
    bias = jnp.full((1, count * BLOCK), biases[-1], F32)
    for r in reversed(range(count - 1)):
        bias = jnp.where(lane < (r + 1) * BLOCK, biases[r], bias)
    return bias


def batches(span, heads, step):
    for first in range(*span, step):
        yield [(i, h) for i in range(first, min(span[1], first + step)) for h in range(heads)]


def rows_of(i):
    return pl.ds(i * BLOCK, BLOCK)


def picked_of(i):
    return pl.ds(i * R * BLOCK, R * BLOCK)


def cols_of(h):
    return pl.ds(h * DH, DH)


def dot_t(a, b):
    return lax.dot_general(a, b, (((1,), (1,)), ((), ())), preferred_element_type=F32)


def eye():
    shape = (BLOCK, BLOCK)
    return lax.broadcasted_iota(I32, shape, 0) == lax.broadcasted_iota(I32, shape, 1)


def flatten(columns, diagonal):
    return [jnp.sum(jnp.where(diagonal, x, 0.0), axis=0, keepdims=True) for x in columns]


def attend(queries, sets):
    scale = 1.0 / math.sqrt(DH)
    s = [
        [dot_t(q, ks) * scale + bias if bias is not None else dot_t(q, ks) * scale
         for ks, vs, bias in group]
        for q, group in zip(queries, sets)
    ]
    top = [[jnp.max(x, axis=1, keepdims=True) for x in group] for group in s]
    top = [functools.reduce(jnp.maximum, group) for group in top]
    w = [[jnp.exp(x - t) for x in group] for group, t in zip(s, top)]
    total = [sum(jnp.sum(x, axis=1, keepdims=True) for x in group) for group in w]
    part = [
        sum(
            jnp.dot(x.astype(BF16), vs, preferred_element_type=F32)
            for x, (ks, vs, bias) in zip(ws, group)
        )
        for ws, group in zip(w, sets)
    ]
    return part, top, total


def far_kernel(n, cap, per, heads, span, arrive_ref, place_ref, q_ref, *refs):
    half, plane = n // 2, n // 4
    first, second = refs[:plane], (refs[plane:half], refs[half : half + plane])
    out_ref, held, keys, vals, glob, ends, stat, pieces = refs[half + plane + 1 :]
    me = lax.axis_index("seq")
    d = lax.bitwise_xor(me, half)
    diagonal = eye()
    stat[...] = jnp.zeros_like(stat)
    size = cap * BLOCK
    sources = [((ref, 0), (ref, size)) for ref in first]
    sources += [((x, 0), (y, 0)) for x, y in zip(*second)]
    biases = choose(n, cap, per, span, arrive_ref, d, sources, held, keys, vals)
    glob_bias = widen(shared_blocks(n, per, place_ref, *second, size, glob, ends))
    inside = lax.bitwise_and(me, half - 1)
    end_bias = [jnp.where(inside == x, 0.0, NONE) for x in (0, half - 1)]
    low, high = span
    count = high - low
    for pairs in batches(span, heads, 3):
        sets = []
        for i, h in pairs:
            cols = cols_of(h)
            group = [
                (keys[picked_of(i), cols], vals[picked_of(i), cols], widen(biases[i])),
                (glob[: G * BLOCK, cols], glob[G * BLOCK :, cols], glob_bias),
            ]
            for e, edge in enumerate((0, per - 1)):
                if i == edge:
                    at = e * 2 * BLOCK
                    group.append(
                        (ends[at : at + BLOCK, cols], ends[at + BLOCK : at + 2 * BLOCK, cols],
                         end_bias[e])
                    )
            sets.append(group)
        part, top, total = attend([q_ref[rows_of(i), cols_of(h)] for i, h in pairs], sets)
        for x, t, (i, h) in zip(part, total, pairs):
            out_ref[rows_of(i - low), cols_of(h)] = (x / t).astype(BF16)
        for c, columns in enumerate((top, total)):
            for x, (i, h) in zip(flatten(columns, diagonal), pairs):
                stat[i - low : i - low + 1, pl.ds(h * DH + c * BLOCK, BLOCK)] = x
    rest = stat[...]
    pieces[...] = jnp.zeros_like(pieces)
    for p in range(PIECES):
        piece = rest.astype(BF16).astype(F32)
        rest = rest - piece
        pieces[p * count : (p + 1) * count] = piece[:count]
    out_ref[pl.ds(count * BLOCK, pieces.shape[0])] = pieces[...].astype(BF16)


def stat_rows(per):
    return -(-per // 8) * 8


def piece_rows(per):
    return -(-PIECES * per // 16) * 16


def scratches(n, cap, per, columns):
    return (
        [pltpu.VMEM((n // 2, 2 * cap * BLOCK, columns), BF16)]
        + [pltpu.VMEM((per * R * BLOCK, columns), BF16)] * 2
        + [pltpu.VMEM((2 * G * BLOCK, columns), BF16), pltpu.VMEM((4 * BLOCK, columns), BF16)]
    )


def far_part(n, cap, per, span, arrive, places, q, got, earlier):
    columns = q.shape[1]
    count = span[1] - span[0]
    heads = columns // DH
    return pl.pallas_call(
        functools.partial(far_kernel, n, cap, per, heads, span),
        out_shape=jax.ShapeDtypeStruct((count * BLOCK + piece_rows(count), columns), BF16),
        in_specs=[spec(SMEM)] * 2 + [spec()] * (1 + len(got)) + [spec(pl.ANY)],
        out_specs=spec(),
        scratch_shapes=scratches(n, cap, per, columns)
        + [pltpu.VMEM((stat_rows(count), columns), F32)]
        + [pltpu.VMEM((piece_rows(count), columns), F32)],
        compiler_params=params(16),
        cost_estimate=HEAVY,
        name="far_part",
    )(arrive, places, q, *got, earlier)


def store_part(heads, pairs, part, top, total, part_ref, stat_ref, diagonal):
    for x, (i, h) in zip(part, pairs):
        part_ref[rows_of(i), cols_of(h)] = x
    for c, columns in enumerate((top, total)):
        for x, (i, h) in zip(flatten(columns, diagonal), pairs):
            stat_ref[i : i + 1, pl.ds(h * DH + c * BLOCK, BLOCK)] = x


def near_kernel(n, cap, per, heads, place_ref, q_ref, k_ref, v_ref, *refs):
    half, plane = n // 2, n // 4
    second = refs[:plane], refs[plane:half]
    part_ref, stat_ref, glob, ends, keys, vals = refs[half + 1 :]
    me = lax.axis_index("seq")
    rows = per * BLOCK
    diagonal = eye()
    stat_ref[...] = jnp.zeros_like(stat_ref)
    size = cap * BLOCK
    glob_bias = widen(shared_blocks(n, per, place_ref, *second, size, glob, ends))
    keys[:BLOCK] = ends[:BLOCK]
    vals[:BLOCK] = ends[BLOCK : 2 * BLOCK]
    keys[pl.ds(BLOCK, rows)] = k_ref[...]
    vals[pl.ds(BLOCK, rows)] = v_ref[...]
    keys[pl.ds(BLOCK + rows, BLOCK)] = ends[2 * BLOCK : 3 * BLOCK]
    vals[pl.ds(BLOCK + rows, BLOCK)] = ends[3 * BLOCK :]
    inside = lax.bitwise_and(me, half - 1)
    first_bias, last_bias = [jnp.where(inside == x, NONE, 0.0) for x in (0, half - 1)]
    for pairs in batches((0, per), heads, 2):
        sets = []
        for i, h in pairs:
            window, cols = pl.ds(i * BLOCK, 3 * BLOCK), cols_of(h)
            bias = None
            if i in (0, per - 1):
                bias = widen([first_bias if i == 0 else 0.0, 0.0, last_bias if i else 0.0])
            sets.append(
                [
                    (keys[window, cols], vals[window, cols], bias),
                    (glob[: G * BLOCK, cols], glob[G * BLOCK :, cols], glob_bias),
                ]
            )
        parts = attend([q_ref[rows_of(i), cols_of(h)] for i, h in pairs], sets)
        store_part(heads, pairs, *parts, part_ref, stat_ref, diagonal)


def part_shapes(per, columns):
    return (
        jax.ShapeDtypeStruct((per * BLOCK, columns), F32),
        jax.ShapeDtypeStruct((stat_rows(per), columns), F32),
    )


def near_part(n, cap, per, places, q, k, v, shared, earlier):
    rows, columns = q.shape
    heads = columns // DH
    return pl.pallas_call(
        functools.partial(near_kernel, n, cap, per, heads),
        out_shape=part_shapes(per, columns),
        in_specs=[spec(SMEM)] + [spec()] * (3 + len(shared)) + [spec(pl.ANY)],
        out_specs=(spec(), spec()),
        scratch_shapes=scratches(n, cap, per, columns)[3:]
        + [pltpu.VMEM((rows + 2 * BLOCK, columns), BF16)] * 2,
        compiler_params=params(16),
        cost_estimate=LIGHT,
        name="near_part",
    )(places, q, k, v, *shared, earlier)


def rand_kernel(n, cap, per, heads, arrive_ref, q_ref, *refs):
    plane = n // 4
    part_ref, stat_ref, held, keys, vals = refs[plane:]
    diagonal = eye()
    stat_ref[...] = jnp.zeros_like(stat_ref)
    me = lax.axis_index("seq")
    size = cap * BLOCK
    sources = [
        ((ref, 2 * side * size), (ref, (2 * side + 1) * size))
        for side in range(2)
        for ref in refs[:plane]
    ]
    biases = choose(n, cap, per, (0, per), arrive_ref, me, sources, held, keys, vals)
    for pairs in batches((0, per), heads, 4):
        sets = [
            [(keys[picked_of(i), cols_of(h)], vals[picked_of(i), cols_of(h)], widen(biases[i]))]
            for i, h in pairs
        ]
        parts = attend([q_ref[rows_of(i), cols_of(h)] for i, h in pairs], sets)
        store_part(heads, pairs, *parts, part_ref, stat_ref, diagonal)


def rand_part(n, cap, per, arrive, q, got):
    columns = q.shape[1]
    return pl.pallas_call(
        functools.partial(rand_kernel, n, cap, per, columns // DH),
        out_shape=part_shapes(per, columns),
        in_specs=[spec(SMEM), spec()] + [spec()] * len(got),
        out_specs=(spec(), spec()),
        scratch_shapes=scratches(n, cap, per, columns)[:3],
        compiler_params=params(16),
        cost_estimate=HEAVY,
        name="rand_part",
    )(arrive, q, *got)


def context_kernel(
    span, heads, near_ref, near_stat_ref, rand_ref, rand_stat_ref, far_ref, out_ref, pieces
):
    low, high = span
    count = high - low
    pieces[...] = far_ref[pl.ds(count * BLOCK, pieces.shape[0])].astype(F32)
    far = sum(pieces[p * count : (p + 1) * count] for p in range(PIECES))
    stats = (near_stat_ref[low:high], rand_stat_ref[low:high], far)
    weights = []
    for h in range(heads):
        tops = [x[:, h * DH : h * DH + BLOCK] for x in stats]
        sums = [x[:, h * DH + BLOCK : (h + 1) * DH] for x in stats]
        top = functools.reduce(jnp.maximum, tops)
        w = [jnp.exp(x - top) for x in tops]
        total = sum(x * y for x, y in zip(w, sums))
        w[2] = w[2] * sums[2]
        weights.append([jnp.transpose(x / total) for x in w])
    for i in range(count):
        for h, ws in enumerate(weights):
            rows, here, cols = rows_of(low + i), rows_of(i), cols_of(h)
            parts = (near_ref[rows, cols], rand_ref[rows, cols], far_ref[here, cols].astype(F32))
            out_ref[here, cols] = sum(x * w[:, i : i + 1] for x, w in zip(parts, ws)).astype(BF16)


def contexts(span, near, near_stat, rand, rand_stat, far):
    columns = near.shape[1]
    count = span[1] - span[0]
    return pl.pallas_call(
        functools.partial(context_kernel, span, columns // DH),
        out_shape=jax.ShapeDtypeStruct((count * BLOCK, columns), BF16),
        in_specs=[spec()] * 5,
        out_specs=spec(),
        scratch_shapes=[pltpu.VMEM((piece_rows(count), columns), F32)],
        compiler_params=params(8),
        cost_estimate=LIGHT,
        name="contexts",
    )(near, near_stat, rand, rand_stat, far)


def project_kernel(span, count, steps, *refs):
    parts, w_ref, (out_ref, joined, product, sems) = refs[:count], refs[count], refs[-4:]
    me = lax.axis_index("head")
    columns = parts[0].shape[1]
    for step, rows_ref in enumerate(parts):
        owner = lax.rem(me + step, count)
        for h in range(count):
            @pl.when(owner == h)
            def _(h=h, rows_ref=rows_ref):
                joined[:, pl.ds(h * columns, columns)] = rows_ref[...]
    size = joined.shape[0] // steps
    copies = []
    for step in range(steps):
        rows = pl.ds(step * size, size)
        product[rows] = jnp.dot(
            joined[rows], w_ref[...], preferred_element_type=F32
        ).astype(BF16)
        target = out_ref.at[pl.ds(span[0] * BLOCK + step * size, size)]
        copies.append(pltpu.make_async_copy(product.at[rows], target, sems.at[step]))
        copies[-1].start()
    for copy in copies:
        copy.wait()


def project(span, tokens, parts, w_out, done=None):
    rows = parts[0].shape[0]
    wide = w_out.shape[1]
    steps = 4
    before = [] if done is None else [done]
    return pl.pallas_call(
        functools.partial(project_kernel, span, len(parts), steps),
        out_shape=jax.ShapeDtypeStruct((tokens, wide), BF16),
        in_specs=[spec()] * (len(parts) + 1) + [spec(pl.ANY)] * len(before),
        out_specs=spec(pl.ANY),
        scratch_shapes=[
            pltpu.VMEM((rows, w_out.shape[0]), BF16),
            pltpu.VMEM((rows, wide), BF16),
            pltpu.SemaphoreType.DMA((steps,)),
        ],
        input_output_aliases={len(parts) + 1: 0} if before else {},
        compiler_params=params(16),
        cost_estimate=LIGHT,
        name="project",
    )(*parts, w_out, *before)


def on_device(queries, keys, values, rand_group, rand_offset, glob_blocks, w_out):
    tokens_dev = queries.shape[0]
    per = tokens_dev // BLOCK
    n = lax.axis_size("seq")
    heads = lax.axis_size("head")
    cap = max(2, (rand_group.shape[0] // n * R + n - 1) // n)

    mates = [(i, i ^ (n // 4)) for i in range(n)]
    partners = [(i, i ^ (n // 2)) for i in range(n)]
    mate_k = lax.ppermute(keys, "seq", mates)
    mate_v = lax.ppermute(values, "seq", mates)
    spots, arrive = ranks(n, per, cap, rand_group.T, rand_offset.T)
    rows = {(0, 0): keys, (0, 1): values}
    lists = ((0, True, (0, 1)),)
    first = exchange(gather(n, per, cap, lists, spots, rows), n)
    later_q = lax.optimization_barrier((queries, *first[1:4]))[0]
    far_q = lax.ppermute(later_q, "seq", partners)
    rows = {(0, 0): keys, (1, 0): mate_k}
    lists = ((1, True, (0,)),)
    second_k = exchange(gather(n, per, cap, lists, spots, rows, [glob_blocks], first[1:4]), n)
    rows = {(0, 1): values, (1, 1): mate_v}
    lists = ((1, True, (1,)),)
    sent = gather(n, per, cap, lists, spots, rows, [glob_blocks], second_k[1:2])
    second = second_k + exchange(sent, n)
    rows = {(0, 0): keys, (0, 1): values, (1, 0): mate_k, (1, 1): mate_v}
    lists = ((0, False, (0, 1)), (1, False, (0, 1)))
    third = gather(n, per, cap, lists, spots, rows, (), sent[:1])
    middle = per * 7 // 17
    spans = ((0, middle), (middle, per))
    fars = []
    earlier = third[0]
    for span in spans:
        earlier = far_part(
            n, cap, per, span, arrive, glob_blocks, far_q, first + second, earlier
        )
        fars.append(lax.ppermute(earlier, "seq", partners))
    third = exchange(third, n)
    near, near_stat = near_part(n, cap, per, glob_blocks, queries, keys, values, second, earlier)
    rand, rand_stat = rand_part(n, cap, per, arrive, queries, third)
    out = None
    for span, far in zip(spans, fars):
        context = contexts(span, near, near_stat, rand, rand_stat, far)
        others = [
            lax.ppermute(context, "head", [((i + s) % heads, i) for i in range(heads)])
            for s in range(1, heads)
        ]
        out = project(span, tokens_dev, [context] + others, w_out, out)
    return out


def solution(mesh):
    return jax.shard_map(
        on_device,
        mesh=mesh,
        in_specs=(
            P("seq", "head"),
            P("seq", "head"),
            P("seq", "head"),
            P(),
            P(),
            P(),
            P(None, "head"),
        ),
        out_specs=P("seq", "head"),
        check_vma=False,
    )
```

```python
import functools
import math

import jax
import jax.numpy as jnp
from jax import lax
from jax.experimental import pallas as pl
from jax.experimental.pallas import tpu as pltpu
from jax.sharding import PartitionSpec as P

DH = 128
BLOCK = 64
R = 3
G = 2
VMEM = pltpu.MemorySpace.VMEM
SMEM = pltpu.MemorySpace.SMEM
BF16 = jnp.bfloat16
F32 = jnp.float32
I32 = jnp.int32
NONE = -1e30
PIECES = 3


def params(mib):
    return pltpu.CompilerParams(vmem_limit_bytes=mib * 1024 * 1024)


LIGHT = pl.CostEstimate(flops=1, bytes_accessed=1, transcendentals=0)
HEAVY = pl.CostEstimate(flops=4 * 10**9, bytes_accessed=1, transcendentals=0)


def spec(space=VMEM):
    return pl.BlockSpec(memory_space=space)


def rank_kernel(n, per, cap, g_ref, o_ref, spot_ref, arrive_ref, g_pad, o_pad):
    me = lax.axis_index("seq")
    nb = g_ref.shape[1]
    wide = g_pad.shape[1]
    tall = spot_ref.shape[0]
    g_pad[...] = jnp.full(g_pad.shape, -1, I32)
    o_pad[...] = jnp.zeros(o_pad.shape, I32)
    g_pad[:R, :nb] = g_ref[...]
    o_pad[:R, :nb] = o_ref[...]
    g = g_pad[...]
    lane = lax.broadcasted_iota(I32, g.shape, 1)
    place = lane
    for d in range(1, n):
        place = jnp.where(lane >= d * per, lane - d * per, place)
    rank = jnp.zeros(g.shape, I32)
    for s in range(1, per):
        back = pltpu.roll(g, s, axis=1)
        ahead = place >= s
        for r in range(R):
            same = jnp.broadcast_to(back[r : r + 1, :], g.shape) == g
            rank = rank + jnp.where(ahead & same, 1, 0)
    arrive_ref[...] = g * cap + rank
    row = lax.broadcasted_iota(I32, (tall, wide), 0)
    spots = jnp.zeros((tall, wide), F32)
    for side in range(2):
        named = jnp.where(g == lax.bitwise_xor(me, side * (n // 4)), o_pad[...], 0)
        for s in range(cap):
            picked = jnp.where(rank == s, named, 0).astype(F32)
            total = jnp.sum(picked, axis=0, keepdims=True)
            here = row == side * cap + s
            spots = spots + jnp.where(here, jnp.broadcast_to(total, (tall, wide)), 0.0)
    token = lax.broadcasted_iota(I32, (wide, 128), 0)
    first = lax.broadcasted_iota(I32, (wide, 128), 1) * per
    belongs = jnp.where((token >= first) & (token < first + per), 1.0, 0.0)
    spot_ref[...] = jnp.dot(
        spots.astype(BF16), belongs.astype(BF16), preferred_element_type=F32
    ).astype(I32)


def ranks(n, per, cap, groups, offsets):
    nb = groups.shape[1]
    wide = -(-nb // 128) * 128
    tall = -(-2 * cap // 8) * 8
    return pl.pallas_call(
        functools.partial(rank_kernel, n, per, cap),
        out_shape=(
            jax.ShapeDtypeStruct((tall, 128), I32),
            jax.ShapeDtypeStruct((8, wide), I32),
        ),
        in_specs=[spec(), spec()],
        out_specs=(spec(), spec()),
        scratch_shapes=[pltpu.VMEM((8, wide), I32), pltpu.VMEM((8, wide), I32)],
        compiler_params=params(4),
        cost_estimate=LIGHT,
        name="ranks",
    )(groups, offsets)


def gather_kernel(n, per, cap, lists, shared, names, spot_ref, *refs):
    plane = n // 4
    me = lax.axis_index("seq")
    sources, outs = dict(zip(names, refs)), refs[-plane:]
    for k, out_ref in enumerate(outs):
        at = 0
        for side, far, parts in lists:
            d = lax.bitwise_xor(me, k + (n // 2 if far else 0))
            for c in parts:
                for s in range(cap):
                    start = spot_ref[side * cap + s, d] * BLOCK
                    rows = pl.ds(pl.multiple_of(start, BLOCK), BLOCK)
                    out_ref[pl.ds(at, BLOCK)] = sources[side, c][rows]
                    at += BLOCK
        if shared:
            (c,) = lists[0][2]
            place_ref = refs[len(names)]
            shared_rows(n, per, k, at, place_ref, sources[0, c], sources[1, c], out_ref)


def shared_rows(n, per, k, at, place_ref, own_ref, mate_ref, out_ref):
    plane = n // 4
    me = lax.axis_index("seq")
    for g in range(G):
        owner = lax.div(place_ref[g], per)
        start = pl.multiple_of((place_ref[g] - owner * per) * BLOCK, BLOCK)
        rows = pl.ds(start, BLOCK)
        mine = lax.bitwise_and(lax.bitwise_xor(owner, me), plane) == 0
        out_ref[pl.ds(at + g * BLOCK, BLOCK)] = jnp.where(mine, own_ref[rows], mate_ref[rows])
    place = lax.bitwise_and(me, plane - 1)
    target = lax.bitwise_xor(place, k)
    is_before = lax.rem(place + 1, plane) == target
    is_end = jnp.where(is_before, target == 0, target == plane - 1)
    rows = pl.ds(pl.multiple_of(jnp.where(is_before, (per - 1) * BLOCK, 0), BLOCK), BLOCK)
    out_ref[pl.ds(at + G * BLOCK, BLOCK)] = jnp.where(is_end, mate_ref[rows], own_ref[rows])


def gather(n, per, cap, lists, spots, sources, shared=(), earlier=()):
    plane = n // 4
    names, arrays = tuple(sources), list(sources.values())
    rows = sum(len(parts) for _, _, parts in lists) * cap * BLOCK
    rows += (G + 1) * BLOCK if shared else 0
    out = jax.ShapeDtypeStruct((rows, arrays[0].shape[1]), BF16)
    return pl.pallas_call(
        functools.partial(gather_kernel, n, per, cap, lists, bool(shared), names),
        out_shape=(out,) * plane,
        in_specs=[spec(SMEM)]
        + [spec()] * len(arrays)
        + [spec(SMEM)] * len(shared)
        + [spec(pl.ANY)] * len(earlier),
        out_specs=(spec(),) * plane,
        compiler_params=params(8),
        cost_estimate=LIGHT,
        name="gather_blocks",
    )(spots, *arrays, *shared, *earlier)


def exchange(parts, n):
    got = [parts[0]]
    for k in range(1, n // 4):
        got.append(lax.ppermute(parts[k], "seq", [(i, i ^ k) for i in range(n)]))
    return got


def choose(n, cap, per, span, arrive_ref, d, sources, held, keys, vals):
    half = n // 2
    me = lax.axis_index("seq")
    for k, pair in enumerate(sources):
        for c, (ref, row) in enumerate(pair):
            held[k, pl.ds(c * cap * BLOCK, cap * BLOCK)] = ref[pl.ds(row, cap * BLOCK)]
    biases = {}
    for i in range(*span):
        row = []
        for r in range(R):
            spot = arrive_ref[r, d * per + i]
            group = lax.div(spot, cap)
            differ = lax.bitwise_xor(group, me)
            here = differ < half
            slot = jnp.where(here, spot - group * cap, 0)
            k = jnp.where(here, differ, 0)
            at = pl.ds((i * R + r) * BLOCK, BLOCK)
            keys[at] = held[k, pl.ds(pl.multiple_of(slot * BLOCK, BLOCK), BLOCK), :]
            vals[at] = held[k, pl.ds(pl.multiple_of((cap + slot) * BLOCK, BLOCK), BLOCK), :]
            row.append(jnp.where(here, 0.0, NONE))
        biases[i] = row
    return biases


def shared_blocks(n, per, place_ref, key_refs, val_refs, skip, glob, ends):
    plane = n // 4
    me = lax.axis_index("seq")
    place = lax.bitwise_and(me, plane - 1)
    biases = []
    for g in range(G):
        differ = lax.bitwise_xor(lax.div(place_ref[g], per), me)
        for p, pair in enumerate(zip(key_refs, val_refs)):
            @pl.when(lax.bitwise_and(differ, plane - 1) == p)
            def _(g=g, pair=pair):
                for c, ref in enumerate(pair):
                    at = pl.ds((c * G + g) * BLOCK, BLOCK)
                    glob[at] = ref[pl.ds(skip + g * BLOCK, BLOCK)]
        biases.append(jnp.where(differ < n // 2, 0.0, NONE))
    for e, neighbour in enumerate((place + plane - 1, place + 1)):
        k = lax.bitwise_xor(place, lax.bitwise_and(neighbour, plane - 1))
        for p, pair in enumerate(zip(key_refs, val_refs)):
            @pl.when(k == p)
            def _(e=e, pair=pair):
                for c, ref in enumerate(pair):
                    at = pl.ds((2 * e + c) * BLOCK, BLOCK)
                    ends[at] = ref[pl.ds(skip + G * BLOCK, BLOCK)]
    return biases


def widen(biases):
    count = len(biases)
    lane = lax.broadcasted_iota(I32, (1, count * BLOCK), 1)
    bias = jnp.full((1, count * BLOCK), biases[-1], F32)
    for r in reversed(range(count - 1)):
        bias = jnp.where(lane < (r + 1) * BLOCK, biases[r], bias)
    return bias


def batches(span, heads, step):
    for first in range(*span, step):
        yield [(i, h) for i in range(first, min(span[1], first + step)) for h in range(heads)]


def rows_of(i):
    return pl.ds(i * BLOCK, BLOCK)


def picked_of(i):
    return pl.ds(i * R * BLOCK, R * BLOCK)


def cols_of(h):
    return pl.ds(h * DH, DH)


def dot_t(a, b):
    return lax.dot_general(a, b, (((1,), (1,)), ((), ())), preferred_element_type=F32)


def eye():
    shape = (BLOCK, BLOCK)
    return lax.broadcasted_iota(I32, shape, 0) == lax.broadcasted_iota(I32, shape, 1)


def flatten(columns, diagonal):
    return [jnp.sum(jnp.where(diagonal, x, 0.0), axis=0, keepdims=True) for x in columns]


def attend(queries, sets):
    scale = 1.0 / math.sqrt(DH)
    s = [
        [dot_t(q, ks) * scale + bias if bias is not None else dot_t(q, ks) * scale
         for ks, vs, bias in group]
        for q, group in zip(queries, sets)
    ]
    top = [[jnp.max(x, axis=1, keepdims=True) for x in group] for group in s]
    top = [functools.reduce(jnp.maximum, group) for group in top]
    w = [[jnp.exp(x - t) for x in group] for group, t in zip(s, top)]
    total = [sum(jnp.sum(x, axis=1, keepdims=True) for x in group) for group in w]
    part = [
        sum(
            jnp.dot(x.astype(BF16), vs, preferred_element_type=F32)
            for x, (ks, vs, bias) in zip(ws, group)
        )
        for ws, group in zip(w, sets)
    ]
    return part, top, total


def far_kernel(n, cap, per, heads, span, arrive_ref, place_ref, q_ref, *refs):
    half, plane = n // 2, n // 4
    first, second = refs[:plane], (refs[plane:half], refs[half : half + plane])
    out_ref, held, keys, vals, glob, ends, stat, pieces = refs[half + plane + 1 :]
    me = lax.axis_index("seq")
    d = lax.bitwise_xor(me, half)
    diagonal = eye()
    stat[...] = jnp.zeros_like(stat)
    size = cap * BLOCK
    sources = [((ref, 0), (ref, size)) for ref in first]
    sources += [((x, 0), (y, 0)) for x, y in zip(*second)]
    biases = choose(n, cap, per, span, arrive_ref, d, sources, held, keys, vals)
    glob_bias = widen(shared_blocks(n, per, place_ref, *second, size, glob, ends))
    inside = lax.bitwise_and(me, half - 1)
    end_bias = [jnp.where(inside == x, 0.0, NONE) for x in (0, half - 1)]
    low, high = span
    count = high - low
    for pairs in batches(span, heads, 3):
        sets = []
        for i, h in pairs:
            cols = cols_of(h)
            group = [
                (keys[picked_of(i), cols], vals[picked_of(i), cols], widen(biases[i])),
                (glob[: G * BLOCK, cols], glob[G * BLOCK :, cols], glob_bias),
            ]
            for e, edge in enumerate((0, per - 1)):
                if i == edge:
                    at = e * 2 * BLOCK
                    group.append(
                        (ends[at : at + BLOCK, cols], ends[at + BLOCK : at + 2 * BLOCK, cols],
                         end_bias[e])
                    )
            sets.append(group)
        part, top, total = attend([q_ref[rows_of(i), cols_of(h)] for i, h in pairs], sets)
        for x, t, (i, h) in zip(part, total, pairs):
            out_ref[rows_of(i - low), cols_of(h)] = (x / t).astype(BF16)
        for c, columns in enumerate((top, total)):
            for x, (i, h) in zip(flatten(columns, diagonal), pairs):
                stat[i - low : i - low + 1, pl.ds(h * DH + c * BLOCK, BLOCK)] = x
    rest = stat[...]
    pieces[...] = jnp.zeros_like(pieces)
    for p in range(PIECES):
        piece = rest.astype(BF16).astype(F32)
        rest = rest - piece
        pieces[p * count : (p + 1) * count] = piece[:count]
    out_ref[pl.ds(count * BLOCK, pieces.shape[0])] = pieces[...].astype(BF16)


def stat_rows(per):
    return -(-per // 8) * 8


def piece_rows(per):
    return -(-PIECES * per // 16) * 16


def scratches(n, cap, per, columns):
    return (
        [pltpu.VMEM((n // 2, 2 * cap * BLOCK, columns), BF16)]
        + [pltpu.VMEM((per * R * BLOCK, columns), BF16)] * 2
        + [pltpu.VMEM((2 * G * BLOCK, columns), BF16), pltpu.VMEM((4 * BLOCK, columns), BF16)]
    )


def far_part(n, cap, per, span, arrive, places, q, got, earlier):
    columns = q.shape[1]
    count = span[1] - span[0]
    heads = columns // DH
    return pl.pallas_call(
        functools.partial(far_kernel, n, cap, per, heads, span),
        out_shape=jax.ShapeDtypeStruct((count * BLOCK + piece_rows(count), columns), BF16),
        in_specs=[spec(SMEM)] * 2 + [spec()] * (1 + len(got)) + [spec(pl.ANY)],
        out_specs=spec(),
        scratch_shapes=scratches(n, cap, per, columns)
        + [pltpu.VMEM((stat_rows(count), columns), F32)]
        + [pltpu.VMEM((piece_rows(count), columns), F32)],
        compiler_params=params(16),
        cost_estimate=HEAVY,
        name="far_part",
    )(arrive, places, q, *got, earlier)


def store_part(heads, pairs, part, top, total, part_ref, stat_ref, diagonal):
    for x, (i, h) in zip(part, pairs):
        part_ref[rows_of(i), cols_of(h)] = x
    for c, columns in enumerate((top, total)):
        for x, (i, h) in zip(flatten(columns, diagonal), pairs):
            stat_ref[i : i + 1, pl.ds(h * DH + c * BLOCK, BLOCK)] = x


def near_kernel(n, cap, per, heads, place_ref, q_ref, k_ref, v_ref, *refs):
    half, plane = n // 2, n // 4
    second = refs[:plane], refs[plane:half]
    part_ref, stat_ref, glob, ends, keys, vals = refs[half + 1 :]
    me = lax.axis_index("seq")
    rows = per * BLOCK
    diagonal = eye()
    stat_ref[...] = jnp.zeros_like(stat_ref)
    size = cap * BLOCK
    glob_bias = widen(shared_blocks(n, per, place_ref, *second, size, glob, ends))
    keys[:BLOCK] = ends[:BLOCK]
    vals[:BLOCK] = ends[BLOCK : 2 * BLOCK]
    keys[pl.ds(BLOCK, rows)] = k_ref[...]
    vals[pl.ds(BLOCK, rows)] = v_ref[...]
    keys[pl.ds(BLOCK + rows, BLOCK)] = ends[2 * BLOCK : 3 * BLOCK]
    vals[pl.ds(BLOCK + rows, BLOCK)] = ends[3 * BLOCK :]
    inside = lax.bitwise_and(me, half - 1)
    first_bias, last_bias = [jnp.where(inside == x, NONE, 0.0) for x in (0, half - 1)]
    for pairs in batches((0, per), heads, 2):
        sets = []
        for i, h in pairs:
            window, cols = pl.ds(i * BLOCK, 3 * BLOCK), cols_of(h)
            bias = None
            if i in (0, per - 1):
                bias = widen([first_bias if i == 0 else 0.0, 0.0, last_bias if i else 0.0])
            sets.append(
                [
                    (keys[window, cols], vals[window, cols], bias),
                    (glob[: G * BLOCK, cols], glob[G * BLOCK :, cols], glob_bias),
                ]
            )
        parts = attend([q_ref[rows_of(i), cols_of(h)] for i, h in pairs], sets)
        store_part(heads, pairs, *parts, part_ref, stat_ref, diagonal)


def part_shapes(per, columns):
    return (
        jax.ShapeDtypeStruct((per * BLOCK, columns), F32),
        jax.ShapeDtypeStruct((stat_rows(per), columns), F32),
    )


def near_part(n, cap, per, places, q, k, v, shared, earlier):
    rows, columns = q.shape
    heads = columns // DH
    return pl.pallas_call(
        functools.partial(near_kernel, n, cap, per, heads),
        out_shape=part_shapes(per, columns),
        in_specs=[spec(SMEM)] + [spec()] * (3 + len(shared)) + [spec(pl.ANY)],
        out_specs=(spec(), spec()),
        scratch_shapes=scratches(n, cap, per, columns)[3:]
        + [pltpu.VMEM((rows + 2 * BLOCK, columns), BF16)] * 2,
        compiler_params=params(16),
        cost_estimate=LIGHT,
        name="near_part",
    )(places, q, k, v, *shared, earlier)


def rand_kernel(n, cap, per, heads, arrive_ref, q_ref, *refs):
    plane = n // 4
    part_ref, stat_ref, held, keys, vals = refs[plane:]
    diagonal = eye()
    stat_ref[...] = jnp.zeros_like(stat_ref)
    me = lax.axis_index("seq")
    size = cap * BLOCK
    sources = [
        ((ref, 2 * side * size), (ref, (2 * side + 1) * size))
        for side in range(2)
        for ref in refs[:plane]
    ]
    biases = choose(n, cap, per, (0, per), arrive_ref, me, sources, held, keys, vals)
    for pairs in batches((0, per), heads, 4):
        sets = [
            [(keys[picked_of(i), cols_of(h)], vals[picked_of(i), cols_of(h)], widen(biases[i]))]
            for i, h in pairs
        ]
        parts = attend([q_ref[rows_of(i), cols_of(h)] for i, h in pairs], sets)
        store_part(heads, pairs, *parts, part_ref, stat_ref, diagonal)


def rand_part(n, cap, per, arrive, q, got):
    columns = q.shape[1]
    return pl.pallas_call(
        functools.partial(rand_kernel, n, cap, per, columns // DH),
        out_shape=part_shapes(per, columns),
        in_specs=[spec(SMEM), spec()] + [spec()] * len(got),
        out_specs=(spec(), spec()),
        scratch_shapes=scratches(n, cap, per, columns)[:3],
        compiler_params=params(16),
        cost_estimate=HEAVY,
        name="rand_part",
    )(arrive, q, *got)


def context_kernel(
    span, heads, near_ref, near_stat_ref, rand_ref, rand_stat_ref, far_ref, out_ref, pieces
):
    low, high = span
    count = high - low
    pieces[...] = far_ref[pl.ds(count * BLOCK, pieces.shape[0])].astype(F32)
    far = sum(pieces[p * count : (p + 1) * count] for p in range(PIECES))
    stats = (near_stat_ref[low:high], rand_stat_ref[low:high], far)
    weights = []
    for h in range(heads):
        tops = [x[:, h * DH : h * DH + BLOCK] for x in stats]
        sums = [x[:, h * DH + BLOCK : (h + 1) * DH] for x in stats]
        top = functools.reduce(jnp.maximum, tops)
        w = [jnp.exp(x - top) for x in tops]
        total = sum(x * y for x, y in zip(w, sums))
        w[2] = w[2] * sums[2]
        weights.append([jnp.transpose(x / total) for x in w])
    for i in range(count):
        for h, ws in enumerate(weights):
            rows, here, cols = rows_of(low + i), rows_of(i), cols_of(h)
            parts = (near_ref[rows, cols], rand_ref[rows, cols], far_ref[here, cols].astype(F32))
            out_ref[here, cols] = sum(x * w[:, i : i + 1] for x, w in zip(parts, ws)).astype(BF16)


def contexts(span, near, near_stat, rand, rand_stat, far):
    columns = near.shape[1]
    count = span[1] - span[0]
    return pl.pallas_call(
        functools.partial(context_kernel, span, columns // DH),
        out_shape=jax.ShapeDtypeStruct((count * BLOCK, columns), BF16),
        in_specs=[spec()] * 5,
        out_specs=spec(),
        scratch_shapes=[pltpu.VMEM((piece_rows(count), columns), F32)],
        compiler_params=params(8),
        cost_estimate=LIGHT,
        name="contexts",
    )(near, near_stat, rand, rand_stat, far)


def project_kernel(span, count, steps, *refs):
    parts, w_ref, (out_ref, joined, product, sems) = refs[:count], refs[count], refs[-4:]
    me = lax.axis_index("head")
    columns = parts[0].shape[1]
    for step, rows_ref in enumerate(parts):
        owner = lax.rem(me + step, count)
        for h in range(count):
            @pl.when(owner == h)
            def _(h=h, rows_ref=rows_ref):
                joined[:, pl.ds(h * columns, columns)] = rows_ref[...]
    size = joined.shape[0] // steps
    copies = []
    for step in range(steps):
        rows = pl.ds(step * size, size)
        product[rows] = jnp.dot(
            joined[rows], w_ref[...], preferred_element_type=F32
        ).astype(BF16)
        target = out_ref.at[pl.ds(span[0] * BLOCK + step * size, size)]
        copies.append(pltpu.make_async_copy(product.at[rows], target, sems.at[step]))
        copies[-1].start()
    for copy in copies:
        copy.wait()


def project(span, tokens, parts, w_out, done=None):
    rows = parts[0].shape[0]
    wide = w_out.shape[1]
    steps = 2
    before = [] if done is None else [done]
    return pl.pallas_call(
        functools.partial(project_kernel, span, len(parts), steps),
        out_shape=jax.ShapeDtypeStruct((tokens, wide), BF16),
        in_specs=[spec()] * (len(parts) + 1) + [spec(pl.ANY)] * len(before),
        out_specs=spec(pl.ANY),
        scratch_shapes=[
            pltpu.VMEM((rows, w_out.shape[0]), BF16),
            pltpu.VMEM((rows, wide), BF16),
            pltpu.SemaphoreType.DMA((steps,)),
        ],
        input_output_aliases={len(parts) + 1: 0} if before else {},
        compiler_params=params(16),
        cost_estimate=LIGHT,
        name="project",
    )(*parts, w_out, *before)


def on_device(queries, keys, values, rand_group, rand_offset, glob_blocks, w_out):
    tokens_dev = queries.shape[0]
    per = tokens_dev // BLOCK
    n = lax.axis_size("seq")
    heads = lax.axis_size("head")
    cap = max(2, (rand_group.shape[0] // n * R + n - 1) // n)

    mates = [(i, i ^ (n // 4)) for i in range(n)]
    partners = [(i, i ^ (n // 2)) for i in range(n)]
    mate_k = lax.ppermute(keys, "seq", mates)
    mate_v = lax.ppermute(values, "seq", mates)
    spots, arrive = ranks(n, per, cap, rand_group.T, rand_offset.T)
    rows = {(0, 0): keys, (0, 1): values}
    lists = ((0, True, (0, 1)),)
    first = exchange(gather(n, per, cap, lists, spots, rows), n)
    later_q = lax.optimization_barrier((queries, *first[1:4]))[0]
    far_q = lax.ppermute(later_q, "seq", partners)
    rows = {(0, 0): keys, (1, 0): mate_k}
    lists = ((1, True, (0,)),)
    second_k = exchange(gather(n, per, cap, lists, spots, rows, [glob_blocks], first[1:4]), n)
    rows = {(0, 1): values, (1, 1): mate_v}
    lists = ((1, True, (1,)),)
    sent = gather(n, per, cap, lists, spots, rows, [glob_blocks], second_k[1:2])
    second = second_k + exchange(sent, n)
    rows = {(0, 0): keys, (0, 1): values, (1, 0): mate_k, (1, 1): mate_v}
    lists = ((0, False, (0, 1)), (1, False, (0, 1)))
    third = gather(n, per, cap, lists, spots, rows, (), sent[:1])
    middle = (per + 1) // 2
    spans = ((0, middle), (middle, per))
    fars = []
    earlier = third[0]
    for span in spans:
        earlier = far_part(
            n, cap, per, span, arrive, glob_blocks, far_q, first + second, earlier
        )
        fars.append(lax.ppermute(earlier, "seq", partners))
    third = exchange(third, n)
    near, near_stat = near_part(n, cap, per, glob_blocks, queries, keys, values, second, earlier)
    rand, rand_stat = rand_part(n, cap, per, arrive, queries, third)
    out = None
    for span, far in zip(spans, fars):
        context = contexts(span, near, near_stat, rand, rand_stat, far)
        others = [
            lax.ppermute(context, "head", [((i + s) % heads, i) for i in range(heads)])
            for s in range(1, heads)
        ]
        out = project(span, tokens_dev, [context] + others, w_out, out)
    return out


def solution(mesh):
    return jax.shard_map(
        on_device,
        mesh=mesh,
        in_specs=(
            P("seq", "head"),
            P("seq", "head"),
            P("seq", "head"),
            P(),
            P(),
            P(),
            P(None, "head"),
        ),
        out_specs=P("seq", "head"),
        check_vma=False,
    )
```
